32 devices in a mesh: space: 16 (over z, y, x), chan: 2 (over core).
Axes of the slice: x: 2, y: 2, z: 4, core: 2. Of those that a mesh axis runs over, the one named last changes fastest.
Arguments:
- features: bfloat16 [128, 512, 128], P('space', None, 'chan'), may hold values from -6 to 6
- heights: int32 [128, 64], P('space'), may hold values from 0 to 8
- neighbours: int32 [16, 26], P('space'), may hold values from -1 to 15, as said below
- w_conv: bfloat16 [27, 128, 128], replicated, may hold values from -0.109375 to 0.109375
- w_down: bfloat16 [8, 128, 256], replicated, may hold values from -0.1875 to 0.1875
- cotangent: bfloat16 [16, 512, 256], P('space'), may hold values from -12 to 12
Outputs:
- coarse: bfloat16 [16, 512, 256], P('space', None, 'chan')
- grad_conv: float32 [27, 128, 128], P(None, 'chan')
- grad_down: float32 [8, 128, 256], P(None, None, 'chan')
- grad_features: bfloat16 [128, 512, 128], P('space', None, 'chan')
The draws below stay inside these ranges and needn't reach their ends.
Inputs may be any that keep to these rules, and one draw needn't show every extreme that they name: neighbours[s, k] is the block at offset d_k from block s (the 26 offsets of the finite set (-1,0,1)^3 without the anchor, lexicographic in (x, y, z)), or -1 where no block is there; if neighbours[s, k] = q then neighbours[q, 25 - k] = s; distinct offsets name distinct blocks; blocks lie on a strip two positions wide and two high and are numbered in order of x, then y, then z, so that every neighbour q of s has 1 <= |q - s| <= 7.
All inputs are finite; a program needn't handle non-finite values.
Results may differ from the reference program's by a relative error of at most 0.005.
Values may be sent and summed in bfloat16 or wider, within the bound.
No kernel may reach another device: no remote copies, remote signals or barrier semaphores. Data moves between devices by JAX's collectives and lax.ppermute only.
A program may use at most 320 MiB of HBM per device.

```python
import jax
import jax.numpy as jnp
from jax import lax

C = 128
CO = 256
BLOCKS = 16
BRICKS = 128
FOOTX = 8


def draw_neighbours(key, part):
    key = jax.random.fold_in(key, 11)
    total = 2 * BLOCKS
    places = jnp.arange(total, dtype=jnp.int32)
    noise = jax.random.randint(key, (total,), 0, 1 << 20, dtype=jnp.int32)
    scores = noise * total + places
    chosen = jnp.argsort(scores)[:BLOCKS].astype(jnp.int32)
    cells = jnp.sort(chosen).astype(jnp.int32)
    coord_x = places // 4
    coord_y = places // 2 % 2
    coord_z = places % 2
    table = jnp.full((total,), -1, jnp.int32).at[cells].set(jnp.arange(BLOCKS, dtype=jnp.int32))
    result = []
    for along_x in (-1, 0, 1):
        for along_y in (-1, 0, 1):
            for along_z in (-1, 0, 1):
                if (along_x, along_y, along_z) != (0, 0, 0):
                    next_x = coord_x[cells] + along_x
                    next_y = coord_y[cells] + along_y
                    next_z = coord_z[cells] + along_z
                    inside = (next_x >= 0) & (next_x < FOOTX) & (next_y >= 0) & (next_y < 2) & (next_z >= 0) & (next_z < 2)
                    place = (jnp.clip(next_x, 0, FOOTX - 1) * 2 + jnp.clip(next_y, 0, 1)) * 2 + jnp.clip(next_z, 0, 1)
                    result.append(jnp.where(inside, table[place], -1))
    return jnp.stack(result, axis=1).astype(jnp.int32)


def plant(array, rng, least, high):
    index_at = [jax.random.randint(jax.random.fold_in(rng, axis), (), 0, length) for axis, length in enumerate(array.shape)]
    widest = array.shape.index(max(array.shape))
    beside = index_at[:widest] + [(index_at[widest] + 1) % array.shape[widest]] + index_at[widest + 1:]
    return array.at[tuple(index_at)].set(least).at[tuple(beside)].set(high)


def level_of(stream_key, shape, pieces, low, high):
    def one(axis_at, parts):
        draws = jax.random.uniform(jax.random.fold_in(jax.random.fold_in(stream_key, 6), axis_at), (parts,), jnp.float32, low / len(pieces), high / len(pieces))
        return jnp.repeat(jnp.exp(draws), shape[axis_at] // parts).reshape((-1,) + (1,) * (len(shape) - axis_at - 1))

    gain = one(*pieces[0])
    for cut in pieces[1:]:
        gain = gain * one(*cut)
    return gain


def normal_values(rng, extent, width, reach, cuts=(), held_as=jnp.bfloat16):
    values = width * jax.random.normal(rng, extent, jnp.float32)
    if cuts:
        values = values * level_of(rng, extent, cuts, -0.22, 0.18)
    return jnp.clip(values, -reach, reach).astype(held_as)


def setup_inputs(seed: int = 0) -> dict:
    splits = jax.random.split(jax.random.key(seed), 7)
    features = normal_values(splits[0], (BRICKS, 512, C), 1.0, 6.0, ((0, 16), (2, 2)))
    heights = plant(jax.random.randint(splits[1], (BRICKS, 64), 0, 9), jax.random.fold_in(splits[1], 1), 0, 8).astype(jnp.int32)
    neighbours = draw_neighbours(jax.random.fold_in(splits[6], 71), 0)
    w_conv = normal_values(splits[3], (27, C, C), (27 * C) ** -0.5, 0.109375)
    w_down = normal_values(splits[4], (8, C, CO), (8 * C) ** -0.5, 0.1875)
    cotangent = normal_values(splits[5], (BLOCKS, 512, CO), 2.0, 12.0, ((0, 16),))
    return {"features": features, "heights": heights, "neighbours": neighbours, "w_conv": w_conv, "w_down": w_down, "cotangent": cotangent}


OFFSETS = [(along_x, along_y, along_z) for along_x in (-1, 0, 1) for along_y in (-1, 0, 1) for along_z in (-1, 0, 1)]
DIRECTIONS = [offset for offset in OFFSETS if offset != (0, 0, 0)]


def blocks_of(bricks):
    count_blocks = bricks.shape[0] // 8
    channels = bricks.shape[-1]
    shaped = bricks.reshape(count_blocks, 2, 2, 2, 8, 8, 8, channels)
    return shaped.transpose(0, 3, 4, 2, 5, 1, 6, 7).reshape(count_blocks, 16, 16, 16, channels)


def bricks_of(volumes):
    count_blocks = volumes.shape[0]
    channels = volumes.shape[-1]
    shaped = volumes.reshape(count_blocks, 2, 8, 2, 8, 2, 8, channels)
    return shaped.transpose(0, 5, 3, 1, 2, 4, 6, 7).reshape(count_blocks * 8, 512, channels)


def pad_all(volumes, neighbours):
    padded = jnp.pad(volumes, ((0, 0), (1, 1), (1, 1), (1, 1), (0, 0)))
    for number, offset in enumerate(DIRECTIONS):
        source = tuple(slice(0, 1) if step_one == 1 else slice(15, 16) if step_one == -1 else slice(0, 16) for step_one in offset)
        target = tuple(slice(17, 18) if step_one == 1 else slice(0, 1) if step_one == -1 else slice(1, 17) for step_one in offset)
        other = neighbours[:, number]
        window = volumes[jnp.maximum(other, 0).astype(jnp.int32)][(slice(None),) + source]
        window = window * (other >= 0).astype(volumes.dtype)[:, None, None, None, None]
        padded = padded.at[(slice(None),) + target].set(window)
    return padded


def conv_block(padded, weights, sign):
    inputs = padded.shape[-1]
    summed = jnp.zeros((4096, weights.shape[-1]), jnp.float32)
    for number, (along_x, along_y, along_z) in enumerate(OFFSETS):
        window = padded[1 + sign * along_x:17 + sign * along_x, 1 + sign * along_y:17 + sign * along_y, 1 + sign * along_z:17 + sign * along_z]
        summed = summed + jnp.dot(window.reshape(4096, inputs), weights[number], preferred_element_type=jnp.float32)
    return summed


def tap_sums(padded, grad_rows):
    inputs = padded.shape[-1]
    result = []
    for along_x, along_y, along_z in OFFSETS:
        window = padded[1 + along_x:17 + along_x, 1 + along_y:17 + along_y, 1 + along_z:17 + along_z]
        result.append(jnp.dot(window.reshape(4096, inputs).T, grad_rows, preferred_element_type=jnp.float32))
    return jnp.stack(result)


def reference(features, heights, neighbours, w_conv, w_down, cotangent):
    levels = jnp.arange(8, dtype=jnp.int32)
    active = (levels[None, None, :] < heights[:, :, None]).astype(jnp.bfloat16).reshape(BRICKS, 512, 1)
    volumes = blocks_of(features * active)
    masks = blocks_of(active)
    padded = pad_all(volumes, neighbours)
    flat_down = w_down.reshape(8 * C, CO)

    def forward(carry, inputs):
        grad_conv, grad_down = carry
        pad_one, mask_one, upstream = inputs
        mask_rows = mask_one.reshape(4096, 1).astype(jnp.float32)
        pre = conv_block(pad_one, w_conv, 1) * mask_rows
        hidden = jax.nn.silu(pre).astype(jnp.bfloat16)
        patches = hidden.reshape(8, 2, 8, 2, 8, 2, C).transpose(0, 2, 4, 1, 3, 5, 6).reshape(512, 8 * C)
        coarse_one = jnp.dot(patches, flat_down, preferred_element_type=jnp.float32).astype(jnp.bfloat16)
        grad_down = grad_down + jnp.dot(patches.T, upstream, preferred_element_type=jnp.float32)
        grad_patches = jnp.dot(upstream, flat_down.T, preferred_element_type=jnp.float32)
        grad_hidden = grad_patches.reshape(8, 8, 8, 2, 2, 2, C).transpose(0, 3, 1, 4, 2, 5, 6).reshape(4096, C)
        sigmoid_pre = jax.nn.sigmoid(pre)
        grad_pre = (grad_hidden * sigmoid_pre * (1.0 + pre * (1.0 - sigmoid_pre)) * mask_rows).astype(jnp.bfloat16)
        grad_conv = grad_conv + tap_sums(pad_one, grad_pre)
        return (grad_conv, grad_down), (coarse_one, grad_pre.reshape(16, 16, 16, C))

    initial = (jnp.zeros((27, C, C), jnp.float32), jnp.zeros((8 * C, CO), jnp.float32))
    (grad_conv, grad_down), (coarse, grad_pre) = lax.scan(forward, initial, (padded, masks, cotangent))
    grad_padded = pad_all(grad_pre, neighbours)
    back_weights = w_conv.transpose(0, 2, 1)

    def backward(inputs):
        pad_one, mask_one = inputs
        rows = conv_block(pad_one, back_weights, -1) * mask_one.reshape(4096, 1).astype(jnp.float32)
        return rows.astype(jnp.bfloat16).reshape(16, 16, 16, C)

    grad_input = lax.map(backward, (grad_padded, masks))
    grad_features = bricks_of(grad_input)
    return coarse, grad_conv / BLOCKS, (grad_down / BLOCKS).reshape(8, C, CO), grad_features
```

```python
import jax
import jax.numpy as jnp
from jax import lax
from jax.sharding import PartitionSpec as P

OFFSETS = [
    (along_x, along_y, along_z)
    for along_x in (-1, 0, 1)
    for along_y in (-1, 0, 1)
    for along_z in (-1, 0, 1)
]
DIRECTIONS = [offset for offset in OFFSETS if offset != (0, 0, 0)]


def to_block(bricks):
    channels = bricks.shape[-1]
    shaped = bricks.reshape(2, 2, 2, 8, 8, 8, channels)
    return shaped.transpose(2, 3, 1, 4, 0, 5, 6).reshape(16, 16, 16, channels)


def from_block(volume):
    channels = volume.shape[-1]
    shaped = volume.reshape(2, 8, 2, 8, 2, 8, channels)
    return shaped.transpose(4, 2, 0, 1, 3, 5, 6).reshape(8, 512, channels)


def sender_slices(offset):
    return tuple(
        (
            slice(15, 16) if step_one == 1 else slice(0, 1) if step_one == -1 else slice(0, 16)
            for step_one in offset
        )
    )


def target_slices(offset):
    return tuple(
        (
            slice(17, 18) if step_one == 1 else slice(0, 1) if step_one == -1 else slice(1, 17)
            for step_one in offset
        )
    )


def groups_of(devices, start):
    return [[(start + 8 * g + i) % devices for i in range(8)] for g in range(devices // 8)]


def exchange(volume, neighbour_row, own):
    devices = lax.axis_size("space")
    stacked = region_stack(volume)
    numbers = jnp.arange(26, dtype=jnp.int32) + 1

    def chosen_for(targets):
        hit = (neighbour_row[None, :] == targets[:, None]).astype(jnp.int32)
        chosen = jnp.sum(hit * numbers[None, :], axis=1) - 1
        return jnp.where(chosen < 0, 26, chosen)

    faces = []
    for start in (0, 4):
        group = (own - start + devices) % devices // 8
        targets = (start + 8 * group + jnp.arange(8, dtype=jnp.int32)) % devices
        sent = jnp.take(stacked, chosen_for(targets), axis=0)
        faces.append(
            lax.all_to_all(
                sent, "space", 0, 0, axis_index_groups=groups_of(devices, start), tiled=True
            )
        )
    everyone = jnp.arange(devices, dtype=jnp.int32)
    edges = lax.all_to_all(
        jnp.take(stacked[:, :16], chosen_for(everyone), axis=0), "space", 0, 0, tiled=True
    )
    return faces[0], faces[1], edges


def region_stack(volume):
    channels = volume.shape[-1]
    regions = []
    for offset in DIRECTIONS:
        region = volume[sender_slices(offset)].reshape(-1, channels)
        regions.append(jnp.pad(region, ((0, 256 - region.shape[0]), (0, 0))))
    regions.append(jnp.zeros((256, channels), volume.dtype))
    return jnp.stack(regions)


def assemble(volume, received, neighbour_row, own):
    channels = volume.shape[-1]
    devices = lax.axis_size("space")
    padded = jnp.pad(volume, ((1, 1), (1, 1), (1, 1), (0, 0)))
    present = (neighbour_row >= 0).astype(volume.dtype)
    other = jnp.maximum(neighbour_row, 0)
    same = own // 8 == other // 8
    first, second, edges = received
    slot_one = other % 8
    slot_two = (other + devices - 4) % devices % 8
    joined = jnp.concatenate([first, second])
    slot = jnp.where(same, slot_one, 8 + slot_two)
    for number, offset in enumerate(DIRECTIONS):
        slices = target_slices(offset)
        extent = tuple((1 if step_one != 0 else 16 for step_one in offset))
        voxel_count = extent[0] * extent[1] * extent[2]
        if voxel_count == 256:
            piece = lax.dynamic_index_in_dim(joined, slot[number], 0, keepdims=False)
        else:
            piece = lax.dynamic_index_in_dim(edges, other[number], 0, keepdims=False)
        piece = piece[:voxel_count] * present[number]
        padded = padded.at[slices].set(piece.reshape(extent + (channels,)))
    return padded


def sum_over_blocks(parts):
    devices = lax.axis_size("space")
    rows = jnp.concatenate([part.reshape(-1, 128) for part in parts]).astype(jnp.bfloat16)
    count = rows.shape[0]
    share = -(-count // devices)
    rows = jnp.pad(rows, ((0, share * devices - count), (0, 0)))
    terms = lax.all_to_all(rows.reshape(devices, share, 128), "space", 0, 0, tiled=True)
    own_sum = jnp.sum(terms.astype(jnp.float32), axis=0) / devices
    whole = lax.all_gather(own_sum.astype(jnp.bfloat16), "space", axis=0, tiled=True)
    result = []
    at = 0
    for part in parts:
        height = part.size // 128
        result.append(whole[at : at + height].astype(jnp.float32).reshape(part.shape))
        at += height
    return result


def tap_columns(padded, half_start, along_x, sign):
    inputs = padded.shape[-1]
    start_x = half_start + 1 + sign * along_x
    columns = []
    for along_y in (-1, 0, 1):
        for along_z in (-1, 0, 1):
            window = padded[
                start_x : start_x + 8,
                1 + sign * along_y : 17 + sign * along_y,
                1 + sign * along_z : 17 + sign * along_z,
            ]
            columns.append(window.reshape(2048, inputs))
    return jnp.concatenate(columns, axis=1)


def conv_taps(padded, weights, sign):
    inputs = padded.shape[-1]
    outputs = weights.shape[-1]
    halves = []
    for half_start in (0, 8):
        summed = jnp.zeros((2048, outputs), jnp.float32)
        for along_x in (-1, 0, 1):
            gathered = tap_columns(padded, half_start, along_x, sign)
            tap_start = (along_x + 1) * 9
            summed = summed + jnp.dot(
                gathered,
                weights[tap_start : tap_start + 9].reshape(9 * inputs, outputs),
                preferred_element_type=jnp.float32,
            )
        halves.append(summed)
    return jnp.concatenate(halves, axis=0)


def tap_gradient(padded, grad_rows):
    inputs = padded.shape[-1]
    result = []
    for along_x in (-1, 0, 1):
        summed = jnp.zeros((9 * inputs, grad_rows.shape[-1]), jnp.float32)
        for half_start in (0, 8):
            gathered = tap_columns(padded, half_start, along_x, 1)
            rows_part = grad_rows[half_start * 256 : half_start * 256 + 2048]
            summed = summed + lax.dot_general(
                gathered, rows_part, (((0,), (0,)), ((), ())), preferred_element_type=jnp.float32
            )
        result.append(summed.reshape(9, inputs, -1))
    return jnp.concatenate(result, axis=0)


def local(features, heights, neighbours, w_conv, w_down, cotangent):
    groups = lax.axis_size("chan")
    member = lax.axis_index("chan")
    own_block = lax.axis_index("space")
    channels = w_conv.shape[1]
    own_in = features.shape[-1]
    out_all = w_down.shape[-1]
    own_out = out_all // groups
    neighbour_row = neighbours[0]
    levels = jnp.arange(8, dtype=jnp.int32)
    active_bricks = (
        (levels[None, None, :] < heights[:, :, None]).astype(jnp.bfloat16).reshape(8, 512, 1)
    )
    active = to_block(active_bricks).reshape(4096, 1).astype(jnp.float32)
    volume = to_block(features * active_bricks)
    received = exchange(volume, neighbour_row, own_block)
    padded = assemble(volume, received, neighbour_row, own_block)
    conv_rows = lax.dynamic_slice_in_dim(w_conv, member * own_in, own_in, 1)
    partial_pre = conv_taps(padded, conv_rows, 1)
    pre = lax.psum(partial_pre, "chan") * active
    hidden = jax.nn.silu(pre).astype(jnp.bfloat16)
    patches = (
        hidden.reshape(8, 2, 8, 2, 8, 2, channels)
        .transpose(0, 2, 4, 1, 3, 5, 6)
        .reshape(512, 8 * channels)
    )
    down_flat = w_down.reshape(8 * channels, out_all)
    down_own = lax.dynamic_slice_in_dim(down_flat, member * own_out, own_out, 1)
    coarse = jnp.dot(patches, down_own, preferred_element_type=jnp.float32).astype(jnp.bfloat16)
    upstream = cotangent[0]
    upstream_own = lax.dynamic_slice_in_dim(upstream, member * own_out, own_out, 1)
    grad_down_part = lax.dot_general(
        patches, upstream_own, (((0,), (0,)), ((), ())), preferred_element_type=jnp.float32
    ).reshape(8, channels, own_out)
    grad_patches = lax.dot_general(
        upstream, down_flat, (((1,), (1,)), ((), ())), preferred_element_type=jnp.float32
    )
    grad_hidden = (
        grad_patches.reshape(8, 8, 8, 2, 2, 2, channels)
        .transpose(0, 3, 1, 4, 2, 5, 6)
        .reshape(4096, channels)
    )
    sigmoid_pre = jax.nn.sigmoid(pre)
    grad_pre = (grad_hidden * sigmoid_pre * (1.0 + pre * (1.0 - sigmoid_pre)) * active).astype(
        jnp.bfloat16
    )
    grad_conv_part = tap_gradient(padded, grad_pre)
    grad_conv, grad_down = sum_over_blocks([grad_conv_part, grad_down_part])
    grad_volume = grad_pre.reshape(16, 16, 16, channels)
    arriving = exchange(grad_volume, neighbour_row, own_block)
    grad_padded = assemble(grad_volume, arriving, neighbour_row, own_block)
    back_weights = conv_rows.transpose(0, 2, 1)
    grad_input = conv_taps(grad_padded, back_weights, -1)
    grad_features = from_block(
        (grad_input * active).astype(jnp.bfloat16).reshape(16, 16, 16, own_in)
    )
    return (coarse[None], grad_conv, grad_down, grad_features)


def solution(mesh):
    placed = (
        P("space", None, "chan"),
        P("space", None),
        P("space", None),
        P(),
        P(),
        P("space", None, None),
    )
    return jax.shard_map(
        local,
        mesh=mesh,
        in_specs=placed,
        out_specs=(
            P("space", None, "chan"),
            P(None, "chan", None),
            P(None, None, "chan"),
            P("space", None, "chan"),
        ),
        check_vma=False,
    )
```

```python
import functools

import jax
import jax.numpy as jnp
from jax import lax
from jax.experimental import pallas as pl
from jax.experimental.pallas import tpu as pltpu
from jax.sharding import PartitionSpec as P

OFFSETS = [
    (along_x, along_y, along_z)
    for along_x in (-1, 0, 1)
    for along_y in (-1, 0, 1)
    for along_z in (-1, 0, 1)
]
DIRECTIONS = [offset for offset in OFFSETS if offset != (0, 0, 0)]
FILL_ORDER = sorted(range(26), key=lambda k: (abs(DIRECTIONS[k][2]), k))
BIG = 48 * 1024 * 1024
F32 = jnp.float32
BF16 = jnp.bfloat16


def vmem():
    return pl.BlockSpec(memory_space=pltpu.VMEM)


def smem():
    return pl.BlockSpec(memory_space=pltpu.SMEM)


def kernel_call(body, outs, specs, scratch=(), flops=0, moved=1 << 22):
    return pl.pallas_call(
        body,
        out_shape=outs,
        in_specs=specs,
        out_specs=jax.tree.map(lambda _: vmem(), outs),
        scratch_shapes=list(scratch),
        compiler_params=pltpu.CompilerParams(vmem_limit_bytes=BIG),
        cost_estimate=pl.CostEstimate(flops=flops, bytes_accessed=moved, transcendentals=0),
    )


def swap_halves(rows):
    return pltpu.roll(rows, 64, 1)


def low_lanes(rows):
    return lax.broadcasted_iota(jnp.int32, rows.shape, 1) < 64


def filled_voxels(heights_ref):
    columns = lax.broadcasted_iota(jnp.int32, (64, 512), 0)
    voxels = lax.broadcasted_iota(jnp.int32, (64, 512), 1)
    spread = (voxels // 8 == columns).astype(F32)
    tall = jnp.dot(heights_ref[...].astype(F32), spread, preferred_element_type=F32)
    level = lax.broadcasted_iota(jnp.int32, tall.shape, 1) % 8
    return (level.astype(F32) < tall).astype(F32)


def fill_slots(rows_ref, near_ref, slots_ref):
    for k, (dx, dy, dz) in enumerate(DIRECTIONS):
        block = near_ref[0, k]
        xh = 7 if dx == 1 else 0
        y = 15 if dy == 1 else 0
        z = 15 if dz == 1 else 0

        @pl.when(block >= 0)
        def _(dx=dx, dy=dy, dz=dz, xh=xh, y=y, z=z, block=block):
            zeros = [d == 0 for d in (dx, dy, dz)]
            if zeros == [False, True, True]:
                plane = rows_ref[xh * 256 : xh * 256 + 256, :]
                first, second = plane[:128], plane[128:]
                if dx == -1:
                    second = swap_halves(second)
                else:
                    first = swap_halves(first)
                region = jnp.where(low_lanes(first), first, second)
            elif zeros == [True, False, True]:
                region = jnp.concatenate(
                    [rows_ref[x * 256 + y * 16 : x * 256 + y * 16 + 16, :] for x in range(8)]
                )
            elif zeros == [True, True, False]:
                region = rows_ref[pl.ds(z, 128, stride=16), :]
            elif zeros == [False, False, True]:
                region = rows_ref[xh * 256 + y * 16 : xh * 256 + y * 16 + 16, :]
            elif zeros == [False, True, False]:
                region = rows_ref[pl.ds(xh * 256 + z, 16, stride=16), :]
            elif zeros == [True, False, False]:
                line = rows_ref[pl.ds(y * 16 + z, 8, stride=256), :]
                region = jnp.concatenate([line, line])
            else:
                at = xh * 256 + y * 16 + z
                region = jnp.broadcast_to(rows_ref[at : at + 1, :], (16, 128))
            slots_ref[block, 0 : region.shape[0], :] = region.astype(BF16)


def put_lines(padded_ref, places, rows):
    count = rows.shape[0]
    level = lax.broadcasted_iota(jnp.int32, rows.shape, 0) % 16
    below = jnp.where(level == 0, 0.0, pltpu.roll(rows, 1, 0)).astype(BF16)
    above = jnp.where(level == 15, 0.0, pltpu.roll(rows, count - 1, 0)).astype(BF16)
    here = rows.astype(BF16)
    at = 0
    for x, row, height in places:
        for j, part in enumerate((below, here, above)):
            padded_ref[x, row : row + height, j * 128 : j * 128 + 128] = part[at : at + height]
        at += height


def put_ends(padded_ref, x, row, rows, dz):
    lines = rows.shape[0]
    j = 0 if dz == -1 else 2
    end = 0 if dz == -1 else 15
    lanes = slice(j * 128, j * 128 + 128)
    old = padded_ref[x, row : row + 16 * lines, lanes].astype(F32).reshape(lines, 16, 128)
    level = lax.broadcasted_iota(jnp.int32, old.shape, 1)
    new = jnp.where(level == end, rows.reshape(lines, 1, 128), old)
    padded_ref[x, row : row + 16 * lines, lanes] = new.reshape(16 * lines, 128).astype(BF16)


def clear_margin(padded_ref):
    empty = jnp.zeros((288, 384), BF16)
    padded_ref[0] = empty
    padded_ref[17] = empty
    line = jnp.zeros((16, 384), BF16)
    for x in range(1, 17):
        padded_ref[x, 0:16, :] = line
        padded_ref[x, 272:288, :] = line


def fill_margin(padded_ref, near_ref, own_ref, other_ref):
    for k in FILL_ORDER:
        dx, dy, dz = DIRECTIONS[k]
        block = near_ref[0, k]
        x = 17 if dx == 1 else 0
        y = 17 if dy == 1 else 0

        @pl.when(block >= 0)
        def _(dx=dx, dy=dy, dz=dz, x=x, y=y, block=block):
            zeros = [d == 0 for d in (dx, dy, dz)]
            height = 128 if zeros.count(True) == 2 else 16
            own = own_ref[block, 0:height, :].astype(F32)
            other = other_ref[block, 0:height, :].astype(F32)

            def first():
                return jnp.where(low_lanes(own), own, swap_halves(other))

            def second():
                return jnp.where(low_lanes(own), swap_halves(own), other)

            if zeros == [False, True, True]:
                put_lines(padded_ref, [(x, 16, 256)], jnp.concatenate([first(), second()]))
            elif zeros == [True, False, True]:
                places = [(at + 1, y * 16, 16) for at in range(16)]
                put_lines(padded_ref, places, jnp.concatenate([first(), second()]))
            elif zeros == [False, False, True]:
                put_lines(padded_ref, [(x, y * 16, 16)], first() if dx == 1 else second())
            elif zeros == [True, True, False]:
                for half, rows in enumerate((first(), second())):
                    for at in range(8):
                        put_ends(
                            padded_ref, half * 8 + at + 1, 16, rows[at * 16 : at * 16 + 16], dz
                        )
            elif zeros == [False, True, False]:
                put_ends(padded_ref, x, 16, first() if dx == 1 else second(), dz)
            elif zeros == [True, False, False]:
                for half, rows in enumerate((first(), second())):
                    for at in range(8):
                        put_ends(
                            padded_ref, half * 8 + at + 1, y * 16, rows[at : at + 1], dz
                        )
            else:
                rows = first() if dx == 1 else second()
                put_ends(padded_ref, x, y * 16, rows[0:1], dz)


def send_features(near_ref, heights_ref, features_ref, slots_ref, rows_ref):
    filled = filled_voxels(heights_ref)
    for oy in range(2):
        for oz in range(2):
            pair = []
            for ox in range(2):
                brick = ox + 2 * oy + 4 * oz
                pair.append(features_ref[brick].astype(F32) * filled[brick : brick + 1])
            turned = jnp.concatenate(pair).T
            for vx in range(8):
                for vy in range(8):
                    at = vx * 256 + (8 * oy + vy) * 16 + 8 * oz
                    source = (vx * 8 + vy) * 8
                    rows_ref[at : at + 8, :] = turned[source : source + 8]
    fill_slots(rows_ref, near_ref, slots_ref)


def lay_out(
    heights_ref, own_ref, other_ref, cot_ref, down_ref,
    padded_ref, active_ref, slope_ref, rows_ref, mask_ref
):
    filled = filled_voxels(heights_ref)
    upright = filled.T
    for brick in range(8):
        ox, oy, oz = brick % 2, brick // 2 % 2, brick // 4
        both = jnp.concatenate([own_ref[brick].astype(F32), other_ref[brick].astype(F32)])
        turned = (both * filled[brick : brick + 1]).T
        mask = jnp.broadcast_to(upright[:, brick : brick + 1], (512, 128))
        for vx in range(8):
            for vy in range(8):
                at = (8 * ox + vx) * 256 + (8 * oy + vy) * 16 + 8 * oz
                source = (vx * 8 + vy) * 8
                rows_ref[at : at + 8, :] = turned[source : source + 8]
                mask_ref[at : at + 8, :] = mask[source : source + 8]
    clear_margin(padded_ref)
    for x in range(16):
        put_lines(padded_ref, [(x + 1, 16, 256)], rows_ref[x * 256 : x * 256 + 256, :])
        active_ref[x * 256 : x * 256 + 256, :] = mask_ref[x * 256 : x * 256 + 256, :].astype(BF16)
    for tap in range(8):
        tx, ty, tz = tap // 4, tap // 2 % 2, tap % 2
        part = lax.dot_general(
            cot_ref[...],
            down_ref[tap * 128 : tap * 128 + 128, :],
            (((1,), (1,)), ((), ())),
            preferred_element_type=F32,
        )
        for ux in range(8):
            for uy in range(8):
                at = (2 * ux + tx) * 256 + (2 * uy + ty) * 16 + tz
                source = (ux * 8 + uy) * 8
                slope_ref[pl.ds(at, 8, stride=2), :] = part[source : source + 8]


def forward(
    near_ref, laid_ref, own_ref, other_ref, active_ref, slope_ref, conv_ref, down_ref, cot_ref,
    padded_ref, coarse_ref, grad_down_ref, grad_pre_ref, slots_ref,
    hidden_ref, grad_ref, packed_ref
):
    padded_ref[...] = laid_ref[...]
    fill_margin(padded_ref, near_ref, own_ref, other_ref)

    def step(group, carry):
        lhs = []
        for pair in range(2):
            pieces = []
            for p in range(4):
                for ey in range(3):
                    pieces.append(
                        padded_ref[group * 4 + pair * 2 + p, ey * 16 : ey * 16 + 256, :]
                    )
            lhs.append(jnp.concatenate(pieces, axis=1))
        summed = jnp.dot(jnp.concatenate(lhs), conv_ref[...], preferred_element_type=F32)
        for pair in range(2):
            for phase in range(2):
                at = pl.multiple_of((group * 4 + pair * 2 + phase) * 256, 256)
                rows = pl.ds(at, 256)
                pre = summed[pair * 256 : pair * 256 + 256, phase * 128 : phase * 128 + 128]
                active = active_ref[rows, :].astype(F32)
                pre = pre * active
                sigmoid = 1.0 / (1.0 + jnp.exp(-pre))
                hidden_ref[rows, :] = pre * sigmoid
                grad = slope_ref[rows, :] * sigmoid * (1.0 + pre * (1.0 - sigmoid)) * active
                grad_ref[rows, :] = grad
                grad_pre_ref[rows, :] = grad.astype(BF16)
        return carry

    lax.fori_loop(0, 4, step, 0)

    for x in range(8):
        low = grad_ref[x * 256 : x * 256 + 256, :]
        high = grad_ref[2048 + x * 256 : 2048 + x * 256 + 256, :]
        packed_ref[x * 256 : x * 256 + 256, :] = jnp.where(
            low_lanes(low), low, swap_halves(high)
        )
    fill_slots(packed_ref, near_ref, slots_ref)

    patches = []
    for tap in range(8):
        tx, ty, tz = tap // 4, tap // 2 % 2, tap % 2
        pieces = []
        for ux in range(8):
            for uy in range(8):
                at = (2 * ux + tx) * 256 + (2 * uy + ty) * 16 + tz
                pieces.append(hidden_ref[pl.ds(at, 8, stride=2), :])
        patches.append(jnp.concatenate(pieces).astype(BF16))
    patches = jnp.concatenate(patches, axis=1)
    coarse = jnp.dot(patches, down_ref[...], preferred_element_type=F32)
    coarse_ref[...] = coarse[:, :128].astype(BF16)
    own_cot = cot_ref[:, 0:128].astype(F32).T.astype(BF16)
    grad_down = jnp.dot(own_cot, patches, preferred_element_type=F32)
    for tap in range(8):
        part = grad_down[:, tap * 128 : tap * 128 + 128].T
        grad_down_ref[tap * 128 : tap * 128 + 128, :] = part.astype(BF16)


def conv_gradient(padded_ref, grad_pre_ref, out_ref, own_ref, turned_ref):
    turned_ref[:, 0:512] = jnp.zeros((128, 512), BF16)
    turned_ref[:, 4608:5120] = jnp.zeros((128, 512), BF16)
    for x in range(16):
        plane = grad_pre_ref[x * 256 : x * 256 + 256, :].astype(F32)
        turned_ref[:, 512 + x * 256 : 768 + x * 256] = plane.T.astype(BF16)
    for x in range(18):
        below = padded_ref[x, :, 0:128].astype(F32)
        here = padded_ref[x, :, 128:256].astype(F32)
        both = jnp.where(low_lanes(below), below, swap_halves(here))
        own_ref[x, :, 0:128] = both.astype(BF16)
        own_ref[x, :, 128:256] = padded_ref[x, :, 256:384]
    lhs = jnp.concatenate(
        [turned_ref[:, (2 - ex) * 256 : (2 - ex) * 256 + 4608] for ex in range(3)]
    )
    for ey in range(3):
        rhs = own_ref[:, ey * 16 : ey * 16 + 256, :].reshape(4608, 256)
        summed = jnp.dot(lhs, rhs, preferred_element_type=F32)
        for ex in range(3):
            part = summed[ex * 128 : ex * 128 + 128].T
            at = (ex * 3 + ey) * 192
            out_ref[at : at + 192, :] = part[0:192].astype(BF16)


def backward(
    near_ref, grad_pre_ref, own_ref, other_ref, active_ref, back_ref, out_ref, padded_ref
):
    clear_margin(padded_ref)
    for x in range(16):
        rows = grad_pre_ref[x * 256 : x * 256 + 256, :].astype(F32)
        put_lines(padded_ref, [(x + 1, 16, 256)], rows)
    fill_margin(padded_ref, near_ref, own_ref, other_ref)
    for half in range(2):
        lhs = []
        for quad in range(2):
            pieces = []
            for p in range(6):
                for ey in range(3):
                    pieces.append(
                        padded_ref[half * 8 + quad * 4 + p, ey * 16 : ey * 16 + 256, :]
                    )
            lhs.append(jnp.concatenate(pieces, axis=1))
        summed = jnp.dot(jnp.concatenate(lhs), back_ref[...], preferred_element_type=F32)
        for quad in range(2):
            for two in range(2):
                part = summed[quad * 256 : quad * 256 + 256, two * 128 : two * 128 + 128]
                x = half * 8 + quad * 4 + two * 2
                even = active_ref[x * 256 : x * 256 + 256, :].astype(F32)
                odd = active_ref[x * 256 + 256 : x * 256 + 512, :].astype(F32)
                part = part * jnp.where(low_lanes(part), even, odd)
                for oy in range(2):
                    rows = [
                        part[(8 * oy + vy) * 16 + 8 * oz : (8 * oy + vy) * 16 + 8 * oz + 8]
                        for oz in range(2)
                        for vy in range(8)
                    ]
                    turned = jnp.concatenate(rows).T
                    first, second = turned[:64], turned[64:]
                    lanes = slice(x % 8 * 64, x % 8 * 64 + 128)
                    brick = half + 2 * oy
                    near = jnp.where(low_lanes(first), first, swap_halves(second))
                    far = jnp.where(low_lanes(first), swap_halves(first), second)
                    out_ref[brick, :, lanes] = near.astype(BF16)
                    out_ref[brick + 4, :, lanes] = far.astype(BF16)


def finish(member_ref, sums_ref, conv_ref, down_ref):
    shift = member_ref[0] * 64
    for tap in range(27):
        rows = sums_ref[tap * 64 : tap * 64 + 64, :].astype(F32)
        conv_ref[tap] = pltpu.roll(rows, shift, 1)
    for tap in range(8):
        rows = sums_ref[1728 + tap * 128 : 1728 + tap * 128 + 128, :].astype(F32)
        down_ref[tap, pl.ds(shift, 64), :] = rows[:64]
        down_ref[tap, pl.ds(64 - shift, 64), :] = rows[64:]


def over_chan(block):
    return lax.ppermute(block, "chan", [(0, 1), (1, 0)])


def to_all(slots):
    return lax.all_to_all(slots, "space", 0, 0, tiled=True)


def local(features, heights, neighbours, w_conv, w_down, cotangent):
    devices = lax.axis_size("space")
    member = lax.axis_index("chan")

    def own_first(whole, axis):
        half = whole.shape[axis] // 2
        return jnp.where(member == 0, whole, jnp.roll(whole, half, axis))

    def out(*shape, dtype=BF16):
        return jax.ShapeDtypeStruct(shape, dtype)

    turned = features.transpose(0, 2, 1)
    slots = kernel_call(
        send_features,
        out(devices, 128, 128),
        [smem(), vmem(), vmem()],
        [pltpu.VMEM((2048, 128), F32)],
    )(neighbours, heights, turned)
    came = to_all(slots)
    other_turned = over_chan(turned)

    conv = own_first(own_first(w_conv, 1), 2)
    down = own_first(own_first(w_down, 1), 2).reshape(1024, 256)
    cot = own_first(cotangent[0], 1)
    slabs = conv.reshape(3, 1152, 128)
    two_phase = jnp.concatenate(
        [jnp.pad(slabs, ((q, 1 - q), (0, 0), (0, 0))) for q in range(2)], axis=2
    ).reshape(4608, 256)
    back = conv[::-1, :64].transpose(0, 2, 1).reshape(3, 1152, 64)
    four_phase = jnp.concatenate(
        [jnp.pad(back, ((q, 3 - q), (0, 0), (0, 0))) for q in range(4)], axis=2
    ).reshape(6912, 256)

    laid, active, slope = kernel_call(
        lay_out,
        (out(18, 288, 384), out(4096, 128), out(4096, 128, dtype=F32)),
        [vmem()] * 5,
        [pltpu.VMEM((4096, 128), F32), pltpu.VMEM((4096, 128), F32)],
        flops=1 << 28,
    )(heights, turned, other_turned, cot, down)
    came_other = over_chan(came)

    padded, coarse, grad_down_part, grad_pre, grad_slots = kernel_call(
        forward,
        (
            out(18, 288, 384),
            out(512, 128),
            out(1024, 128),
            out(4096, 128),
            out(devices, 128, 128),
        ),
        [smem()] + [vmem()] * 8,
        [
            pltpu.VMEM((4096, 128), F32),
            pltpu.VMEM((4096, 128), F32),
            pltpu.VMEM((2048, 128), F32),
        ],
        flops=5 << 30,
    )(neighbours, laid, came, came_other, active, slope, two_phase, down, cot)
    grad_came = to_all(grad_slots)

    grad_conv_part = kernel_call(
        conv_gradient,
        out(1728, 128),
        [vmem()] * 2,
        [pltpu.VMEM((18, 288, 256), BF16), pltpu.VMEM((128, 5120), BF16)],
        flops=3 << 30,
    )(padded, grad_pre)

    terms = jnp.concatenate([grad_conv_part, grad_down_part])
    share = -(-2752 // (devices * 16)) * 16
    terms = jnp.pad(terms, ((0, share * devices - 2752), (0, 0)))
    arrived = to_all(terms.reshape(devices, share, 128))
    own_sum = (jnp.sum(arrived.astype(F32), axis=0) / devices).astype(BF16)
    sums = to_all(jnp.broadcast_to(own_sum[None], (devices, share, 128)))

    grad_came_other = over_chan(grad_came)
    grad_features = kernel_call(
        backward,
        out(8, 64, 512),
        [smem()] + [vmem()] * 5,
        [pltpu.VMEM((18, 288, 384), BF16)],
        flops=5 << 30,
    )(neighbours, grad_pre, grad_came, grad_came_other, active, four_phase)

    grad_conv, grad_down = kernel_call(
        finish,
        (out(27, 64, 128, dtype=F32), out(8, 128, 128, dtype=F32)),
        [smem(), vmem()],
    )(member.reshape(1), sums.reshape(-1, 128))
    return coarse[None], grad_conv, grad_down, grad_features.transpose(0, 2, 1)


def solution(mesh):
    placed = (
        P("space", None, "chan"),
        P("space", None),
        P("space", None),
        P(),
        P(),
        P("space", None, None),
    )
    return jax.shard_map(
        local,
        mesh=mesh,
        in_specs=placed,
        out_specs=(
            P("space", None, "chan"),
            P(None, "chan", None),
            P(None, None, "chan"),
            P("space", None, "chan"),
        ),
        check_vma=False,
    )
```

```python
import jax
import jax.numpy as jnp
from jax import lax
from jax.experimental import pallas as pl
from jax.experimental.pallas import tpu as pltpu
from jax.sharding import PartitionSpec as P

OFFSETS = [
    (along_x, along_y, along_z)
    for along_x in (-1, 0, 1)
    for along_y in (-1, 0, 1)
    for along_z in (-1, 0, 1)
]
DIRECTIONS = [offset for offset in OFFSETS if offset != (0, 0, 0)]
FILL_ORDER = sorted(range(26), key=lambda k: (abs(DIRECTIONS[k][2]), k))
F32 = jnp.float32
BF16 = jnp.bfloat16


def vmem():
    return pl.BlockSpec(memory_space=pltpu.VMEM)


def smem():
    return pl.BlockSpec(memory_space=pltpu.SMEM)


def hbm():
    return pl.BlockSpec(memory_space=pltpu.HBM)


def kernel_call(body, outs, specs, scratch=(), flops=0, moved=1 << 22, mib=28):
    return pl.pallas_call(
        body,
        out_shape=outs,
        in_specs=specs,
        out_specs=jax.tree.map(lambda _: vmem(), outs),
        scratch_shapes=list(scratch),
        compiler_params=pltpu.CompilerParams(vmem_limit_bytes=mib * 1024 * 1024),
        cost_estimate=pl.CostEstimate(flops=flops, bytes_accessed=moved, transcendentals=0),
    )


def swap_halves(rows):
    return pltpu.roll(rows, 64, 1)


def low_lanes(rows):
    return lax.broadcasted_iota(jnp.int32, rows.shape, 1) < 64


def filled_voxels(heights_ref):
    columns = lax.broadcasted_iota(jnp.int32, (64, 512), 0)
    voxels = lax.broadcasted_iota(jnp.int32, (64, 512), 1)
    spread = (voxels // 8 == columns).astype(F32)
    tall = jnp.dot(heights_ref[...].astype(F32), spread, preferred_element_type=F32)
    level = lax.broadcasted_iota(jnp.int32, tall.shape, 1) % 8
    return (level.astype(F32) < tall).astype(F32)


def fill_slots(rows_ref, near_ref, slots_ref, start=0):
    for k, (dx, dy, dz) in enumerate(DIRECTIONS):
        block = near_ref[0, k]
        xh = 7 if dx == 1 else 0
        y = 15 if dy == 1 else 0
        z = 15 if dz == 1 else 0

        @pl.when(block >= 0)
        def _(dx=dx, dy=dy, dz=dz, xh=xh, y=y, z=z, block=block):
            zeros = [d == 0 for d in (dx, dy, dz)]
            if zeros == [False, True, True]:
                plane = rows_ref[xh * 256 : xh * 256 + 256, :]
                first, second = plane[:128], plane[128:]
                if dx == -1:
                    second = swap_halves(second)
                else:
                    first = swap_halves(first)
                region = jnp.where(low_lanes(first), first, second)
            elif zeros == [True, False, True]:
                region = jnp.concatenate(
                    [rows_ref[x * 256 + y * 16 : x * 256 + y * 16 + 16, :] for x in range(8)]
                )
            elif zeros == [True, True, False]:
                region = rows_ref[pl.ds(z, 128, stride=16), :]
            elif zeros == [False, False, True]:
                region = rows_ref[xh * 256 + y * 16 : xh * 256 + y * 16 + 16, :]
            elif zeros == [False, True, False]:
                region = rows_ref[pl.ds(xh * 256 + z, 16, stride=16), :]
            elif zeros == [True, False, False]:
                line = rows_ref[pl.ds(y * 16 + z, 8, stride=256), :]
                region = jnp.concatenate([line, line])
            else:
                at = xh * 256 + y * 16 + z
                region = jnp.broadcast_to(rows_ref[at : at + 1, :], (16, 128))
            slots_ref[block, start : start + region.shape[0], :] = region.astype(BF16)


def put_lines(padded_ref, places, rows):
    count = rows.shape[0]
    level = lax.broadcasted_iota(jnp.int32, rows.shape, 0) % 16
    below = jnp.where(level == 0, 0.0, pltpu.roll(rows, 1, 0)).astype(BF16)
    above = jnp.where(level == 15, 0.0, pltpu.roll(rows, count - 1, 0)).astype(BF16)
    here = rows.astype(BF16)
    at = 0
    for x, row, height in places:
        for j, part in enumerate((below, here, above)):
            padded_ref[x, row : row + height, j * 128 : j * 128 + 128] = part[at : at + height]
        at += height


def put_ends(padded_ref, x, row, rows, dz):
    lines = rows.shape[0]
    j = 0 if dz == -1 else 2
    end = 0 if dz == -1 else 15
    lanes = slice(j * 128, j * 128 + 128)
    old = padded_ref[x, row : row + 16 * lines, lanes].astype(F32).reshape(lines, 16, 128)
    level = lax.broadcasted_iota(jnp.int32, old.shape, 1)
    new = jnp.where(level == end, rows.reshape(lines, 1, 128), old)
    padded_ref[x, row : row + 16 * lines, lanes] = new.reshape(16 * lines, 128).astype(BF16)


def clear_margin(padded_ref):
    empty = jnp.zeros((288, 384), BF16)
    padded_ref[0] = empty
    padded_ref[17] = empty
    line = jnp.zeros((16, 384), BF16)
    for x in range(1, 17):
        padded_ref[x, 0:16, :] = line
        padded_ref[x, 272:288, :] = line


def fill_margin(padded_ref, near_ref, own_ref, other_ref, start=0):
    for k in FILL_ORDER:
        dx, dy, dz = DIRECTIONS[k]
        block = near_ref[0, k]
        x = 17 if dx == 1 else 0
        y = 17 if dy == 1 else 0

        @pl.when(block >= 0)
        def _(dx=dx, dy=dy, dz=dz, x=x, y=y, block=block):
            zeros = [d == 0 for d in (dx, dy, dz)]
            height = 128 if zeros.count(True) == 2 else 16
            own = own_ref[block, start : start + height, :].astype(F32)
            other = other_ref[block, 0:height, :].astype(F32)

            def first():
                return jnp.where(low_lanes(own), own, swap_halves(other))

            def second():
                return jnp.where(low_lanes(own), swap_halves(own), other)

            if zeros == [False, True, True]:
                put_lines(padded_ref, [(x, 16, 256)], jnp.concatenate([first(), second()]))
            elif zeros == [True, False, True]:
                places = [(at + 1, y * 16, 16) for at in range(16)]
                put_lines(padded_ref, places, jnp.concatenate([first(), second()]))
            elif zeros == [False, False, True]:
                put_lines(padded_ref, [(x, y * 16, 16)], first() if dx == 1 else second())
            elif zeros == [True, True, False]:
                for half, rows in enumerate((first(), second())):
                    for at in range(8):
                        put_ends(
                            padded_ref, half * 8 + at + 1, 16, rows[at * 16 : at * 16 + 16], dz
                        )
            elif zeros == [False, True, False]:
                put_ends(padded_ref, x, 16, first() if dx == 1 else second(), dz)
            elif zeros == [True, False, False]:
                for half, rows in enumerate((first(), second())):
                    for at in range(8):
                        put_ends(
                            padded_ref, half * 8 + at + 1, y * 16, rows[at : at + 1], dz
                        )
            else:
                rows = first() if dx == 1 else second()
                put_ends(padded_ref, x, y * 16, rows[0:1], dz)


def send_features(
    near_hbm, heights_hbm, features_hbm, slots_ref,
    near_ref, heights_ref, features_ref, rows_ref, arrived
):
    copies = [
        pltpu.make_async_copy(near_hbm, near_ref, arrived.at[8]),
        pltpu.make_async_copy(heights_hbm, heights_ref, arrived.at[9]),
    ]
    order = (0, 1, 2, 3, 4, 5, 6, 7)
    bricks = [
        pltpu.make_async_copy(features_hbm.at[i], features_ref.at[i], arrived.at[i]) for i in order
    ]
    for copy in copies + bricks:
        copy.start()
    copies[1].wait()
    filled = filled_voxels(heights_ref)
    for oz in range(2):
        for oy in range(2):
            pair = []
            for ox in range(2):
                brick = ox + 2 * oy + 4 * oz
                bricks[brick].wait()
                pair.append(features_ref[brick].astype(F32) * filled[brick : brick + 1])
            turned = jnp.concatenate(pair).T
            for vx in range(8):
                for vy in range(8):
                    at = vx * 256 + (8 * oy + vy) * 16 + 8 * oz
                    source = (vx * 8 + vy) * 8
                    rows_ref[at : at + 8, :] = turned[source : source + 8]
    copies[0].wait()
    fill_slots(rows_ref, near_ref, slots_ref)


def weights(member_ref, conv_ref, down_in_ref, cot_in_ref, two_ref, four_ref, down_ref, cot_ref):
    shift = member_ref[0] * 64
    empty = jnp.zeros((128, 128), BF16)
    for yz in range(9):
        taps = []
        for ex in range(3):
            tap = conv_ref[ex * 9 + yz].astype(F32)
            taps.append(pltpu.roll(pltpu.roll(tap, shift, 0), shift, 1))
        whole = [empty] + [tap.astype(BF16) for tap in taps] + [empty]
        for p in range(4):
            rows = slice((p * 9 + yz) * 128, (p * 9 + yz) * 128 + 128)
            two_ref[rows, 0:128] = whole[p + 1] if p < 3 else empty
            two_ref[rows, 128:256] = whole[p]
        none = jnp.zeros((64, 128), F32)
        own = [none] + [taps[2 - ex][:64] for ex in range(3)] + [none]
        pairs = [jnp.concatenate([own[i + 1], own[i]]).T.astype(BF16) for i in range(4)]
        for p in range(6):
            at = (p * 9 + 8 - yz) * 128
            four_ref[at : at + 128, 0:128] = pairs[p] if p < 4 else empty
            four_ref[at : at + 128, 128:256] = pairs[p - 2] if p >= 2 else empty
    for tap in range(8):
        rows = down_in_ref[tap].astype(F32)
        rows = pltpu.roll(rows, shift, 0)
        down_ref[tap * 128 : tap * 128 + 128, :] = pltpu.roll(rows, 2 * shift, 1).astype(BF16)
    cot_ref[...] = pltpu.roll(cot_in_ref[...].astype(F32), 2 * shift, 1).astype(BF16)


def lay_out(
    heights_ref, own_ref, other_ref, cot_ref, down_ref, conv_ref,
    padded_ref, active_ref, slope_ref, pre_ref, rows_ref, mask_ref
):
    filled = filled_voxels(heights_ref)
    upright = filled.T
    for brick in range(8):
        ox, oy, oz = brick % 2, brick // 2 % 2, brick // 4
        both = jnp.concatenate([own_ref[brick].astype(F32), other_ref[brick].astype(F32)])
        turned = (both * filled[brick : brick + 1]).T
        mask = jnp.broadcast_to(upright[:, brick : brick + 1], (512, 128))
        for vx in range(8):
            for vy in range(8):
                at = (8 * ox + vx) * 256 + (8 * oy + vy) * 16 + 8 * oz
                source = (vx * 8 + vy) * 8
                rows_ref[at : at + 8, :] = turned[source : source + 8]
                mask_ref[at : at + 8, :] = mask[source : source + 8]
    clear_margin(padded_ref)
    for x in range(16):
        put_lines(padded_ref, [(x + 1, 16, 256)], rows_ref[x * 256 : x * 256 + 256, :])
        active_ref[x * 256 : x * 256 + 256, :] = mask_ref[x * 256 : x * 256 + 256, :].astype(BF16)
    for tap in range(8):
        tx, ty, tz = tap // 4, tap // 2 % 2, tap % 2
        part = lax.dot_general(
            cot_ref[...],
            down_ref[tap * 128 : tap * 128 + 128, :],
            (((1,), (1,)), ((), ())),
            preferred_element_type=F32,
        )
        for ux in range(8):
            for uy in range(8):
                at = (2 * ux + tx) * 256 + (2 * uy + ty) * 16 + tz
                source = (ux * 8 + uy) * 8
                rows = pl.ds(at, 8, stride=2)
                slope_ref[rows, :] = part[source : source + 8] * mask_ref[rows, :]


    def step(group, carry):
        lhs = []
        for pair in range(2):
            pieces = []
            for p in range(4):
                for ey in range(3):
                    pieces.append(
                        padded_ref[group * 4 + pair * 2 + p, ey * 16 : ey * 16 + 256, :]
                    )
            lhs.append(jnp.concatenate(pieces, axis=1))
        summed = jnp.dot(jnp.concatenate(lhs), conv_ref[...], preferred_element_type=F32)
        for pair in range(2):
            for phase in range(2):
                at = pl.multiple_of((group * 4 + pair * 2 + phase) * 256, 256)
                pre_ref[pl.ds(at, 256), :] = summed[
                    pair * 256 : pair * 256 + 256, phase * 128 : phase * 128 + 128
                ]
        return carry

    lax.fori_loop(0, 4, step, 0)


def add_margin(padded_ref, near_ref, own_ref, other_ref, conv_ref, pre_ref):
    def tap(ex, ey, ez):
        at = ((ex * 3 + ey) * 3 + ez) * 128
        return conv_ref[at : at + 128, 0:128]

    for x, ex in ((0, 0), (17, 2)):
        lhs = jnp.concatenate(
            [padded_ref[x, ey * 16 : ey * 16 + 256, :] for ey in range(3)], axis=1
        )
        rhs = conv_ref[ex * 1152 : ex * 1152 + 1152, 0:128]
        at = 0 if x == 0 else 15 * 256
        pre_ref[at : at + 256, :] += jnp.dot(lhs, rhs, preferred_element_type=F32)
    none = jnp.zeros((16, 384), BF16)
    for y, ey in ((0, 0), (17, 2)):
        lhs = jnp.concatenate(
            [
                jnp.concatenate(
                    [
                        padded_ref[x + ex, y * 16 : y * 16 + 16, :] if 1 <= x + ex <= 16 else none
                        for x in range(16)
                    ]
                )
                for ex in range(3)
            ],
            axis=1,
        )
        rhs = jnp.concatenate([tap(ex, ey, ez) for ex in range(3) for ez in range(3)])
        added = jnp.dot(lhs, rhs, preferred_element_type=F32)
        for x in range(16):
            at = x * 256 + (0 if y == 0 else 240)
            pre_ref[at : at + 16, :] += added[x * 16 : x * 16 + 16]
    for k in (DIRECTIONS.index((0, 0, -1)), DIRECTIONS.index((0, 0, 1))):
        block = near_ref[0, k]
        ez = 0 if DIRECTIONS[k][2] == -1 else 2

        @pl.when(block >= 0)
        def _(block=block, ez=ez):
            own = own_ref[block].astype(F32)
            other = other_ref[block].astype(F32)
            face = jnp.concatenate(
                [
                    jnp.where(low_lanes(own), own, swap_halves(other)),
                    jnp.where(low_lanes(own), swap_halves(own), other),
                ]
            )
            line = lax.broadcasted_iota(jnp.int32, face.shape, 0) % 16
            shifted = [
                jnp.where(line == 0, 0.0, pltpu.roll(face, 1, 0)),
                face,
                jnp.where(line == 15, 0.0, pltpu.roll(face, 255, 0)),
            ]
            border = jnp.zeros((16, 128), F32)
            lhs = []
            for ex in range(3):
                for part in shifted:
                    if ex == 0:
                        part = jnp.concatenate([border, part[:240]])
                    elif ex == 2:
                        part = jnp.concatenate([part[16:], border])
                    lhs.append(part.astype(BF16))
            rhs = jnp.concatenate([tap(ex, ey, ez) for ex in range(3) for ey in range(3)])
            added = jnp.dot(jnp.concatenate(lhs, axis=1), rhs, preferred_element_type=F32)
            rows = pl.ds(0 if ez == 0 else 15, 256, stride=16)
            pre_ref[rows, :] = pre_ref[rows, :] + added


def forward(
    near_ref, laid_ref, own_ref, other_ref, active_ref, slope_ref, inner_ref, conv_ref, down_ref,
    cot_ref,
    coarse_ref, grad_pre_ref, slots_ref,
    padded_ref, pre_ref, grad_ref, packed_ref, lanes_ref, turned_ref
):
    padded_ref[...] = laid_ref[...]
    pre_ref[...] = inner_ref[...]
    fill_margin(padded_ref, near_ref, own_ref, other_ref)
    add_margin(padded_ref, near_ref, own_ref, other_ref, conv_ref, pre_ref)

    turned_ref[:, 0:512] = jnp.zeros((128, 512), BF16)
    turned_ref[:, 4608:5120] = jnp.zeros((128, 512), BF16)
    for x in range(16):
        rows = slice(x * 256, x * 256 + 256)
        pre = pre_ref[rows, :] * active_ref[rows, :].astype(F32)
        sigmoid = 1.0 / (1.0 + jnp.exp(-pre))
        pre_ref[rows, :] = pre * sigmoid
        grad = slope_ref[rows, :] * sigmoid * (1.0 + pre * (1.0 - sigmoid))
        grad_ref[rows, :] = grad
        grad_pre_ref[rows, :] = grad.astype(BF16)
        turned_ref[:, 512 + x * 256 : 768 + x * 256] = grad.T.astype(BF16)

    share = slots_ref.shape[1] - 128
    for x in range(8):
        low = grad_ref[x * 256 : x * 256 + 256, :]
        high = grad_ref[2048 + x * 256 : 2048 + x * 256 + 256, :]
        packed_ref[x * 256 : x * 256 + 256, :] = jnp.where(
            low_lanes(low), low, swap_halves(high)
        )
    fill_slots(packed_ref, near_ref, slots_ref, share)

    def put_terms(at, rows):
        while rows.shape[0]:
            owner, row = at // share, at % share
            count = min(rows.shape[0], share - row)
            slots_ref[owner, row : row + count, :] = rows[:count]
            rows = rows[count:]
            at += count

    for x in range(18):
        below = padded_ref[x, :, 0:128].astype(F32)
        here = padded_ref[x, :, 128:256].astype(F32)
        both = jnp.where(low_lanes(below), below, swap_halves(here))
        lanes_ref[x, :, 0:128] = both.astype(BF16)
        lanes_ref[x, :, 128:256] = padded_ref[x, :, 256:384]
    lhs = jnp.concatenate(
        [turned_ref[:, (2 - ex) * 256 : (2 - ex) * 256 + 4608] for ex in range(3)]
    )
    for ey in range(3):
        rhs = lanes_ref[:, ey * 16 : ey * 16 + 256, :].reshape(4608, 256)
        summed = jnp.dot(lhs, rhs, preferred_element_type=F32)
        for ex in range(3):
            part = summed[ex * 128 : ex * 128 + 128].T
            put_terms((ex * 3 + ey) * 192, part[0:192].astype(BF16))

    patches = []
    for tap in range(8):
        tx, ty, tz = tap // 4, tap // 2 % 2, tap % 2
        pieces = []
        for ux in range(8):
            for uy in range(8):
                at = (2 * ux + tx) * 256 + (2 * uy + ty) * 16 + tz
                pieces.append(pre_ref[pl.ds(at, 8, stride=2), :])
        patches.append(jnp.concatenate(pieces).astype(BF16))
    patches = jnp.concatenate(patches, axis=1)
    coarse = jnp.dot(patches, down_ref[...], preferred_element_type=F32)
    coarse_ref[...] = coarse[:, :128].astype(BF16)
    own_cot = cot_ref[:, 0:128].astype(F32).T.astype(BF16)
    grad_down = jnp.dot(own_cot, patches, preferred_element_type=F32)
    for tap in range(8):
        part = grad_down[:, tap * 128 : tap * 128 + 128].T
        put_terms(1728 + tap * 128, part.astype(BF16))


def total(slots_ref, out_ref):
    devices, share, _ = out_ref.shape
    summed = slots_ref[0, 0:share, :].astype(F32)
    for device in range(1, devices):
        summed = summed + slots_ref[device, 0:share, :].astype(F32)
    summed = (summed / devices).astype(BF16)
    for device in range(devices):
        out_ref[device] = summed


def backward(
    near_ref, grad_pre_ref, own_ref, other_ref, active_ref, back_ref, out_ref, padded_ref
):
    clear_margin(padded_ref)
    for x in range(16):
        rows = grad_pre_ref[x * 256 : x * 256 + 256, :].astype(F32)
        put_lines(padded_ref, [(x + 1, 16, 256)], rows)
    fill_margin(padded_ref, near_ref, own_ref, other_ref, own_ref.shape[1] - 128)
    for half in range(2):
        lhs = []
        for quad in range(2):
            pieces = []
            for p in range(6):
                for ey in range(3):
                    pieces.append(
                        padded_ref[half * 8 + quad * 4 + p, ey * 16 : ey * 16 + 256, :]
                    )
            lhs.append(jnp.concatenate(pieces, axis=1))
        summed = jnp.dot(jnp.concatenate(lhs), back_ref[...], preferred_element_type=F32)
        for quad in range(2):
            for two in range(2):
                part = summed[quad * 256 : quad * 256 + 256, two * 128 : two * 128 + 128]
                x = half * 8 + quad * 4 + two * 2
                even = active_ref[x * 256 : x * 256 + 256, :].astype(F32)
                odd = active_ref[x * 256 + 256 : x * 256 + 512, :].astype(F32)
                part = part * jnp.where(low_lanes(part), even, odd)
                for oy in range(2):
                    rows = [
                        part[(8 * oy + vy) * 16 + 8 * oz : (8 * oy + vy) * 16 + 8 * oz + 8]
                        for oz in range(2)
                        for vy in range(8)
                    ]
                    turned = jnp.concatenate(rows).T
                    first, second = turned[:64], turned[64:]
                    lanes = slice(x % 8 * 64, x % 8 * 64 + 128)
                    brick = half + 2 * oy
                    near = jnp.where(low_lanes(first), first, swap_halves(second))
                    far = jnp.where(low_lanes(first), swap_halves(first), second)
                    out_ref[brick, :, lanes] = near.astype(BF16)
                    out_ref[brick + 4, :, lanes] = far.astype(BF16)


def finish(member_ref, sums_ref, conv_ref, down_ref):
    shift = member_ref[0] * 64
    for tap in range(27):
        rows = sums_ref[tap * 64 : tap * 64 + 64, :].astype(F32)
        conv_ref[tap] = pltpu.roll(rows, shift, 1)
    for tap in range(8):
        rows = sums_ref[1728 + tap * 128 : 1728 + tap * 128 + 128, :].astype(F32)
        down_ref[tap, pl.ds(shift, 64), :] = rows[:64]
        down_ref[tap, pl.ds(64 - shift, 64), :] = rows[64:]


def over_chan(block):
    return lax.ppermute(block, "chan", [(0, 1), (1, 0)])


def to_all(slots):
    return lax.all_to_all(slots, "space", 0, 0, tiled=True)


def local(features, heights, neighbours, w_conv, w_down, cotangent):
    devices = lax.axis_size("space")
    member = lax.axis_index("chan")

    def out(*shape, dtype=BF16):
        return jax.ShapeDtypeStruct(shape, dtype)

    turned = features.transpose(0, 2, 1)
    slots = kernel_call(
        send_features,
        out(devices, 128, 128),
        [hbm()] * 3,
        [
            pltpu.SMEM(neighbours.shape, jnp.int32),
            pltpu.VMEM(heights.shape, jnp.int32),
            pltpu.VMEM(turned.shape, BF16),
            pltpu.VMEM((2048, 128), F32),
            pltpu.SemaphoreType.DMA((10,)),
        ],
        mib=16,
    )(neighbours, heights, turned)
    came = to_all(slots)
    other_turned = over_chan(turned)

    two_phase, four_phase, down, cot = kernel_call(
        weights,
        (out(4608, 256), out(6912, 256), out(1024, 256), out(512, 256)),
        [smem()] + [vmem()] * 3,
        flops=1 << 28,
    )(member.reshape(1), w_conv, w_down, cotangent[0])
    laid, active, slope, inner = kernel_call(
        lay_out,
        (
            out(18, 288, 384),
            out(4096, 128),
            out(4096, 128, dtype=F32),
            out(4096, 128, dtype=F32),
        ),
        [vmem()] * 6,
        [pltpu.VMEM((4096, 128), F32), pltpu.VMEM((4096, 128), F32)],
        flops=5 << 30,
    )(heights, turned, other_turned, cot, down, two_phase)
    came, inner = lax.optimization_barrier((came, inner))
    came_other = over_chan(came)

    share = -(-2752 // (devices * 16)) * 16
    coarse, grad_pre, terms = kernel_call(
        forward,
        (out(512, 128), out(4096, 128), out(devices, share + 128, 128)),
        [smem()] + [vmem()] * 9,
        [
            pltpu.VMEM((18, 288, 384), BF16),
            pltpu.VMEM((4096, 128), F32),
            pltpu.VMEM((4096, 128), F32),
            pltpu.VMEM((2048, 128), F32),
            pltpu.VMEM((18, 288, 256), BF16),
            pltpu.VMEM((128, 5120), BF16),
        ],
        flops=5 << 30,
        mib=36,
    )(neighbours, laid, came, came_other, active, slope, inner, two_phase, down, cot)

    arrived = to_all(terms)
    sums = to_all(
        kernel_call(total, out(devices, share, 128), [vmem()], mib=16)(arrived)
    )
    arrived_other = over_chan(arrived[:, share:])
    grad_features = kernel_call(
        backward,
        out(8, 64, 512),
        [smem()] + [vmem()] * 5,
        [pltpu.VMEM((18, 288, 384), BF16)],
        flops=5 << 30,
    )(neighbours, grad_pre, arrived, arrived_other, active, four_phase)

    grad_conv, grad_down = kernel_call(
        finish,
        (out(27, 64, 128, dtype=F32), out(8, 128, 128, dtype=F32)),
        [smem(), vmem()],
        mib=16,
    )(member.reshape(1), sums.reshape(-1, 128))
    return coarse[None], grad_conv, grad_down, grad_features.transpose(0, 2, 1)


def solution(mesh):
    placed = (
        P("space", None, "chan"),
        P("space", None),
        P("space", None),
        P(),
        P(),
        P("space", None, None),
    )
    return jax.shard_map(
        local,
        mesh=mesh,
        in_specs=placed,
        out_specs=(
            P("space", None, "chan"),
            P(None, "chan", None),
            P(None, None, "chan"),
            P("space", None, "chan"),
        ),
        check_vma=False,
    )
```

```python
import jax
import jax.numpy as jnp
from jax import lax
from jax.experimental import pallas as pl
from jax.experimental.pallas import tpu as pltpu
from jax.sharding import PartitionSpec as P

OFFSETS = [
    (along_x, along_y, along_z)
    for along_x in (-1, 0, 1)
    for along_y in (-1, 0, 1)
    for along_z in (-1, 0, 1)
]
DIRECTIONS = [offset for offset in OFFSETS if offset != (0, 0, 0)]
FILL_ORDER = sorted(range(26), key=lambda k: (abs(DIRECTIONS[k][2]), k))
F32 = jnp.float32
BF16 = jnp.bfloat16


def vmem():
    return pl.BlockSpec(memory_space=pltpu.VMEM)


def smem():
    return pl.BlockSpec(memory_space=pltpu.SMEM)


def hbm():
    return pl.BlockSpec(memory_space=pltpu.HBM)


def kernel_call(body, outs, specs, scratch=(), flops=0, moved=1 << 22):
    return pl.pallas_call(
        body,
        out_shape=outs,
        in_specs=specs,
        out_specs=jax.tree.map(lambda _: vmem(), outs),
        scratch_shapes=list(scratch),
        compiler_params=pltpu.CompilerParams(vmem_limit_bytes=17 * 1024 * 1024),
        cost_estimate=pl.CostEstimate(flops=flops, bytes_accessed=moved, transcendentals=0),
    )


def swap_halves(rows):
    return pltpu.roll(rows, 64, 1)


def low_lanes(rows):
    return lax.broadcasted_iota(jnp.int32, rows.shape, 1) < 64


def filled_voxels(heights_ref):
    columns = lax.broadcasted_iota(jnp.int32, (64, 512), 0)
    voxels = lax.broadcasted_iota(jnp.int32, (64, 512), 1)
    spread = (voxels // 8 == columns).astype(F32)
    tall = jnp.dot(heights_ref[...].astype(F32), spread, preferred_element_type=F32)
    level = lax.broadcasted_iota(jnp.int32, tall.shape, 1) % 8
    return (level.astype(F32) < tall).astype(F32)


def fill_slots(rows_ref, near_ref, slots_ref, start=0, faces=True):
    for k, (dx, dy, dz) in enumerate(DIRECTIONS):
        block = near_ref[0, k]
        xh = 7 if dx == 1 else 0
        y = 15 if dy == 1 else 0
        z = 15 if dz == 1 else 0
        if not faces and (dx, dy, dz).count(0) == 2:
            continue

        @pl.when(block >= 0)
        def _(dx=dx, dy=dy, dz=dz, xh=xh, y=y, z=z, block=block):
            zeros = [d == 0 for d in (dx, dy, dz)]
            if zeros == [False, True, True]:
                plane = rows_ref[xh * 256 : xh * 256 + 256, :]
                first, second = plane[:128], plane[128:]
                if dx == -1:
                    second = swap_halves(second)
                else:
                    first = swap_halves(first)
                region = jnp.where(low_lanes(first), first, second)
            elif zeros == [True, False, True]:
                region = jnp.concatenate(
                    [rows_ref[x * 256 + y * 16 : x * 256 + y * 16 + 16, :] for x in range(8)]
                )
            elif zeros == [True, True, False]:
                region = rows_ref[pl.ds(z, 128, stride=16), :]
            elif zeros == [False, False, True]:
                region = rows_ref[xh * 256 + y * 16 : xh * 256 + y * 16 + 16, :]
            elif zeros == [False, True, False]:
                region = rows_ref[pl.ds(xh * 256 + z, 16, stride=16), :]
            elif zeros == [True, False, False]:
                line = rows_ref[pl.ds(y * 16 + z, 8, stride=256), :]
                region = jnp.concatenate([line, line])
            else:
                at = xh * 256 + y * 16 + z
                region = jnp.broadcast_to(rows_ref[at : at + 1, :], (16, 128))
            slots_ref[block, start : start + region.shape[0], :] = region.astype(BF16)


def fill_faces(rows_ref, near_ref, place_ref, faces_ref):
    member, own = place_ref[0], place_ref[1]
    for k, (dx, dy, dz) in enumerate(DIRECTIONS):
        if (dx, dy, dz).count(0) != 2:
            continue
        block = near_ref[0, k]
        distance = jnp.where(member == 0, block - own, own - block)
        end = 15 if dx + dy + dz == 1 else 0

        @pl.when((block >= 0) & (distance >= 1))
        def _(dx=dx, dy=dy, end=end, distance=distance):
            if dx:
                region = rows_ref[end * 256 : end * 256 + 256, :]
            elif dy:
                region = jnp.concatenate(
                    [rows_ref[x * 256 + end * 16 : x * 256 + end * 16 + 16, :] for x in range(16)]
                )
            else:
                region = rows_ref[pl.ds(end, 256, stride=16), :]
            faces_ref[distance - 1] = region.astype(BF16)


def put_lines(padded_ref, places, rows):
    count = rows.shape[0]
    level = lax.broadcasted_iota(jnp.int32, rows.shape, 0) % 16
    below = jnp.where(level == 0, 0.0, pltpu.roll(rows, 1, 0)).astype(BF16)
    above = jnp.where(level == 15, 0.0, pltpu.roll(rows, count - 1, 0)).astype(BF16)
    here = rows.astype(BF16)
    at = 0
    for x, row, height in places:
        for j, part in enumerate((below, here, above)):
            padded_ref[x, row : row + height, j * 128 : j * 128 + 128] = part[at : at + height]
        at += height


def put_ends(padded_ref, x, row, rows, dz):
    lines = rows.shape[0]
    j = 0 if dz == -1 else 2
    end = 0 if dz == -1 else 15
    lanes = slice(j * 128, j * 128 + 128)
    old = padded_ref[x, row : row + 16 * lines, lanes].astype(F32).reshape(lines, 16, 128)
    level = lax.broadcasted_iota(jnp.int32, old.shape, 1)
    new = jnp.where(level == end, rows.reshape(lines, 1, 128), old)
    padded_ref[x, row : row + 16 * lines, lanes] = new.reshape(16 * lines, 128).astype(BF16)


def clear_margin(padded_ref):
    empty = jnp.zeros((288, 384), BF16)
    padded_ref[0] = empty
    padded_ref[17] = empty
    line = jnp.zeros((16, 384), BF16)
    for x in range(1, 17):
        padded_ref[x, 0:16, :] = line
        padded_ref[x, 272:288, :] = line


def put_region(padded_ref, offset, rows):
    dx, dy, dz = offset
    zeros = [d == 0 for d in offset]
    x = 17 if dx == 1 else 0
    y = 17 if dy == 1 else 0
    if zeros == [False, True, True]:
        put_lines(padded_ref, [(x, 16, 256)], rows)
    elif zeros == [True, False, True]:
        put_lines(padded_ref, [(at + 1, y * 16, 16) for at in range(16)], rows)
    elif zeros == [False, False, True]:
        put_lines(padded_ref, [(x, y * 16, 16)], rows)
    elif zeros == [True, True, False]:
        for at in range(16):
            put_ends(padded_ref, at + 1, 16, rows[at * 16 : at * 16 + 16], dz)
    elif zeros == [False, True, False]:
        put_ends(padded_ref, x, 16, rows, dz)
    elif zeros == [True, False, False]:
        for at in range(16):
            put_ends(padded_ref, at + 1, y * 16, rows[at : at + 1], dz)
    else:
        put_ends(padded_ref, x, y * 16, rows[0:1], dz)


def fill_margin(padded_ref, near_ref, own_ref, other_ref, start=0, faces=None):
    for k in FILL_ORDER:
        offset = DIRECTIONS[k]
        block = near_ref[0, k]
        face = offset.count(0) == 2
        if face and faces is not None:
            place_ref, own_faces_ref, other_faces_ref = faces
            member = place_ref[0]
            away = place_ref[1] - block
            here = jnp.where(away > 0, 0, 1) == member
            slot = jnp.abs(away) - 1

            @pl.when((block >= 0) & here)
            def _(offset=offset, slot=slot):
                put_region(padded_ref, offset, own_faces_ref[slot].astype(F32))

            @pl.when((block >= 0) & jnp.logical_not(here))
            def _(offset=offset, slot=slot):
                rows = swap_halves(other_faces_ref[slot].astype(F32))
                put_region(padded_ref, offset, rows)

            continue

        @pl.when(block >= 0)
        def _(offset=offset, block=block, face=face):
            height = 128 if face else 16
            own = own_ref[block, start : start + height, :].astype(F32)
            other = other_ref[block, 0:height, :].astype(F32)
            first = jnp.where(low_lanes(own), own, swap_halves(other))
            second = jnp.where(low_lanes(own), swap_halves(own), other)
            if face:
                rows = jnp.concatenate([first, second])
            elif offset[0] == 0:
                rows = jnp.concatenate([first[:8], second[:8]])
            else:
                rows = first if offset[0] == 1 else second
            put_region(padded_ref, offset, rows)


def send_features(
    near_hbm, heights_hbm, features_hbm, slots_ref,
    near_ref, heights_ref, features_ref, rows_ref, arrived
):
    copies = [
        pltpu.make_async_copy(near_hbm, near_ref, arrived.at[8]),
        pltpu.make_async_copy(heights_hbm, heights_ref, arrived.at[9]),
    ]
    order = (0, 1, 2, 3, 4, 5, 6, 7)
    bricks = [
        pltpu.make_async_copy(features_hbm.at[i], features_ref.at[i], arrived.at[i]) for i in order
    ]
    for copy in copies + bricks:
        copy.start()
    copies[1].wait()
    filled = filled_voxels(heights_ref)
    for oz in range(2):
        for oy in range(2):
            pair = []
            for ox in range(2):
                brick = ox + 2 * oy + 4 * oz
                bricks[brick].wait()
                pair.append(features_ref[brick].astype(F32) * filled[brick : brick + 1])
            turned = jnp.concatenate(pair).T
            for vx in range(8):
                for vy in range(8):
                    at = vx * 256 + (8 * oy + vy) * 16 + 8 * oz
                    source = (vx * 8 + vy) * 8
                    rows_ref[at : at + 8, :] = turned[source : source + 8]
    copies[0].wait()
    fill_slots(rows_ref, near_ref, slots_ref)


def weights(member_ref, conv_ref, down_in_ref, cot_in_ref, two_ref, four_ref, down_ref, cot_ref):
    shift = member_ref[0] * 64
    empty = jnp.zeros((128, 128), BF16)
    for yz in range(9):
        taps = []
        for ex in range(3):
            tap = conv_ref[ex * 9 + yz].astype(F32)
            taps.append(pltpu.roll(pltpu.roll(tap, shift, 0), shift, 1))
        whole = [empty] + [tap.astype(BF16) for tap in taps] + [empty]
        for p in range(4):
            rows = slice((p * 9 + yz) * 128, (p * 9 + yz) * 128 + 128)
            two_ref[rows, 0:128] = whole[p + 1] if p < 3 else empty
            two_ref[rows, 128:256] = whole[p]
        none = jnp.zeros((64, 128), F32)
        own = [none] + [taps[2 - ex][:64] for ex in range(3)] + [none]
        pairs = [jnp.concatenate([own[i + 1], own[i]]).T.astype(BF16) for i in range(4)]
        for p in range(6):
            at = (p * 9 + 8 - yz) * 128
            four_ref[at : at + 128, 0:128] = pairs[p] if p < 4 else empty
            four_ref[at : at + 128, 128:256] = pairs[p - 2] if p >= 2 else empty
    for tap in range(8):
        rows = down_in_ref[tap].astype(F32)
        rows = pltpu.roll(rows, shift, 0)
        down_ref[tap * 128 : tap * 128 + 128, :] = pltpu.roll(rows, 2 * shift, 1).astype(BF16)
    cot_ref[...] = pltpu.roll(cot_in_ref[...].astype(F32), 2 * shift, 1).astype(BF16)


def lay_out(
    heights_ref, own_ref, other_ref, cot_ref, down_ref, conv_ref,
    padded_ref, active_ref, slope_ref, pre_ref, rows_ref, mask_ref
):
    filled = filled_voxels(heights_ref)
    upright = filled.T
    for brick in range(8):
        ox, oy, oz = brick % 2, brick // 2 % 2, brick // 4
        both = jnp.concatenate([own_ref[brick].astype(F32), other_ref[brick].astype(F32)])
        turned = (both * filled[brick : brick + 1]).T
        mask = jnp.broadcast_to(upright[:, brick : brick + 1], (512, 128))
        for vx in range(8):
            for vy in range(8):
                at = (8 * ox + vx) * 256 + (8 * oy + vy) * 16 + 8 * oz
                source = (vx * 8 + vy) * 8
                rows_ref[at : at + 8, :] = turned[source : source + 8]
                mask_ref[at : at + 8, :] = mask[source : source + 8]
    clear_margin(padded_ref)
    for x in range(16):
        put_lines(padded_ref, [(x + 1, 16, 256)], rows_ref[x * 256 : x * 256 + 256, :])
        active_ref[x * 256 : x * 256 + 256, :] = mask_ref[x * 256 : x * 256 + 256, :].astype(BF16)
    for tap in range(8):
        tx, ty, tz = tap // 4, tap // 2 % 2, tap % 2
        part = lax.dot_general(
            cot_ref[...],
            down_ref[tap * 128 : tap * 128 + 128, :],
            (((1,), (1,)), ((), ())),
            preferred_element_type=F32,
        )
        for ux in range(8):
            for uy in range(8):
                at = (2 * ux + tx) * 256 + (2 * uy + ty) * 16 + tz
                source = (ux * 8 + uy) * 8
                rows = pl.ds(at, 8, stride=2)
                slope_ref[rows, :] = part[source : source + 8] * mask_ref[rows, :]


    def step(group, carry):
        lhs = []
        for pair in range(2):
            pieces = []
            for p in range(4):
                for ey in range(3):
                    pieces.append(
                        padded_ref[group * 4 + pair * 2 + p, ey * 16 : ey * 16 + 256, :]
                    )
            lhs.append(jnp.concatenate(pieces, axis=1))
        summed = jnp.dot(jnp.concatenate(lhs), conv_ref[...], preferred_element_type=F32)
        for pair in range(2):
            for phase in range(2):
                at = pl.multiple_of((group * 4 + pair * 2 + phase) * 256, 256)
                pre_ref[pl.ds(at, 256), :] = summed[
                    pair * 256 : pair * 256 + 256, phase * 128 : phase * 128 + 128
                ]
        return carry

    lax.fori_loop(0, 4, step, 0)


def add_margin(padded_ref, near_ref, own_ref, other_ref, conv_ref, pre_ref):
    def tap(ex, ey, ez):
        at = ((ex * 3 + ey) * 3 + ez) * 128
        return conv_ref[at : at + 128, 0:128]

    for x, ex in ((0, 0), (17, 2)):
        lhs = jnp.concatenate(
            [padded_ref[x, ey * 16 : ey * 16 + 256, :] for ey in range(3)], axis=1
        )
        rhs = conv_ref[ex * 1152 : ex * 1152 + 1152, 0:128]
        at = 0 if x == 0 else 15 * 256
        pre_ref[at : at + 256, :] += jnp.dot(lhs, rhs, preferred_element_type=F32)
    none = jnp.zeros((16, 384), BF16)
    for y, ey in ((0, 0), (17, 2)):
        lhs = jnp.concatenate(
            [
                jnp.concatenate(
                    [
                        padded_ref[x + ex, y * 16 : y * 16 + 16, :] if 1 <= x + ex <= 16 else none
                        for x in range(16)
                    ]
                )
                for ex in range(3)
            ],
            axis=1,
        )
        rhs = jnp.concatenate([tap(ex, ey, ez) for ex in range(3) for ez in range(3)])
        added = jnp.dot(lhs, rhs, preferred_element_type=F32)
        for x in range(16):
            at = x * 256 + (0 if y == 0 else 240)
            pre_ref[at : at + 16, :] += added[x * 16 : x * 16 + 16]
    for k in (DIRECTIONS.index((0, 0, -1)), DIRECTIONS.index((0, 0, 1))):
        block = near_ref[0, k]
        ez = 0 if DIRECTIONS[k][2] == -1 else 2

        @pl.when(block >= 0)
        def _(block=block, ez=ez):
            own = own_ref[block].astype(F32)
            other = other_ref[block].astype(F32)
            face = jnp.concatenate(
                [
                    jnp.where(low_lanes(own), own, swap_halves(other)),
                    jnp.where(low_lanes(own), swap_halves(own), other),
                ]
            )
            line = lax.broadcasted_iota(jnp.int32, face.shape, 0) % 16
            shifted = [
                jnp.where(line == 0, 0.0, pltpu.roll(face, 1, 0)),
                face,
                jnp.where(line == 15, 0.0, pltpu.roll(face, 255, 0)),
            ]
            border = jnp.zeros((16, 128), F32)
            lhs = []
            for ex in range(3):
                for part in shifted:
                    if ex == 0:
                        part = jnp.concatenate([border, part[:240]])
                    elif ex == 2:
                        part = jnp.concatenate([part[16:], border])
                    lhs.append(part.astype(BF16))
            rhs = jnp.concatenate([tap(ex, ey, ez) for ex in range(3) for ey in range(3)])
            added = jnp.dot(jnp.concatenate(lhs, axis=1), rhs, preferred_element_type=F32)
            rows = pl.ds(0 if ez == 0 else 15, 256, stride=16)
            pre_ref[rows, :] = pre_ref[rows, :] + added


def forward(
    near_ref, place_ref, laid_ref, own_ref, other_ref, active_ref, slope_ref, inner_ref, conv_ref,
    down_ref, cot_ref,
    coarse_ref, grad_pre_ref, slots_ref, faces_ref,
    padded_ref, pre_ref, grad_ref, packed_ref, lanes_ref, turned_ref
):
    padded_ref[...] = laid_ref[...]
    pre_ref[...] = inner_ref[...]
    fill_margin(padded_ref, near_ref, own_ref, other_ref)
    add_margin(padded_ref, near_ref, own_ref, other_ref, conv_ref, pre_ref)

    turned_ref[:, 0:512] = jnp.zeros((128, 512), BF16)
    turned_ref[:, 4608:5120] = jnp.zeros((128, 512), BF16)
    for x in range(16):
        rows = slice(x * 256, x * 256 + 256)
        pre = pre_ref[rows, :] * active_ref[rows, :].astype(F32)
        sigmoid = 1.0 / (1.0 + jnp.exp(-pre))
        pre_ref[rows, :] = pre * sigmoid
        grad = slope_ref[rows, :] * sigmoid * (1.0 + pre * (1.0 - sigmoid))
        grad_ref[rows, :] = grad
        grad_pre_ref[rows, :] = grad.astype(BF16)
        turned_ref[:, 512 + x * 256 : 768 + x * 256] = grad.T.astype(BF16)

    fill_faces(grad_ref, near_ref, place_ref, faces_ref)
    share = slots_ref.shape[1] - 16
    for x in range(8):
        low = grad_ref[x * 256 : x * 256 + 256, :]
        high = grad_ref[2048 + x * 256 : 2048 + x * 256 + 256, :]
        packed_ref[x * 256 : x * 256 + 256, :] = jnp.where(
            low_lanes(low), low, swap_halves(high)
        )
    fill_slots(packed_ref, near_ref, slots_ref, share, faces=False)

    def put_terms(at, rows):
        while rows.shape[0]:
            owner, row = at // share, at % share
            count = min(rows.shape[0], share - row)
            slots_ref[owner, row : row + count, :] = rows[:count]
            rows = rows[count:]
            at += count

    for x in range(18):
        below = padded_ref[x, :, 0:128].astype(F32)
        here = padded_ref[x, :, 128:256].astype(F32)
        both = jnp.where(low_lanes(below), below, swap_halves(here))
        lanes_ref[x, :, 0:128] = both.astype(BF16)
        lanes_ref[x, :, 128:256] = padded_ref[x, :, 256:384]
    lhs = jnp.concatenate(
        [turned_ref[:, (2 - ex) * 256 : (2 - ex) * 256 + 4608] for ex in range(3)]
    )
    for ey in range(3):
        rhs = lanes_ref[:, ey * 16 : ey * 16 + 256, :].reshape(4608, 256)
        summed = jnp.dot(lhs, rhs, preferred_element_type=F32)
        for ex in range(3):
            part = summed[ex * 128 : ex * 128 + 128].T
            put_terms((ex * 3 + ey) * 192, part[0:192].astype(BF16))

    patches = []
    for tap in range(8):
        tx, ty, tz = tap // 4, tap // 2 % 2, tap % 2
        pieces = []
        for ux in range(8):
            for uy in range(8):
                at = (2 * ux + tx) * 256 + (2 * uy + ty) * 16 + tz
                pieces.append(pre_ref[pl.ds(at, 8, stride=2), :])
        patches.append(jnp.concatenate(pieces).astype(BF16))
    patches = jnp.concatenate(patches, axis=1)
    coarse = jnp.dot(patches, down_ref[...], preferred_element_type=F32)
    coarse_ref[...] = coarse[:, :128].astype(BF16)
    own_cot = cot_ref[:, 0:128].astype(F32).T.astype(BF16)
    grad_down = jnp.dot(own_cot, patches, preferred_element_type=F32)
    for tap in range(8):
        part = grad_down[:, tap * 128 : tap * 128 + 128].T
        put_terms(1728 + tap * 128, part.astype(BF16))


def total(slots_ref, out_ref):
    devices, share, _ = out_ref.shape
    summed = slots_ref[0, 0:share, :].astype(F32)
    for device in range(1, devices):
        summed = summed + slots_ref[device, 0:share, :].astype(F32)
    summed = (summed / devices).astype(BF16)
    for device in range(devices):
        out_ref[device] = summed


def backward(
    near_ref, place_ref, grad_pre_ref, own_ref, other_ref, own_faces_ref, other_faces_ref,
    active_ref, back_ref, out_ref, padded_ref
):
    clear_margin(padded_ref)
    for x in range(16):
        rows = grad_pre_ref[x * 256 : x * 256 + 256, :].astype(F32)
        put_lines(padded_ref, [(x + 1, 16, 256)], rows)
    fill_margin(
        padded_ref, near_ref, own_ref, other_ref, own_ref.shape[1] - 16,
        (place_ref, own_faces_ref, other_faces_ref),
    )
    for half in range(2):
        lhs = []
        for quad in range(2):
            pieces = []
            for p in range(6):
                for ey in range(3):
                    pieces.append(
                        padded_ref[half * 8 + quad * 4 + p, ey * 16 : ey * 16 + 256, :]
                    )
            lhs.append(jnp.concatenate(pieces, axis=1))
        summed = jnp.dot(jnp.concatenate(lhs), back_ref[...], preferred_element_type=F32)
        for quad in range(2):
            for two in range(2):
                part = summed[quad * 256 : quad * 256 + 256, two * 128 : two * 128 + 128]
                x = half * 8 + quad * 4 + two * 2
                even = active_ref[x * 256 : x * 256 + 256, :].astype(F32)
                odd = active_ref[x * 256 + 256 : x * 256 + 512, :].astype(F32)
                part = part * jnp.where(low_lanes(part), even, odd)
                for oy in range(2):
                    rows = [
                        part[(8 * oy + vy) * 16 + 8 * oz : (8 * oy + vy) * 16 + 8 * oz + 8]
                        for oz in range(2)
                        for vy in range(8)
                    ]
                    turned = jnp.concatenate(rows).T
                    first, second = turned[:64], turned[64:]
                    lanes = slice(x % 8 * 64, x % 8 * 64 + 128)
                    brick = half + 2 * oy
                    near = jnp.where(low_lanes(first), first, swap_halves(second))
                    far = jnp.where(low_lanes(first), swap_halves(first), second)
                    out_ref[brick, :, lanes] = near.astype(BF16)
                    out_ref[brick + 4, :, lanes] = far.astype(BF16)


def finish(member_ref, sums_ref, conv_ref, down_ref):
    shift = member_ref[0] * 64
    for tap in range(27):
        rows = sums_ref[tap * 64 : tap * 64 + 64, :].astype(F32)
        conv_ref[tap] = pltpu.roll(rows, shift, 1)
    for tap in range(8):
        rows = sums_ref[1728 + tap * 128 : 1728 + tap * 128 + 128, :].astype(F32)
        down_ref[tap, pl.ds(shift, 64), :] = rows[:64]
        down_ref[tap, pl.ds(64 - shift, 64), :] = rows[64:]


def over_space(block, distance):
    blocks = range(lax.axis_size("space"))
    route = [(2 * i, 2 * (i + distance)) for i in blocks if i + distance in blocks]
    route += [(2 * i + 1, 2 * (i - distance) + 1) for i in blocks if i - distance in blocks]
    return lax.ppermute(block, ("space", "chan"), route)


def over_chan(block):
    return lax.ppermute(block, "chan", [(0, 1), (1, 0)])


def to_all(slots):
    return lax.all_to_all(slots, "space", 0, 0, tiled=True)


def local(features, heights, neighbours, w_conv, w_down, cotangent):
    devices = lax.axis_size("space")
    member = lax.axis_index("chan")

    def out(*shape, dtype=BF16):
        return jax.ShapeDtypeStruct(shape, dtype)

    turned = features.transpose(0, 2, 1)
    slots = kernel_call(
        send_features,
        out(devices, 128, 128),
        [hbm()] * 3,
        [
            pltpu.SMEM(neighbours.shape, jnp.int32),
            pltpu.VMEM(heights.shape, jnp.int32),
            pltpu.VMEM(turned.shape, BF16),
            pltpu.VMEM((2048, 128), F32),
            pltpu.SemaphoreType.DMA((10,)),
        ],
    )(*(pltpu.with_memory_space_constraint(x, pltpu.HBM) for x in (neighbours, heights, turned)))
    came = to_all(slots)
    other_turned = over_chan(turned)

    two_phase, four_phase, down, cot = kernel_call(
        weights,
        (out(4608, 256), out(6912, 256), out(1024, 256), out(512, 256)),
        [smem()] + [vmem()] * 3,
        flops=1 << 28,
    )(member.reshape(1), w_conv, w_down, cotangent[0])
    laid, active, slope, inner = kernel_call(
        lay_out,
        (
            out(18, 288, 384),
            out(4096, 128),
            out(4096, 128, dtype=F32),
            out(4096, 128, dtype=F32),
        ),
        [vmem()] * 6,
        [pltpu.VMEM((4096, 128), F32), pltpu.VMEM((4096, 128), F32)],
        flops=5 << 30,
    )(heights, turned, other_turned, cot, down, two_phase)
    came, inner = lax.optimization_barrier((came, inner))
    came_other = over_chan(came)

    share = -(-2752 // (devices * 16)) * 16
    place = jnp.stack([member, lax.axis_index("space")]).astype(jnp.int32)
    coarse, grad_pre, terms, faces = kernel_call(
        forward,
        (out(512, 128), out(4096, 128), out(devices, share + 16, 128), out(4, 256, 128)),
        [smem()] * 2 + [vmem()] * 9,
        [
            pltpu.VMEM((18, 288, 384), BF16),
            pltpu.VMEM((4096, 128), F32),
            pltpu.VMEM((4096, 128), F32),
            pltpu.VMEM((2048, 128), F32),
            pltpu.VMEM((18, 288, 256), BF16),
            pltpu.VMEM((128, 5120), BF16),
        ],
        flops=5 << 30,
    )(neighbours, place, laid, came, came_other, active, slope, inner, two_phase, down, cot)

    arrived = to_all(terms)
    sums = to_all(
        kernel_call(total, out(devices, share, 128), [vmem()])(arrived)
    )
    arrived_other = over_chan(arrived[:, share:])
    came_faces = jnp.stack([over_space(faces[i], i + 1) for i in range(4)])
    other_faces = over_chan(came_faces)
    grad_features = kernel_call(
        backward,
        out(8, 64, 512),
        [smem()] * 2 + [vmem()] * 7,
        [pltpu.VMEM((18, 288, 384), BF16)],
        flops=5 << 30,
    )(
        neighbours, place, grad_pre, arrived, arrived_other, came_faces, other_faces, active,
        four_phase,
    )

    grad_conv, grad_down = kernel_call(
        finish,
        (out(27, 64, 128, dtype=F32), out(8, 128, 128, dtype=F32)),
        [smem(), vmem()],
    )(member.reshape(1), sums.reshape(-1, 128))
    return coarse[None], grad_conv, grad_down, grad_features.transpose(0, 2, 1)


def solution(mesh):
    placed = (
        P("space", None, "chan"),
        P("space", None),
        P("space", None),
        P(),
        P(),
        P("space", None, None),
    )
    return jax.shard_map(
        local,
        mesh=mesh,
        in_specs=placed,
        out_specs=(
            P("space", None, "chan"),
            P(None, "chan", None),
            P(None, None, "chan"),
            P("space", None, "chan"),
        ),
        check_vma=False,
    )
```

```python
import jax
import jax.numpy as jnp
from jax import lax
from jax.experimental import pallas as pl
from jax.experimental.pallas import tpu as pltpu
from jax.sharding import PartitionSpec as P

OFFSETS = [
    (along_x, along_y, along_z)
    for along_x in (-1, 0, 1)
    for along_y in (-1, 0, 1)
    for along_z in (-1, 0, 1)
]
DIRECTIONS = [offset for offset in OFFSETS if offset != (0, 0, 0)]
FILL_ORDER = sorted(range(26), key=lambda k: (abs(DIRECTIONS[k][2]), k))
F32 = jnp.float32
BF16 = jnp.bfloat16


def vmem():
    return pl.BlockSpec(memory_space=pltpu.VMEM)


def smem():
    return pl.BlockSpec(memory_space=pltpu.SMEM)


def hbm():
    return pl.BlockSpec(memory_space=pltpu.HBM)


def kernel_call(body, outs, specs, out_specs, scratch=(), flops=0, mib=16):
    call = pl.pallas_call(
        body,
        out_shape=outs,
        in_specs=specs,
        out_specs=out_specs,
        scratch_shapes=list(scratch),
        compiler_params=pltpu.CompilerParams(vmem_limit_bytes=mib * 1024 * 1024),
        cost_estimate=pl.CostEstimate(flops=flops, bytes_accessed=1 << 22, transcendentals=0),
    )

    def run(*operands):
        placed = []
        for spec, operand in zip(specs, operands):
            if spec.memory_space == pltpu.HBM:
                operand = pltpu.with_memory_space_constraint(operand, pltpu.HBM)
            placed.append(operand)
        return call(*placed)

    return run


def start_all(pairs, arrived):
    copies = [
        pltpu.make_async_copy(source, target, arrived.at[i])
        for i, (source, target) in enumerate(pairs)
    ]
    for copy in copies:
        copy.start()
    return copies


def swap_halves(rows):
    return pltpu.roll(rows, 64, 1)


def low_lanes(rows):
    return lax.broadcasted_iota(jnp.int32, rows.shape, 1) < 64


def filled_voxels(heights_ref):
    columns = lax.broadcasted_iota(jnp.int32, (64, 512), 0)
    voxels = lax.broadcasted_iota(jnp.int32, (64, 512), 1)
    spread = (voxels // 8 == columns).astype(F32)
    tall = jnp.dot(heights_ref[...].astype(F32), spread, preferred_element_type=F32)
    level = lax.broadcasted_iota(jnp.int32, tall.shape, 1) % 8
    return (level.astype(F32) < tall).astype(F32)


def fill_slots(rows_ref, near_ref, slots_ref, start=0, faces=True):
    for k, (dx, dy, dz) in enumerate(DIRECTIONS):
        block = near_ref[0, k]
        xh = 7 if dx == 1 else 0
        y = 15 if dy == 1 else 0
        z = 15 if dz == 1 else 0
        if not faces and (dx, dy, dz).count(0) == 2:
            continue

        @pl.when(block >= 0)
        def _(dx=dx, dy=dy, dz=dz, xh=xh, y=y, z=z, block=block):
            zeros = [d == 0 for d in (dx, dy, dz)]
            if zeros == [False, True, True]:
                plane = rows_ref[xh * 256 : xh * 256 + 256, :]
                first, second = plane[:128], plane[128:]
                if dx == -1:
                    second = swap_halves(second)
                else:
                    first = swap_halves(first)
                region = jnp.where(low_lanes(first), first, second)
            elif zeros == [True, False, True]:
                region = jnp.concatenate(
                    [rows_ref[x * 256 + y * 16 : x * 256 + y * 16 + 16, :] for x in range(8)]
                )
            elif zeros == [True, True, False]:
                region = rows_ref[pl.ds(z, 128, stride=16), :]
            elif zeros == [False, False, True]:
                region = rows_ref[xh * 256 + y * 16 : xh * 256 + y * 16 + 16, :]
            elif zeros == [False, True, False]:
                region = rows_ref[pl.ds(xh * 256 + z, 16, stride=16), :]
            elif zeros == [True, False, False]:
                line = rows_ref[pl.ds(y * 16 + z, 8, stride=256), :]
                region = jnp.concatenate([line, line])
            else:
                at = xh * 256 + y * 16 + z
                region = jnp.broadcast_to(rows_ref[at : at + 1, :], (16, 128))
            slots_ref[block, start : start + region.shape[0], :] = region.astype(BF16)


def fill_faces(rows_ref, near_ref, place_ref, faces_ref):
    member, own = place_ref[0], place_ref[1]
    for k, (dx, dy, dz) in enumerate(DIRECTIONS):
        if (dx, dy, dz).count(0) != 2:
            continue
        block = near_ref[0, k]
        distance = jnp.where(member == 0, block - own, own - block)
        end = 15 if dx + dy + dz == 1 else 0

        @pl.when((block >= 0) & (distance >= 1))
        def _(dx=dx, dy=dy, end=end, distance=distance):
            if dx:
                region = rows_ref[end * 256 : end * 256 + 256, :]
            elif dy:
                region = jnp.concatenate(
                    [rows_ref[x * 256 + end * 16 : x * 256 + end * 16 + 16, :] for x in range(16)]
                )
            else:
                region = rows_ref[pl.ds(end, 256, stride=16), :]
            faces_ref[distance - 1] = region.astype(BF16)


def put_lines(padded_ref, places, rows):
    count = rows.shape[0]
    level = lax.broadcasted_iota(jnp.int32, rows.shape, 0) % 16
    below = jnp.where(level == 0, 0.0, pltpu.roll(rows, 1, 0)).astype(BF16)
    above = jnp.where(level == 15, 0.0, pltpu.roll(rows, count - 1, 0)).astype(BF16)
    here = rows.astype(BF16)
    at = 0
    for x, row, height in places:
        for j, part in enumerate((below, here, above)):
            padded_ref[x, row : row + height, j * 128 : j * 128 + 128] = part[at : at + height]
        at += height


def put_ends(padded_ref, x, row, rows, dz):
    lines = rows.shape[0]
    j = 0 if dz == -1 else 2
    end = 0 if dz == -1 else 15
    lanes = slice(j * 128, j * 128 + 128)
    old = padded_ref[x, row : row + 16 * lines, lanes].astype(F32).reshape(lines, 16, 128)
    level = lax.broadcasted_iota(jnp.int32, old.shape, 1)
    new = jnp.where(level == end, rows.reshape(lines, 1, 128), old)
    padded_ref[x, row : row + 16 * lines, lanes] = new.reshape(16 * lines, 128).astype(BF16)


def clear_margin(padded_ref):
    empty = jnp.zeros((288, 384), BF16)
    padded_ref[0] = empty
    padded_ref[17] = empty
    line = jnp.zeros((16, 384), BF16)
    for x in range(1, 17):
        padded_ref[x, 0:16, :] = line
        padded_ref[x, 272:288, :] = line


def put_region(padded_ref, offset, rows):
    dx, dy, dz = offset
    zeros = [d == 0 for d in offset]
    x = 17 if dx == 1 else 0
    y = 17 if dy == 1 else 0
    if zeros == [False, True, True]:
        put_lines(padded_ref, [(x, 16, 256)], rows)
    elif zeros == [True, False, True]:
        put_lines(padded_ref, [(at + 1, y * 16, 16) for at in range(16)], rows)
    elif zeros == [False, False, True]:
        put_lines(padded_ref, [(x, y * 16, 16)], rows)
    elif zeros == [True, True, False]:
        for at in range(16):
            put_ends(padded_ref, at + 1, 16, rows[at * 16 : at * 16 + 16], dz)
    elif zeros == [False, True, False]:
        put_ends(padded_ref, x, 16, rows, dz)
    elif zeros == [True, False, False]:
        for at in range(16):
            put_ends(padded_ref, at + 1, y * 16, rows[at : at + 1], dz)
    else:
        put_ends(padded_ref, x, y * 16, rows[0:1], dz)


def fill_margin(padded_ref, near_ref, own_ref, other_ref, start=0, faces=None):
    for k in FILL_ORDER:
        offset = DIRECTIONS[k]
        block = near_ref[0, k]
        face = offset.count(0) == 2
        if face and faces is not None:
            place_ref, own_faces_ref, other_faces_ref = faces
            member = place_ref[0]
            away = place_ref[1] - block
            here = jnp.where(away > 0, 0, 1) == member
            slot = jnp.abs(away) - 1

            @pl.when((block >= 0) & here)
            def _(offset=offset, slot=slot):
                put_region(padded_ref, offset, own_faces_ref[slot].astype(F32))

            @pl.when((block >= 0) & jnp.logical_not(here))
            def _(offset=offset, slot=slot):
                rows = swap_halves(other_faces_ref[slot].astype(F32))
                put_region(padded_ref, offset, rows)

            continue

        @pl.when(block >= 0)
        def _(offset=offset, block=block, face=face):
            height = 128 if face else 16
            own = own_ref[block, start : start + height, :].astype(F32)
            other = other_ref[block, 0:height, :].astype(F32)
            first = jnp.where(low_lanes(own), own, swap_halves(other))
            second = jnp.where(low_lanes(own), swap_halves(own), other)
            if face:
                rows = jnp.concatenate([first, second])
            elif offset[0] == 0:
                rows = jnp.concatenate([first[:8], second[:8]])
            else:
                rows = first if offset[0] == 1 else second
            put_region(padded_ref, offset, rows)


def send_features(
    near_hbm, heights_hbm, features_hbm, slots_ref,
    near_ref, heights_ref, features_ref, rows_ref, arrived
):
    copies = [
        pltpu.make_async_copy(near_hbm, near_ref, arrived.at[8]),
        pltpu.make_async_copy(heights_hbm, heights_ref, arrived.at[9]),
    ]
    order = (0, 1, 2, 3, 4, 5, 6, 7)
    bricks = [
        pltpu.make_async_copy(features_hbm.at[i], features_ref.at[i], arrived.at[i]) for i in order
    ]
    for copy in copies + bricks:
        copy.start()
    copies[1].wait()
    filled = filled_voxels(heights_ref)
    for oz in range(2):
        for oy in range(2):
            pair = []
            for ox in range(2):
                brick = ox + 2 * oy + 4 * oz
                bricks[brick].wait()
                pair.append(features_ref[brick].astype(F32) * filled[brick : brick + 1])
            turned = jnp.concatenate(pair).T
            for vx in range(8):
                for vy in range(8):
                    at = vx * 256 + (8 * oy + vy) * 16 + 8 * oz
                    source = (vx * 8 + vy) * 8
                    rows_ref[at : at + 8, :] = turned[source : source + 8]
    copies[0].wait()
    fill_slots(rows_ref, near_ref, slots_ref)


def weights(shift, conv_ref, down_in_ref, cot_in_ref, two_ref, four_ref, down_ref, cot_ref):
    empty = jnp.zeros((128, 128), BF16)
    for yz in range(9):
        taps = []
        for ex in range(3):
            tap = conv_ref[ex * 9 + yz].astype(F32)
            taps.append(pltpu.roll(pltpu.roll(tap, shift, 0), shift, 1))
        whole = [empty] + [tap.astype(BF16) for tap in taps] + [empty]
        for p in range(4):
            rows = slice((p * 9 + yz) * 128, (p * 9 + yz) * 128 + 128)
            two_ref[rows, 0:128] = whole[p + 1] if p < 3 else empty
            two_ref[rows, 128:256] = whole[p]
        none = jnp.zeros((64, 128), F32)
        own = [none] + [taps[2 - ex][:64] for ex in range(3)] + [none]
        pairs = [jnp.concatenate([own[i + 1], own[i]]).T.astype(BF16) for i in range(4)]
        for p in range(6):
            at = (p * 9 + 8 - yz) * 128
            four_ref[at : at + 128, 0:128] = pairs[p] if p < 4 else empty
            four_ref[at : at + 128, 128:256] = pairs[p - 2] if p >= 2 else empty
    for tap in range(8):
        rows = down_in_ref[tap].astype(F32)
        rows = pltpu.roll(rows, shift, 0)
        down_ref[tap * 128 : tap * 128 + 128, :] = pltpu.roll(rows, 2 * shift, 1).astype(BF16)
    cot_ref[...] = pltpu.roll(cot_in_ref[...].astype(F32), 2 * shift, 1).astype(BF16)


def prepare(
    place_ref, conv_hbm, down_hbm, cot_hbm, heights_hbm, own_hbm, other_hbm,
    lanes_hbm, active_hbm, slope_hbm, inner_hbm, taps_hbm, four_hbm, down_out_hbm, cot_out_hbm,
    conv_in_ref, down_in_ref, cot_in_ref, heights_ref, own_ref, other_ref,
    two_ref, four_ref, down_ref, cot_ref, padded_ref, rows_ref, mask_ref, lanes_ref, active_ref,
    slope_ref, inner_ref, arrived, left, left_inner
):
    came = start_all(
        [
            (conv_hbm, conv_in_ref),
            (down_hbm, down_in_ref),
            (cot_hbm, cot_in_ref),
            (heights_hbm, heights_ref),
            (own_hbm, own_ref),
            (other_hbm, other_ref),
        ],
        arrived,
    )
    gone = [
        pltpu.make_async_copy(source, target, left.at[i])
        for i, (source, target) in enumerate(
            [
                (two_ref.at[0:3456, 0:128], taps_hbm),
                (four_ref, four_hbm),
                (down_ref, down_out_hbm),
                (cot_ref, cot_out_hbm),
                (lanes_ref, lanes_hbm),
                (active_ref, active_hbm),
                (slope_ref, slope_hbm),
            ]
        )
    ]
    for copy in came[:3]:
        copy.wait()
    weights(
        place_ref[0] * 64, conv_in_ref, down_in_ref, cot_in_ref, two_ref, four_ref, down_ref, cot_ref
    )
    for copy in gone[:4]:
        copy.start()
    for copy in came[3:]:
        copy.wait()
    filled = filled_voxels(heights_ref)
    upright = filled.T
    for brick in range(8):
        ox, oy, oz = brick % 2, brick // 2 % 2, brick // 4
        both = jnp.concatenate([own_ref[brick].astype(F32), other_ref[brick].astype(F32)])
        turned = (both * filled[brick : brick + 1]).T
        mask = jnp.broadcast_to(upright[:, brick : brick + 1], (512, 128))
        for vx in range(8):
            for vy in range(8):
                at = (8 * ox + vx) * 256 + (8 * oy + vy) * 16 + 8 * oz
                source = (vx * 8 + vy) * 8
                rows_ref[at : at + 8, :] = turned[source : source + 8]
                mask_ref[at : at + 8, :] = mask[source : source + 8]
    clear_margin(padded_ref)
    for x in range(16):
        put_lines(padded_ref, [(x + 1, 16, 256)], rows_ref[x * 256 : x * 256 + 256, :])
        active_ref[x * 256 : x * 256 + 256, :] = mask_ref[x * 256 : x * 256 + 256, :].astype(BF16)
    for x in range(18):
        below = padded_ref[x, :, 0:128].astype(F32)
        here = padded_ref[x, :, 128:256].astype(F32)
        both = jnp.where(low_lanes(below), below, swap_halves(here))
        lanes_ref[x, :, 0:128] = both.astype(BF16)
        lanes_ref[x, :, 128:256] = padded_ref[x, :, 256:384]
    gone[4].start()
    gone[5].start()
    for tap in range(8):
        tx, ty, tz = tap // 4, tap // 2 % 2, tap % 2
        part = lax.dot_general(
            cot_ref[...],
            down_ref[tap * 128 : tap * 128 + 128, :],
            (((1,), (1,)), ((), ())),
            preferred_element_type=F32,
        )
        for ux in range(8):
            for uy in range(8):
                at = (2 * ux + tx) * 256 + (2 * uy + ty) * 16 + tz
                source = (ux * 8 + uy) * 8
                rows = pl.ds(at, 8, stride=2)
                slope_ref[rows, :] = part[source : source + 8] * mask_ref[rows, :]
    gone[6].start()

    def leave(group):
        rows = pl.ds(pl.multiple_of(group * 1024, 1024), 1024)
        return pltpu.make_async_copy(
            inner_ref.at[rows], inner_hbm.at[rows], left_inner.at[group]
        )


    def step(group, carry):
        lhs = []
        for pair in range(2):
            pieces = []
            for p in range(4):
                for ey in range(3):
                    pieces.append(
                        padded_ref[group * 4 + pair * 2 + p, ey * 16 : ey * 16 + 256, :]
                    )
            lhs.append(jnp.concatenate(pieces, axis=1))
        summed = jnp.dot(jnp.concatenate(lhs), two_ref[...], preferred_element_type=F32)
        for pair in range(2):
            for phase in range(2):
                at = pl.multiple_of((group * 4 + pair * 2 + phase) * 256, 256)
                inner_ref[pl.ds(at, 256), :] = summed[
                    pair * 256 : pair * 256 + 256, phase * 128 : phase * 128 + 128
                ]
        leave(group).start()
        return carry

    lax.fori_loop(0, 4, step, 0)
    for copy in gone:
        copy.wait()
    for group in range(4):
        leave(group).wait()


def add_margin(padded_ref, near_ref, own_ref, other_ref, taps_ref, pre_ref):
    def tap(ex, ey, ez):
        at = ((ex * 3 + ey) * 3 + ez) * 128
        return taps_ref[at : at + 128, :]

    for x, ex in ((0, 0), (17, 2)):
        lhs = jnp.concatenate(
            [padded_ref[x, ey * 16 : ey * 16 + 256, :] for ey in range(3)], axis=1
        )
        rhs = taps_ref[ex * 1152 : ex * 1152 + 1152, :]
        at = 0 if x == 0 else 15 * 256
        pre_ref[at : at + 256, :] += jnp.dot(lhs, rhs, preferred_element_type=F32)
    none = jnp.zeros((16, 384), BF16)
    for y, ey in ((0, 0), (17, 2)):
        lhs = jnp.concatenate(
            [
                jnp.concatenate(
                    [
                        padded_ref[x + ex, y * 16 : y * 16 + 16, :] if 1 <= x + ex <= 16 else none
                        for x in range(16)
                    ]
                )
                for ex in range(3)
            ],
            axis=1,
        )
        rhs = jnp.concatenate([tap(ex, ey, ez) for ex in range(3) for ez in range(3)])
        added = jnp.dot(lhs, rhs, preferred_element_type=F32)
        for x in range(16):
            at = x * 256 + (0 if y == 0 else 240)
            pre_ref[at : at + 16, :] += added[x * 16 : x * 16 + 16]
    for k in (DIRECTIONS.index((0, 0, -1)), DIRECTIONS.index((0, 0, 1))):
        block = near_ref[0, k]
        ez = 0 if DIRECTIONS[k][2] == -1 else 2

        @pl.when(block >= 0)
        def _(block=block, ez=ez):
            own = own_ref[block].astype(F32)
            other = other_ref[block].astype(F32)
            face = jnp.concatenate(
                [
                    jnp.where(low_lanes(own), own, swap_halves(other)),
                    jnp.where(low_lanes(own), swap_halves(own), other),
                ]
            )
            line = lax.broadcasted_iota(jnp.int32, face.shape, 0) % 16
            shifted = [
                jnp.where(line == 0, 0.0, pltpu.roll(face, 1, 0)),
                face,
                jnp.where(line == 15, 0.0, pltpu.roll(face, 255, 0)),
            ]
            border = jnp.zeros((16, 128), F32)
            lhs = []
            for ex in range(3):
                for part in shifted:
                    if ex == 0:
                        part = jnp.concatenate([border, part[:240]])
                    elif ex == 2:
                        part = jnp.concatenate([part[16:], border])
                    lhs.append(part.astype(BF16))
            rhs = jnp.concatenate([tap(ex, ey, ez) for ex in range(3) for ey in range(3)])
            added = jnp.dot(jnp.concatenate(lhs, axis=1), rhs, preferred_element_type=F32)
            rows = pl.ds(0 if ez == 0 else 15, 256, stride=16)
            pre_ref[rows, :] = pre_ref[rows, :] + added


def forward(
    near_ref, place_ref, own_ref, other_ref,
    lanes_hbm, active_hbm, slope_hbm, inner_hbm, taps_hbm, down_hbm, cot_hbm,
    slots_ref, faces_ref, coarse_hbm, grad_pre_hbm,
    padded_ref, pre_ref, grad_ref, packed_ref, turned_ref, lanes_ref, active_ref, slope_ref,
    taps_ref, down_ref, cot_ref, coarse_ref, grad_pre_ref, arrived, left
):
    came = start_all(
        [
            (taps_hbm, taps_ref),
            (inner_hbm, pre_ref),
            (active_hbm, active_ref),
            (slope_hbm, slope_ref),
            (lanes_hbm, lanes_ref),
            (down_hbm, down_ref),
            (cot_hbm, cot_ref),
        ],
        arrived,
    )
    padded_ref[...] = jnp.zeros(padded_ref.shape, BF16)
    fill_margin(padded_ref, near_ref, own_ref, other_ref)
    came[0].wait()
    came[1].wait()
    add_margin(padded_ref, near_ref, own_ref, other_ref, taps_ref, pre_ref)
    came[2].wait()
    came[3].wait()

    turned_ref[:, 0:512] = jnp.zeros((128, 512), BF16)
    turned_ref[:, 4608:5120] = jnp.zeros((128, 512), BF16)
    for x in range(16):
        rows = slice(x * 256, x * 256 + 256)
        pre = pre_ref[rows, :] * active_ref[rows, :].astype(F32)
        sigmoid = 1.0 / (1.0 + jnp.exp(-pre))
        pre_ref[rows, :] = pre * sigmoid
        grad = slope_ref[rows, :] * sigmoid * (1.0 + pre * (1.0 - sigmoid))
        grad_ref[rows, :] = grad
        grad_pre_ref[rows, :] = grad.astype(BF16)
        turned_ref[:, 512 + x * 256 : 768 + x * 256] = grad.T.astype(BF16)

    gone = [
        pltpu.make_async_copy(grad_pre_ref, grad_pre_hbm, left.at[0]),
        pltpu.make_async_copy(coarse_ref, coarse_hbm, left.at[1]),
    ]
    gone[0].start()
    fill_faces(grad_ref, near_ref, place_ref, faces_ref)
    share = slots_ref.shape[1] - 16
    for x in range(8):
        low = grad_ref[x * 256 : x * 256 + 256, :]
        high = grad_ref[2048 + x * 256 : 2048 + x * 256 + 256, :]
        packed_ref[x * 256 : x * 256 + 256, :] = jnp.where(
            low_lanes(low), low, swap_halves(high)
        )
    fill_slots(packed_ref, near_ref, slots_ref, share, faces=False)

    def put_terms(at, rows):
        while rows.shape[0]:
            owner, row = at // share, at % share
            count = min(rows.shape[0], share - row)
            slots_ref[owner, row : row + count, :] = rows[:count]
            rows = rows[count:]
            at += count

    came[4].wait()
    for x in range(18):
        below = padded_ref[x, :, 0:128].astype(F32)
        here = padded_ref[x, :, 128:256].astype(F32)
        both = jnp.where(low_lanes(below), below, swap_halves(here))
        lanes_ref[x, :, 0:128] += both.astype(BF16)
        lanes_ref[x, :, 128:256] += padded_ref[x, :, 256:384]
    lhs = jnp.concatenate(
        [turned_ref[:, (2 - ex) * 256 : (2 - ex) * 256 + 4608] for ex in range(3)]
    )
    for ey in range(3):
        rhs = lanes_ref[:, ey * 16 : ey * 16 + 256, :].reshape(4608, 256)
        summed = jnp.dot(lhs, rhs, preferred_element_type=F32)
        for ex in range(3):
            part = summed[ex * 128 : ex * 128 + 128].T
            put_terms((ex * 3 + ey) * 192, part[0:192].astype(BF16))

    came[5].wait()
    came[6].wait()
    patches = []
    for tap in range(8):
        tx, ty, tz = tap // 4, tap // 2 % 2, tap % 2
        pieces = []
        for ux in range(8):
            for uy in range(8):
                at = (2 * ux + tx) * 256 + (2 * uy + ty) * 16 + tz
                pieces.append(pre_ref[pl.ds(at, 8, stride=2), :])
        patches.append(jnp.concatenate(pieces).astype(BF16))
    patches = jnp.concatenate(patches, axis=1)
    coarse = jnp.dot(patches, down_ref[...], preferred_element_type=F32)
    coarse_ref[...] = coarse[:, :128].astype(BF16)
    gone[1].start()
    own_cot = cot_ref[:, 0:128].astype(F32).T.astype(BF16)
    grad_down = jnp.dot(own_cot, patches, preferred_element_type=F32)
    for tap in range(8):
        part = grad_down[:, tap * 128 : tap * 128 + 128].T
        put_terms(1728 + tap * 128, part.astype(BF16))
    for copy in gone:
        copy.wait()


def total(slots_ref, out_ref):
    devices, share, _ = out_ref.shape
    summed = slots_ref[0, 0:share, :].astype(F32)
    for device in range(1, devices):
        summed = summed + slots_ref[device, 0:share, :].astype(F32)
    summed = (summed / devices).astype(BF16)
    for device in range(devices):
        out_ref[device] = summed


def backward(
    near_ref, place_ref, own_ref, other_ref, own_faces_ref, other_faces_ref,
    grad_pre_hbm, active_hbm, back_hbm, out_ref,
    padded_ref, grad_pre_ref, active_ref, back_ref, arrived
):
    came = start_all(
        [(grad_pre_hbm, grad_pre_ref), (back_hbm, back_ref), (active_hbm, active_ref)], arrived
    )
    clear_margin(padded_ref)
    came[0].wait()
    for x in range(16):
        rows = grad_pre_ref[x * 256 : x * 256 + 256, :].astype(F32)
        put_lines(padded_ref, [(x + 1, 16, 256)], rows)
    fill_margin(
        padded_ref, near_ref, own_ref, other_ref, own_ref.shape[1] - 16,
        (place_ref, own_faces_ref, other_faces_ref),
    )
    came[1].wait()
    came[2].wait()
    for half in range(2):
        lhs = []
        for quad in range(2):
            pieces = []
            for p in range(6):
                for ey in range(3):
                    pieces.append(
                        padded_ref[half * 8 + quad * 4 + p, ey * 16 : ey * 16 + 256, :]
                    )
            lhs.append(jnp.concatenate(pieces, axis=1))
        summed = jnp.dot(jnp.concatenate(lhs), back_ref[...], preferred_element_type=F32)
        for quad in range(2):
            for two in range(2):
                part = summed[quad * 256 : quad * 256 + 256, two * 128 : two * 128 + 128]
                x = half * 8 + quad * 4 + two * 2
                even = active_ref[x * 256 : x * 256 + 256, :].astype(F32)
                odd = active_ref[x * 256 + 256 : x * 256 + 512, :].astype(F32)
                part = part * jnp.where(low_lanes(part), even, odd)
                for oy in range(2):
                    rows = [
                        part[(8 * oy + vy) * 16 + 8 * oz : (8 * oy + vy) * 16 + 8 * oz + 8]
                        for oz in range(2)
                        for vy in range(8)
                    ]
                    turned = jnp.concatenate(rows).T
                    first, second = turned[:64], turned[64:]
                    lanes = slice(x % 8 * 64, x % 8 * 64 + 128)
                    brick = half + 2 * oy
                    near = jnp.where(low_lanes(first), first, swap_halves(second))
                    far = jnp.where(low_lanes(first), swap_halves(first), second)
                    out_ref[brick, :, lanes] = near.astype(BF16)
                    out_ref[brick + 4, :, lanes] = far.astype(BF16)


def finish(place_ref, sums_ref, conv_ref, down_ref):
    shift = place_ref[0] * 64
    for tap in range(27):
        rows = sums_ref[tap * 64 : tap * 64 + 64, :].astype(F32)
        conv_ref[tap] = pltpu.roll(rows, shift, 1)
    for tap in range(8):
        rows = sums_ref[1728 + tap * 128 : 1728 + tap * 128 + 128, :].astype(F32)
        down_ref[tap, pl.ds(shift, 64), :] = rows[:64]
        down_ref[tap, pl.ds(64 - shift, 64), :] = rows[64:]


def over_space(block, distance):
    blocks = range(lax.axis_size("space"))
    route = [(2 * i, 2 * (i + distance)) for i in blocks if i + distance in blocks]
    route += [(2 * i + 1, 2 * (i - distance) + 1) for i in blocks if i - distance in blocks]
    return lax.ppermute(block, ("space", "chan"), route)


def over_chan(block):
    return lax.ppermute(block, "chan", [(0, 1), (1, 0)])


def to_all(slots):
    return lax.all_to_all(slots, "space", 0, 0, tiled=True)


def local(features, heights, neighbours, w_conv, w_down, cotangent):
    devices = lax.axis_size("space")
    member = lax.axis_index("chan")

    def out(*shape, dtype=BF16):
        return jax.ShapeDtypeStruct(shape, dtype)

    def held_out(*shape, dtype=BF16):
        return pltpu.HBM(shape, dtype)

    def memory(*shape, dtype=BF16):
        return pltpu.VMEM(shape, dtype)

    def copies(count):
        return pltpu.SemaphoreType.DMA((count,))

    place = jnp.stack([member, lax.axis_index("space")]).astype(jnp.int32)
    turned = features.transpose(0, 2, 1)
    slots = kernel_call(
        send_features,
        out(devices, 128, 128),
        [hbm()] * 3,
        vmem(),
        [
            pltpu.SMEM(neighbours.shape, jnp.int32),
            memory(8, 64, dtype=jnp.int32),
            memory(8, 64, 512),
            memory(2048, 128, dtype=F32),
            copies(10),
        ],
    )(neighbours, heights, turned)
    came = to_all(slots)
    other_turned = over_chan(turned)

    held = [
        held_out(18, 288, 256),
        held_out(4096, 128),
        held_out(4096, 128, dtype=F32),
        held_out(4096, 128, dtype=F32),
        held_out(3456, 128),
        held_out(6912, 256),
        held_out(1024, 256),
        held_out(512, 256),
    ]
    lanes, active, slope, inner, taps, four_phase, down, cot = kernel_call(
        prepare,
        held,
        [smem()] + [hbm()] * 5 + [pl.BlockSpec(memory_space=pl.ANY)],
        [hbm()] * 8,
        [
            memory(27, 128, 128),
            memory(8, 128, 256),
            memory(512, 256),
            memory(8, 64, dtype=jnp.int32),
            memory(8, 64, 512),
            memory(8, 64, 512),
            memory(4608, 256),
            memory(6912, 256),
            memory(1024, 256),
            memory(512, 256),
            memory(18, 288, 384),
            memory(4096, 128, dtype=F32),
            memory(4096, 128, dtype=F32),
            memory(18, 288, 256),
            memory(4096, 128),
            memory(4096, 128, dtype=F32),
            memory(4096, 128, dtype=F32),
            copies(6),
            copies(7),
            copies(4),
        ],
        flops=5 << 30,
        mib=36,
    )(place, w_conv, w_down, cotangent[0], heights, turned, other_turned)
    came, inner = lax.optimization_barrier((came, inner))
    came_other = over_chan(came)

    share = -(-2752 // (devices * 16)) * 16
    terms, faces, coarse, grad_pre = kernel_call(
        forward,
        [
            out(devices, share + 16, 128),
            out(4, 256, 128),
            held_out(512, 128),
            held_out(4096, 128),
        ],
        [smem()] * 2 + [vmem()] * 2 + [hbm()] * 7,
        [vmem()] * 2 + [hbm()] * 2,
        [
            memory(18, 288, 384),
            memory(4096, 128, dtype=F32),
            memory(4096, 128, dtype=F32),
            memory(2048, 128, dtype=F32),
            memory(128, 5120),
            memory(18, 288, 256),
            memory(4096, 128),
            memory(4096, 128, dtype=F32),
            memory(3456, 128),
            memory(1024, 256),
            memory(512, 256),
            memory(512, 128),
            memory(4096, 128),
            copies(7),
            copies(2),
        ],
        flops=5 << 30,
        mib=32,
    )(
        neighbours, place, came, came_other, lanes, active, slope, inner, taps, down, cot
    )

    arrived = to_all(terms)
    came_faces = jnp.stack([over_space(faces[i], i + 1) for i in range(4)])
    other_faces = over_chan(came_faces)
    arrived, came_faces, other_faces = lax.optimization_barrier(
        (arrived, came_faces, other_faces)
    )
    sums = to_all(
        kernel_call(total, out(devices, share, 128), [vmem()], vmem())(arrived)
    )
    arrived_other = over_chan(arrived[:, share:])
    grad_features = kernel_call(
        backward,
        out(8, 64, 512),
        [smem()] * 2 + [vmem()] * 4 + [hbm()] * 3,
        vmem(),
        [
            memory(18, 288, 384),
            memory(4096, 128),
            memory(4096, 128),
            memory(6912, 256),
            copies(3),
        ],
        flops=5 << 30,
        mib=24,
    )(
        neighbours, place, arrived, arrived_other, came_faces, other_faces, grad_pre, active,
        four_phase,
    )

    grad_conv, grad_down = kernel_call(
        finish,
        [out(27, 64, 128, dtype=F32), out(8, 128, 128, dtype=F32)],
        [smem(), vmem()],
        [vmem()] * 2,
    )(place, sums.reshape(-1, 128))
    return coarse[None], grad_conv, grad_down, grad_features.transpose(0, 2, 1)


def solution(mesh):
    placed = (
        P("space", None, "chan"),
        P("space", None),
        P("space", None),
        P(),
        P(),
        P("space", None, None),
    )
    return jax.shard_map(
        local,
        mesh=mesh,
        in_specs=placed,
        out_specs=(
            P("space", None, "chan"),
            P(None, "chan", None),
            P(None, None, "chan"),
            P("space", None, "chan"),
        ),
        check_vma=False,
    )
```

```python
import jax
import jax.numpy as jnp
from jax import lax
from jax.experimental import pallas as pl
from jax.experimental.pallas import tpu as pltpu
from jax.sharding import PartitionSpec as P

OFFSETS = [
    (along_x, along_y, along_z)
    for along_x in (-1, 0, 1)
    for along_y in (-1, 0, 1)
    for along_z in (-1, 0, 1)
]
DIRECTIONS = [offset for offset in OFFSETS if offset != (0, 0, 0)]
FILL_ORDER = sorted(range(26), key=lambda k: (abs(DIRECTIONS[k][2]), k))
F32 = jnp.float32
BF16 = jnp.bfloat16


def vmem():
    return pl.BlockSpec(memory_space=pltpu.VMEM)


def smem():
    return pl.BlockSpec(memory_space=pltpu.SMEM)


def hbm():
    return pl.BlockSpec(memory_space=pltpu.HBM)


def kernel_call(body, outs, specs, out_specs, scratch=(), flops=0, mib=16):
    call = pl.pallas_call(
        body,
        out_shape=outs,
        in_specs=specs,
        out_specs=out_specs,
        scratch_shapes=list(scratch),
        compiler_params=pltpu.CompilerParams(vmem_limit_bytes=mib * 1024 * 1024),
        cost_estimate=pl.CostEstimate(flops=flops, bytes_accessed=1 << 22, transcendentals=0),
    )

    def run(*operands):
        placed = []
        for spec, operand in zip(specs, operands):
            if spec.memory_space == pltpu.HBM:
                operand = pltpu.with_memory_space_constraint(operand, pltpu.HBM)
            placed.append(operand)
        return call(*placed)

    return run


def start_all(pairs, arrived):
    copies = [
        pltpu.make_async_copy(source, target, arrived.at[i])
        for i, (source, target) in enumerate(pairs)
    ]
    for copy in copies:
        copy.start()
    return copies


def swap_halves(rows):
    return pltpu.roll(rows, 64, 1)


def low_lanes(rows):
    return lax.broadcasted_iota(jnp.int32, rows.shape, 1) < 64


def filled_voxels(heights_ref):
    columns = lax.broadcasted_iota(jnp.int32, (64, 512), 0)
    voxels = lax.broadcasted_iota(jnp.int32, (64, 512), 1)
    spread = (voxels // 8 == columns).astype(F32)
    tall = jnp.dot(heights_ref[...].astype(F32), spread, preferred_element_type=F32)
    level = lax.broadcasted_iota(jnp.int32, tall.shape, 1) % 8
    return (level.astype(F32) < tall).astype(F32)


def fill_slots(rows_ref, near_ref, slots_ref, start=0, faces=True):
    for k, (dx, dy, dz) in enumerate(DIRECTIONS):
        block = near_ref[0, k]
        xh = 7 if dx == 1 else 0
        y = 15 if dy == 1 else 0
        z = 15 if dz == 1 else 0
        if not faces and (dx, dy, dz).count(0) == 2:
            continue

        @pl.when(block >= 0)
        def _(dx=dx, dy=dy, dz=dz, xh=xh, y=y, z=z, block=block):
            zeros = [d == 0 for d in (dx, dy, dz)]
            if zeros == [False, True, True]:
                plane = rows_ref[xh * 256 : xh * 256 + 256, :]
                first, second = plane[:128], plane[128:]
                if dx == -1:
                    second = swap_halves(second)
                else:
                    first = swap_halves(first)
                region = jnp.where(low_lanes(first), first, second)
            elif zeros == [True, False, True]:
                region = jnp.concatenate(
                    [rows_ref[x * 256 + y * 16 : x * 256 + y * 16 + 16, :] for x in range(8)]
                )
            elif zeros == [True, True, False]:
                region = rows_ref[pl.ds(z, 128, stride=16), :]
            elif zeros == [False, False, True]:
                region = rows_ref[xh * 256 + y * 16 : xh * 256 + y * 16 + 16, :]
            elif zeros == [False, True, False]:
                region = rows_ref[pl.ds(xh * 256 + z, 16, stride=16), :]
            elif zeros == [True, False, False]:
                line = rows_ref[pl.ds(y * 16 + z, 8, stride=256), :]
                region = jnp.concatenate([line, line])
            else:
                at = xh * 256 + y * 16 + z
                region = jnp.broadcast_to(rows_ref[at : at + 1, :], (16, 128))
            slots_ref[block, start : start + region.shape[0], :] = region.astype(BF16)


def fill_faces(rows_ref, near_ref, place_ref, faces_ref):
    member, own = place_ref[0], place_ref[1]
    for k, (dx, dy, dz) in enumerate(DIRECTIONS):
        if (dx, dy, dz).count(0) != 2:
            continue
        block = near_ref[0, k]
        distance = jnp.where(member == 0, block - own, own - block)
        end = 15 if dx + dy + dz == 1 else 0

        @pl.when((block >= 0) & (distance >= 1))
        def _(dx=dx, dy=dy, end=end, distance=distance):
            if dx:
                region = rows_ref[end * 256 : end * 256 + 256, :]
            elif dy:
                region = jnp.concatenate(
                    [rows_ref[x * 256 + end * 16 : x * 256 + end * 16 + 16, :] for x in range(16)]
                )
            else:
                region = rows_ref[pl.ds(end, 256, stride=16), :]
            faces_ref[distance - 1] = region.astype(BF16)


class Whole:
    def __init__(self, ref):
        self.ref = ref

    def at(self, x, row, height):
        return self.ref, x, row


class Margin:
    def __init__(self, planes_ref, lines_ref):
        self.planes_ref, self.lines_ref = planes_ref, lines_ref

    def at(self, x, row, height):
        if x in (0, 17):
            return self.planes_ref, x // 17, row
        return self.lines_ref, row // 272, (x - 1) * 16


def put_lines(padded, places, rows):
    count = rows.shape[0]
    level = lax.broadcasted_iota(jnp.int32, rows.shape, 0) % 16
    below = jnp.where(level == 0, 0.0, pltpu.roll(rows, 1, 0)).astype(BF16)
    above = jnp.where(level == 15, 0.0, pltpu.roll(rows, count - 1, 0)).astype(BF16)
    here = rows.astype(BF16)
    at = 0
    for x, row, height in places:
        ref, plane, first = padded.at(x, row, height)
        for j, part in enumerate((below, here, above)):
            ref[plane, first : first + height, j * 128 : j * 128 + 128] = part[at : at + height]
        at += height


def put_ends(padded, x, row, rows, dz):
    lines = rows.shape[0]
    j = 0 if dz == -1 else 2
    end = 0 if dz == -1 else 15
    lanes = slice(j * 128, j * 128 + 128)
    ref, plane, first = padded.at(x, row, 16 * lines)
    span = slice(first, first + 16 * lines)
    old = ref[plane, span, lanes].astype(F32).reshape(lines, 16, 128)
    level = lax.broadcasted_iota(jnp.int32, old.shape, 1)
    new = jnp.where(level == end, rows.reshape(lines, 1, 128), old)
    ref[plane, span, lanes] = new.reshape(16 * lines, 128).astype(BF16)


def clear_margin(padded_ref):
    empty = jnp.zeros((288, 384), BF16)
    padded_ref[0] = empty
    padded_ref[17] = empty
    line = jnp.zeros((16, 384), BF16)
    for x in range(1, 17):
        padded_ref[x, 0:16, :] = line
        padded_ref[x, 272:288, :] = line


def put_region(padded, offset, rows):
    dx, dy, dz = offset
    zeros = [d == 0 for d in offset]
    x = 17 if dx == 1 else 0
    y = 17 if dy == 1 else 0
    if zeros == [False, True, True]:
        put_lines(padded, [(x, 16, 256)], rows)
    elif zeros == [True, False, True]:
        put_lines(padded, [(at + 1, y * 16, 16) for at in range(16)], rows)
    elif zeros == [False, False, True]:
        put_lines(padded, [(x, y * 16, 16)], rows)
    elif zeros == [True, True, False]:
        for at in range(16):
            put_ends(padded, at + 1, 16, rows[at * 16 : at * 16 + 16], dz)
    elif zeros == [False, True, False]:
        put_ends(padded, x, 16, rows, dz)
    elif zeros == [True, False, False]:
        for at in range(16):
            put_ends(padded, at + 1, y * 16, rows[at : at + 1], dz)
    else:
        put_ends(padded, x, y * 16, rows[0:1], dz)


def fill_margin(padded, near_ref, own_ref, other_ref, start=0, faces=None, z_faces=True):
    for k in FILL_ORDER:
        offset = DIRECTIONS[k]
        block = near_ref[0, k]
        face = offset.count(0) == 2
        if face and offset[2] and not z_faces:
            continue
        if face and faces is not None:
            place_ref, own_faces_ref, other_faces_ref = faces
            member = place_ref[0]
            away = place_ref[1] - block
            here = jnp.where(away > 0, 0, 1) == member
            slot = jnp.abs(away) - 1

            @pl.when((block >= 0) & here)
            def _(offset=offset, slot=slot):
                put_region(padded, offset, own_faces_ref[slot].astype(F32))

            @pl.when((block >= 0) & jnp.logical_not(here))
            def _(offset=offset, slot=slot):
                rows = swap_halves(other_faces_ref[slot].astype(F32))
                put_region(padded, offset, rows)

            continue

        @pl.when(block >= 0)
        def _(offset=offset, block=block, face=face):
            height = 128 if face else 16
            own = own_ref[block, start : start + height, :].astype(F32)
            other = other_ref[block, 0:height, :].astype(F32)
            first = jnp.where(low_lanes(own), own, swap_halves(other))
            second = jnp.where(low_lanes(own), swap_halves(own), other)
            if face:
                rows = jnp.concatenate([first, second])
            elif offset[0] == 0:
                rows = jnp.concatenate([first[:8], second[:8]])
            else:
                rows = first if offset[0] == 1 else second
            put_region(padded, offset, rows)


def send_features(
    near_hbm, heights_hbm, features_hbm, slots_ref,
    near_ref, heights_ref, features_ref, rows_ref, arrived
):
    copies = [
        pltpu.make_async_copy(near_hbm, near_ref, arrived.at[8]),
        pltpu.make_async_copy(heights_hbm, heights_ref, arrived.at[9]),
    ]
    order = (0, 1, 2, 3, 4, 5, 6, 7)
    bricks = [
        pltpu.make_async_copy(features_hbm.at[i], features_ref.at[i], arrived.at[i]) for i in order
    ]
    for copy in copies + bricks:
        copy.start()
    copies[1].wait()
    filled = filled_voxels(heights_ref)
    for oz in range(2):
        for oy in range(2):
            pair = []
            for ox in range(2):
                brick = ox + 2 * oy + 4 * oz
                bricks[brick].wait()
                pair.append(features_ref[brick].astype(F32) * filled[brick : brick + 1])
            turned = jnp.concatenate(pair).T
            for vx in range(8):
                for vy in range(8):
                    at = vx * 256 + (8 * oy + vy) * 16 + 8 * oz
                    source = (vx * 8 + vy) * 8
                    rows_ref[at : at + 8, :] = turned[source : source + 8]
    copies[0].wait()
    fill_slots(rows_ref, near_ref, slots_ref)


def own_first_taps(shift, conv_ref, yz):
    taps = []
    for ex in range(3):
        tap = conv_ref[ex * 9 + yz].astype(F32)
        taps.append(pltpu.roll(pltpu.roll(tap, shift, 0), shift, 1))
    return taps


def forward_weights(shift, conv_ref, down_in_ref, cot_in_ref, two_ref, down_ref, cot_ref):
    empty = jnp.zeros((128, 128), BF16)
    for yz in range(9):
        taps = own_first_taps(shift, conv_ref, yz)
        whole = [empty] + [tap.astype(BF16) for tap in taps] + [empty]
        for p in range(4):
            rows = slice((p * 9 + yz) * 128, (p * 9 + yz) * 128 + 128)
            two_ref[rows, 0:128] = whole[p + 1] if p < 3 else empty
            two_ref[rows, 128:256] = whole[p]
    for tap in range(8):
        rows = down_in_ref[tap].astype(F32)
        rows = pltpu.roll(rows, shift, 0)
        down_ref[tap * 128 : tap * 128 + 128, :] = pltpu.roll(rows, 2 * shift, 1).astype(BF16)
    cot_ref[...] = pltpu.roll(cot_in_ref[...].astype(F32), 2 * shift, 1).astype(BF16)


def backward_weights(shift, conv_ref, four_ref):
    empty = jnp.zeros((128, 128), BF16)
    none = jnp.zeros((64, 128), F32)
    for yz in range(9):
        taps = own_first_taps(shift, conv_ref, yz)
        own = [none] + [taps[2 - ex][:64] for ex in range(3)] + [none]
        pairs = [jnp.concatenate([own[i + 1], own[i]]).T.astype(BF16) for i in range(4)]
        for p in range(6):
            at = (p * 9 + 8 - yz) * 128
            four_ref[at : at + 128, 0:128] = pairs[p] if p < 4 else empty
            four_ref[at : at + 128, 128:256] = pairs[p - 2] if p >= 2 else empty


def own_lanes(triple):
    below, here = triple[:, 0:128].astype(F32), triple[:, 128:256].astype(F32)
    both = jnp.where(low_lanes(below), below, swap_halves(here)).astype(BF16)
    return both, triple[:, 256:384]


def prepare(
    place_ref, conv_hbm, down_hbm, cot_hbm, heights_hbm, own_hbm, other_hbm,
    lanes_hbm, active_hbm, slope_hbm, inner_hbm, taps_hbm, down_out_hbm, cot_out_hbm,
    conv_in_ref, down_in_ref, cot_in_ref, heights_ref, own_ref, other_ref,
    two_ref, down_ref, cot_ref, padded_ref, rows_ref, mask_ref, lanes_ref, active_ref,
    slope_ref, inner_ref, arrived, left, left_inner
):
    came = start_all(
        [
            (conv_hbm, conv_in_ref),
            (down_hbm, down_in_ref),
            (cot_hbm, cot_in_ref),
            (heights_hbm, heights_ref),
            (own_hbm, own_ref),
            (other_hbm, other_ref),
        ],
        arrived,
    )
    gone = [
        pltpu.make_async_copy(source, target, left.at[i])
        for i, (source, target) in enumerate(
            [
                (two_ref.at[0:3456, 0:128], taps_hbm),
                (down_ref, down_out_hbm),
                (cot_ref, cot_out_hbm),
                (lanes_ref, lanes_hbm),
                (active_ref, active_hbm),
                (slope_ref, slope_hbm),
            ]
        )
    ]
    for copy in came[:3]:
        copy.wait()
    forward_weights(
        place_ref[0] * 64, conv_in_ref, down_in_ref, cot_in_ref, two_ref, down_ref, cot_ref
    )
    for copy in gone[:3]:
        copy.start()
    for copy in came[3:]:
        copy.wait()
    filled = filled_voxels(heights_ref)
    upright = filled.T
    for brick in range(8):
        ox, oy, oz = brick % 2, brick // 2 % 2, brick // 4
        both = jnp.concatenate([own_ref[brick].astype(F32), other_ref[brick].astype(F32)])
        turned = (both * filled[brick : brick + 1]).T
        mask = jnp.broadcast_to(upright[:, brick : brick + 1], (512, 128))
        for vx in range(8):
            for vy in range(8):
                at = (8 * ox + vx) * 256 + (8 * oy + vy) * 16 + 8 * oz
                source = (vx * 8 + vy) * 8
                rows_ref[at : at + 8, :] = turned[source : source + 8]
                mask_ref[at : at + 8, :] = mask[source : source + 8]
    clear_margin(padded_ref)
    for x in range(16):
        put_lines(Whole(padded_ref), [(x + 1, 16, 256)], rows_ref[x * 256 : x * 256 + 256, :])
        active_ref[x * 256 : x * 256 + 256, :] = mask_ref[x * 256 : x * 256 + 256, :].astype(BF16)
    for x in range(18):
        lanes_ref[x, :, 0:128], lanes_ref[x, :, 128:256] = own_lanes(padded_ref[x])
    gone[3].start()
    gone[4].start()
    for tap in range(8):
        tx, ty, tz = tap // 4, tap // 2 % 2, tap % 2
        part = lax.dot_general(
            cot_ref[...],
            down_ref[tap * 128 : tap * 128 + 128, :],
            (((1,), (1,)), ((), ())),
            preferred_element_type=F32,
        )
        for ux in range(8):
            for uy in range(8):
                at = (2 * ux + tx) * 256 + (2 * uy + ty) * 16 + tz
                source = (ux * 8 + uy) * 8
                rows = pl.ds(at, 8, stride=2)
                slope_ref[rows, :] = part[source : source + 8] * mask_ref[rows, :]
    gone[5].start()

    def leave(group):
        rows = pl.ds(pl.multiple_of(group * 1024, 1024), 1024)
        return pltpu.make_async_copy(
            inner_ref.at[rows], inner_hbm.at[rows], left_inner.at[group]
        )


    def step(group, carry):
        lhs = []
        for pair in range(2):
            pieces = []
            for p in range(4):
                for ey in range(3):
                    pieces.append(
                        padded_ref[group * 4 + pair * 2 + p, ey * 16 : ey * 16 + 256, :]
                    )
            lhs.append(jnp.concatenate(pieces, axis=1))
        summed = jnp.dot(jnp.concatenate(lhs), two_ref[...], preferred_element_type=F32)
        for pair in range(2):
            for phase in range(2):
                at = pl.multiple_of((group * 4 + pair * 2 + phase) * 256, 256)
                inner_ref[pl.ds(at, 256), :] = summed[
                    pair * 256 : pair * 256 + 256, phase * 128 : phase * 128 + 128
                ]
        leave(group).start()
        return carry

    lax.fori_loop(0, 4, step, 0)
    for copy in gone:
        copy.wait()
    for group in range(4):
        leave(group).wait()


def add_margin(planes_ref, lines_ref, near_ref, own_ref, other_ref, taps_ref, pre_ref, lanes_ref):
    def tap(ex, ey, ez):
        at = ((ex * 3 + ey) * 3 + ez) * 128
        return taps_ref[at : at + 128, :]

    for side, ex in ((0, 0), (1, 2)):
        lhs = jnp.concatenate(
            [planes_ref[side, ey * 16 : ey * 16 + 256, :] for ey in range(3)], axis=1
        )
        rhs = taps_ref[ex * 1152 : ex * 1152 + 1152, :]
        at = side * 15 * 256
        pre_ref[at : at + 256, :] += jnp.dot(lhs, rhs, preferred_element_type=F32)
    none = jnp.zeros((16, 384), BF16)
    for side, ey in ((0, 0), (1, 2)):
        lines = lines_ref[side]
        lhs = jnp.concatenate(
            [
                jnp.concatenate([none, lines[:240]]),
                lines,
                jnp.concatenate([lines[16:], none]),
            ],
            axis=1,
        )
        rhs = jnp.concatenate([tap(ex, ey, ez) for ex in range(3) for ez in range(3)])
        added = jnp.dot(lhs, rhs, preferred_element_type=F32)
        for x in range(16):
            at = x * 256 + side * 240
            pre_ref[at : at + 16, :] += added[x * 16 : x * 16 + 16]
    for k in (DIRECTIONS.index((0, 0, -1)), DIRECTIONS.index((0, 0, 1))):
        block = near_ref[0, k]
        ez = 0 if DIRECTIONS[k][2] == -1 else 2

        @pl.when(block >= 0)
        def _(block=block, ez=ez):
            own = own_ref[block].astype(F32)
            other = other_ref[block].astype(F32)
            face = jnp.concatenate(
                [
                    jnp.where(low_lanes(own), own, swap_halves(other)),
                    jnp.where(low_lanes(own), swap_halves(own), other),
                ]
            )
            line = lax.broadcasted_iota(jnp.int32, face.shape, 0) % 16
            shifted = [
                jnp.where(line == 0, 0.0, pltpu.roll(face, 1, 0)),
                face,
                jnp.where(line == 15, 0.0, pltpu.roll(face, 255, 0)),
            ]
            border = jnp.zeros((16, 128), F32)
            lhs = []
            for ex in range(3):
                for part in shifted:
                    if ex == 0:
                        part = jnp.concatenate([border, part[:240]])
                    elif ex == 2:
                        part = jnp.concatenate([part[16:], border])
                    lhs.append(part.astype(BF16))
            rhs = jnp.concatenate([tap(ex, ey, ez) for ex in range(3) for ey in range(3)])
            added = jnp.dot(jnp.concatenate(lhs, axis=1), rhs, preferred_element_type=F32)
            rows = pl.ds(0 if ez == 0 else 15, 256, stride=16)
            pre_ref[rows, :] = pre_ref[rows, :] + added
            lanes = slice(ez * 64, ez * 64 + 128)
            for x in range(16):
                old = lanes_ref[x + 1, 16:272, lanes].astype(F32).reshape(16, 16, 128)
                level = lax.broadcasted_iota(jnp.int32, old.shape, 1)
                lane = lax.broadcasted_iota(jnp.int32, old.shape, 2)
                here = (level == (0 if ez == 0 else 15)) & (lane < 64)
                new = jnp.where(here, face[x * 16 : x * 16 + 16].reshape(16, 1, 128), old)
                lanes_ref[x + 1, 16:272, lanes] = new.reshape(256, 128).astype(BF16)


def forward(
    near_ref, place_ref, own_ref, other_ref,
    lanes_hbm, active_hbm, slope_hbm, inner_hbm, taps_hbm, down_hbm, cot_hbm,
    slots_ref, faces_ref, coarse_hbm, grad_pre_hbm,
    planes_ref, lines_ref, pre_ref, grad_ref, packed_ref, turned_ref, lanes_ref, active_ref,
    slope_ref, taps_ref, down_ref, cot_ref, coarse_ref, grad_pre_ref, arrived, left
):
    came = start_all(
        [
            (taps_hbm, taps_ref),
            (inner_hbm, pre_ref),
            (active_hbm, active_ref),
            (slope_hbm, slope_ref),
            (lanes_hbm, lanes_ref),
            (down_hbm, down_ref),
            (cot_hbm, cot_ref),
        ],
        arrived,
    )
    planes_ref[...] = jnp.zeros(planes_ref.shape, BF16)
    lines_ref[...] = jnp.zeros(lines_ref.shape, BF16)
    margin = Margin(planes_ref, lines_ref)
    fill_margin(margin, near_ref, own_ref, other_ref, z_faces=False)
    came[4].wait()
    for side in range(2):
        x = side * 17
        lanes_ref[x, :, 0:128], lanes_ref[x, :, 128:256] = own_lanes(planes_ref[side])
        both, above = own_lanes(lines_ref[side])
        rows = slice(side * 272, side * 272 + 16)
        for x in range(16):
            lanes_ref[x + 1, rows, 0:128] = both[x * 16 : x * 16 + 16]
            lanes_ref[x + 1, rows, 128:256] = above[x * 16 : x * 16 + 16]
    came[0].wait()
    came[1].wait()
    add_margin(planes_ref, lines_ref, near_ref, own_ref, other_ref, taps_ref, pre_ref, lanes_ref)
    came[2].wait()
    came[3].wait()

    turned_ref[:, 0:512] = jnp.zeros((128, 512), BF16)
    turned_ref[:, 4608:5120] = jnp.zeros((128, 512), BF16)
    for x in range(16):
        rows = slice(x * 256, x * 256 + 256)
        pre = pre_ref[rows, :] * active_ref[rows, :].astype(F32)
        sigmoid = 0.5 + 0.5 * jnp.tanh(0.5 * pre)
        pre_ref[rows, :] = pre * sigmoid
        grad = slope_ref[rows, :] * sigmoid * (1.0 + pre * (1.0 - sigmoid))
        grad_ref[rows, :] = grad
        grad_pre_ref[rows, :] = grad.astype(BF16)
        turned_ref[:, 512 + x * 256 : 768 + x * 256] = grad.T.astype(BF16)

    gone = [
        pltpu.make_async_copy(grad_pre_ref, grad_pre_hbm, left.at[0]),
        pltpu.make_async_copy(coarse_ref, coarse_hbm, left.at[1]),
    ]
    gone[0].start()
    fill_faces(grad_ref, near_ref, place_ref, faces_ref)
    share = slots_ref.shape[1] - 16
    for x in range(8):
        low = grad_ref[x * 256 : x * 256 + 256, :]
        high = grad_ref[2048 + x * 256 : 2048 + x * 256 + 256, :]
        packed_ref[x * 256 : x * 256 + 256, :] = jnp.where(
            low_lanes(low), low, swap_halves(high)
        )
    fill_slots(packed_ref, near_ref, slots_ref, share, faces=False)

    def put_terms(at, rows):
        while rows.shape[0]:
            owner, row = at // share, at % share
            count = min(rows.shape[0], share - row)
            slots_ref[owner, row : row + count, :] = rows[:count]
            rows = rows[count:]
            at += count

    lhs = jnp.concatenate(
        [turned_ref[:, (2 - ex) * 256 : (2 - ex) * 256 + 4608] for ex in range(3)]
    )
    for ey in range(3):
        rhs = lanes_ref[:, ey * 16 : ey * 16 + 256, :].reshape(4608, 256)
        summed = jnp.dot(lhs, rhs, preferred_element_type=F32)
        for ex in range(3):
            part = summed[ex * 128 : ex * 128 + 128].T
            put_terms((ex * 3 + ey) * 192, part[0:192].astype(BF16))

    came[5].wait()
    came[6].wait()
    patches = []
    for tap in range(8):
        tx, ty, tz = tap // 4, tap // 2 % 2, tap % 2
        pieces = []
        for ux in range(8):
            for uy in range(8):
                at = (2 * ux + tx) * 256 + (2 * uy + ty) * 16 + tz
                pieces.append(pre_ref[pl.ds(at, 8, stride=2), :])
        patches.append(jnp.concatenate(pieces).astype(BF16))
    patches = jnp.concatenate(patches, axis=1)
    coarse = jnp.dot(patches, down_ref[...], preferred_element_type=F32)
    coarse_ref[...] = coarse[:, :128].astype(BF16)
    gone[1].start()
    own_cot = cot_ref[:, 0:128].astype(F32).T.astype(BF16)
    grad_down = jnp.dot(own_cot, patches, preferred_element_type=F32)
    for tap in range(8):
        part = grad_down[:, tap * 128 : tap * 128 + 128].T
        put_terms(1728 + tap * 128, part.astype(BF16))
    for copy in gone:
        copy.wait()


def total(slots_ref, out_ref):
    devices, share, _ = out_ref.shape
    summed = slots_ref[0, 0:share, :].astype(F32)
    for device in range(1, devices):
        summed = summed + slots_ref[device, 0:share, :].astype(F32)
    summed = (summed / devices).astype(BF16)
    for device in range(devices):
        out_ref[device] = summed


def backward(
    near_ref, place_ref, own_ref, other_ref, own_faces_ref, other_faces_ref,
    grad_pre_hbm, active_hbm, conv_hbm, out_ref,
    padded_ref, grad_pre_ref, active_ref, conv_ref, back_ref, arrived
):
    came = start_all(
        [(conv_hbm, conv_ref), (grad_pre_hbm, grad_pre_ref), (active_hbm, active_ref)], arrived
    )
    came[0].wait()
    backward_weights(place_ref[0] * 64, conv_ref, back_ref)
    clear_margin(padded_ref)
    came[1].wait()
    for x in range(16):
        rows = grad_pre_ref[x * 256 : x * 256 + 256, :].astype(F32)
        put_lines(Whole(padded_ref), [(x + 1, 16, 256)], rows)
    fill_margin(
        Whole(padded_ref), near_ref, own_ref, other_ref, own_ref.shape[1] - 16,
        (place_ref, own_faces_ref, other_faces_ref),
    )
    came[2].wait()
    for half in range(2):
        lhs = []
        for quad in range(2):
            pieces = []
            for p in range(6):
                for ey in range(3):
                    pieces.append(
                        padded_ref[half * 8 + quad * 4 + p, ey * 16 : ey * 16 + 256, :]
                    )
            lhs.append(jnp.concatenate(pieces, axis=1))
        summed = jnp.dot(jnp.concatenate(lhs), back_ref[...], preferred_element_type=F32)
        for quad in range(2):
            for two in range(2):
                part = summed[quad * 256 : quad * 256 + 256, two * 128 : two * 128 + 128]
                x = half * 8 + quad * 4 + two * 2
                even = active_ref[x * 256 : x * 256 + 256, :].astype(F32)
                odd = active_ref[x * 256 + 256 : x * 256 + 512, :].astype(F32)
                part = part * jnp.where(low_lanes(part), even, odd)
                for oy in range(2):
                    rows = [
                        part[(8 * oy + vy) * 16 + 8 * oz : (8 * oy + vy) * 16 + 8 * oz + 8]
                        for oz in range(2)
                        for vy in range(8)
                    ]
                    turned = jnp.concatenate(rows).T
                    first, second = turned[:64], turned[64:]
                    lanes = slice(x % 8 * 64, x % 8 * 64 + 128)
                    brick = half + 2 * oy
                    near = jnp.where(low_lanes(first), first, swap_halves(second))
                    far = jnp.where(low_lanes(first), swap_halves(first), second)
                    out_ref[brick, :, lanes] = near.astype(BF16)
                    out_ref[brick + 4, :, lanes] = far.astype(BF16)


def finish(place_ref, sums_ref, conv_hbm, down_hbm, conv_ref, down_ref, left):
    shift = place_ref[0] * 64
    gone = [
        pltpu.make_async_copy(conv_ref.at[i : i + 9], conv_hbm.at[i : i + 9], left.at[i // 9])
        for i in (0, 9, 18)
    ]
    gone.append(pltpu.make_async_copy(down_ref, down_hbm, left.at[3]))
    for tap in range(27):
        rows = sums_ref[tap * 64 : tap * 64 + 64, :].astype(F32)
        conv_ref[tap] = pltpu.roll(rows, shift, 1)
        if tap % 9 == 8:
            gone[tap // 9].start()
    for tap in range(8):
        rows = sums_ref[1728 + tap * 128 : 1728 + tap * 128 + 128, :].astype(F32)
        down_ref[tap, pl.ds(shift, 64), :] = rows[:64]
        down_ref[tap, pl.ds(64 - shift, 64), :] = rows[64:]
    gone[3].start()
    for copy in gone:
        copy.wait()


def over_space(block, distance):
    blocks = range(lax.axis_size("space"))
    route = [(2 * i, 2 * (i + distance)) for i in blocks if i + distance in blocks]
    route += [(2 * i + 1, 2 * (i - distance) + 1) for i in blocks if i - distance in blocks]
    return lax.ppermute(block, ("space", "chan"), route)


def over_chan(block):
    return lax.ppermute(block, "chan", [(0, 1), (1, 0)])


def to_all(slots):
    return lax.all_to_all(slots, "space", 0, 0, tiled=True)


def local(features, heights, neighbours, w_conv, w_down, cotangent):
    devices = lax.axis_size("space")
    member = lax.axis_index("chan")

    def out(*shape, dtype=BF16):
        return jax.ShapeDtypeStruct(shape, dtype)

    def held_out(*shape, dtype=BF16):
        return pltpu.HBM(shape, dtype)

    def memory(*shape, dtype=BF16):
        return pltpu.VMEM(shape, dtype)

    def copies(count):
        return pltpu.SemaphoreType.DMA((count,))

    place = jnp.stack([member, lax.axis_index("space")]).astype(jnp.int32)
    turned = features.transpose(0, 2, 1)
    slots = kernel_call(
        send_features,
        out(devices, 128, 128),
        [hbm()] * 3,
        vmem(),
        [
            pltpu.SMEM(neighbours.shape, jnp.int32),
            memory(8, 64, dtype=jnp.int32),
            memory(8, 64, 512),
            memory(2048, 128, dtype=F32),
            copies(10),
        ],
    )(neighbours, heights, turned)
    came = to_all(slots)
    other_turned = over_chan(turned)

    held = [
        held_out(18, 288, 256),
        held_out(4096, 128),
        held_out(4096, 128, dtype=F32),
        held_out(4096, 128, dtype=F32),
        held_out(3456, 128),
        held_out(1024, 256),
        held_out(512, 256),
    ]
    lanes, active, slope, inner, taps, down, cot = kernel_call(
        prepare,
        held,
        [smem()] + [hbm()] * 5 + [pl.BlockSpec(memory_space=pl.ANY)],
        [hbm()] * 7,
        [
            memory(27, 128, 128),
            memory(8, 128, 256),
            memory(512, 256),
            memory(8, 64, dtype=jnp.int32),
            memory(8, 64, 512),
            memory(8, 64, 512),
            memory(4608, 256),
            memory(1024, 256),
            memory(512, 256),
            memory(18, 288, 384),
            memory(4096, 128, dtype=F32),
            memory(4096, 128, dtype=F32),
            memory(18, 288, 256),
            memory(4096, 128),
            memory(4096, 128, dtype=F32),
            memory(4096, 128, dtype=F32),
            copies(6),
            copies(6),
            copies(4),
        ],
        flops=5 << 30,
        mib=36,
    )(place, w_conv, w_down, cotangent[0], heights, turned, other_turned)
    came, inner = lax.optimization_barrier((came, inner))
    came_other = over_chan(came)

    share = -(-2752 // (devices * 16)) * 16
    terms, faces, coarse, grad_pre = kernel_call(
        forward,
        [
            out(devices, share + 16, 128),
            out(4, 256, 128),
            held_out(512, 128),
            held_out(4096, 128),
        ],
        [smem()] * 2 + [vmem()] * 2 + [hbm()] * 7,
        [vmem()] * 2 + [hbm()] * 2,
        [
            memory(2, 288, 384),
            memory(2, 256, 384),
            memory(4096, 128, dtype=F32),
            memory(4096, 128, dtype=F32),
            memory(2048, 128, dtype=F32),
            memory(128, 5120),
            memory(18, 288, 256),
            memory(4096, 128),
            memory(4096, 128, dtype=F32),
            memory(3456, 128),
            memory(1024, 256),
            memory(512, 256),
            memory(512, 128),
            memory(4096, 128),
            copies(7),
            copies(2),
        ],
        flops=5 << 30,
        mib=32,
    )(
        neighbours, place, came, came_other, lanes, active, slope, inner, taps, down, cot
    )

    arrived = to_all(terms)
    came_faces = [over_space(faces[i], i + 1) for i in range(4)]
    arrived, *came_faces = lax.optimization_barrier((arrived, *came_faces))
    came_faces = jnp.stack(came_faces)
    other_faces = over_chan(came_faces)
    sums = to_all(
        kernel_call(total, out(devices, share, 128), [vmem()], vmem())(arrived)
    )
    arrived_other = over_chan(arrived[:, share:])
    grad_features = kernel_call(
        backward,
        out(8, 64, 512),
        [smem()] * 2 + [vmem()] * 4 + [hbm()] * 3,
        vmem(),
        [
            memory(18, 288, 384),
            memory(4096, 128),
            memory(4096, 128),
            memory(27, 128, 128),
            memory(6912, 256),
            copies(3),
        ],
        flops=5 << 30,
        mib=24,
    )(
        neighbours, place, arrived, arrived_other, came_faces, other_faces, grad_pre, active,
        w_conv,
    )

    grad_conv, grad_down = kernel_call(
        finish,
        [held_out(27, 64, 128, dtype=F32), held_out(8, 128, 128, dtype=F32)],
        [smem(), vmem()],
        [hbm()] * 2,
        [memory(27, 64, 128, dtype=F32), memory(8, 128, 128, dtype=F32), copies(4)],
    )(place, sums.reshape(-1, 128))
    return coarse[None], grad_conv, grad_down, grad_features.transpose(0, 2, 1)


def solution(mesh):
    placed = (
        P("space", None, "chan"),
        P("space", None),
        P("space", None),
        P(),
        P(),
        P("space", None, None),
    )
    return jax.shard_map(
        local,
        mesh=mesh,
        in_specs=placed,
        out_specs=(
            P("space", None, "chan"),
            P(None, "chan", None),
            P(None, None, "chan"),
            P("space", None, "chan"),
        ),
        check_vma=False,
    )
```

```python
import jax
import jax.numpy as jnp
from jax import lax
from jax.experimental import pallas as pl
from jax.experimental.pallas import tpu as pltpu
from jax.sharding import PartitionSpec as P

OFFSETS = [
    (along_x, along_y, along_z)
    for along_x in (-1, 0, 1)
    for along_y in (-1, 0, 1)
    for along_z in (-1, 0, 1)
]
DIRECTIONS = [offset for offset in OFFSETS if offset != (0, 0, 0)]
FILL_ORDER = sorted(range(26), key=lambda k: (abs(DIRECTIONS[k][2]), k))
F32 = jnp.float32
BF16 = jnp.bfloat16


def vmem():
    return pl.BlockSpec(memory_space=pltpu.VMEM)


def smem():
    return pl.BlockSpec(memory_space=pltpu.SMEM)


def hbm():
    return pl.BlockSpec(memory_space=pltpu.HBM)


def kernel_call(body, outs, specs, out_specs, scratch=(), flops=0, mib=16):
    call = pl.pallas_call(
        body,
        out_shape=outs,
        in_specs=specs,
        out_specs=out_specs,
        scratch_shapes=list(scratch),
        compiler_params=pltpu.CompilerParams(vmem_limit_bytes=mib * 1024 * 1024),
        cost_estimate=pl.CostEstimate(flops=flops, bytes_accessed=1 << 22, transcendentals=0),
    )

    def run(*operands):
        placed = []
        for spec, operand in zip(specs, operands):
            if spec.memory_space == pltpu.HBM:
                operand = pltpu.with_memory_space_constraint(operand, pltpu.HBM)
            placed.append(operand)
        return call(*placed)

    return run


def start_all(pairs, arrived):
    copies = [
        pltpu.make_async_copy(source, target, arrived.at[i])
        for i, (source, target) in enumerate(pairs)
    ]
    for copy in copies:
        copy.start()
    return copies


def swap_halves(rows):
    return pltpu.roll(rows, 64, 1)


def low_lanes(rows):
    return lax.broadcasted_iota(jnp.int32, rows.shape, 1) < 64


def filled_voxels(heights_ref):
    columns = lax.broadcasted_iota(jnp.int32, (64, 512), 0)
    voxels = lax.broadcasted_iota(jnp.int32, (64, 512), 1)
    spread = (voxels // 8 == columns).astype(F32)
    tall = jnp.dot(heights_ref[...].astype(F32), spread, preferred_element_type=F32)
    level = lax.broadcasted_iota(jnp.int32, tall.shape, 1) % 8
    return (level.astype(F32) < tall).astype(F32)


def fill_slots(rows_ref, near_ref, slots_ref, start=0, faces=True):
    for k, (dx, dy, dz) in enumerate(DIRECTIONS):
        block = near_ref[0, k]
        xh = 7 if dx == 1 else 0
        y = 15 if dy == 1 else 0
        z = 15 if dz == 1 else 0
        if not faces and (dx, dy, dz).count(0) == 2:
            continue

        @pl.when(block >= 0)
        def _(dx=dx, dy=dy, dz=dz, xh=xh, y=y, z=z, block=block):
            zeros = [d == 0 for d in (dx, dy, dz)]
            if zeros == [False, True, True]:
                plane = rows_ref[xh * 256 : xh * 256 + 256, :]
                first, second = plane[:128], plane[128:]
                if dx == -1:
                    second = swap_halves(second)
                else:
                    first = swap_halves(first)
                region = jnp.where(low_lanes(first), first, second)
            elif zeros == [True, False, True]:
                region = jnp.concatenate(
                    [rows_ref[x * 256 + y * 16 : x * 256 + y * 16 + 16, :] for x in range(8)]
                )
            elif zeros == [True, True, False]:
                region = rows_ref[pl.ds(z, 128, stride=16), :]
            elif zeros == [False, False, True]:
                region = rows_ref[xh * 256 + y * 16 : xh * 256 + y * 16 + 16, :]
            elif zeros == [False, True, False]:
                region = rows_ref[pl.ds(xh * 256 + z, 16, stride=16), :]
            elif zeros == [True, False, False]:
                line = rows_ref[pl.ds(y * 16 + z, 8, stride=256), :]
                region = jnp.concatenate([line, line])
            else:
                at = xh * 256 + y * 16 + z
                region = jnp.broadcast_to(rows_ref[at : at + 1, :], (16, 128))
            slots_ref[block, start : start + region.shape[0], :] = region.astype(BF16)


def fill_faces(rows_ref, near_ref, place_ref, faces_ref):
    member, own = place_ref[0], place_ref[1]
    for k, (dx, dy, dz) in enumerate(DIRECTIONS):
        if (dx, dy, dz).count(0) != 2:
            continue
        block = near_ref[0, k]
        distance = jnp.where(member == 0, block - own, own - block)
        end = 15 if dx + dy + dz == 1 else 0

        @pl.when((block >= 0) & (distance >= 1))
        def _(dx=dx, dy=dy, end=end, distance=distance):
            if dx:
                region = rows_ref[end * 256 : end * 256 + 256, :]
            elif dy:
                region = jnp.concatenate(
                    [rows_ref[x * 256 + end * 16 : x * 256 + end * 16 + 16, :] for x in range(16)]
                )
            else:
                region = rows_ref[pl.ds(end, 256, stride=16), :]
            faces_ref[distance - 1] = region.astype(BF16)


class Whole:
    def __init__(self, ref):
        self.ref = ref

    def at(self, x, row, height):
        return self.ref, x, row


class Margin:
    def __init__(self, planes_ref, lines_ref):
        self.planes_ref, self.lines_ref = planes_ref, lines_ref

    def at(self, x, row, height):
        if x in (0, 17):
            return self.planes_ref, x // 17, row
        return self.lines_ref, row // 272, (x - 1) * 16


def put_lines(padded, places, rows):
    count = rows.shape[0]
    level = lax.broadcasted_iota(jnp.int32, rows.shape, 0) % 16
    below = jnp.where(level == 0, 0.0, pltpu.roll(rows, 1, 0)).astype(BF16)
    above = jnp.where(level == 15, 0.0, pltpu.roll(rows, count - 1, 0)).astype(BF16)
    here = rows.astype(BF16)
    at = 0
    for x, row, height in places:
        ref, plane, first = padded.at(x, row, height)
        for j, part in enumerate((below, here, above)):
            ref[plane, first : first + height, j * 128 : j * 128 + 128] = part[at : at + height]
        at += height


def put_ends(padded, x, row, rows, dz):
    lines = rows.shape[0]
    j = 0 if dz == -1 else 2
    end = 0 if dz == -1 else 15
    lanes = slice(j * 128, j * 128 + 128)
    ref, plane, first = padded.at(x, row, 16 * lines)
    span = slice(first, first + 16 * lines)
    old = ref[plane, span, lanes].astype(F32).reshape(lines, 16, 128)
    level = lax.broadcasted_iota(jnp.int32, old.shape, 1)
    new = jnp.where(level == end, rows.reshape(lines, 1, 128), old)
    ref[plane, span, lanes] = new.reshape(16 * lines, 128).astype(BF16)


def clear_margin(padded_ref):
    empty = jnp.zeros((288, 384), BF16)
    padded_ref[0] = empty
    padded_ref[17] = empty
    line = jnp.zeros((16, 384), BF16)
    for x in range(1, 17):
        padded_ref[x, 0:16, :] = line
        padded_ref[x, 272:288, :] = line


def put_region(padded, offset, rows):
    dx, dy, dz = offset
    zeros = [d == 0 for d in offset]
    x = 17 if dx == 1 else 0
    y = 17 if dy == 1 else 0
    if zeros == [False, True, True]:
        put_lines(padded, [(x, 16, 256)], rows)
    elif zeros == [True, False, True]:
        put_lines(padded, [(at + 1, y * 16, 16) for at in range(16)], rows)
    elif zeros == [False, False, True]:
        put_lines(padded, [(x, y * 16, 16)], rows)
    elif zeros == [True, True, False]:
        for at in range(16):
            put_ends(padded, at + 1, 16, rows[at * 16 : at * 16 + 16], dz)
    elif zeros == [False, True, False]:
        put_ends(padded, x, 16, rows, dz)
    elif zeros == [True, False, False]:
        for at in range(16):
            put_ends(padded, at + 1, y * 16, rows[at : at + 1], dz)
    else:
        put_ends(padded, x, y * 16, rows[0:1], dz)


def face_source(place_ref, block):
    away = place_ref[1] - block
    return jnp.where(away > 0, 0, 1) == place_ref[0], jnp.clip(jnp.abs(away) - 1, 0, 3)


def fill_margin(padded, near_ref, own_ref, other_ref, start=0, faces=None, z_faces=True):
    for k in FILL_ORDER:
        offset = DIRECTIONS[k]
        block = near_ref[0, k]
        face = offset.count(0) == 2
        if face and offset[2] and not z_faces:
            continue
        if face and faces is not None:
            place_ref, own_faces_ref, other_faces_ref = faces
            here, slot = face_source(place_ref, block)

            @pl.when((block >= 0) & here)
            def _(offset=offset, slot=slot):
                put_region(padded, offset, own_faces_ref[slot].astype(F32))

            @pl.when((block >= 0) & jnp.logical_not(here))
            def _(offset=offset, slot=slot):
                rows = swap_halves(other_faces_ref[slot].astype(F32))
                put_region(padded, offset, rows)

            continue

        @pl.when(block >= 0)
        def _(offset=offset, block=block, face=face):
            height = 128 if face else 16
            own = own_ref[block, start : start + height, :].astype(F32)
            other = other_ref[block, 0:height, :].astype(F32)
            first = jnp.where(low_lanes(own), own, swap_halves(other))
            second = jnp.where(low_lanes(own), swap_halves(own), other)
            if face:
                rows = jnp.concatenate([first, second])
            elif offset[0] == 0:
                rows = jnp.concatenate([first[:8], second[:8]])
            else:
                rows = first if offset[0] == 1 else second
            put_region(padded, offset, rows)


def send_features(
    near_hbm, heights_hbm, features_hbm, slots_ref,
    near_ref, heights_ref, features_ref, rows_ref, arrived
):
    copies = [
        pltpu.make_async_copy(near_hbm, near_ref, arrived.at[8]),
        pltpu.make_async_copy(heights_hbm, heights_ref, arrived.at[9]),
    ]
    order = (0, 1, 2, 3, 4, 5, 6, 7)
    bricks = [
        pltpu.make_async_copy(features_hbm.at[i], features_ref.at[i], arrived.at[i]) for i in order
    ]
    for copy in copies + bricks:
        copy.start()
    copies[1].wait()
    filled = filled_voxels(heights_ref)
    for oz in range(2):
        for oy in range(2):
            pair = []
            for ox in range(2):
                brick = ox + 2 * oy + 4 * oz
                bricks[brick].wait()
                pair.append(features_ref[brick].astype(F32) * filled[brick : brick + 1])
            turned = jnp.concatenate(pair).T
            for vx in range(8):
                for vy in range(8):
                    at = vx * 256 + (8 * oy + vy) * 16 + 8 * oz
                    source = (vx * 8 + vy) * 8
                    rows_ref[at : at + 8, :] = turned[source : source + 8]
    copies[0].wait()
    fill_slots(rows_ref, near_ref, slots_ref)


def own_first_taps(shift, conv_ref, yz):
    taps = []
    for ex in range(3):
        tap = conv_ref[ex * 9 + yz].astype(F32)
        taps.append(pltpu.roll(pltpu.roll(tap, shift, 0), shift, 1))
    return taps


def forward_weights(shift, conv_ref, down_in_ref, cot_in_ref, two_ref, down_ref, cot_ref):
    empty = jnp.zeros((128, 128), BF16)
    for yz in range(9):
        taps = own_first_taps(shift, conv_ref, yz)
        whole = [empty] + [tap.astype(BF16) for tap in taps] + [empty]
        for p in range(4):
            rows = slice((p * 9 + yz) * 128, (p * 9 + yz) * 128 + 128)
            two_ref[rows, 0:128] = whole[p + 1] if p < 3 else empty
            two_ref[rows, 128:256] = whole[p]
    for tap in range(8):
        rows = down_in_ref[tap].astype(F32)
        rows = pltpu.roll(rows, shift, 0)
        down_ref[tap * 128 : tap * 128 + 128, :] = pltpu.roll(rows, 2 * shift, 1).astype(BF16)
    cot_ref[...] = pltpu.roll(cot_in_ref[...].astype(F32), 2 * shift, 1).astype(BF16)


def backward_weights(shift, conv_ref, four_ref, taps_ref):
    empty = jnp.zeros((128, 128), BF16)
    none = jnp.zeros((64, 128), F32)
    for yz in range(9):
        taps = own_first_taps(shift, conv_ref, yz)
        own = [none] + [taps[2 - ex][:64] for ex in range(3)] + [none]
        pairs = [jnp.concatenate([own[i + 1], own[i]]).T.astype(BF16) for i in range(4)]
        for p in range(6):
            at = (p * 9 + 8 - yz) * 128
            four_ref[at : at + 128, 0:128] = pairs[p] if p < 4 else empty
            four_ref[at : at + 128, 128:256] = pairs[p - 2] if p >= 2 else empty
        for ex in range(3):
            at = (ex * 9 + 8 - yz) * 128
            wide = pairs[ex] if ex == 0 else jnp.where(low_lanes(empty), pairs[ex], empty)
            taps_ref[at : at + 128, :] = wide


def own_lanes(triple):
    below, here = triple[:, 0:128].astype(F32), triple[:, 128:256].astype(F32)
    both = jnp.where(low_lanes(below), below, swap_halves(here)).astype(BF16)
    return both, triple[:, 256:384]


def prepare(
    place_ref, conv_hbm, down_hbm, cot_hbm, heights_hbm, own_hbm, other_hbm,
    lanes_hbm, active_hbm, slope_hbm, inner_hbm, taps_hbm, down_out_hbm, cot_out_hbm,
    conv_in_ref, down_in_ref, cot_in_ref, heights_ref, own_ref, other_ref,
    two_ref, down_ref, cot_ref, padded_ref, rows_ref, mask_ref, lanes_ref, active_ref,
    slope_ref, inner_ref, arrived, left, left_inner
):
    came = start_all(
        [
            (conv_hbm, conv_in_ref),
            (down_hbm, down_in_ref),
            (cot_hbm, cot_in_ref),
            (heights_hbm, heights_ref),
            (own_hbm, own_ref),
            (other_hbm, other_ref),
        ],
        arrived,
    )
    gone = [
        pltpu.make_async_copy(source, target, left.at[i])
        for i, (source, target) in enumerate(
            [
                (two_ref.at[0:3456, 0:128], taps_hbm),
                (down_ref, down_out_hbm),
                (cot_ref, cot_out_hbm),
                (lanes_ref, lanes_hbm),
                (active_ref, active_hbm),
                (slope_ref, slope_hbm),
            ]
        )
    ]
    for copy in came[:3]:
        copy.wait()
    forward_weights(
        place_ref[0] * 64, conv_in_ref, down_in_ref, cot_in_ref, two_ref, down_ref, cot_ref
    )
    for copy in gone[:3]:
        copy.start()
    for copy in came[3:]:
        copy.wait()
    filled = filled_voxels(heights_ref)
    upright = filled.T
    for brick in range(8):
        ox, oy, oz = brick % 2, brick // 2 % 2, brick // 4
        both = jnp.concatenate([own_ref[brick].astype(F32), other_ref[brick].astype(F32)])
        turned = (both * filled[brick : brick + 1]).T
        mask = jnp.broadcast_to(upright[:, brick : brick + 1], (512, 128))
        for vx in range(8):
            for vy in range(8):
                at = (8 * ox + vx) * 256 + (8 * oy + vy) * 16 + 8 * oz
                source = (vx * 8 + vy) * 8
                rows_ref[at : at + 8, :] = turned[source : source + 8]
                mask_ref[at : at + 8, :] = mask[source : source + 8]
    clear_margin(padded_ref)
    for x in range(16):
        put_lines(Whole(padded_ref), [(x + 1, 16, 256)], rows_ref[x * 256 : x * 256 + 256, :])
        active_ref[x * 256 : x * 256 + 256, :] = mask_ref[x * 256 : x * 256 + 256, :].astype(BF16)
    for x in range(18):
        lanes_ref[x, :, 0:128], lanes_ref[x, :, 128:256] = own_lanes(padded_ref[x])
    gone[3].start()
    gone[4].start()
    for tap in range(8):
        tx, ty, tz = tap // 4, tap // 2 % 2, tap % 2
        part = lax.dot_general(
            cot_ref[...],
            down_ref[tap * 128 : tap * 128 + 128, :],
            (((1,), (1,)), ((), ())),
            preferred_element_type=F32,
        )
        for ux in range(8):
            for uy in range(8):
                at = (2 * ux + tx) * 256 + (2 * uy + ty) * 16 + tz
                source = (ux * 8 + uy) * 8
                rows = pl.ds(at, 8, stride=2)
                slope_ref[rows, :] = part[source : source + 8] * mask_ref[rows, :]
    gone[5].start()

    def leave(group):
        rows = pl.ds(pl.multiple_of(group * 1024, 1024), 1024)
        return pltpu.make_async_copy(
            inner_ref.at[rows], inner_hbm.at[rows], left_inner.at[group]
        )


    def step(group, carry):
        lhs = []
        for pair in range(2):
            pieces = []
            for p in range(4):
                for ey in range(3):
                    pieces.append(
                        padded_ref[group * 4 + pair * 2 + p, ey * 16 : ey * 16 + 256, :]
                    )
            lhs.append(jnp.concatenate(pieces, axis=1))
        summed = jnp.dot(jnp.concatenate(lhs), two_ref[...], preferred_element_type=F32)
        for pair in range(2):
            for phase in range(2):
                at = pl.multiple_of((group * 4 + pair * 2 + phase) * 256, 256)
                inner_ref[pl.ds(at, 256), :] = summed[
                    pair * 256 : pair * 256 + 256, phase * 128 : phase * 128 + 128
                ]
        leave(group).start()
        return carry

    lax.fori_loop(0, 4, step, 0)
    for copy in gone:
        copy.wait()
    for group in range(4):
        leave(group).wait()


def tap_rows(taps_ref, taps):
    starts = [((ex * 3 + ey) * 3 + ez) * 128 for ex, ey, ez in taps]
    return jnp.concatenate([taps_ref[at : at + 128, :] for at in starts])


def margin_planes(planes_ref, taps_ref):
    sums = []
    for side, ex in ((0, 0), (1, 2)):
        lhs = jnp.concatenate(
            [planes_ref[side, ey * 16 : ey * 16 + 256, :] for ey in range(3)], axis=1
        )
        rhs = taps_ref[ex * 1152 : ex * 1152 + 1152, :]
        sums.append(jnp.dot(lhs, rhs, preferred_element_type=F32))
    return sums


def margin_lines(lines_ref, taps_ref):
    sums = []
    none = jnp.zeros((16, 384), BF16)
    for side, ey in ((0, 0), (1, 2)):
        lines = lines_ref[side]
        lhs = jnp.concatenate(
            [
                jnp.concatenate([none, lines[:240]]),
                lines,
                jnp.concatenate([lines[16:], none]),
            ],
            axis=1,
        )
        rhs = tap_rows(taps_ref, [(ex, ey, ez) for ex in range(3) for ez in range(3)])
        sums.append(jnp.dot(lhs, rhs, preferred_element_type=F32))
    return sums


def margin_ends(face, ez, taps_ref):
    line = lax.broadcasted_iota(jnp.int32, face.shape, 0) % 16
    shifted = [
        jnp.where(line == 0, 0.0, pltpu.roll(face, 1, 0)),
        face,
        jnp.where(line == 15, 0.0, pltpu.roll(face, 255, 0)),
    ]
    border = jnp.zeros((16, 128), F32)
    lhs = []
    for ex in range(3):
        for part in shifted:
            if ex == 0:
                part = jnp.concatenate([border, part[:240]])
            elif ex == 2:
                part = jnp.concatenate([part[16:], border])
            lhs.append(part.astype(BF16))
    rhs = tap_rows(taps_ref, [(ex, ey, ez) for ex in range(3) for ey in range(3)])
    return jnp.dot(jnp.concatenate(lhs, axis=1), rhs, preferred_element_type=F32)


Z_FACES = ((DIRECTIONS.index((0, 0, -1)), 0), (DIRECTIONS.index((0, 0, 1)), 2))


def joined_face(own_ref, other_ref, block):
    own = own_ref[block].astype(F32)
    other = other_ref[block].astype(F32)
    return jnp.concatenate(
        [
            jnp.where(low_lanes(own), own, swap_halves(other)),
            jnp.where(low_lanes(own), swap_halves(own), other),
        ]
    )


def add_margin(planes_ref, lines_ref, near_ref, own_ref, other_ref, taps_ref, pre_ref):
    for side, added in enumerate(margin_planes(planes_ref, taps_ref)):
        at = side * 15 * 256
        pre_ref[at : at + 256, :] += added
    for side, added in enumerate(margin_lines(lines_ref, taps_ref)):
        for x in range(16):
            at = x * 256 + side * 240
            pre_ref[at : at + 16, :] += added[x * 16 : x * 16 + 16]
    for k, ez in Z_FACES:
        block = near_ref[0, k]

        @pl.when(block >= 0)
        def _(block=block, ez=ez):
            added = margin_ends(joined_face(own_ref, other_ref, block), ez, taps_ref)
            rows = pl.ds(0 if ez == 0 else 15, 256, stride=16)
            pre_ref[rows, :] = pre_ref[rows, :] + added


def put_own_margin(planes_ref, lines_ref, near_ref, own_ref, other_ref, lanes_ref):
    for side in range(2):
        plane = side * 17
        lanes_ref[plane, :, 0:128], lanes_ref[plane, :, 128:256] = own_lanes(planes_ref[side])
        both, above = own_lanes(lines_ref[side])
        rows = slice(side * 272, side * 272 + 16)
        for x in range(16):
            lanes_ref[x + 1, rows, 0:128] = both[x * 16 : x * 16 + 16]
            lanes_ref[x + 1, rows, 128:256] = above[x * 16 : x * 16 + 16]
    for k, ez in Z_FACES:
        block = near_ref[0, k]

        @pl.when(block >= 0)
        def _(block=block, ez=ez):
            face = joined_face(own_ref, other_ref, block)
            lanes = slice(ez * 64, ez * 64 + 128)
            for x in range(16):
                old = lanes_ref[x + 1, 16:272, lanes].astype(F32).reshape(16, 16, 128)
                level = lax.broadcasted_iota(jnp.int32, old.shape, 1)
                lane = lax.broadcasted_iota(jnp.int32, old.shape, 2)
                here = (level == (0 if ez == 0 else 15)) & (lane < 64)
                new = jnp.where(here, face[x * 16 : x * 16 + 16].reshape(16, 1, 128), old)
                lanes_ref[x + 1, 16:272, lanes] = new.reshape(256, 128).astype(BF16)


def forward(
    near_ref, place_ref, own_ref, other_ref,
    lanes_hbm, active_hbm, slope_hbm, inner_hbm, taps_hbm, down_hbm, cot_hbm,
    slots_ref, faces_ref, coarse_hbm, grad_pre_hbm,
    planes_ref, lines_ref, pre_ref, grad_ref, packed_ref, turned_ref, lanes_ref, active_ref,
    slope_ref, taps_ref, down_ref, cot_ref, coarse_ref, grad_pre_ref, arrived, left
):
    came = start_all(
        [
            (taps_hbm, taps_ref),
            (inner_hbm, pre_ref),
            (active_hbm, active_ref),
            (slope_hbm, slope_ref),
            (lanes_hbm, lanes_ref),
            (down_hbm, down_ref),
            (cot_hbm, cot_ref),
        ],
        arrived,
    )
    planes_ref[...] = jnp.zeros(planes_ref.shape, BF16)
    lines_ref[...] = jnp.zeros(lines_ref.shape, BF16)
    margin = Margin(planes_ref, lines_ref)
    fill_margin(margin, near_ref, own_ref, other_ref, z_faces=False)
    came[0].wait()
    came[1].wait()
    add_margin(planes_ref, lines_ref, near_ref, own_ref, other_ref, taps_ref, pre_ref)
    came[2].wait()
    came[3].wait()

    turned_ref[:, 0:512] = jnp.zeros((128, 512), BF16)
    turned_ref[:, 4608:5120] = jnp.zeros((128, 512), BF16)
    for x in range(16):
        rows = slice(x * 256, x * 256 + 256)
        pre = pre_ref[rows, :] * active_ref[rows, :].astype(F32)
        sigmoid = 0.5 + 0.5 * jnp.tanh(0.5 * pre)
        pre_ref[rows, :] = pre * sigmoid
        grad = slope_ref[rows, :] * sigmoid * (1.0 + pre * (1.0 - sigmoid))
        grad_ref[rows, :] = grad
        grad = grad.astype(BF16)
        grad_pre_ref[rows, :] = grad
        turned_ref[:, 512 + x * 256 : 768 + x * 256] = grad.T

    gone = [
        pltpu.make_async_copy(grad_pre_ref, grad_pre_hbm, left.at[0]),
        pltpu.make_async_copy(coarse_ref, coarse_hbm, left.at[1]),
    ]
    gone[0].start()
    fill_faces(grad_ref, near_ref, place_ref, faces_ref)
    share = slots_ref.shape[1] - 16
    for x in range(8):
        low = grad_ref[x * 256 : x * 256 + 256, :]
        high = grad_ref[2048 + x * 256 : 2048 + x * 256 + 256, :]
        packed_ref[x * 256 : x * 256 + 256, :] = jnp.where(
            low_lanes(low), low, swap_halves(high)
        )
    fill_slots(packed_ref, near_ref, slots_ref, share, faces=False)

    def put_terms(at, rows):
        while rows.shape[0]:
            owner, row = at // share, at % share
            count = min(rows.shape[0], share - row)
            slots_ref[owner, row : row + count, :] = rows[:count]
            rows = rows[count:]
            at += count

    came[4].wait()
    put_own_margin(planes_ref, lines_ref, near_ref, own_ref, other_ref, lanes_ref)
    lhs = jnp.concatenate(
        [turned_ref[:, (2 - ex) * 256 : (2 - ex) * 256 + 4608] for ex in range(3)]
    )
    for ey in range(3):
        rhs = lanes_ref[:, ey * 16 : ey * 16 + 256, :].reshape(4608, 256)
        summed = jnp.dot(lhs, rhs, preferred_element_type=F32)
        for ex in range(3):
            part = summed[ex * 128 : ex * 128 + 128].T
            put_terms((ex * 3 + ey) * 192, part[0:192].astype(BF16))

    came[5].wait()
    came[6].wait()
    patches = []
    for tap in range(8):
        tx, ty, tz = tap // 4, tap // 2 % 2, tap % 2
        pieces = []
        for ux in range(8):
            for uy in range(8):
                at = (2 * ux + tx) * 256 + (2 * uy + ty) * 16 + tz
                pieces.append(pre_ref[pl.ds(at, 8, stride=2), :])
        patches.append(jnp.concatenate(pieces).astype(BF16))
    patches = jnp.concatenate(patches, axis=1)
    coarse = jnp.dot(patches, down_ref[...], preferred_element_type=F32)
    coarse_ref[...] = coarse[:, :128].astype(BF16)
    gone[1].start()
    own_cot = cot_ref[:, 0:128].astype(F32).T.astype(BF16)
    grad_down = jnp.dot(own_cot, patches, preferred_element_type=F32)
    for tap in range(8):
        part = grad_down[:, tap * 128 : tap * 128 + 128].T
        put_terms(1728 + tap * 128, part.astype(BF16))
    for copy in gone:
        copy.wait()


def total(slots_ref, out_ref):
    devices, share, _ = out_ref.shape
    summed = slots_ref[0, 0:share, :].astype(F32)
    for device in range(1, devices):
        summed = summed + slots_ref[device, 0:share, :].astype(F32)
    summed = (summed / devices).astype(BF16)
    for device in range(devices):
        out_ref[device] = summed


def backward_inner(
    place_ref, conv_hbm, grad_pre_hbm, inner_hbm, taps_hbm,
    padded_ref, grad_pre_ref, conv_ref, back_ref, inner_ref, taps_ref, arrived, left
):
    came = start_all([(conv_hbm, conv_ref), (grad_pre_hbm, grad_pre_ref)], arrived)
    gone = [
        pltpu.make_async_copy(taps_ref, taps_hbm, left.at[0]),
        pltpu.make_async_copy(inner_ref, inner_hbm, left.at[1]),
    ]
    came[0].wait()
    backward_weights(place_ref[0] * 64, conv_ref, back_ref, taps_ref)
    gone[0].start()
    clear_margin(padded_ref)
    came[1].wait()
    for x in range(16):
        rows = grad_pre_ref[x * 256 : x * 256 + 256, :].astype(F32)
        put_lines(Whole(padded_ref), [(x + 1, 16, 256)], rows)
    for half in range(2):
        lhs = []
        for quad in range(2):
            pieces = []
            for p in range(6):
                for ey in range(3):
                    pieces.append(
                        padded_ref[half * 8 + quad * 4 + p, ey * 16 : ey * 16 + 256, :]
                    )
            lhs.append(jnp.concatenate(pieces, axis=1))
        summed = jnp.dot(jnp.concatenate(lhs), back_ref[...], preferred_element_type=F32)
        for quad in range(2):
            for two in range(2):
                inner_ref[half * 4 + quad * 2 + two] = summed[
                    quad * 256 : quad * 256 + 256, two * 128 : two * 128 + 128
                ]
    gone[1].start()
    for copy in gone:
        copy.wait()


def backward(
    near_ref, place_ref, own_ref, other_ref, own_faces_ref, other_faces_ref,
    inner_hbm, taps_hbm, active_hbm, out_ref,
    planes_ref, lines_ref, inner_ref, taps_ref, active_ref, arrived
):
    came = start_all(
        [(taps_hbm, taps_ref), (inner_hbm, inner_ref), (active_hbm, active_ref)], arrived
    )
    planes_ref[...] = jnp.zeros(planes_ref.shape, BF16)
    lines_ref[...] = jnp.zeros(lines_ref.shape, BF16)
    faces = (place_ref, own_faces_ref, other_faces_ref)
    fill_margin(
        Margin(planes_ref, lines_ref), near_ref, own_ref, other_ref, own_ref.shape[1] - 16,
        faces, z_faces=False,
    )
    came[0].wait()
    came[1].wait()
    first, last = margin_planes(planes_ref, taps_ref)
    inner_ref[0] += first
    inner_ref[7] += swap_halves(last)
    for side, added in enumerate(margin_lines(lines_ref, taps_ref)):
        for pair in range(8):
            even = added[pair * 32 : pair * 32 + 16]
            odd = added[pair * 32 + 16 : pair * 32 + 32]
            inner_ref[pair, side * 240 : side * 240 + 16, :] += even + swap_halves(odd)
    for k, ez in Z_FACES:
        block = near_ref[0, k]
        here, slot = face_source(place_ref, block)

        @pl.when(block >= 0)
        def _(ez=ez, here=here, slot=slot):
            own = own_faces_ref[slot].astype(F32)
            other = swap_halves(other_faces_ref[slot].astype(F32))
            added = margin_ends(jnp.where(here, own, other), ez, taps_ref)
            for pair in range(8):
                even = added[pair * 32 : pair * 32 + 16]
                odd = added[pair * 32 + 16 : pair * 32 + 32]
                rows = pl.ds(0 if ez == 0 else 15, 16, stride=16)
                inner_ref[pair, rows, :] = inner_ref[pair, rows, :] + even + swap_halves(odd)

    came[2].wait()
    for pair in range(8):
        x = pair * 2
        part = inner_ref[pair]
        even = active_ref[x * 256 : x * 256 + 256, :].astype(F32)
        odd = active_ref[x * 256 + 256 : x * 256 + 512, :].astype(F32)
        part = part * jnp.where(low_lanes(part), even, odd)
        for oy in range(2):
            rows = [
                part[(8 * oy + vy) * 16 + 8 * oz : (8 * oy + vy) * 16 + 8 * oz + 8]
                for oz in range(2)
                for vy in range(8)
            ]
            turned = jnp.concatenate(rows).T
            first, second = turned[:64], turned[64:]
            lanes = slice(x % 8 * 64, x % 8 * 64 + 128)
            brick = x // 8 + 2 * oy
            near = jnp.where(low_lanes(first), first, swap_halves(second))
            far = jnp.where(low_lanes(first), swap_halves(first), second)
            out_ref[brick, :, lanes] = near.astype(BF16)
            out_ref[brick + 4, :, lanes] = far.astype(BF16)


def finish(place_ref, sums_ref, conv_ref, down_ref):
    shift = place_ref[0] * 64
    for tap in range(27):
        rows = sums_ref[tap * 64 : tap * 64 + 64, :].astype(F32)
        conv_ref[tap] = pltpu.roll(rows, shift, 1)
    for tap in range(8):
        rows = sums_ref[1728 + tap * 128 : 1728 + tap * 128 + 128, :].astype(F32)
        down_ref[tap, pl.ds(shift, 64), :] = rows[:64]
        down_ref[tap, pl.ds(64 - shift, 64), :] = rows[64:]


def over_space(block, distance):
    blocks = range(lax.axis_size("space"))
    route = [(2 * i, 2 * (i + distance)) for i in blocks if i + distance in blocks]
    route += [(2 * i + 1, 2 * (i - distance) + 1) for i in blocks if i - distance in blocks]
    return lax.ppermute(block, ("space", "chan"), route)


def over_chan(block):
    return lax.ppermute(block, "chan", [(0, 1), (1, 0)])


def to_all(slots):
    return lax.all_to_all(slots, "space", 0, 0, tiled=True)


def local(features, heights, neighbours, w_conv, w_down, cotangent):
    devices = lax.axis_size("space")
    member = lax.axis_index("chan")

    def out(*shape, dtype=BF16):
        return jax.ShapeDtypeStruct(shape, dtype)

    def held_out(*shape, dtype=BF16):
        return pltpu.HBM(shape, dtype)

    def memory(*shape, dtype=BF16):
        return pltpu.VMEM(shape, dtype)

    def copies(count):
        return pltpu.SemaphoreType.DMA((count,))

    place = jnp.stack([member, lax.axis_index("space")]).astype(jnp.int32)
    turned = features.transpose(0, 2, 1)
    slots = kernel_call(
        send_features,
        out(devices, 128, 128),
        [hbm()] * 3,
        vmem(),
        [
            pltpu.SMEM(neighbours.shape, jnp.int32),
            memory(8, 64, dtype=jnp.int32),
            memory(8, 64, 512),
            memory(2048, 128, dtype=F32),
            copies(10),
        ],
    )(neighbours, heights, turned)
    came = to_all(slots)
    other_turned = over_chan(turned)

    held = [
        held_out(18, 288, 256),
        held_out(4096, 128),
        held_out(4096, 128, dtype=F32),
        held_out(4096, 128, dtype=F32),
        held_out(3456, 128),
        held_out(1024, 256),
        held_out(512, 256),
    ]
    lanes, active, slope, inner, taps, down, cot = kernel_call(
        prepare,
        held,
        [smem()] + [hbm()] * 5 + [pl.BlockSpec(memory_space=pl.ANY)],
        [hbm()] * 7,
        [
            memory(27, 128, 128),
            memory(8, 128, 256),
            memory(512, 256),
            memory(8, 64, dtype=jnp.int32),
            memory(8, 64, 512),
            memory(8, 64, 512),
            memory(4608, 256),
            memory(1024, 256),
            memory(512, 256),
            memory(18, 288, 384),
            memory(4096, 128, dtype=F32),
            memory(4096, 128, dtype=F32),
            memory(18, 288, 256),
            memory(4096, 128),
            memory(4096, 128, dtype=F32),
            memory(4096, 128, dtype=F32),
            copies(6),
            copies(6),
            copies(4),
        ],
        flops=5 << 30,
        mib=36,
    )(place, w_conv, w_down, cotangent[0], heights, turned, other_turned)
    came, inner = lax.optimization_barrier((came, inner))
    came_other = over_chan(came)

    share = -(-2752 // (devices * 16)) * 16
    terms, faces, coarse, grad_pre = kernel_call(
        forward,
        [
            out(devices, share + 16, 128),
            out(4, 256, 128),
            held_out(512, 128),
            held_out(4096, 128),
        ],
        [smem()] * 2 + [vmem()] * 2 + [hbm()] * 7,
        [vmem()] * 2 + [hbm()] * 2,
        [
            memory(2, 288, 384),
            memory(2, 256, 384),
            memory(4096, 128, dtype=F32),
            memory(4096, 128, dtype=F32),
            memory(2048, 128, dtype=F32),
            memory(128, 5120),
            memory(18, 288, 256),
            memory(4096, 128),
            memory(4096, 128, dtype=F32),
            memory(3456, 128),
            memory(1024, 256),
            memory(512, 256),
            memory(512, 128),
            memory(4096, 128),
            copies(7),
            copies(2),
        ],
        flops=5 << 30,
        mib=32,
    )(
        neighbours, place, came, came_other, lanes, active, slope, inner, taps, down, cot
    )

    arrived = to_all(terms)
    came_faces = [over_space(faces[i], i + 1) for i in range(4)]
    back_inner, back_taps = kernel_call(
        backward_inner,
        [held_out(8, 256, 128, dtype=F32), held_out(3456, 128)],
        [smem()] + [hbm()] * 2,
        [hbm()] * 2,
        [
            memory(18, 288, 384),
            memory(4096, 128),
            memory(27, 128, 128),
            memory(6912, 256),
            memory(8, 256, 128, dtype=F32),
            memory(3456, 128),
            copies(2),
            copies(2),
        ],
        flops=5 << 30,
        mib=24,
    )(place, w_conv, grad_pre)
    arrived, back_inner, *nearest = lax.optimization_barrier(
        (arrived, back_inner, *came_faces[:3])
    )
    came_faces = jnp.stack([*nearest, came_faces[3]])
    other_faces = over_chan(came_faces)
    sums = to_all(
        kernel_call(total, out(devices, share, 128), [vmem()], vmem())(arrived)
    )
    arrived_other = over_chan(arrived[:, share:])
    grad_features = kernel_call(
        backward,
        out(8, 64, 512),
        [smem()] * 2 + [vmem()] * 4 + [hbm()] * 3,
        vmem(),
        [
            memory(2, 288, 384),
            memory(2, 256, 384),
            memory(8, 256, 128, dtype=F32),
            memory(3456, 128),
            memory(4096, 128),
            copies(3),
        ],
        flops=1 << 30,
    )(
        neighbours, place, arrived, arrived_other, came_faces, other_faces, back_inner, back_taps,
        active,
    )

    grad_conv, grad_down = kernel_call(
        finish,
        [out(27, 64, 128, dtype=F32), out(8, 128, 128, dtype=F32)],
        [smem(), vmem()],
        [vmem()] * 2,
    )(place, sums.reshape(-1, 128))
    return coarse[None], grad_conv, grad_down, grad_features.transpose(0, 2, 1)


def solution(mesh):
    placed = (
        P("space", None, "chan"),
        P("space", None),
        P("space", None),
        P(),
        P(),
        P("space", None, None),
    )
    return jax.shard_map(
        local,
        mesh=mesh,
        in_specs=placed,
        out_specs=(
            P("space", None, "chan"),
            P(None, "chan", None),
            P(None, None, "chan"),
            P("space", None, "chan"),
        ),
        check_vma=False,
    )
```

```python
import jax
import jax.numpy as jnp
from jax import lax
from jax.experimental import pallas as pl
from jax.experimental.pallas import tpu as pltpu
from jax.sharding import PartitionSpec as P

OFFSETS = [
    (along_x, along_y, along_z)
    for along_x in (-1, 0, 1)
    for along_y in (-1, 0, 1)
    for along_z in (-1, 0, 1)
]
DIRECTIONS = [offset for offset in OFFSETS if offset != (0, 0, 0)]
FILL_ORDER = sorted(range(26), key=lambda k: (abs(DIRECTIONS[k][2]), k))
INACTIVE = -1e30
F32 = jnp.float32
BF16 = jnp.bfloat16


def vmem():
    return pl.BlockSpec(memory_space=pltpu.VMEM)


def smem():
    return pl.BlockSpec(memory_space=pltpu.SMEM)


def hbm():
    return pl.BlockSpec(memory_space=pltpu.HBM)


def kernel_call(body, outs, specs, out_specs, scratch=(), flops=0, mib=16):
    call = pl.pallas_call(
        body,
        out_shape=outs,
        in_specs=specs,
        out_specs=out_specs,
        scratch_shapes=list(scratch),
        compiler_params=pltpu.CompilerParams(vmem_limit_bytes=mib * 1024 * 1024),
        cost_estimate=pl.CostEstimate(flops=flops, bytes_accessed=1 << 22, transcendentals=0),
    )

    def run(*operands):
        placed = []
        for spec, operand in zip(specs, operands):
            if spec.memory_space == pltpu.HBM:
                operand = pltpu.with_memory_space_constraint(operand, pltpu.HBM)
            placed.append(operand)
        return call(*placed)

    return run


def start_all(pairs, arrived):
    copies = [
        pltpu.make_async_copy(source, target, arrived.at[i])
        for i, (source, target) in enumerate(pairs)
    ]
    for copy in copies:
        copy.start()
    return copies


def swap_halves(rows):
    return pltpu.roll(rows, 64, 1)


def low_lanes(rows):
    return lax.broadcasted_iota(jnp.int32, rows.shape, 1) < 64


def filled_voxels(heights_ref):
    columns = lax.broadcasted_iota(jnp.int32, (64, 512), 0)
    voxels = lax.broadcasted_iota(jnp.int32, (64, 512), 1)
    spread = (voxels // 8 == columns).astype(F32)
    tall = jnp.dot(heights_ref[...].astype(F32), spread, preferred_element_type=F32)
    level = lax.broadcasted_iota(jnp.int32, tall.shape, 1) % 8
    return (level.astype(F32) < tall).astype(F32)


def fill_slots(rows_ref, near_ref, slots_ref, start=0, faces=True):
    for k, (dx, dy, dz) in enumerate(DIRECTIONS):
        block = near_ref[0, k]
        xh = 7 if dx == 1 else 0
        y = 15 if dy == 1 else 0
        z = 15 if dz == 1 else 0
        if not faces and (dx, dy, dz).count(0) == 2:
            continue

        @pl.when(block >= 0)
        def _(dx=dx, dy=dy, dz=dz, xh=xh, y=y, z=z, block=block):
            zeros = [d == 0 for d in (dx, dy, dz)]
            if zeros == [False, True, True]:
                plane = rows_ref[xh * 256 : xh * 256 + 256, :]
                first, second = plane[:128], plane[128:]
                if dx == -1:
                    second = swap_halves(second)
                else:
                    first = swap_halves(first)
                region = jnp.where(low_lanes(first), first, second)
            elif zeros == [True, False, True]:
                region = jnp.concatenate(
                    [rows_ref[x * 256 + y * 16 : x * 256 + y * 16 + 16, :] for x in range(8)]
                )
            elif zeros == [True, True, False]:
                region = rows_ref[pl.ds(z, 128, stride=16), :]
            elif zeros == [False, False, True]:
                region = rows_ref[xh * 256 + y * 16 : xh * 256 + y * 16 + 16, :]
            elif zeros == [False, True, False]:
                region = rows_ref[pl.ds(xh * 256 + z, 16, stride=16), :]
            elif zeros == [True, False, False]:
                line = rows_ref[pl.ds(y * 16 + z, 8, stride=256), :]
                region = jnp.concatenate([line, line])
            else:
                at = xh * 256 + y * 16 + z
                region = jnp.broadcast_to(rows_ref[at : at + 1, :], (16, 128))
            slots_ref[block, start : start + region.shape[0], :] = region.astype(BF16)


def fill_faces(rows_ref, near_ref, place, faces_ref):
    member, own = place
    for k, (dx, dy, dz) in enumerate(DIRECTIONS):
        if (dx, dy, dz).count(0) != 2:
            continue
        block = near_ref[0, k]
        distance = jnp.where(member == 0, block - own, own - block)
        end = 15 if dx + dy + dz == 1 else 0

        @pl.when((block >= 0) & (distance >= 1))
        def _(dx=dx, dy=dy, end=end, distance=distance):
            if dx:
                region = rows_ref[end * 256 : end * 256 + 256, :]
            elif dy:
                region = jnp.concatenate(
                    [rows_ref[x * 256 + end * 16 : x * 256 + end * 16 + 16, :] for x in range(16)]
                )
            else:
                region = rows_ref[pl.ds(end, 256, stride=16), :]
            faces_ref[distance - 1] = region.astype(BF16)


class Whole:
    def __init__(self, ref):
        self.ref = ref

    def at(self, x, row, height):
        return self.ref, x, row


class Margin:
    def __init__(self, planes_ref, lines_ref):
        self.planes_ref, self.lines_ref = planes_ref, lines_ref

    def at(self, x, row, height):
        if x in (0, 17):
            return self.planes_ref, x // 17, row
        return self.lines_ref, row // 272, (x - 1) * 16


def put_lines(padded, places, rows):
    count = rows.shape[0]
    level = lax.broadcasted_iota(jnp.int32, rows.shape, 0) % 16
    below = jnp.where(level == 0, 0.0, pltpu.roll(rows, 1, 0)).astype(BF16)
    above = jnp.where(level == 15, 0.0, pltpu.roll(rows, count - 1, 0)).astype(BF16)
    here = rows.astype(BF16)
    at = 0
    for x, row, height in places:
        ref, plane, first = padded.at(x, row, height)
        for j, part in enumerate((below, here, above)):
            ref[plane, first : first + height, j * 128 : j * 128 + 128] = part[at : at + height]
        at += height


def put_ends(padded, x, row, rows, dz):
    lines = rows.shape[0]
    j = 0 if dz == -1 else 2
    end = 0 if dz == -1 else 15
    lanes = slice(j * 128, j * 128 + 128)
    ref, plane, first = padded.at(x, row, 16 * lines)
    span = slice(first, first + 16 * lines)
    old = ref[plane, span, lanes].astype(F32).reshape(lines, 16, 128)
    level = lax.broadcasted_iota(jnp.int32, old.shape, 1)
    new = jnp.where(level == end, rows.reshape(lines, 1, 128), old)
    ref[plane, span, lanes] = new.reshape(16 * lines, 128).astype(BF16)


def clear_margin(padded_ref):
    empty = jnp.zeros((288, 384), BF16)
    padded_ref[0] = empty
    padded_ref[17] = empty
    line = jnp.zeros((16, 384), BF16)
    for x in range(1, 17):
        padded_ref[x, 0:16, :] = line
        padded_ref[x, 272:288, :] = line


def put_region(padded, offset, rows):
    dx, dy, dz = offset
    zeros = [d == 0 for d in offset]
    x = 17 if dx == 1 else 0
    y = 17 if dy == 1 else 0
    if zeros == [False, True, True]:
        put_lines(padded, [(x, 16, 256)], rows)
    elif zeros == [True, False, True]:
        put_lines(padded, [(at + 1, y * 16, 16) for at in range(16)], rows)
    elif zeros == [False, False, True]:
        put_lines(padded, [(x, y * 16, 16)], rows)
    elif zeros == [True, True, False]:
        for at in range(16):
            put_ends(padded, at + 1, 16, rows[at * 16 : at * 16 + 16], dz)
    elif zeros == [False, True, False]:
        put_ends(padded, x, 16, rows, dz)
    elif zeros == [True, False, False]:
        for at in range(16):
            put_ends(padded, at + 1, y * 16, rows[at : at + 1], dz)
    else:
        put_ends(padded, x, y * 16, rows[0:1], dz)


def face_source(place, block):
    away = place[1] - block
    return jnp.where(away > 0, 0, 1) == place[0], jnp.clip(jnp.abs(away) - 1, 0, 3)


def fill_margin(padded, near_ref, own_ref, other_ref, start=0, faces=None, z_faces=True):
    for k in FILL_ORDER:
        offset = DIRECTIONS[k]
        block = near_ref[0, k]
        face = offset.count(0) == 2
        if face and offset[2] and not z_faces:
            continue
        if face and faces is not None:
            place, own_faces_ref, other_faces_ref = faces
            here, slot = face_source(place, block)

            @pl.when((block >= 0) & here)
            def _(offset=offset, slot=slot):
                put_region(padded, offset, own_faces_ref[slot].astype(F32))

            @pl.when((block >= 0) & jnp.logical_not(here))
            def _(offset=offset, slot=slot):
                rows = swap_halves(other_faces_ref[slot].astype(F32))
                put_region(padded, offset, rows)

            continue

        @pl.when(block >= 0)
        def _(offset=offset, block=block, face=face):
            height = 128 if face else 16
            own = own_ref[block, start : start + height, :].astype(F32)
            other = other_ref[block, 0:height, :].astype(F32)
            first = jnp.where(low_lanes(own), own, swap_halves(other))
            second = jnp.where(low_lanes(own), swap_halves(own), other)
            if face:
                rows = jnp.concatenate([first, second])
            elif offset[0] == 0:
                rows = jnp.concatenate([first[:8], second[:8]])
            else:
                rows = first if offset[0] == 1 else second
            put_region(padded, offset, rows)


def send_features(
    near_hbm, heights_hbm, features_hbm, slots_ref,
    near_ref, heights_ref, features_ref, rows_ref, arrived
):
    copies = [
        pltpu.make_async_copy(near_hbm, near_ref, arrived.at[8]),
        pltpu.make_async_copy(heights_hbm, heights_ref, arrived.at[9]),
    ]
    order = (0, 1, 2, 3, 4, 5, 6, 7)
    bricks = [
        pltpu.make_async_copy(features_hbm.at[i], features_ref.at[i], arrived.at[i]) for i in order
    ]
    for copy in copies + bricks:
        copy.start()
    copies[1].wait()
    filled = filled_voxels(heights_ref)
    for oz in range(2):
        for oy in range(2):
            pair = []
            for ox in range(2):
                brick = ox + 2 * oy + 4 * oz
                bricks[brick].wait()
                pair.append(features_ref[brick].astype(F32) * filled[brick : brick + 1])
            turned = jnp.concatenate(pair).T
            for vx in range(8):
                for vy in range(8):
                    at = vx * 256 + (8 * oy + vy) * 16 + 8 * oz
                    source = (vx * 8 + vy) * 8
                    rows_ref[at : at + 8, :] = turned[source : source + 8]
    copies[0].wait()
    fill_slots(rows_ref, near_ref, slots_ref)


def own_first_taps(shift, conv_ref, yz):
    taps = []
    for ex in range(3):
        tap = conv_ref[ex * 9 + yz].astype(F32)
        taps.append(pltpu.roll(pltpu.roll(tap, shift, 0), shift, 1))
    return taps


def forward_weights(shift, conv_ref, down_in_ref, cot_in_ref, two_ref, down_ref, cot_ref):
    empty = jnp.zeros((128, 128), BF16)
    for yz in range(9):
        taps = own_first_taps(shift, conv_ref, yz)
        whole = [empty] + [tap.astype(BF16) for tap in taps] + [empty]
        for p in range(4):
            rows = slice((p * 9 + yz) * 128, (p * 9 + yz) * 128 + 128)
            two_ref[rows, 0:128] = whole[p + 1] if p < 3 else empty
            two_ref[rows, 128:256] = whole[p]
    for tap in range(8):
        rows = down_in_ref[tap].astype(F32)
        rows = pltpu.roll(rows, shift, 0)
        down_ref[tap * 128 : tap * 128 + 128, :] = pltpu.roll(rows, 2 * shift, 1).astype(BF16)
    cot_ref[...] = pltpu.roll(cot_in_ref[...].astype(F32), 2 * shift, 1).astype(BF16)


def backward_weights(shift, conv_ref, four_ref):
    empty = jnp.zeros((128, 128), BF16)
    none = jnp.zeros((64, 128), F32)
    for yz in range(9):
        taps = own_first_taps(shift, conv_ref, yz)
        own = [none] + [taps[2 - ex][:64] for ex in range(3)] + [none]
        pairs = [jnp.concatenate([own[i + 1], own[i]]).T.astype(BF16) for i in range(4)]
        for p in range(6):
            at = (p * 9 + 8 - yz) * 128
            four_ref[at : at + 128, 0:128] = pairs[p] if p < 4 else empty
            four_ref[at : at + 128, 128:256] = pairs[p - 2] if p >= 2 else empty


def own_lanes(triple):
    below, here = triple[:, 0:128].astype(F32), triple[:, 128:256].astype(F32)
    both = jnp.where(low_lanes(below), below, swap_halves(here)).astype(BF16)
    return both, triple[:, 256:384]


def prepare(
    core_ref, conv_hbm, down_hbm, cot_hbm, heights_hbm, own_hbm, other_hbm,
    lanes_hbm, active_hbm, slope_hbm, inner_hbm, taps_hbm, down_out_hbm, cot_out_hbm,
    conv_in_ref, down_in_ref, cot_in_ref, heights_ref, own_ref, other_ref,
    two_ref, down_ref, cot_ref, padded_ref, rows_ref, mask_ref, lanes_ref, active_ref,
    slope_ref, inner_ref, slope_wide_ref, arrived, left, left_inner
):
    came = start_all(
        [
            (conv_hbm, conv_in_ref),
            (down_hbm, down_in_ref),
            (cot_hbm, cot_in_ref),
            (heights_hbm, heights_ref),
            (own_hbm, own_ref),
            (other_hbm, other_ref),
        ],
        arrived,
    )
    gone = [
        pltpu.make_async_copy(source, target, left.at[i])
        for i, (source, target) in enumerate(
            [
                (two_ref.at[0:3456, 0:128], taps_hbm),
                (down_ref, down_out_hbm),
                (cot_ref, cot_out_hbm),
                (lanes_ref, lanes_hbm),
                (active_ref, active_hbm),
                (slope_ref, slope_hbm),
            ]
        )
    ]
    for copy in came[:3]:
        copy.wait()
    forward_weights(
        core_ref[0] * 64, conv_in_ref, down_in_ref, cot_in_ref, two_ref, down_ref, cot_ref
    )
    for copy in gone[:3]:
        copy.start()
    for copy in came[3:]:
        copy.wait()
    filled = filled_voxels(heights_ref)
    upright = filled.T
    for brick in range(8):
        ox, oy, oz = brick % 2, brick // 2 % 2, brick // 4
        both = jnp.concatenate([own_ref[brick].astype(F32), other_ref[brick].astype(F32)])
        turned = (both * filled[brick : brick + 1]).T
        mask = jnp.broadcast_to(upright[:, brick : brick + 1], (512, 128))
        for vx in range(8):
            for vy in range(8):
                at = (8 * ox + vx) * 256 + (8 * oy + vy) * 16 + 8 * oz
                source = (vx * 8 + vy) * 8
                rows_ref[at : at + 8, :] = turned[source : source + 8]
                mask_ref[at : at + 8, :] = mask[source : source + 8]
    clear_margin(padded_ref)
    for x in range(16):
        put_lines(Whole(padded_ref), [(x + 1, 16, 256)], rows_ref[x * 256 : x * 256 + 256, :])
        active_ref[x * 256 : x * 256 + 256, :] = mask_ref[x * 256 : x * 256 + 256, :].astype(BF16)
    for x in range(18):
        lanes_ref[x, :, 0:128], lanes_ref[x, :, 128:256] = own_lanes(padded_ref[x])
    gone[3].start()
    gone[4].start()
    for tap in range(8):
        tx, ty, tz = tap // 4, tap // 2 % 2, tap % 2
        part = lax.dot_general(
            cot_ref[...],
            down_ref[tap * 128 : tap * 128 + 128, :],
            (((1,), (1,)), ((), ())),
            preferred_element_type=F32,
        )
        for ux in range(8):
            for uy in range(8):
                at = (2 * ux + tx) * 256 + (2 * uy + ty) * 16 + tz
                source = (ux * 8 + uy) * 8
                rows = pl.ds(at, 8, stride=2)
                slope_wide_ref[rows, :] = part[source : source + 8] * mask_ref[rows, :]
    slope_ref[...] = slope_wide_ref[...].astype(BF16)
    gone[5].start()

    def leave(group):
        rows = pl.ds(pl.multiple_of(group * 1024, 1024), 1024)
        return pltpu.make_async_copy(
            inner_ref.at[rows], inner_hbm.at[rows], left_inner.at[group]
        )


    def step(group, carry):
        lhs = []
        for pair in range(2):
            pieces = []
            for p in range(4):
                for ey in range(3):
                    pieces.append(
                        padded_ref[group * 4 + pair * 2 + p, ey * 16 : ey * 16 + 256, :]
                    )
            lhs.append(jnp.concatenate(pieces, axis=1))
        summed = jnp.dot(jnp.concatenate(lhs), two_ref[...], preferred_element_type=F32)
        for pair in range(2):
            for phase in range(2):
                at = pl.multiple_of((group * 4 + pair * 2 + phase) * 256, 256)
                part = summed[pair * 256 : pair * 256 + 256, phase * 128 : phase * 128 + 128]
                rows = pl.ds(at, 256)
                inner_ref[rows, :] = jnp.where(mask_ref[rows, :] > 0, part, INACTIVE)
        leave(group).start()
        return carry

    lax.fori_loop(0, 4, step, 0)
    for copy in gone:
        copy.wait()
    for group in range(4):
        leave(group).wait()


def tap_rows(taps_ref, taps):
    starts = [((ex * 3 + ey) * 3 + ez) * 128 for ex, ey, ez in taps]
    return jnp.concatenate([taps_ref[at : at + 128, :] for at in starts])


def margin_planes(planes_ref, taps_ref):
    sums = []
    for side, ex in ((0, 0), (1, 2)):
        lhs = jnp.concatenate(
            [planes_ref[side, ey * 16 : ey * 16 + 256, :] for ey in range(3)], axis=1
        )
        rhs = taps_ref[ex * 1152 : ex * 1152 + 1152, :]
        sums.append(jnp.dot(lhs, rhs, preferred_element_type=F32))
    return sums


def margin_lines(lines_ref, taps_ref):
    sums = []
    none = jnp.zeros((16, 384), BF16)
    for side, ey in ((0, 0), (1, 2)):
        lines = lines_ref[side]
        lhs = jnp.concatenate(
            [
                jnp.concatenate([none, lines[:240]]),
                lines,
                jnp.concatenate([lines[16:], none]),
            ],
            axis=1,
        )
        rhs = tap_rows(taps_ref, [(ex, ey, ez) for ex in range(3) for ez in range(3)])
        sums.append(jnp.dot(lhs, rhs, preferred_element_type=F32))
    return sums


def margin_ends(face, ez, taps_ref):
    line = lax.broadcasted_iota(jnp.int32, face.shape, 0) % 16
    shifted = [
        jnp.where(line == 0, 0.0, pltpu.roll(face, 1, 0)),
        face,
        jnp.where(line == 15, 0.0, pltpu.roll(face, 255, 0)),
    ]
    border = jnp.zeros((16, 128), F32)
    lhs = []
    for ex in range(3):
        for part in shifted:
            if ex == 0:
                part = jnp.concatenate([border, part[:240]])
            elif ex == 2:
                part = jnp.concatenate([part[16:], border])
            lhs.append(part.astype(BF16))
    rhs = tap_rows(taps_ref, [(ex, ey, ez) for ex in range(3) for ey in range(3)])
    return jnp.dot(jnp.concatenate(lhs, axis=1), rhs, preferred_element_type=F32)


Z_FACES = ((DIRECTIONS.index((0, 0, -1)), 0), (DIRECTIONS.index((0, 0, 1)), 2))


def joined_face(own_ref, other_ref, block):
    own = own_ref[block].astype(F32)
    other = other_ref[block].astype(F32)
    return jnp.concatenate(
        [
            jnp.where(low_lanes(own), own, swap_halves(other)),
            jnp.where(low_lanes(own), swap_halves(own), other),
        ]
    )


def add_margin(planes_ref, lines_ref, near_ref, own_ref, other_ref, taps_ref, pre_ref):
    for side, added in enumerate(margin_planes(planes_ref, taps_ref)):
        at = side * 15 * 256
        pre_ref[at : at + 256, :] += added
    for side, added in enumerate(margin_lines(lines_ref, taps_ref)):
        for x in range(16):
            at = x * 256 + side * 240
            pre_ref[at : at + 16, :] += added[x * 16 : x * 16 + 16]
    for k, ez in Z_FACES:
        block = near_ref[0, k]

        @pl.when(block >= 0)
        def _(block=block, ez=ez):
            added = margin_ends(joined_face(own_ref, other_ref, block), ez, taps_ref)
            rows = pl.ds(0 if ez == 0 else 15, 256, stride=16)
            pre_ref[rows, :] = pre_ref[rows, :] + added


def put_own_margin(planes_ref, lines_ref, near_ref, own_ref, other_ref, lanes_ref):
    for side in range(2):
        plane = side * 17
        lanes_ref[plane, :, 0:128], lanes_ref[plane, :, 128:256] = own_lanes(planes_ref[side])
        both, above = own_lanes(lines_ref[side])
        rows = slice(side * 272, side * 272 + 16)
        for x in range(16):
            lanes_ref[x + 1, rows, 0:128] = both[x * 16 : x * 16 + 16]
            lanes_ref[x + 1, rows, 128:256] = above[x * 16 : x * 16 + 16]
    for k, ez in Z_FACES:
        block = near_ref[0, k]

        @pl.when(block >= 0)
        def _(block=block, ez=ez):
            face = joined_face(own_ref, other_ref, block)
            lanes = slice(ez * 64, ez * 64 + 128)
            for x in range(16):
                old = lanes_ref[x + 1, 16:272, lanes].astype(F32).reshape(16, 16, 128)
                level = lax.broadcasted_iota(jnp.int32, old.shape, 1)
                lane = lax.broadcasted_iota(jnp.int32, old.shape, 2)
                here = (level == (0 if ez == 0 else 15)) & (lane < 64)
                new = jnp.where(here, face[x * 16 : x * 16 + 16].reshape(16, 1, 128), old)
                lanes_ref[x + 1, 16:272, lanes] = new.reshape(256, 128).astype(BF16)


def forward(
    near_ref, core_ref, at_ref, own_ref, other_ref, taps_ref, inner_ref, slope_ref,
    lanes_hbm, down_hbm, cot_hbm,
    slots_hbm, faces_ref, coarse_hbm, grad_pre_hbm,
    planes_ref, lines_ref, pre_ref, grad_ref, packed_ref, turned_ref, lanes_ref,
    down_ref, cot_ref, coarse_ref, grad_pre_ref, slots_ref, arrived, left, left_slots
):
    came = start_all(
        [(lanes_hbm, lanes_ref), (down_hbm, down_ref), (cot_hbm, cot_ref)], arrived
    )
    pre_ref[...] = inner_ref[...]
    planes_ref[...] = jnp.zeros(planes_ref.shape, BF16)
    lines_ref[...] = jnp.zeros(lines_ref.shape, BF16)
    margin = Margin(planes_ref, lines_ref)
    fill_margin(margin, near_ref, own_ref, other_ref, z_faces=False)
    add_margin(planes_ref, lines_ref, near_ref, own_ref, other_ref, taps_ref, pre_ref)

    turned_ref[:, 0:512] = jnp.zeros((128, 512), BF16)
    turned_ref[:, 4608:5120] = jnp.zeros((128, 512), BF16)
    for x in range(16):
        rows = slice(x * 256, x * 256 + 256)
        pre = pre_ref[rows, :]
        sigmoid = 0.5 + 0.5 * jnp.tanh(0.5 * pre)
        pre_ref[rows, :] = jnp.where(pre > 0.5 * INACTIVE, pre * sigmoid, 0.0)
        grad = slope_ref[rows, :].astype(F32) * sigmoid * (1.0 + pre * (1.0 - sigmoid))
        grad_ref[rows, :] = grad
        grad = grad.astype(BF16)
        grad_pre_ref[rows, :] = grad
        turned_ref[:, 512 + x * 256 : 768 + x * 256] = grad.T

    gone = [
        pltpu.make_async_copy(grad_pre_ref, grad_pre_hbm, left.at[0]),
        pltpu.make_async_copy(coarse_ref, coarse_hbm, left.at[1]),
    ]
    gone[0].start()
    fill_faces(grad_ref, near_ref, (core_ref[0], at_ref[0]), faces_ref)
    share = slots_ref.shape[1] - 16
    for x in range(8):
        low = grad_ref[x * 256 : x * 256 + 256, :]
        high = grad_ref[2048 + x * 256 : 2048 + x * 256 + 256, :]
        packed_ref[x * 256 : x * 256 + 256, :] = jnp.where(
            low_lanes(low), low, swap_halves(high)
        )
    fill_slots(packed_ref, near_ref, slots_ref, share, faces=False)

    def put_terms(at, rows):
        while rows.shape[0]:
            owner, row = at // share, at % share
            count = min(rows.shape[0], share - row)
            slots_ref[owner, row : row + count, :] = rows[:count]
            rows = rows[count:]
            at += count

    ends = [1024 // share] + [(1024 + 576 * i) // share for i in (1, 2)] + [slots_ref.shape[0]]
    leaving = [
        pltpu.make_async_copy(
            slots_ref.at[first:last], slots_hbm.at[first:last], left_slots.at[i]
        )
        for i, (first, last) in enumerate(zip([0] + ends, ends))
    ]

    came[1].wait()
    came[2].wait()
    patches = []
    for tap in range(8):
        tx, ty, tz = tap // 4, tap // 2 % 2, tap % 2
        pieces = []
        for ux in range(8):
            for uy in range(8):
                at = (2 * ux + tx) * 256 + (2 * uy + ty) * 16 + tz
                pieces.append(pre_ref[pl.ds(at, 8, stride=2), :])
        patches.append(jnp.concatenate(pieces).astype(BF16))
    patches = jnp.concatenate(patches, axis=1)
    coarse = jnp.dot(patches, down_ref[...], preferred_element_type=F32)
    coarse_ref[...] = coarse[:, :128].astype(BF16)
    gone[1].start()
    own_cot = cot_ref[:, 0:128].astype(F32).T.astype(BF16)
    grad_down = jnp.dot(own_cot, patches, preferred_element_type=F32)
    for tap in range(8):
        part = grad_down[:, tap * 128 : tap * 128 + 128].T
        put_terms(tap * 128, part.astype(BF16))
    leaving[0].start()

    came[0].wait()
    put_own_margin(planes_ref, lines_ref, near_ref, own_ref, other_ref, lanes_ref)
    lhs = jnp.concatenate(
        [turned_ref[:, (2 - ex) * 256 : (2 - ex) * 256 + 4608] for ex in range(3)]
    )
    for ey in range(3):
        rhs = lanes_ref[:, ey * 16 : ey * 16 + 256, :].reshape(4608, 256)
        summed = jnp.dot(lhs, rhs, preferred_element_type=F32)
        for ex in range(3):
            part = summed[ex * 128 : ex * 128 + 128].T
            put_terms(1024 + (ey * 3 + ex) * 192, part[0:192].astype(BF16))
        leaving[ey + 1].start()
    for copy in gone + leaving:
        copy.wait()


def fetch(taps_hbm, inner_hbm, slope_hbm, taps_ref, inner_ref, slope_ref, arrived):
    for copy in start_all(
        [(taps_hbm, taps_ref), (inner_hbm, inner_ref), (slope_hbm, slope_ref)], arrived
    ):
        copy.wait()


def total(slots_ref, out_ref):
    devices, share, _ = out_ref.shape
    summed = slots_ref[0, 0:share, :].astype(F32)
    for device in range(1, devices):
        summed = summed + slots_ref[device, 0:share, :].astype(F32)
    summed = (summed / devices).astype(BF16)
    for device in range(devices):
        out_ref[device] = summed


def backward(
    near_ref, core_ref, at_ref, own_ref, other_ref, own_faces_ref, other_faces_ref,
    grad_pre_hbm, active_hbm, conv_hbm, out_ref,
    padded_ref, grad_pre_ref, active_ref, conv_ref, back_ref, arrived
):
    came = start_all(
        [(conv_hbm, conv_ref), (grad_pre_hbm, grad_pre_ref), (active_hbm, active_ref)], arrived
    )
    came[0].wait()
    backward_weights(core_ref[0] * 64, conv_ref, back_ref)
    clear_margin(padded_ref)
    came[1].wait()
    for x in range(16):
        rows = grad_pre_ref[x * 256 : x * 256 + 256, :].astype(F32)
        put_lines(Whole(padded_ref), [(x + 1, 16, 256)], rows)
    fill_margin(
        Whole(padded_ref), near_ref, own_ref, other_ref, own_ref.shape[1] - 16,
        ((core_ref[0], at_ref[0]), own_faces_ref, other_faces_ref),
    )
    came[2].wait()
    for half in range(2):
        lhs = []
        for quad in range(2):
            pieces = []
            for p in range(6):
                for ey in range(3):
                    pieces.append(
                        padded_ref[half * 8 + quad * 4 + p, ey * 16 : ey * 16 + 256, :]
                    )
            lhs.append(jnp.concatenate(pieces, axis=1))
        summed = jnp.dot(jnp.concatenate(lhs), back_ref[...], preferred_element_type=F32)
        for quad in range(2):
            for two in range(2):
                part = summed[quad * 256 : quad * 256 + 256, two * 128 : two * 128 + 128]
                x = half * 8 + quad * 4 + two * 2
                even = active_ref[x * 256 : x * 256 + 256, :].astype(F32)
                odd = active_ref[x * 256 + 256 : x * 256 + 512, :].astype(F32)
                part = part * jnp.where(low_lanes(part), even, odd)
                for oy in range(2):
                    rows = [
                        part[(8 * oy + vy) * 16 + 8 * oz : (8 * oy + vy) * 16 + 8 * oz + 8]
                        for oz in range(2)
                        for vy in range(8)
                    ]
                    turned = jnp.concatenate(rows).T
                    first, second = turned[:64], turned[64:]
                    lanes = slice(x % 8 * 64, x % 8 * 64 + 128)
                    brick = half + 2 * oy
                    near = jnp.where(low_lanes(first), first, swap_halves(second))
                    far = jnp.where(low_lanes(first), swap_halves(first), second)
                    out_ref[brick, :, lanes] = near.astype(BF16)
                    out_ref[brick + 4, :, lanes] = far.astype(BF16)


def finish(core_ref, sums_ref, conv_ref, down_ref):
    shift = core_ref[0] * 64
    for tap in range(27):
        ex, ey, ez = tap // 9, tap // 3 % 3, tap % 3
        at = 1024 + ((ey * 3 + ex) * 3 + ez) * 64
        rows = sums_ref[at : at + 64, :].astype(F32)
        conv_ref[tap] = pltpu.roll(rows, shift, 1)
    for tap in range(8):
        rows = sums_ref[tap * 128 : tap * 128 + 128, :].astype(F32)
        down_ref[tap, pl.ds(shift, 64), :] = rows[:64]
        down_ref[tap, pl.ds(64 - shift, 64), :] = rows[64:]


def over_space(block, distance):
    blocks = range(lax.axis_size("space"))
    route = [(2 * i, 2 * (i + distance)) for i in blocks if i + distance in blocks]
    route += [(2 * i + 1, 2 * (i - distance) + 1) for i in blocks if i - distance in blocks]
    return lax.ppermute(block, ("space", "chan"), route)


def over_chan(block):
    return lax.ppermute(block, "chan", [(0, 1), (1, 0)])


def to_all(slots):
    return lax.all_to_all(slots, "space", 0, 0, tiled=True)


def local(features, heights, neighbours, w_conv, w_down, cotangent):
    devices = lax.axis_size("space")
    member = lax.axis_index("chan")

    def out(*shape, dtype=BF16):
        return jax.ShapeDtypeStruct(shape, dtype)

    def held_out(*shape, dtype=BF16):
        return pltpu.HBM(shape, dtype)

    def memory(*shape, dtype=BF16):
        return pltpu.VMEM(shape, dtype)

    def copies(count):
        return pltpu.SemaphoreType.DMA((count,))

    core = member.reshape(1)
    place = (core, lax.axis_index("space").reshape(1))
    turned = features.transpose(0, 2, 1)
    slots = kernel_call(
        send_features,
        out(devices, 128, 128),
        [hbm()] * 3,
        vmem(),
        [
            pltpu.SMEM(neighbours.shape, jnp.int32),
            memory(8, 64, dtype=jnp.int32),
            memory(8, 64, 512),
            memory(2048, 128, dtype=F32),
            copies(10),
        ],
    )(neighbours, heights, turned)
    came = to_all(slots)
    other_turned = over_chan(turned)

    held = [
        held_out(18, 288, 256),
        held_out(4096, 128),
        held_out(4096, 128),
        held_out(4096, 128, dtype=F32),
        held_out(3456, 128),
        held_out(1024, 256),
        held_out(512, 256),
    ]
    lanes, active, slope, inner, taps, down, cot = kernel_call(
        prepare,
        held,
        [smem()] + [hbm()] * 5 + [pl.BlockSpec(memory_space=pl.ANY)],
        [hbm()] * 7,
        [
            memory(27, 128, 128),
            memory(8, 128, 256),
            memory(512, 256),
            memory(8, 64, dtype=jnp.int32),
            memory(8, 64, 512),
            memory(8, 64, 512),
            memory(4608, 256),
            memory(1024, 256),
            memory(512, 256),
            memory(18, 288, 384),
            memory(4096, 128, dtype=F32),
            memory(4096, 128, dtype=F32),
            memory(18, 288, 256),
            memory(4096, 128),
            memory(4096, 128),
            memory(4096, 128, dtype=F32),
            memory(4096, 128, dtype=F32),
            copies(6),
            copies(6),
            copies(4),
        ],
        flops=5 << 30,
        mib=36,
    )(core, w_conv, w_down, cotangent[0], heights, turned, other_turned)
    came, taps, inner, slope = lax.optimization_barrier((came, taps, inner, slope))
    came_other = over_chan(came)
    taps, inner, slope = kernel_call(
        fetch,
        [out(3456, 128), out(4096, 128, dtype=F32), out(4096, 128)],
        [hbm()] * 3,
        [vmem()] * 3,
        [copies(3)],
    )(taps, inner, slope)

    share = -(-2752 // (devices * 16)) * 16
    terms, faces, coarse, grad_pre = kernel_call(
        forward,
        [
            held_out(devices, share + 16, 128),
            out(4, 256, 128),
            held_out(512, 128),
            held_out(4096, 128),
        ],
        [smem()] * 3 + [vmem()] * 5 + [hbm()] * 3,
        [hbm(), vmem(), hbm(), hbm()],
        [
            memory(2, 288, 384),
            memory(2, 256, 384),
            memory(4096, 128, dtype=F32),
            memory(4096, 128, dtype=F32),
            memory(2048, 128, dtype=F32),
            memory(128, 5120),
            memory(18, 288, 256),
            memory(1024, 256),
            memory(512, 256),
            memory(512, 128),
            memory(4096, 128),
            memory(devices, share + 16, 128),
            copies(3),
            copies(2),
            copies(4),
        ],
        flops=5 << 30,
        mib=24,
    )(
        neighbours, *place, came, came_other, taps, inner, slope, lanes, down, cot
    )

    arrived = to_all(terms)
    came_faces = [over_space(faces[i], i + 1) for i in range(4)]
    arrived, *came_faces = lax.optimization_barrier((arrived, *came_faces))
    came_faces = jnp.stack(came_faces)
    other_faces = over_chan(came_faces)
    sums = to_all(
        kernel_call(total, out(devices, share, 128), [vmem()], vmem())(arrived)
    )
    arrived_other = over_chan(arrived[:, share:])
    grad_features = kernel_call(
        backward,
        out(8, 64, 512),
        [smem()] * 3 + [vmem()] * 4 + [hbm()] * 3,
        vmem(),
        [
            memory(18, 288, 384),
            memory(4096, 128),
            memory(4096, 128),
            memory(27, 128, 128),
            memory(6912, 256),
            copies(3),
        ],
        flops=5 << 30,
        mib=24,
    )(
        neighbours, *place, arrived, arrived_other, came_faces, other_faces, grad_pre, active,
        w_conv,
    )

    grad_conv, grad_down = kernel_call(
        finish,
        [out(27, 64, 128, dtype=F32), out(8, 128, 128, dtype=F32)],
        [smem(), vmem()],
        [vmem()] * 2,
    )(core, sums.reshape(-1, 128))
    return coarse[None], grad_conv, grad_down, grad_features.transpose(0, 2, 1)


def solution(mesh):
    placed = (
        P("space", None, "chan"),
        P("space", None),
        P("space", None),
        P(),
        P(),
        P("space", None, None),
    )
    return jax.shard_map(
        local,
        mesh=mesh,
        in_specs=placed,
        out_specs=(
            P("space", None, "chan"),
            P(None, "chan", None),
            P(None, None, "chan"),
            P("space", None, "chan"),
        ),
        check_vma=False,
    )
```

```python
import functools

import jax
import jax.numpy as jnp
from jax import lax
from jax.experimental import pallas as pl
from jax.experimental.pallas import tpu as pltpu
from jax.sharding import PartitionSpec as P

OFFSETS = [
    (along_x, along_y, along_z)
    for along_x in (-1, 0, 1)
    for along_y in (-1, 0, 1)
    for along_z in (-1, 0, 1)
]
DIRECTIONS = [offset for offset in OFFSETS if offset != (0, 0, 0)]
FILL_ORDER = sorted(range(26), key=lambda k: (abs(DIRECTIONS[k][2]), k))
INACTIVE = -1e30
NEAR, FAR = 4, 7
INNER = 4
F32 = jnp.float32
BF16 = jnp.bfloat16


def vmem():
    return pl.BlockSpec(memory_space=pltpu.VMEM)


def smem():
    return pl.BlockSpec(memory_space=pltpu.SMEM)


def hbm():
    return pl.BlockSpec(memory_space=pltpu.HBM)


def kernel_call(body, outs, specs, out_specs, scratch=(), flops=0, mib=16):
    call = pl.pallas_call(
        body,
        out_shape=outs,
        in_specs=specs,
        out_specs=out_specs,
        scratch_shapes=list(scratch),
        compiler_params=pltpu.CompilerParams(vmem_limit_bytes=mib * 1024 * 1024),
        cost_estimate=pl.CostEstimate(flops=flops, bytes_accessed=1 << 22, transcendentals=0),
    )

    def run(*operands):
        placed = []
        for spec, operand in zip(specs, operands):
            if spec.memory_space == pltpu.HBM:
                operand = pltpu.with_memory_space_constraint(operand, pltpu.HBM)
            placed.append(operand)
        return call(*placed)

    return run


def start_all(pairs, arrived):
    copies = [
        pltpu.make_async_copy(source, target, arrived.at[i])
        for i, (source, target) in enumerate(pairs)
    ]
    for copy in copies:
        copy.start()
    return copies


def swap_halves(rows):
    return pltpu.roll(rows, 64, 1)


def low_lanes(rows):
    return lax.broadcasted_iota(jnp.int32, rows.shape, 1) < 64


def filled_voxels(heights_ref):
    columns = lax.broadcasted_iota(jnp.int32, (64, 512), 0)
    voxels = lax.broadcasted_iota(jnp.int32, (64, 512), 1)
    spread = (voxels // 8 == columns).astype(F32)
    tall = jnp.dot(heights_ref[...].astype(F32), spread, preferred_element_type=F32)
    level = lax.broadcasted_iota(jnp.int32, tall.shape, 1) % 8
    return (level.astype(F32) < tall).astype(F32)


def fill_slots(rows_ref, near_ref, slots_ref):
    for k, (dx, dy, dz) in enumerate(DIRECTIONS):
        block = near_ref[0, k]
        xh = 7 if dx == 1 else 0
        y = 15 if dy == 1 else 0
        z = 15 if dz == 1 else 0

        @pl.when(block >= 0)
        def _(dx=dx, dy=dy, dz=dz, xh=xh, y=y, z=z, block=block):
            zeros = [d == 0 for d in (dx, dy, dz)]
            if zeros == [False, True, True]:
                plane = rows_ref[xh * 256 : xh * 256 + 256, :]
                first, second = plane[:128], plane[128:]
                if dx == -1:
                    second = swap_halves(second)
                else:
                    first = swap_halves(first)
                region = jnp.where(low_lanes(first), first, second)
            elif zeros == [True, False, True]:
                region = jnp.concatenate(
                    [rows_ref[x * 256 + y * 16 : x * 256 + y * 16 + 16, :] for x in range(8)]
                )
            elif zeros == [True, True, False]:
                region = rows_ref[pl.ds(z, 128, stride=16), :]
            elif zeros == [False, False, True]:
                region = rows_ref[xh * 256 + y * 16 : xh * 256 + y * 16 + 16, :]
            elif zeros == [False, True, False]:
                region = rows_ref[pl.ds(xh * 256 + z, 16, stride=16), :]
            elif zeros == [True, False, False]:
                line = rows_ref[pl.ds(y * 16 + z, 8, stride=256), :]
                region = jnp.concatenate([line, line])
            else:
                at = xh * 256 + y * 16 + z
                region = jnp.broadcast_to(rows_ref[at : at + 1, :], (16, 128))
            slots_ref[block, 0 : region.shape[0], :] = region.astype(BF16)


def fill_regions(rows_ref, near_ref, place, near_out_ref, far_out_ref):
    member, own = place
    for k, (dx, dy, dz) in enumerate(DIRECTIONS):
        block = near_ref[0, k]
        distance = jnp.where(member == 0, block - own, own - block)
        face = (dx, dy, dz).count(0) == 2
        x, y, z = (15 if d == 1 else 0 for d in (dx, dy, dz))
        wanted = (block >= 0) & (distance >= 1)

        def region(dx=dx, dy=dy, dz=dz, x=x, y=y, z=z):
            zeros = [d == 0 for d in (dx, dy, dz)]
            if zeros == [False, True, True]:
                rows = rows_ref[x * 256 : x * 256 + 256, :]
            elif zeros == [True, False, True]:
                rows = jnp.concatenate(
                    [rows_ref[at * 256 + y * 16 : at * 256 + y * 16 + 16, :] for at in range(16)]
                )
            elif zeros == [True, True, False]:
                rows = rows_ref[pl.ds(z, 256, stride=16), :]
            elif zeros == [False, False, True]:
                rows = rows_ref[x * 256 + y * 16 : x * 256 + y * 16 + 16, :]
            elif zeros == [False, True, False]:
                rows = rows_ref[pl.ds(x * 256 + z, 16, stride=16), :]
            elif zeros == [True, False, False]:
                rows = rows_ref[pl.ds(y * 16 + z, 16, stride=256), :]
            else:
                at = x * 256 + y * 16 + z
                rows = jnp.broadcast_to(rows_ref[at : at + 1, :], (16, 128))
            return rows.astype(BF16)

        @pl.when(wanted & (distance <= NEAR))
        def _(region=region, distance=distance, height=256 if face else 16):
            near_out_ref[distance - 1, 0:height, :] = region()

        if not face:

            @pl.when(wanted & (distance > NEAR))
            def _(region=region, distance=distance):
                far_out_ref[distance - 1 - NEAR] = region()


class Whole:
    def __init__(self, ref):
        self.ref = ref

    def at(self, x, row, height):
        return self.ref, x, row


class Margin:
    def __init__(self, planes_ref, lines_ref):
        self.planes_ref, self.lines_ref = planes_ref, lines_ref

    def at(self, x, row, height):
        if x in (0, 17):
            return self.planes_ref, x // 17, row
        return self.lines_ref, row // 272, (x - 1) * 16


def put_lines(padded, places, rows):
    count = rows.shape[0]
    level = lax.broadcasted_iota(jnp.int32, rows.shape, 0) % 16
    below = jnp.where(level == 0, 0.0, pltpu.roll(rows, 1, 0)).astype(BF16)
    above = jnp.where(level == 15, 0.0, pltpu.roll(rows, count - 1, 0)).astype(BF16)
    here = rows.astype(BF16)
    at = 0
    for x, row, height in places:
        ref, plane, first = padded.at(x, row, height)
        for j, part in enumerate((below, here, above)):
            ref[plane, first : first + height, j * 128 : j * 128 + 128] = part[at : at + height]
        at += height


def put_ends(padded, x, row, rows, dz):
    lines = rows.shape[0]
    j = 0 if dz == -1 else 2
    end = 0 if dz == -1 else 15
    lanes = slice(j * 128, j * 128 + 128)
    ref, plane, first = padded.at(x, row, 16 * lines)
    span = slice(first, first + 16 * lines)
    old = ref[plane, span, lanes].astype(F32).reshape(lines, 16, 128)
    level = lax.broadcasted_iota(jnp.int32, old.shape, 1)
    new = jnp.where(level == end, rows.reshape(lines, 1, 128), old)
    ref[plane, span, lanes] = new.reshape(16 * lines, 128).astype(BF16)


def clear_margin(padded_ref):
    empty = jnp.zeros((288, 384), BF16)
    padded_ref[0] = empty
    padded_ref[17] = empty
    line = jnp.zeros((16, 384), BF16)
    for x in range(1, 17):
        padded_ref[x, 0:16, :] = line
        padded_ref[x, 272:288, :] = line


def put_region(padded, offset, rows):
    dx, dy, dz = offset
    zeros = [d == 0 for d in offset]
    x = 17 if dx == 1 else 0
    y = 17 if dy == 1 else 0
    if zeros == [False, True, True]:
        put_lines(padded, [(x, 16, 256)], rows)
    elif zeros == [True, False, True]:
        put_lines(padded, [(at + 1, y * 16, 16) for at in range(16)], rows)
    elif zeros == [False, False, True]:
        put_lines(padded, [(x, y * 16, 16)], rows)
    elif zeros == [True, True, False]:
        for at in range(16):
            put_ends(padded, at + 1, 16, rows[at * 16 : at * 16 + 16], dz)
    elif zeros == [False, True, False]:
        put_ends(padded, x, 16, rows, dz)
    elif zeros == [True, False, False]:
        for at in range(16):
            put_ends(padded, at + 1, y * 16, rows[at : at + 1], dz)
    else:
        put_ends(padded, x, y * 16, rows[0:1], dz)


def fill_grad_margin(padded, near_ref, place, own_ref, other_ref):
    for k in FILL_ORDER:
        offset = DIRECTIONS[k]
        block = near_ref[0, k]
        height = 256 if offset.count(0) == 2 else 16
        away = place[1] - block
        distance = jnp.abs(away)
        here = jnp.where(away > 0, 0, 1) == place[0]
        far = NEAR * 256 + (distance - 1 - NEAR) * 16
        start = (distance - 1) * 256 if height == 256 else jnp.where(
            distance <= NEAR, (distance - 1) * 256, far
        )

        @pl.when(block >= 0)
        def _(offset=offset, here=here, start=start, height=height):
            span = pl.ds(pl.multiple_of(start, 16), height)
            own = own_ref[span, :].astype(F32)
            other = swap_halves(other_ref[span, :].astype(F32))
            put_region(padded, offset, jnp.where(here, own, other))


def fill_margin(padded, near_ref, own_ref, other_ref):
    for k in FILL_ORDER:
        offset = DIRECTIONS[k]
        block = near_ref[0, k]
        face = offset.count(0) == 2
        if face and offset[2]:
            continue

        @pl.when(block >= 0)
        def _(offset=offset, block=block, face=face):
            height = 128 if face else 16
            own = own_ref[block, 0:height, :].astype(F32)
            other = other_ref[block, 0:height, :].astype(F32)
            first = jnp.where(low_lanes(own), own, swap_halves(other))
            second = jnp.where(low_lanes(own), swap_halves(own), other)
            if face:
                rows = jnp.concatenate([first, second])
            elif offset[0] == 0:
                rows = jnp.concatenate([first[:8], second[:8]])
            else:
                rows = first if offset[0] == 1 else second
            put_region(padded, offset, rows)


def send_features(
    near_hbm, heights_hbm, features_hbm, slots_ref,
    near_ref, heights_ref, features_ref, rows_ref, arrived
):
    copies = [
        pltpu.make_async_copy(near_hbm, near_ref, arrived.at[8]),
        pltpu.make_async_copy(heights_hbm, heights_ref, arrived.at[9]),
    ]
    order = (0, 1, 2, 3, 4, 5, 6, 7)
    bricks = [
        pltpu.make_async_copy(features_hbm.at[i], features_ref.at[i], arrived.at[i]) for i in order
    ]
    for copy in copies + bricks:
        copy.start()
    copies[1].wait()
    filled = filled_voxels(heights_ref)
    for oz in range(2):
        for oy in range(2):
            pair = []
            for ox in range(2):
                brick = ox + 2 * oy + 4 * oz
                bricks[brick].wait()
                pair.append(features_ref[brick].astype(F32) * filled[brick : brick + 1])
            turned = jnp.concatenate(pair).T
            for vx in range(8):
                for vy in range(8):
                    at = vx * 256 + (8 * oy + vy) * 16 + 8 * oz
                    source = (vx * 8 + vy) * 8
                    rows_ref[at : at + 8, :] = turned[source : source + 8]
    copies[0].wait()
    fill_slots(rows_ref, near_ref, slots_ref)


def own_first_taps(shift, conv_ref, yz):
    taps = []
    for ex in range(3):
        tap = conv_ref[ex * 9 + yz].astype(F32)
        taps.append(pltpu.roll(pltpu.roll(tap, shift, 0), shift, 1))
    return taps


def forward_weights(shift, conv_ref, down_in_ref, cot_in_ref, two_ref, down_ref, cot_ref):
    empty = jnp.zeros((128, 128), BF16)
    for yz in range(9):
        taps = own_first_taps(shift, conv_ref, yz)
        whole = [empty] + [tap.astype(BF16) for tap in taps] + [empty]
        for p in range(4):
            rows = slice((p * 9 + yz) * 128, (p * 9 + yz) * 128 + 128)
            two_ref[rows, 0:128] = whole[p + 1] if p < 3 else empty
            two_ref[rows, 128:256] = whole[p]
    for tap in range(8):
        rows = down_in_ref[tap].astype(F32)
        rows = pltpu.roll(rows, shift, 0)
        down_ref[tap * 128 : tap * 128 + 128, :] = pltpu.roll(rows, 2 * shift, 1).astype(BF16)
    cot_ref[...] = pltpu.roll(cot_in_ref[...].astype(F32), 2 * shift, 1).astype(BF16)


def backward_weights(shift, conv_ref, four_ref):
    empty = jnp.zeros((128, 128), BF16)
    none = jnp.zeros((64, 128), F32)
    for yz in range(9):
        taps = own_first_taps(shift, conv_ref, yz)
        own = [none] + [taps[2 - ex][:64] for ex in range(3)] + [none]
        pairs = [jnp.concatenate([own[i + 1], own[i]]).T.astype(BF16) for i in range(4)]
        for p in range(6):
            at = (p * 9 + 8 - yz) * 128
            four_ref[at : at + 128, 0:128] = pairs[p] if p < 4 else empty
            four_ref[at : at + 128, 128:256] = pairs[p - 2] if p >= 2 else empty


def own_lanes(triple):
    below, here = triple[:, 0:128].astype(F32), triple[:, 128:256].astype(F32)
    both = jnp.where(low_lanes(below), below, swap_halves(here)).astype(BF16)
    return both, triple[:, 256:384]


def prepare(
    core_ref, conv_hbm, down_hbm, cot_hbm, heights_hbm, own_hbm, other_hbm,
    lanes_hbm, active_hbm, slope_hbm, inner_hbm, taps_hbm, down_out_hbm, cot_out_hbm,
    conv_in_ref, down_in_ref, cot_in_ref, heights_ref, own_ref, other_ref,
    two_ref, down_ref, cot_ref, padded_ref, rows_ref, mask_ref, lanes_ref, active_ref,
    slope_ref, inner_ref, arrived, left, left_inner
):
    came = start_all(
        [
            (conv_hbm, conv_in_ref),
            (down_hbm, down_in_ref),
            (cot_hbm, cot_in_ref),
            (heights_hbm, heights_ref),
            (own_hbm, own_ref),
            (other_hbm, other_ref),
        ],
        arrived,
    )
    gone = [
        pltpu.make_async_copy(source, target, left.at[i])
        for i, (source, target) in enumerate(
            [
                (two_ref.at[0:3456, 0:128], taps_hbm),
                (down_ref, down_out_hbm),
                (cot_ref, cot_out_hbm),
                (lanes_ref, lanes_hbm),
                (active_ref, active_hbm),
                (slope_ref, slope_hbm),
            ]
        )
    ]
    for copy in came[:3]:
        copy.wait()
    forward_weights(
        core_ref[0] * 64, conv_in_ref, down_in_ref, cot_in_ref, two_ref, down_ref, cot_ref
    )
    for copy in gone[:3]:
        copy.start()
    for copy in came[3:]:
        copy.wait()
    filled = filled_voxels(heights_ref)
    upright = filled.T
    for brick in range(8):
        ox, oy, oz = brick % 2, brick // 2 % 2, brick // 4
        both = jnp.concatenate([own_ref[brick].astype(F32), other_ref[brick].astype(F32)])
        turned = (both * filled[brick : brick + 1]).T
        mask = jnp.broadcast_to(upright[:, brick : brick + 1], (512, 128))
        for vx in range(8):
            for vy in range(8):
                at = (8 * ox + vx) * 256 + (8 * oy + vy) * 16 + 8 * oz
                source = (vx * 8 + vy) * 8
                rows_ref[at : at + 8, :] = turned[source : source + 8]
                mask_ref[at : at + 8, :] = mask[source : source + 8]
    clear_margin(padded_ref)
    for x in range(16):
        put_lines(Whole(padded_ref), [(x + 1, 16, 256)], rows_ref[x * 256 : x * 256 + 256, :])
        active_ref[x * 256 : x * 256 + 256, :] = mask_ref[x * 256 : x * 256 + 256, :].astype(BF16)
    for x in range(18):
        lanes_ref[x, :, 0:128], lanes_ref[x, :, 128:256] = own_lanes(padded_ref[x])
    gone[3].start()
    gone[4].start()
    for tap in range(8):
        tx, ty, tz = tap // 4, tap // 2 % 2, tap % 2
        part = lax.dot_general(
            cot_ref[...],
            down_ref[tap * 128 : tap * 128 + 128, :],
            (((1,), (1,)), ((), ())),
            preferred_element_type=F32,
        )
        for ux in range(8):
            for uy in range(8):
                at = (2 * ux + tx) * 256 + (2 * uy + ty) * 16 + tz
                source = (ux * 8 + uy) * 8
                rows = pl.ds(at, 8, stride=2)
                slope_ref[rows, :] = part[source : source + 8] * mask_ref[rows, :]
    gone[5].start()

    def leave(group):
        rows = pl.ds(pl.multiple_of(group * 1024, 1024), 1024)
        return pltpu.make_async_copy(
            inner_ref.at[rows], inner_hbm.at[rows], left_inner.at[group]
        )


    def step(group, carry):
        lhs = []
        for pair in range(2):
            pieces = []
            for p in range(4):
                for ey in range(3):
                    pieces.append(
                        padded_ref[group * 4 + pair * 2 + p, ey * 16 : ey * 16 + 256, :]
                    )
            lhs.append(jnp.concatenate(pieces, axis=1))
        summed = jnp.dot(jnp.concatenate(lhs), two_ref[...], preferred_element_type=F32)
        for pair in range(2):
            for phase in range(2):
                at = pl.multiple_of((group * 4 + pair * 2 + phase) * 256, 256)
                part = summed[pair * 256 : pair * 256 + 256, phase * 128 : phase * 128 + 128]
                rows = pl.ds(at, 256)
                inner_ref[rows, :] = jnp.where(mask_ref[rows, :] > 0, part, INACTIVE)
        leave(group).start()
        return carry

    lax.fori_loop(0, 4, step, 0)
    for copy in gone:
        copy.wait()
    for group in range(4):
        leave(group).wait()


def tap_rows(taps_ref, taps):
    starts = [((ex * 3 + ey) * 3 + ez) * 128 for ex, ey, ez in taps]
    return jnp.concatenate([taps_ref[at : at + 128, :] for at in starts])


def margin_planes(planes_ref, taps_ref):
    sums = []
    for side, ex in ((0, 0), (1, 2)):
        lhs = jnp.concatenate(
            [planes_ref[side, ey * 16 : ey * 16 + 256, :] for ey in range(3)], axis=1
        )
        rhs = taps_ref[ex * 1152 : ex * 1152 + 1152, :]
        sums.append(jnp.dot(lhs, rhs, preferred_element_type=F32))
    return sums


def margin_lines(lines_ref, taps_ref):
    sums = []
    none = jnp.zeros((16, 384), BF16)
    for side, ey in ((0, 0), (1, 2)):
        lines = lines_ref[side]
        lhs = jnp.concatenate(
            [
                jnp.concatenate([none, lines[:240]]),
                lines,
                jnp.concatenate([lines[16:], none]),
            ],
            axis=1,
        )
        rhs = tap_rows(taps_ref, [(ex, ey, ez) for ex in range(3) for ez in range(3)])
        sums.append(jnp.dot(lhs, rhs, preferred_element_type=F32))
    return sums


def margin_ends(face, ez, taps_ref):
    line = lax.broadcasted_iota(jnp.int32, face.shape, 0) % 16
    shifted = [
        jnp.where(line == 0, 0.0, pltpu.roll(face, 1, 0)),
        face,
        jnp.where(line == 15, 0.0, pltpu.roll(face, 255, 0)),
    ]
    border = jnp.zeros((16, 128), F32)
    lhs = []
    for ex in range(3):
        for part in shifted:
            if ex == 0:
                part = jnp.concatenate([border, part[:240]])
            elif ex == 2:
                part = jnp.concatenate([part[16:], border])
            lhs.append(part.astype(BF16))
    rhs = tap_rows(taps_ref, [(ex, ey, ez) for ex in range(3) for ey in range(3)])
    return jnp.dot(jnp.concatenate(lhs, axis=1), rhs, preferred_element_type=F32)


Z_FACES = ((DIRECTIONS.index((0, 0, -1)), 0), (DIRECTIONS.index((0, 0, 1)), 2))


def joined_face(own_ref, other_ref, block):
    own = own_ref[block].astype(F32)
    other = other_ref[block].astype(F32)
    return jnp.concatenate(
        [
            jnp.where(low_lanes(own), own, swap_halves(other)),
            jnp.where(low_lanes(own), swap_halves(own), other),
        ]
    )


def add_margin(planes_ref, lines_ref, near_ref, own_ref, other_ref, taps_ref, pre_ref):
    for side, added in enumerate(margin_planes(planes_ref, taps_ref)):
        at = side * 15 * 256
        pre_ref[at : at + 256, :] += added
    for side, added in enumerate(margin_lines(lines_ref, taps_ref)):
        for x in range(16):
            at = x * 256 + side * 240
            pre_ref[at : at + 16, :] += added[x * 16 : x * 16 + 16]
    for k, ez in Z_FACES:
        block = near_ref[0, k]

        @pl.when(block >= 0)
        def _(block=block, ez=ez):
            added = margin_ends(joined_face(own_ref, other_ref, block), ez, taps_ref)
            rows = pl.ds(0 if ez == 0 else 15, 256, stride=16)
            pre_ref[rows, :] = pre_ref[rows, :] + added


def put_own_margin(planes_ref, lines_ref, near_ref, own_ref, other_ref, lanes_ref):
    for side in range(2):
        plane = side * 17
        lanes_ref[plane, :, 0:128], lanes_ref[plane, :, 128:256] = own_lanes(planes_ref[side])
        both, above = own_lanes(lines_ref[side])
        rows = slice(side * 272, side * 272 + 16)
        for x in range(16):
            lanes_ref[x + 1, rows, 0:128] = both[x * 16 : x * 16 + 16]
            lanes_ref[x + 1, rows, 128:256] = above[x * 16 : x * 16 + 16]
    for k, ez in Z_FACES:
        block = near_ref[0, k]

        @pl.when(block >= 0)
        def _(block=block, ez=ez):
            face = joined_face(own_ref, other_ref, block)
            lanes = slice(ez * 64, ez * 64 + 128)
            for x in range(16):
                old = lanes_ref[x + 1, 16:272, lanes].astype(F32).reshape(16, 16, 128)
                level = lax.broadcasted_iota(jnp.int32, old.shape, 1)
                lane = lax.broadcasted_iota(jnp.int32, old.shape, 2)
                here = (level == (0 if ez == 0 else 15)) & (lane < 64)
                new = jnp.where(here, face[x * 16 : x * 16 + 16].reshape(16, 1, 128), old)
                lanes_ref[x + 1, 16:272, lanes] = new.reshape(256, 128).astype(BF16)


def forward(
    near_ref, core_ref, at_ref, own_ref, other_ref, taps_ref, inner_ref, slope_ref,
    lanes_hbm, down_hbm, cot_hbm,
    terms_hbm, near_out_ref, far_out_ref, coarse_hbm, grad_pre_hbm,
    planes_ref, lines_ref, pre_ref, grad_ref, turned_ref, lanes_ref,
    down_ref, cot_ref, coarse_ref, grad_pre_ref, terms_ref, arrived, left, left_terms
):
    came = start_all(
        [(lanes_hbm, lanes_ref), (down_hbm, down_ref), (cot_hbm, cot_ref)], arrived
    )
    pre_ref[...] = inner_ref[...]
    planes_ref[...] = jnp.zeros(planes_ref.shape, BF16)
    lines_ref[...] = jnp.zeros(lines_ref.shape, BF16)
    margin = Margin(planes_ref, lines_ref)
    fill_margin(margin, near_ref, own_ref, other_ref)
    add_margin(planes_ref, lines_ref, near_ref, own_ref, other_ref, taps_ref, pre_ref)

    turned_ref[:, 0:512] = jnp.zeros((128, 512), BF16)
    turned_ref[:, 4608:5120] = jnp.zeros((128, 512), BF16)
    for x in range(16):
        rows = slice(x * 256, x * 256 + 256)
        pre = pre_ref[rows, :]
        sigmoid = 0.5 + 0.5 * jnp.tanh(0.5 * pre)
        pre_ref[rows, :] = jnp.where(pre > 0.5 * INACTIVE, pre * sigmoid, 0.0)
        grad = slope_ref[rows, :] * sigmoid * (1.0 + pre * (1.0 - sigmoid))
        grad_ref[rows, :] = grad
        grad = grad.astype(BF16)
        grad_pre_ref[rows, :] = grad
        turned_ref[:, 512 + x * 256 : 768 + x * 256] = grad.T

    gone = [
        pltpu.make_async_copy(grad_pre_ref, grad_pre_hbm, left.at[0]),
        pltpu.make_async_copy(coarse_ref, coarse_hbm, left.at[1]),
    ]
    gone[0].start()
    fill_regions(grad_ref, near_ref, (core_ref[0], at_ref[0]), near_out_ref, far_out_ref)

    def leave(i, first, last):
        return pltpu.make_async_copy(
            terms_ref.at[first:last], terms_hbm.at[first:last], left_terms.at[i]
        )

    ends = [1024, 1600, 2176, terms_ref.shape[0]]
    leaving = [leave(i, first, last) for i, (first, last) in enumerate(zip([0] + ends, ends))]

    came[1].wait()
    came[2].wait()
    patches = []
    for tap in range(8):
        tx, ty, tz = tap // 4, tap // 2 % 2, tap % 2
        pieces = []
        for ux in range(8):
            for uy in range(8):
                at = (2 * ux + tx) * 256 + (2 * uy + ty) * 16 + tz
                pieces.append(pre_ref[pl.ds(at, 8, stride=2), :])
        patches.append(jnp.concatenate(pieces).astype(BF16))
    patches = jnp.concatenate(patches, axis=1)
    coarse = jnp.dot(patches, down_ref[...], preferred_element_type=F32)
    coarse_ref[...] = coarse[:, :128].astype(BF16)
    gone[1].start()
    own_cot = cot_ref[:, 0:128].astype(F32).T.astype(BF16)
    grad_down = jnp.dot(own_cot, patches, preferred_element_type=F32)
    for tap in range(8):
        part = grad_down[:, tap * 128 : tap * 128 + 128].T
        terms_ref[tap * 128 : tap * 128 + 128, :] = part.astype(BF16)
    leaving[0].start()

    came[0].wait()
    put_own_margin(planes_ref, lines_ref, near_ref, own_ref, other_ref, lanes_ref)
    lhs = jnp.concatenate(
        [turned_ref[:, (2 - ex) * 256 : (2 - ex) * 256 + 4608] for ex in range(3)]
    )
    for ey in range(3):
        rhs = lanes_ref[:, ey * 16 : ey * 16 + 256, :].reshape(4608, 256)
        summed = jnp.dot(lhs, rhs, preferred_element_type=F32)
        for ex in range(3):
            part = summed[ex * 128 : ex * 128 + 128].T
            at = 1024 + (ey * 3 + ex) * 192
            terms_ref[at : at + 192, :] = part[0:192].astype(BF16)
        leaving[ey + 1].start()
    for copy in gone + leaving:
        copy.wait()


def fetch(taps_hbm, inner_hbm, slope_hbm, taps_ref, inner_ref, slope_ref, arrived):
    for copy in start_all(
        [(taps_hbm, taps_ref), (inner_hbm, inner_ref), (slope_hbm, slope_ref)], arrived
    ):
        copy.wait()


def total(scale, parts_ref, out_hbm, sum_ref, left):
    summed = parts_ref[0].astype(F32)
    for part in range(1, parts_ref.shape[0]):
        summed = summed + parts_ref[part].astype(F32)
    sum_ref[...] = (summed * scale).astype(BF16)
    repeat(sum_ref, out_hbm, left)


def repeat(rows_ref, out_hbm, left):
    copies = [
        pltpu.make_async_copy(rows_ref, out_hbm.at[i], left.at[i])
        for i in range(out_hbm.shape[0])
    ]
    for copy in copies:
        copy.start()
    for copy in copies:
        copy.wait()


def backward(
    near_ref, core_ref, at_ref, own_ref, other_ref,
    grad_pre_hbm, active_hbm, conv_hbm, out_ref,
    padded_ref, grad_pre_ref, active_ref, conv_ref, back_ref, arrived
):
    came = start_all(
        [(conv_hbm, conv_ref), (grad_pre_hbm, grad_pre_ref), (active_hbm, active_ref)], arrived
    )
    came[0].wait()
    backward_weights(core_ref[0] * 64, conv_ref, back_ref)
    clear_margin(padded_ref)
    came[1].wait()
    for x in range(16):
        rows = grad_pre_ref[x * 256 : x * 256 + 256, :].astype(F32)
        put_lines(Whole(padded_ref), [(x + 1, 16, 256)], rows)
    place = (core_ref[0], at_ref[0])
    fill_grad_margin(Whole(padded_ref), near_ref, place, own_ref, other_ref)
    came[2].wait()
    for half in range(2):
        lhs = []
        for quad in range(2):
            pieces = []
            for p in range(6):
                for ey in range(3):
                    pieces.append(
                        padded_ref[half * 8 + quad * 4 + p, ey * 16 : ey * 16 + 256, :]
                    )
            lhs.append(jnp.concatenate(pieces, axis=1))
        summed = jnp.dot(jnp.concatenate(lhs), back_ref[...], preferred_element_type=F32)
        for quad in range(2):
            for two in range(2):
                part = summed[quad * 256 : quad * 256 + 256, two * 128 : two * 128 + 128]
                x = half * 8 + quad * 4 + two * 2
                even = active_ref[x * 256 : x * 256 + 256, :].astype(F32)
                odd = active_ref[x * 256 + 256 : x * 256 + 512, :].astype(F32)
                part = part * jnp.where(low_lanes(part), even, odd)
                for oy in range(2):
                    rows = [
                        part[(8 * oy + vy) * 16 + 8 * oz : (8 * oy + vy) * 16 + 8 * oz + 8]
                        for oz in range(2)
                        for vy in range(8)
                    ]
                    turned = jnp.concatenate(rows).T
                    first, second = turned[:64], turned[64:]
                    lanes = slice(x % 8 * 64, x % 8 * 64 + 128)
                    brick = half + 2 * oy
                    near = jnp.where(low_lanes(first), first, swap_halves(second))
                    far = jnp.where(low_lanes(first), swap_halves(first), second)
                    out_ref[brick, :, lanes] = near.astype(BF16)
                    out_ref[brick + 4, :, lanes] = far.astype(BF16)


def finish(core_ref, sums_ref, conv_ref, down_ref):
    shift = core_ref[0] * 64
    for tap in range(27):
        ex, ey, ez = tap // 9, tap // 3 % 3, tap % 3
        at = 1024 + ((ey * 3 + ex) * 3 + ez) * 64
        rows = sums_ref[at : at + 64, :].astype(F32)
        conv_ref[tap] = pltpu.roll(rows, shift, 1)
    for tap in range(8):
        rows = sums_ref[tap * 128 : tap * 128 + 128, :].astype(F32)
        down_ref[tap, pl.ds(shift, 64), :] = rows[:64]
        down_ref[tap, pl.ds(64 - shift, 64), :] = rows[64:]


def over_space(block, distance):
    blocks = range(lax.axis_size("space"))
    route = [(2 * i, 2 * (i + distance)) for i in blocks if i + distance in blocks]
    route += [(2 * i + 1, 2 * (i - distance) + 1) for i in blocks if i - distance in blocks]
    return lax.ppermute(block, ("space", "chan"), route)


def over_chan(block):
    return lax.ppermute(block, "chan", [(0, 1), (1, 0)])


def to_all(slots):
    return lax.all_to_all(slots, "space", 0, 0, tiled=True)


def to_group(slots, inner):
    devices = lax.axis_size("space")
    if inner:
        groups = [[i + j for j in range(INNER)] for i in range(0, devices, INNER)]
    else:
        groups = [[i + j for j in range(0, devices, INNER)] for i in range(INNER)]
    return lax.all_to_all(slots, "space", 0, 0, axis_index_groups=groups, tiled=True)


def local(features, heights, neighbours, w_conv, w_down, cotangent):
    devices = lax.axis_size("space")
    member = lax.axis_index("chan")

    def out(*shape, dtype=BF16):
        return jax.ShapeDtypeStruct(shape, dtype)

    def held_out(*shape, dtype=BF16):
        return pltpu.HBM(shape, dtype)

    def memory(*shape, dtype=BF16):
        return pltpu.VMEM(shape, dtype)

    def copies(count):
        return pltpu.SemaphoreType.DMA((count,))

    core = member.reshape(1)
    place = (core, lax.axis_index("space").reshape(1))
    turned = features.transpose(0, 2, 1)
    slots = kernel_call(
        send_features,
        out(devices, 128, 128),
        [hbm()] * 3,
        vmem(),
        [
            pltpu.SMEM(neighbours.shape, jnp.int32),
            memory(8, 64, dtype=jnp.int32),
            memory(8, 64, 512),
            memory(2048, 128, dtype=F32),
            copies(10),
        ],
    )(neighbours, heights, turned)
    came = to_all(slots)
    other_turned = over_chan(turned)

    held = [
        held_out(18, 288, 256),
        held_out(4096, 128),
        held_out(4096, 128, dtype=F32),
        held_out(4096, 128, dtype=F32),
        held_out(3456, 128),
        held_out(1024, 256),
        held_out(512, 256),
    ]
    lanes, active, slope, inner, taps, down, cot = kernel_call(
        prepare,
        held,
        [smem()] + [hbm()] * 5 + [pl.BlockSpec(memory_space=pl.ANY)],
        [hbm()] * 7,
        [
            memory(27, 128, 128),
            memory(8, 128, 256),
            memory(512, 256),
            memory(8, 64, dtype=jnp.int32),
            memory(8, 64, 512),
            memory(8, 64, 512),
            memory(4608, 256),
            memory(1024, 256),
            memory(512, 256),
            memory(18, 288, 384),
            memory(4096, 128, dtype=F32),
            memory(4096, 128, dtype=F32),
            memory(18, 288, 256),
            memory(4096, 128),
            memory(4096, 128, dtype=F32),
            memory(4096, 128, dtype=F32),
            copies(6),
            copies(6),
            copies(4),
        ],
        flops=5 << 30,
        mib=36,
    )(core, w_conv, w_down, cotangent[0], heights, turned, other_turned)
    came, taps, inner, slope = lax.optimization_barrier((came, taps, inner, slope))
    came_other = over_chan(came)
    taps, inner, slope = kernel_call(
        fetch,
        [out(3456, 128), out(4096, 128, dtype=F32), out(4096, 128, dtype=F32)],
        [hbm()] * 3,
        [vmem()] * 3,
        [copies(3)],
    )(taps, inner, slope)

    outer = devices // INNER
    share = -(-2752 // (devices * 16)) * 16
    height = share * outer
    terms, near_out, far_out, coarse, grad_pre = kernel_call(
        forward,
        [
            held_out(INNER * height, 128),
            out(NEAR, 256, 128),
            out(FAR - NEAR, 16, 128),
            held_out(512, 128),
            held_out(4096, 128),
        ],
        [smem()] * 3 + [vmem()] * 5 + [hbm()] * 3,
        [hbm(), vmem(), vmem(), hbm(), hbm()],
        [
            memory(2, 288, 384),
            memory(2, 256, 384),
            memory(4096, 128, dtype=F32),
            memory(4096, 128, dtype=F32),
            memory(128, 5120),
            memory(18, 288, 256),
            memory(1024, 256),
            memory(512, 256),
            memory(512, 128),
            memory(4096, 128),
            memory(INNER * height, 128),
            copies(3),
            copies(2),
            copies(4),
        ],
        flops=5 << 30,
        mib=24,
    )(
        neighbours, *place, came, came_other, taps, inner, slope, lanes, down, cot
    )

    def sum_of(parts, times, scale):
        rows = parts.shape[1]
        return kernel_call(
            functools.partial(total, scale),
            held_out(times, rows, 128),
            [vmem()],
            hbm(),
            [memory(rows, 128), copies(times)],
        )(parts)

    arrived = to_group(terms.reshape(INNER, height, 128), True)
    near_came = [over_space(near_out[i], i + 1) for i in range(NEAR)]
    arrived, *near_came = lax.optimization_barrier((arrived, *near_came))
    part = sum_of(arrived, 1, 1.0).reshape(outer, share, 128)
    arrived = to_group(part, False)
    far_came = [over_space(far_out[i], NEAR + i + 1) for i in range(FAR - NEAR)]
    arrived, *far_came = lax.optimization_barrier((arrived, *far_came))
    whole = to_group(sum_of(arrived, outer, 1.0 / devices), False)
    own_regions = jnp.concatenate(near_came + far_came)
    other_regions = over_chan(own_regions)
    whole, own_regions, other_regions = lax.optimization_barrier(
        (whole, own_regions, other_regions)
    )
    sums = to_group(
        kernel_call(
            repeat, held_out(INNER, height, 128), [vmem()], hbm(), [copies(INNER)]
        )(whole.reshape(height, 128)),
        True,
    )
    grad_features = kernel_call(
        backward,
        out(8, 64, 512),
        [smem()] * 3 + [vmem()] * 2 + [hbm()] * 3,
        vmem(),
        [
            memory(18, 288, 384),
            memory(4096, 128),
            memory(4096, 128),
            memory(27, 128, 128),
            memory(6912, 256),
            copies(3),
        ],
        flops=5 << 30,
        mib=24,
    )(neighbours, *place, own_regions, other_regions, grad_pre, active, w_conv)

    grad_conv, grad_down = kernel_call(
        finish,
        [out(27, 64, 128, dtype=F32), out(8, 128, 128, dtype=F32)],
        [smem(), vmem()],
        [vmem()] * 2,
    )(core, sums.reshape(-1, 128))
    return coarse[None], grad_conv, grad_down, grad_features.transpose(0, 2, 1)


def solution(mesh):
    placed = (
        P("space", None, "chan"),
        P("space", None),
        P("space", None),
        P(),
        P(),
        P("space", None, None),
    )
    return jax.shard_map(
        local,
        mesh=mesh,
        in_specs=placed,
        out_specs=(
            P("space", None, "chan"),
            P(None, "chan", None),
            P(None, None, "chan"),
            P("space", None, "chan"),
        ),
        check_vma=False,
    )
```

```python
import jax
import jax.numpy as jnp
from jax import lax
from jax.experimental import pallas as pl
from jax.experimental.pallas import tpu as pltpu
from jax.sharding import PartitionSpec as P

OFFSETS = [
    (along_x, along_y, along_z)
    for along_x in (-1, 0, 1)
    for along_y in (-1, 0, 1)
    for along_z in (-1, 0, 1)
]
DIRECTIONS = [offset for offset in OFFSETS if offset != (0, 0, 0)]
FILL_ORDER = sorted(range(26), key=lambda k: (abs(DIRECTIONS[k][2]), k))
INACTIVE = -1e30
F32 = jnp.float32
BF16 = jnp.bfloat16


def vmem():
    return pl.BlockSpec(memory_space=pltpu.VMEM)


def smem():
    return pl.BlockSpec(memory_space=pltpu.SMEM)


def hbm():
    return pl.BlockSpec(memory_space=pltpu.HBM)


def kernel_call(body, outs, specs, out_specs, scratch=(), flops=0, mib=16):
    call = pl.pallas_call(
        body,
        out_shape=outs,
        in_specs=specs,
        out_specs=out_specs,
        scratch_shapes=list(scratch),
        compiler_params=pltpu.CompilerParams(vmem_limit_bytes=mib * 1024 * 1024),
        cost_estimate=pl.CostEstimate(flops=flops, bytes_accessed=1 << 22, transcendentals=0),
    )

    def run(*operands):
        placed = []
        for spec, operand in zip(specs, operands):
            if spec.memory_space == pltpu.HBM:
                operand = pltpu.with_memory_space_constraint(operand, pltpu.HBM)
            placed.append(operand)
        return call(*placed)

    return run


def start_all(pairs, arrived):
    copies = [
        pltpu.make_async_copy(source, target, arrived.at[i])
        for i, (source, target) in enumerate(pairs)
    ]
    for copy in copies:
        copy.start()
    return copies


def swap_halves(rows):
    return pltpu.roll(rows, 64, 1)


def low_lanes(rows):
    return lax.broadcasted_iota(jnp.int32, rows.shape, 1) < 64


def filled_voxels(heights_ref):
    columns = lax.broadcasted_iota(jnp.int32, (64, 512), 0)
    voxels = lax.broadcasted_iota(jnp.int32, (64, 512), 1)
    spread = (voxels // 8 == columns).astype(F32)
    tall = jnp.dot(heights_ref[...].astype(F32), spread, preferred_element_type=F32)
    level = lax.broadcasted_iota(jnp.int32, tall.shape, 1) % 8
    return (level.astype(F32) < tall).astype(F32)


def fill_slots(rows_ref, near_ref, slots_ref):
    for k, (dx, dy, dz) in enumerate(DIRECTIONS):
        block = near_ref[0, k]
        xh = 7 if dx == 1 else 0
        y = 15 if dy == 1 else 0
        z = 15 if dz == 1 else 0

        @pl.when(block >= 0)
        def _(dx=dx, dy=dy, dz=dz, xh=xh, y=y, z=z, block=block):
            zeros = [d == 0 for d in (dx, dy, dz)]
            if zeros == [False, True, True]:
                plane = rows_ref[xh * 256 : xh * 256 + 256, :]
                first, second = plane[:128], plane[128:]
                if dx == -1:
                    second = swap_halves(second)
                else:
                    first = swap_halves(first)
                region = jnp.where(low_lanes(first), first, second)
            elif zeros == [True, False, True]:
                region = jnp.concatenate(
                    [rows_ref[x * 256 + y * 16 : x * 256 + y * 16 + 16, :] for x in range(8)]
                )
            elif zeros == [True, True, False]:
                region = rows_ref[pl.ds(z, 128, stride=16), :]
            elif zeros == [False, False, True]:
                region = rows_ref[xh * 256 + y * 16 : xh * 256 + y * 16 + 16, :]
            elif zeros == [False, True, False]:
                region = rows_ref[pl.ds(xh * 256 + z, 16, stride=16), :]
            elif zeros == [True, False, False]:
                line = rows_ref[pl.ds(y * 16 + z, 8, stride=256), :]
                region = jnp.concatenate([line, line])
            else:
                at = xh * 256 + y * 16 + z
                region = jnp.broadcast_to(rows_ref[at : at + 1, :], (16, 128))
            slots_ref[block, 0 : region.shape[0], :] = region.astype(BF16)


def fill_edges(rows_ref, near_ref, slots_ref, start):
    for k, (dx, dy, dz) in enumerate(DIRECTIONS):
        if (dx, dy, dz).count(0) == 2:
            continue
        block = near_ref[0, k]
        x, y, z = (15 if d == 1 else 0 for d in (dx, dy, dz))

        @pl.when(block >= 0)
        def _(dx=dx, dy=dy, dz=dz, x=x, y=y, z=z, block=block):
            if dx == 0:
                line = rows_ref[pl.ds(y * 16 + z, 16, stride=256), :]
                low, high = line[:8], swap_halves(line[8:])
                line = jnp.where(low_lanes(low), low, high)
                rows = jnp.concatenate([line, line])
            elif dz == 0:
                rows = rows_ref[x * 256 + y * 16 : x * 256 + y * 16 + 16, :]
            elif dy == 0:
                rows = rows_ref[pl.ds(x * 256 + z, 16, stride=16), :]
            else:
                at = x * 256 + y * 16 + z
                rows = jnp.broadcast_to(rows_ref[at : at + 1, :], (16, 128))
            if dx == 1:
                rows = swap_halves(rows)
            slots_ref[block, start : start + 16, :] = rows.astype(BF16)


def fill_faces(rows_ref, near_ref, place, faces_ref):
    member, own = place
    for k, (dx, dy, dz) in enumerate(DIRECTIONS):
        if (dx, dy, dz).count(0) != 2:
            continue
        block = near_ref[0, k]
        distance = jnp.where(member == 0, block - own, own - block)
        end = 15 if dx + dy + dz == 1 else 0

        @pl.when((block >= 0) & (distance >= 1))
        def _(dx=dx, dy=dy, end=end, distance=distance):
            if dx:
                region = rows_ref[end * 256 : end * 256 + 256, :]
            elif dy:
                region = jnp.concatenate(
                    [rows_ref[x * 256 + end * 16 : x * 256 + end * 16 + 16, :] for x in range(16)]
                )
            else:
                region = rows_ref[pl.ds(end, 256, stride=16), :]
            faces_ref[distance - 1] = region.astype(BF16)


class Whole:
    def __init__(self, ref):
        self.ref = ref

    def at(self, x, row, height):
        return self.ref, x, row


class Margin:
    def __init__(self, planes_ref, lines_ref):
        self.planes_ref, self.lines_ref = planes_ref, lines_ref

    def at(self, x, row, height):
        if x in (0, 17):
            return self.planes_ref, x // 17, row
        return self.lines_ref, row // 272, (x - 1) * 16


def put_lines(padded, places, rows):
    count = rows.shape[0]
    level = lax.broadcasted_iota(jnp.int32, rows.shape, 0) % 16
    below = jnp.where(level == 0, 0.0, pltpu.roll(rows, 1, 0)).astype(BF16)
    above = jnp.where(level == 15, 0.0, pltpu.roll(rows, count - 1, 0)).astype(BF16)
    here = rows.astype(BF16)
    at = 0
    for x, row, height in places:
        ref, plane, first = padded.at(x, row, height)
        for j, part in enumerate((below, here, above)):
            ref[plane, first : first + height, j * 128 : j * 128 + 128] = part[at : at + height]
        at += height


def put_ends(padded, x, row, rows, dz):
    lines = rows.shape[0]
    j = 0 if dz == -1 else 2
    end = 0 if dz == -1 else 15
    lanes = slice(j * 128, j * 128 + 128)
    ref, plane, first = padded.at(x, row, 16 * lines)
    span = slice(first, first + 16 * lines)
    old = ref[plane, span, lanes].astype(F32).reshape(lines, 16, 128)
    level = lax.broadcasted_iota(jnp.int32, old.shape, 1)
    new = jnp.where(level == end, rows.reshape(lines, 1, 128), old)
    ref[plane, span, lanes] = new.reshape(16 * lines, 128).astype(BF16)


def clear_margin(padded_ref):
    empty = jnp.zeros((288, 384), BF16)
    padded_ref[0] = empty
    padded_ref[17] = empty
    line = jnp.zeros((16, 384), BF16)
    for x in range(1, 17):
        padded_ref[x, 0:16, :] = line
        padded_ref[x, 272:288, :] = line


def put_region(padded, offset, rows):
    dx, dy, dz = offset
    zeros = [d == 0 for d in offset]
    x = 17 if dx == 1 else 0
    y = 17 if dy == 1 else 0
    if zeros == [False, True, True]:
        put_lines(padded, [(x, 16, 256)], rows)
    elif zeros == [True, False, True]:
        put_lines(padded, [(at + 1, y * 16, 16) for at in range(16)], rows)
    elif zeros == [False, False, True]:
        put_lines(padded, [(x, y * 16, 16)], rows)
    elif zeros == [True, True, False]:
        for at in range(16):
            put_ends(padded, at + 1, 16, rows[at * 16 : at * 16 + 16], dz)
    elif zeros == [False, True, False]:
        put_ends(padded, x, 16, rows, dz)
    elif zeros == [True, False, False]:
        for at in range(16):
            put_ends(padded, at + 1, y * 16, rows[at : at + 1], dz)
    else:
        put_ends(padded, x, y * 16, rows[0:1], dz)


def face_source(place, block):
    away = place[1] - block
    return jnp.where(away > 0, 0, 1) == place[0], jnp.clip(jnp.abs(away) - 1, 0, 3)


def fill_margin(padded, near_ref, own_ref, other_ref, start=0, faces=None, z_faces=True):
    for k in FILL_ORDER:
        offset = DIRECTIONS[k]
        block = near_ref[0, k]
        face = offset.count(0) == 2
        if face and offset[2] and not z_faces:
            continue
        if face and faces is not None:
            place, own_faces_ref, other_faces_ref = faces
            here, slot = face_source(place, block)

            @pl.when((block >= 0) & here)
            def _(offset=offset, slot=slot):
                put_region(padded, offset, own_faces_ref[slot].astype(F32))

            @pl.when((block >= 0) & jnp.logical_not(here))
            def _(offset=offset, slot=slot):
                rows = swap_halves(other_faces_ref[slot].astype(F32))
                put_region(padded, offset, rows)

            continue

        @pl.when(block >= 0)
        def _(offset=offset, block=block, face=face):
            height = 128 if face else 16
            own = own_ref[block, start : start + height, :].astype(F32)
            other = other_ref[block, 0:height, :].astype(F32)
            first = jnp.where(low_lanes(own), own, swap_halves(other))
            second = jnp.where(low_lanes(own), swap_halves(own), other)
            if face:
                rows = jnp.concatenate([first, second])
            elif offset[0] == 0:
                rows = jnp.concatenate([first[:8], second[:8]])
            else:
                rows = first if offset[0] == 1 else second
            put_region(padded, offset, rows)


def send_features(
    near_hbm, heights_hbm, features_hbm, slots_ref,
    near_ref, heights_ref, features_ref, rows_ref, arrived
):
    copies = [
        pltpu.make_async_copy(near_hbm, near_ref, arrived.at[8]),
        pltpu.make_async_copy(heights_hbm, heights_ref, arrived.at[9]),
    ]
    order = (0, 1, 2, 3, 4, 5, 6, 7)
    bricks = [
        pltpu.make_async_copy(features_hbm.at[i], features_ref.at[i], arrived.at[i]) for i in order
    ]
    for copy in copies + bricks:
        copy.start()
    copies[1].wait()
    filled = filled_voxels(heights_ref)
    for oz in range(2):
        for oy in range(2):
            pair = []
            for ox in range(2):
                brick = ox + 2 * oy + 4 * oz
                bricks[brick].wait()
                pair.append(features_ref[brick].astype(F32) * filled[brick : brick + 1])
            turned = jnp.concatenate(pair).T
            for vx in range(8):
                for vy in range(8):
                    at = vx * 256 + (8 * oy + vy) * 16 + 8 * oz
                    source = (vx * 8 + vy) * 8
                    rows_ref[at : at + 8, :] = turned[source : source + 8]
    copies[0].wait()
    fill_slots(rows_ref, near_ref, slots_ref)


def own_first_taps(shift, conv_ref, yz):
    taps = []
    for ex in range(3):
        tap = conv_ref[ex * 9 + yz].astype(F32)
        taps.append(pltpu.roll(pltpu.roll(tap, shift, 0), shift, 1))
    return taps


def forward_weights(shift, conv_ref, down_in_ref, cot_in_ref, two_ref, down_ref, cot_ref):
    empty = jnp.zeros((128, 128), BF16)
    for yz in range(9):
        taps = own_first_taps(shift, conv_ref, yz)
        whole = [empty] + [tap.astype(BF16) for tap in taps] + [empty]
        for p in range(4):
            rows = slice((p * 9 + yz) * 128, (p * 9 + yz) * 128 + 128)
            two_ref[rows, 0:128] = whole[p + 1] if p < 3 else empty
            two_ref[rows, 128:256] = whole[p]
    for tap in range(8):
        rows = down_in_ref[tap].astype(F32)
        rows = pltpu.roll(rows, shift, 0)
        down_ref[tap * 128 : tap * 128 + 128, :] = pltpu.roll(rows, 2 * shift, 1).astype(BF16)
    cot_ref[...] = pltpu.roll(cot_in_ref[...].astype(F32), 2 * shift, 1).astype(BF16)


def backward_weights(shift, conv_ref, four_ref):
    empty = jnp.zeros((128, 128), BF16)
    none = jnp.zeros((64, 128), F32)
    for yz in range(9):
        taps = own_first_taps(shift, conv_ref, yz)
        own = [none] + [taps[2 - ex][:64] for ex in range(3)] + [none]
        pairs = [jnp.concatenate([own[i + 1], own[i]]).T.astype(BF16) for i in range(4)]
        for p in range(6):
            at = (p * 9 + 8 - yz) * 128
            four_ref[at : at + 128, 0:128] = pairs[p] if p < 4 else empty
            four_ref[at : at + 128, 128:256] = pairs[p - 2] if p >= 2 else empty


def own_lanes(triple):
    below, here = triple[:, 0:128].astype(F32), triple[:, 128:256].astype(F32)
    both = jnp.where(low_lanes(below), below, swap_halves(here)).astype(BF16)
    return both, triple[:, 256:384]


def prepare(
    core_ref, conv_hbm, down_hbm, cot_hbm, heights_hbm, own_hbm, other_hbm,
    lanes_hbm, active_hbm, slope_hbm, inner_hbm, taps_hbm, down_out_hbm, cot_out_hbm,
    conv_in_ref, down_in_ref, cot_in_ref, heights_ref, own_ref, other_ref,
    two_ref, down_ref, cot_ref, padded_ref, rows_ref, mask_ref, lanes_ref, active_ref,
    slope_ref, inner_ref, arrived, left, left_inner
):
    came = start_all(
        [
            (conv_hbm, conv_in_ref),
            (down_hbm, down_in_ref),
            (cot_hbm, cot_in_ref),
            (heights_hbm, heights_ref),
            (own_hbm, own_ref),
            (other_hbm, other_ref),
        ],
        arrived,
    )
    gone = [
        pltpu.make_async_copy(source, target, left.at[i])
        for i, (source, target) in enumerate(
            [
                (two_ref.at[0:3456, 0:128], taps_hbm),
                (down_ref, down_out_hbm),
                (cot_ref, cot_out_hbm),
                (lanes_ref, lanes_hbm),
                (active_ref, active_hbm),
                (slope_ref, slope_hbm),
            ]
        )
    ]
    for copy in came[:3]:
        copy.wait()
    forward_weights(
        core_ref[0] * 64, conv_in_ref, down_in_ref, cot_in_ref, two_ref, down_ref, cot_ref
    )
    for copy in gone[:3]:
        copy.start()
    for copy in came[3:]:
        copy.wait()
    filled = filled_voxels(heights_ref)
    upright = filled.T
    for brick in range(8):
        ox, oy, oz = brick % 2, brick // 2 % 2, brick // 4
        both = jnp.concatenate([own_ref[brick].astype(F32), other_ref[brick].astype(F32)])
        turned = (both * filled[brick : brick + 1]).T
        mask = jnp.broadcast_to(upright[:, brick : brick + 1], (512, 128))
        for vx in range(8):
            for vy in range(8):
                at = (8 * ox + vx) * 256 + (8 * oy + vy) * 16 + 8 * oz
                source = (vx * 8 + vy) * 8
                rows_ref[at : at + 8, :] = turned[source : source + 8]
                mask_ref[at : at + 8, :] = mask[source : source + 8]
    clear_margin(padded_ref)
    for x in range(16):
        put_lines(Whole(padded_ref), [(x + 1, 16, 256)], rows_ref[x * 256 : x * 256 + 256, :])
        active_ref[x * 256 : x * 256 + 256, :] = mask_ref[x * 256 : x * 256 + 256, :].astype(BF16)
    for x in range(18):
        lanes_ref[x, :, 0:128], lanes_ref[x, :, 128:256] = own_lanes(padded_ref[x])
    gone[3].start()
    gone[4].start()
    for tap in range(8):
        tx, ty, tz = tap // 4, tap // 2 % 2, tap % 2
        part = lax.dot_general(
            cot_ref[...],
            down_ref[tap * 128 : tap * 128 + 128, :],
            (((1,), (1,)), ((), ())),
            preferred_element_type=F32,
        )
        for ux in range(8):
            for uy in range(8):
                at = (2 * ux + tx) * 256 + (2 * uy + ty) * 16 + tz
                source = (ux * 8 + uy) * 8
                rows = pl.ds(at, 8, stride=2)
                slope_ref[rows, :] = part[source : source + 8] * mask_ref[rows, :]
    gone[5].start()

    def leave(group):
        rows = pl.ds(pl.multiple_of(group * 1024, 1024), 1024)
        return pltpu.make_async_copy(
            inner_ref.at[rows], inner_hbm.at[rows], left_inner.at[group]
        )


    def step(group, carry):
        lhs = []
        for pair in range(2):
            pieces = []
            for p in range(4):
                for ey in range(3):
                    pieces.append(
                        padded_ref[group * 4 + pair * 2 + p, ey * 16 : ey * 16 + 256, :]
                    )
            lhs.append(jnp.concatenate(pieces, axis=1))
        summed = jnp.dot(jnp.concatenate(lhs), two_ref[...], preferred_element_type=F32)
        for pair in range(2):
            for phase in range(2):
                at = pl.multiple_of((group * 4 + pair * 2 + phase) * 256, 256)
                part = summed[pair * 256 : pair * 256 + 256, phase * 128 : phase * 128 + 128]
                rows = pl.ds(at, 256)
                inner_ref[rows, :] = jnp.where(mask_ref[rows, :] > 0, part, INACTIVE)
        leave(group).start()
        return carry

    lax.fori_loop(0, 4, step, 0)
    for copy in gone:
        copy.wait()
    for group in range(4):
        leave(group).wait()


def tap_rows(taps_ref, taps):
    starts = [((ex * 3 + ey) * 3 + ez) * 128 for ex, ey, ez in taps]
    return jnp.concatenate([taps_ref[at : at + 128, :] for at in starts])


def margin_planes(planes_ref, taps_ref):
    sums = []
    for side, ex in ((0, 0), (1, 2)):
        lhs = jnp.concatenate(
            [planes_ref[side, ey * 16 : ey * 16 + 256, :] for ey in range(3)], axis=1
        )
        rhs = taps_ref[ex * 1152 : ex * 1152 + 1152, :]
        sums.append(jnp.dot(lhs, rhs, preferred_element_type=F32))
    return sums


def margin_lines(lines_ref, taps_ref):
    sums = []
    none = jnp.zeros((16, 384), BF16)
    for side, ey in ((0, 0), (1, 2)):
        lines = lines_ref[side]
        lhs = jnp.concatenate(
            [
                jnp.concatenate([none, lines[:240]]),
                lines,
                jnp.concatenate([lines[16:], none]),
            ],
            axis=1,
        )
        rhs = tap_rows(taps_ref, [(ex, ey, ez) for ex in range(3) for ez in range(3)])
        sums.append(jnp.dot(lhs, rhs, preferred_element_type=F32))
    return sums


def margin_ends(face, ez, taps_ref):
    line = lax.broadcasted_iota(jnp.int32, face.shape, 0) % 16
    shifted = [
        jnp.where(line == 0, 0.0, pltpu.roll(face, 1, 0)),
        face,
        jnp.where(line == 15, 0.0, pltpu.roll(face, 255, 0)),
    ]
    border = jnp.zeros((16, 128), F32)
    lhs = []
    for ex in range(3):
        for part in shifted:
            if ex == 0:
                part = jnp.concatenate([border, part[:240]])
            elif ex == 2:
                part = jnp.concatenate([part[16:], border])
            lhs.append(part.astype(BF16))
    rhs = tap_rows(taps_ref, [(ex, ey, ez) for ex in range(3) for ey in range(3)])
    return jnp.dot(jnp.concatenate(lhs, axis=1), rhs, preferred_element_type=F32)


Z_FACES = ((DIRECTIONS.index((0, 0, -1)), 0), (DIRECTIONS.index((0, 0, 1)), 2))


def joined_face(own_ref, other_ref, block):
    own = own_ref[block].astype(F32)
    other = other_ref[block].astype(F32)
    return jnp.concatenate(
        [
            jnp.where(low_lanes(own), own, swap_halves(other)),
            jnp.where(low_lanes(own), swap_halves(own), other),
        ]
    )


def add_margin(planes_ref, lines_ref, near_ref, own_ref, other_ref, taps_ref, pre_ref):
    for side, added in enumerate(margin_planes(planes_ref, taps_ref)):
        at = side * 15 * 256
        pre_ref[at : at + 256, :] += added
    for side, added in enumerate(margin_lines(lines_ref, taps_ref)):
        for x in range(16):
            at = x * 256 + side * 240
            pre_ref[at : at + 16, :] += added[x * 16 : x * 16 + 16]
    for k, ez in Z_FACES:
        block = near_ref[0, k]

        @pl.when(block >= 0)
        def _(block=block, ez=ez):
            added = margin_ends(joined_face(own_ref, other_ref, block), ez, taps_ref)
            rows = pl.ds(0 if ez == 0 else 15, 256, stride=16)
            pre_ref[rows, :] = pre_ref[rows, :] + added


def put_own_margin(planes_ref, lines_ref, near_ref, own_ref, other_ref, lanes_ref):
    for side in range(2):
        plane = side * 17
        lanes_ref[plane, :, 0:128], lanes_ref[plane, :, 128:256] = own_lanes(planes_ref[side])
        both, above = own_lanes(lines_ref[side])
        rows = slice(side * 272, side * 272 + 16)
        for x in range(16):
            lanes_ref[x + 1, rows, 0:128] = both[x * 16 : x * 16 + 16]
            lanes_ref[x + 1, rows, 128:256] = above[x * 16 : x * 16 + 16]
    for k, ez in Z_FACES:
        block = near_ref[0, k]

        @pl.when(block >= 0)
        def _(block=block, ez=ez):
            face = joined_face(own_ref, other_ref, block)
            lanes = slice(ez * 64, ez * 64 + 128)
            for x in range(16):
                old = lanes_ref[x + 1, 16:272, lanes].astype(F32).reshape(16, 16, 128)
                level = lax.broadcasted_iota(jnp.int32, old.shape, 1)
                lane = lax.broadcasted_iota(jnp.int32, old.shape, 2)
                here = (level == (0 if ez == 0 else 15)) & (lane < 64)
                new = jnp.where(here, face[x * 16 : x * 16 + 16].reshape(16, 1, 128), old)
                lanes_ref[x + 1, 16:272, lanes] = new.reshape(256, 128).astype(BF16)


def forward(
    near_ref, core_ref, at_ref, own_ref, other_ref, taps_ref, inner_ref,
    slope_hbm, lanes_hbm, down_hbm, cot_hbm,
    slots_hbm, faces_ref, coarse_hbm, grad_pre_hbm,
    planes_ref, lines_ref, pre_ref, grad_ref, turned_ref, slope_ref, lanes_ref,
    down_ref, cot_ref, coarse_ref, grad_pre_ref, slots_ref, arrived, left, left_slots
):
    came = start_all(
        [
            (slope_hbm, slope_ref),
            (lanes_hbm, lanes_ref),
            (down_hbm, down_ref),
            (cot_hbm, cot_ref),
        ],
        arrived,
    )
    pre_ref[...] = inner_ref[...]
    planes_ref[...] = jnp.zeros(planes_ref.shape, BF16)
    lines_ref[...] = jnp.zeros(lines_ref.shape, BF16)
    margin = Margin(planes_ref, lines_ref)
    fill_margin(margin, near_ref, own_ref, other_ref, z_faces=False)
    add_margin(planes_ref, lines_ref, near_ref, own_ref, other_ref, taps_ref, pre_ref)
    came[0].wait()

    turned_ref[:, 0:512] = jnp.zeros((128, 512), BF16)
    turned_ref[:, 4608:5120] = jnp.zeros((128, 512), BF16)
    for x in range(16):
        rows = slice(x * 256, x * 256 + 256)
        pre = pre_ref[rows, :]
        sigmoid = 0.5 + 0.5 * jnp.tanh(0.5 * pre)
        pre_ref[rows, :] = jnp.where(pre > 0.5 * INACTIVE, pre * sigmoid, 0.0)
        grad = slope_ref[rows, :] * sigmoid * (1.0 + pre * (1.0 - sigmoid))
        grad_ref[rows, :] = grad
        grad = grad.astype(BF16)
        grad_pre_ref[rows, :] = grad
        turned_ref[:, 512 + x * 256 : 768 + x * 256] = grad.T

    gone = [
        pltpu.make_async_copy(grad_pre_ref, grad_pre_hbm, left.at[0]),
        pltpu.make_async_copy(coarse_ref, coarse_hbm, left.at[1]),
    ]
    gone[0].start()
    fill_faces(grad_ref, near_ref, (core_ref[0], at_ref[0]), faces_ref)
    share = slots_ref.shape[1] - 16
    fill_edges(grad_ref, near_ref, slots_ref, share)

    def put_terms(at, rows):
        while rows.shape[0]:
            owner, row = at // share, at % share
            count = min(rows.shape[0], share - row)
            slots_ref[owner, row : row + count, :] = rows[:count]
            rows = rows[count:]
            at += count

    ends = [1024 // share] + [(1024 + 576 * i) // share for i in (1, 2)] + [slots_ref.shape[0]]
    leaving = [
        pltpu.make_async_copy(
            slots_ref.at[first:last], slots_hbm.at[first:last], left_slots.at[i]
        )
        for i, (first, last) in enumerate(zip([0] + ends, ends))
    ]

    came[2].wait()
    came[3].wait()
    patches = []
    for tap in range(8):
        tx, ty, tz = tap // 4, tap // 2 % 2, tap % 2
        pieces = []
        for ux in range(8):
            for uy in range(8):
                at = (2 * ux + tx) * 256 + (2 * uy + ty) * 16 + tz
                pieces.append(pre_ref[pl.ds(at, 8, stride=2), :])
        patches.append(jnp.concatenate(pieces).astype(BF16))
    patches = jnp.concatenate(patches, axis=1)
    coarse = jnp.dot(patches, down_ref[...], preferred_element_type=F32)
    coarse_ref[...] = coarse[:, :128].astype(BF16)
    gone[1].start()
    own_cot = cot_ref[:, 0:128].astype(F32).T.astype(BF16)
    grad_down = jnp.dot(own_cot, patches, preferred_element_type=F32)
    for tap in range(8):
        part = grad_down[:, tap * 128 : tap * 128 + 128].T
        put_terms(tap * 128, part.astype(BF16))
    leaving[0].start()

    came[1].wait()
    put_own_margin(planes_ref, lines_ref, near_ref, own_ref, other_ref, lanes_ref)
    lhs = jnp.concatenate(
        [turned_ref[:, (2 - ex) * 256 : (2 - ex) * 256 + 4608] for ex in range(3)]
    )
    for ey in range(3):
        rhs = lanes_ref[:, ey * 16 : ey * 16 + 256, :].reshape(4608, 256)
        summed = jnp.dot(lhs, rhs, preferred_element_type=F32)
        for ex in range(3):
            part = summed[ex * 128 : ex * 128 + 128].T
            put_terms(1024 + (ey * 3 + ex) * 192, part[0:192].astype(BF16))
        leaving[ey + 1].start()
    for copy in gone + leaving:
        copy.wait()


def fetch(taps_hbm, inner_hbm, taps_ref, inner_ref, arrived):
    for copy in start_all([(taps_hbm, taps_ref), (inner_hbm, inner_ref)], arrived):
        copy.wait()


def total(slots_ref, out_hbm, sum_ref, left):
    devices, share, _ = out_hbm.shape
    summed = slots_ref[0, 0:share, :].astype(F32)
    for device in range(1, devices):
        summed = summed + slots_ref[device, 0:share, :].astype(F32)
    sum_ref[...] = (summed / devices).astype(BF16)
    copies = [
        pltpu.make_async_copy(sum_ref, out_hbm.at[i], left.at[i]) for i in range(devices)
    ]
    for copy in copies:
        copy.start()
    for copy in copies:
        copy.wait()


def backward(
    near_ref, core_ref, at_ref, own_ref, other_ref, own_faces_ref, other_faces_ref,
    grad_pre_hbm, active_hbm, conv_hbm, out_ref,
    padded_ref, grad_pre_ref, active_ref, conv_ref, back_ref, arrived
):
    came = start_all(
        [(conv_hbm, conv_ref), (grad_pre_hbm, grad_pre_ref), (active_hbm, active_ref)], arrived
    )
    came[0].wait()
    backward_weights(core_ref[0] * 64, conv_ref, back_ref)
    clear_margin(padded_ref)
    came[1].wait()
    for x in range(16):
        rows = grad_pre_ref[x * 256 : x * 256 + 256, :].astype(F32)
        put_lines(Whole(padded_ref), [(x + 1, 16, 256)], rows)
    fill_margin(
        Whole(padded_ref), near_ref, own_ref, other_ref, own_ref.shape[1] - 16,
        ((core_ref[0], at_ref[0]), own_faces_ref, other_faces_ref),
    )
    came[2].wait()
    for half in range(2):
        lhs = []
        for quad in range(2):
            pieces = []
            for p in range(6):
                for ey in range(3):
                    pieces.append(
                        padded_ref[half * 8 + quad * 4 + p, ey * 16 : ey * 16 + 256, :]
                    )
            lhs.append(jnp.concatenate(pieces, axis=1))
        summed = jnp.dot(jnp.concatenate(lhs), back_ref[...], preferred_element_type=F32)
        for quad in range(2):
            for two in range(2):
                part = summed[quad * 256 : quad * 256 + 256, two * 128 : two * 128 + 128]
                x = half * 8 + quad * 4 + two * 2
                even = active_ref[x * 256 : x * 256 + 256, :].astype(F32)
                odd = active_ref[x * 256 + 256 : x * 256 + 512, :].astype(F32)
                part = part * jnp.where(low_lanes(part), even, odd)
                for oy in range(2):
                    rows = [
                        part[(8 * oy + vy) * 16 + 8 * oz : (8 * oy + vy) * 16 + 8 * oz + 8]
                        for oz in range(2)
                        for vy in range(8)
                    ]
                    turned = jnp.concatenate(rows).T
                    first, second = turned[:64], turned[64:]
                    lanes = slice(x % 8 * 64, x % 8 * 64 + 128)
                    brick = half + 2 * oy
                    near = jnp.where(low_lanes(first), first, swap_halves(second))
                    far = jnp.where(low_lanes(first), swap_halves(first), second)
                    out_ref[brick, :, lanes] = near.astype(BF16)
                    out_ref[brick + 4, :, lanes] = far.astype(BF16)


def finish(core_ref, sums_ref, conv_ref, down_ref):
    shift = core_ref[0] * 64
    for tap in range(27):
        ex, ey, ez = tap // 9, tap // 3 % 3, tap % 3
        at = 1024 + ((ey * 3 + ex) * 3 + ez) * 64
        rows = sums_ref[at : at + 64, :].astype(F32)
        conv_ref[tap] = pltpu.roll(rows, shift, 1)
    for tap in range(8):
        rows = sums_ref[tap * 128 : tap * 128 + 128, :].astype(F32)
        down_ref[tap, pl.ds(shift, 64), :] = rows[:64]
        down_ref[tap, pl.ds(64 - shift, 64), :] = rows[64:]


def over_space(block, distance):
    blocks = range(lax.axis_size("space"))
    route = [(2 * i, 2 * (i + distance)) for i in blocks if i + distance in blocks]
    route += [(2 * i + 1, 2 * (i - distance) + 1) for i in blocks if i - distance in blocks]
    return lax.ppermute(block, ("space", "chan"), route)


def over_chan(block):
    return lax.ppermute(block, "chan", [(0, 1), (1, 0)])


def to_all(slots):
    return lax.all_to_all(slots, "space", 0, 0, tiled=True)


def local(features, heights, neighbours, w_conv, w_down, cotangent):
    devices = lax.axis_size("space")
    member = lax.axis_index("chan")

    def out(*shape, dtype=BF16):
        return jax.ShapeDtypeStruct(shape, dtype)

    def held_out(*shape, dtype=BF16):
        return pltpu.HBM(shape, dtype)

    def memory(*shape, dtype=BF16):
        return pltpu.VMEM(shape, dtype)

    def copies(count):
        return pltpu.SemaphoreType.DMA((count,))

    core = member.reshape(1)
    place = (core, lax.axis_index("space").reshape(1))
    turned = features.transpose(0, 2, 1)
    slots = kernel_call(
        send_features,
        out(devices, 128, 128),
        [hbm()] * 3,
        vmem(),
        [
            pltpu.SMEM(neighbours.shape, jnp.int32),
            memory(8, 64, dtype=jnp.int32),
            memory(8, 64, 512),
            memory(2048, 128, dtype=F32),
            copies(10),
        ],
    )(neighbours, heights, turned)
    came = to_all(slots)
    other_turned = over_chan(turned)

    held = [
        held_out(18, 288, 256),
        held_out(4096, 128),
        held_out(4096, 128, dtype=F32),
        held_out(4096, 128, dtype=F32),
        held_out(3456, 128),
        held_out(1024, 256),
        held_out(512, 256),
    ]
    lanes, active, slope, inner, taps, down, cot = kernel_call(
        prepare,
        held,
        [smem()] + [hbm()] * 5 + [pl.BlockSpec(memory_space=pl.ANY)],
        [hbm()] * 7,
        [
            memory(27, 128, 128),
            memory(8, 128, 256),
            memory(512, 256),
            memory(8, 64, dtype=jnp.int32),
            memory(8, 64, 512),
            memory(8, 64, 512),
            memory(4608, 256),
            memory(1024, 256),
            memory(512, 256),
            memory(18, 288, 384),
            memory(4096, 128, dtype=F32),
            memory(4096, 128, dtype=F32),
            memory(18, 288, 256),
            memory(4096, 128),
            memory(4096, 128, dtype=F32),
            memory(4096, 128, dtype=F32),
            copies(6),
            copies(6),
            copies(4),
        ],
        flops=5 << 30,
        mib=36,
    )(core, w_conv, w_down, cotangent[0], heights, turned, other_turned)
    came, taps, inner = lax.optimization_barrier((came, taps, inner))
    came_other = over_chan(came)
    taps, inner = kernel_call(
        fetch,
        [out(3456, 128), out(4096, 128, dtype=F32)],
        [hbm()] * 2,
        [vmem()] * 2,
        [copies(2)],
    )(taps, inner)

    share = -(-2752 // (devices * 16)) * 16
    terms, faces, coarse, grad_pre = kernel_call(
        forward,
        [
            held_out(devices, share + 16, 128),
            out(4, 256, 128),
            held_out(512, 128),
            held_out(4096, 128),
        ],
        [smem()] * 3 + [vmem()] * 4 + [hbm()] * 4,
        [hbm(), vmem(), hbm(), hbm()],
        [
            memory(2, 288, 384),
            memory(2, 256, 384),
            memory(4096, 128, dtype=F32),
            memory(4096, 128, dtype=F32),
            memory(128, 5120),
            memory(4096, 128, dtype=F32),
            memory(18, 288, 256),
            memory(1024, 256),
            memory(512, 256),
            memory(512, 128),
            memory(4096, 128),
            memory(devices, share + 16, 128),
            copies(4),
            copies(2),
            copies(4),
        ],
        flops=5 << 30,
        mib=24,
    )(
        neighbours, *place, came, came_other, taps, inner, slope, lanes, down, cot
    )

    arrived = to_all(terms)
    came_faces = [over_space(faces[i], i + 1) for i in range(4)]
    arrived, *came_faces = lax.optimization_barrier((arrived, *came_faces))
    came_faces = jnp.stack(came_faces)
    other_faces = over_chan(came_faces)
    sums = to_all(
        kernel_call(
            total,
            held_out(devices, share, 128),
            [vmem()],
            hbm(),
            [memory(share, 128), copies(devices)],
        )(arrived)
    )
    arrived_other = over_chan(arrived[:, share:])
    grad_features = kernel_call(
        backward,
        out(8, 64, 512),
        [smem()] * 3 + [vmem()] * 4 + [hbm()] * 3,
        vmem(),
        [
            memory(18, 288, 384),
            memory(4096, 128),
            memory(4096, 128),
            memory(27, 128, 128),
            memory(6912, 256),
            copies(3),
        ],
        flops=5 << 30,
        mib=24,
    )(
        neighbours, *place, arrived, arrived_other, came_faces, other_faces, grad_pre, active,
        w_conv,
    )

    grad_conv, grad_down = kernel_call(
        finish,
        [out(27, 64, 128, dtype=F32), out(8, 128, 128, dtype=F32)],
        [smem(), vmem()],
        [vmem()] * 2,
    )(core, sums.reshape(-1, 128))
    return coarse[None], grad_conv, grad_down, grad_features.transpose(0, 2, 1)


def solution(mesh):
    placed = (
        P("space", None, "chan"),
        P("space", None),
        P("space", None),
        P(),
        P(),
        P("space", None, None),
    )
    return jax.shard_map(
        local,
        mesh=mesh,
        in_specs=placed,
        out_specs=(
            P("space", None, "chan"),
            P(None, "chan", None),
            P(None, None, "chan"),
            P("space", None, "chan"),
        ),
        check_vma=False,
    )
```

```python
import functools

import jax
import jax.numpy as jnp
from jax import lax
from jax.experimental import pallas as pl
from jax.experimental.pallas import tpu as pltpu
from jax.sharding import PartitionSpec as P

OFFSETS = [
    (along_x, along_y, along_z)
    for along_x in (-1, 0, 1)
    for along_y in (-1, 0, 1)
    for along_z in (-1, 0, 1)
]
DIRECTIONS = [offset for offset in OFFSETS if offset != (0, 0, 0)]
FILL_ORDER = sorted(range(26), key=lambda k: (abs(DIRECTIONS[k][2]), k))
INACTIVE = -1e30
F32 = jnp.float32
BF16 = jnp.bfloat16


def vmem():
    return pl.BlockSpec(memory_space=pltpu.VMEM)


def smem():
    return pl.BlockSpec(memory_space=pltpu.SMEM)


def hbm():
    return pl.BlockSpec(memory_space=pltpu.HBM)


def kernel_call(body, outs, specs, out_specs, scratch=(), flops=0, mib=16):
    call = pl.pallas_call(
        body,
        out_shape=outs,
        in_specs=specs,
        out_specs=out_specs,
        scratch_shapes=list(scratch),
        compiler_params=pltpu.CompilerParams(vmem_limit_bytes=mib * 1024 * 1024),
        cost_estimate=pl.CostEstimate(flops=flops, bytes_accessed=1 << 22, transcendentals=0),
    )

    def run(*operands):
        placed = []
        for spec, operand in zip(specs, operands):
            if spec.memory_space == pltpu.HBM:
                operand = pltpu.with_memory_space_constraint(operand, pltpu.HBM)
            placed.append(operand)
        return call(*placed)

    return run


def start_all(pairs, arrived):
    copies = [
        pltpu.make_async_copy(source, target, arrived.at[i])
        for i, (source, target) in enumerate(pairs)
    ]
    for copy in copies:
        copy.start()
    return copies


def swap_halves(rows):
    return pltpu.roll(rows, 64, 1)


def low_lanes(rows):
    return lax.broadcasted_iota(jnp.int32, rows.shape, 1) < 64


def filled_voxels(heights_ref):
    columns = lax.broadcasted_iota(jnp.int32, (64, 512), 0)
    voxels = lax.broadcasted_iota(jnp.int32, (64, 512), 1)
    spread = (voxels // 8 == columns).astype(F32)
    tall = jnp.dot(heights_ref[...].astype(F32), spread, preferred_element_type=F32)
    level = lax.broadcasted_iota(jnp.int32, tall.shape, 1) % 8
    return (level.astype(F32) < tall).astype(F32)


def fill_slots(rows_ref, near_ref, slots_ref):
    for k, (dx, dy, dz) in enumerate(DIRECTIONS):
        block = near_ref[0, k]
        xh = 7 if dx == 1 else 0
        y = 15 if dy == 1 else 0
        z = 15 if dz == 1 else 0

        @pl.when(block >= 0)
        def _(dx=dx, dy=dy, dz=dz, xh=xh, y=y, z=z, block=block):
            zeros = [d == 0 for d in (dx, dy, dz)]
            if zeros == [False, True, True]:
                plane = rows_ref[xh * 256 : xh * 256 + 256, :]
                first, second = plane[:128], plane[128:]
                if dx == -1:
                    second = swap_halves(second)
                else:
                    first = swap_halves(first)
                region = jnp.where(low_lanes(first), first, second)
            elif zeros == [True, False, True]:
                region = jnp.concatenate(
                    [rows_ref[x * 256 + y * 16 : x * 256 + y * 16 + 16, :] for x in range(8)]
                )
            elif zeros == [True, True, False]:
                region = rows_ref[pl.ds(z, 128, stride=16), :]
            elif zeros == [False, False, True]:
                region = rows_ref[xh * 256 + y * 16 : xh * 256 + y * 16 + 16, :]
            elif zeros == [False, True, False]:
                region = rows_ref[pl.ds(xh * 256 + z, 16, stride=16), :]
            elif zeros == [True, False, False]:
                line = rows_ref[pl.ds(y * 16 + z, 8, stride=256), :]
                region = jnp.concatenate([line, line])
            else:
                at = xh * 256 + y * 16 + z
                region = jnp.broadcast_to(rows_ref[at : at + 1, :], (16, 128))
            slots_ref[block, 0 : region.shape[0], :] = region.astype(BF16)


def fill_edges(rows_ref, near_ref, slots_ref, start):
    for k, (dx, dy, dz) in enumerate(DIRECTIONS):
        if (dx, dy, dz).count(0) == 2:
            continue
        block = near_ref[0, k]
        x, y, z = (15 if d == 1 else 0 for d in (dx, dy, dz))

        @pl.when(block >= 0)
        def _(dx=dx, dy=dy, dz=dz, x=x, y=y, z=z, block=block):
            if dx == 0:
                line = rows_ref[pl.ds(y * 16 + z, 16, stride=256), :]
                low, high = line[:8], swap_halves(line[8:])
                line = jnp.where(low_lanes(low), low, high)
                rows = jnp.concatenate([line, line])
            elif dz == 0:
                rows = rows_ref[x * 256 + y * 16 : x * 256 + y * 16 + 16, :]
            elif dy == 0:
                rows = rows_ref[pl.ds(x * 256 + z, 16, stride=16), :]
            else:
                at = x * 256 + y * 16 + z
                rows = jnp.broadcast_to(rows_ref[at : at + 1, :], (16, 128))
            if dx == 1:
                rows = swap_halves(rows)
            slots_ref[block, start : start + 16, :] = rows.astype(BF16)


def fill_faces(rows_ref, near_ref, place, faces_ref):
    member, own = place
    for k, (dx, dy, dz) in enumerate(DIRECTIONS):
        if (dx, dy, dz).count(0) != 2:
            continue
        block = near_ref[0, k]
        distance = jnp.where(member == 0, block - own, own - block)
        end = 15 if dx + dy + dz == 1 else 0

        @pl.when((block >= 0) & (distance >= 1))
        def _(dx=dx, dy=dy, end=end, distance=distance):
            if dx:
                region = rows_ref[end * 256 : end * 256 + 256, :]
            elif dy:
                region = jnp.concatenate(
                    [rows_ref[x * 256 + end * 16 : x * 256 + end * 16 + 16, :] for x in range(16)]
                )
            else:
                region = rows_ref[pl.ds(end, 256, stride=16), :]
            faces_ref[distance - 1] = region.astype(BF16)


class Whole:
    def __init__(self, ref):
        self.ref = ref

    def at(self, x, row, height):
        return self.ref, x, row


class Margin:
    def __init__(self, planes_ref, lines_ref):
        self.planes_ref, self.lines_ref = planes_ref, lines_ref

    def at(self, x, row, height):
        if x in (0, 17):
            return self.planes_ref, x // 17, row
        return self.lines_ref, row // 272, (x - 1) * 16


def put_lines(padded, places, rows):
    count = rows.shape[0]
    level = lax.broadcasted_iota(jnp.int32, rows.shape, 0) % 16
    below = jnp.where(level == 0, 0.0, pltpu.roll(rows, 1, 0)).astype(BF16)
    above = jnp.where(level == 15, 0.0, pltpu.roll(rows, count - 1, 0)).astype(BF16)
    here = rows.astype(BF16)
    at = 0
    for x, row, height in places:
        ref, plane, first = padded.at(x, row, height)
        for j, part in enumerate((below, here, above)):
            ref[plane, first : first + height, j * 128 : j * 128 + 128] = part[at : at + height]
        at += height


def put_ends(padded, x, row, rows, dz):
    lines = rows.shape[0]
    j = 0 if dz == -1 else 2
    end = 0 if dz == -1 else 15
    lanes = slice(j * 128, j * 128 + 128)
    ref, plane, first = padded.at(x, row, 16 * lines)
    span = slice(first, first + 16 * lines)
    old = ref[plane, span, lanes].astype(F32).reshape(lines, 16, 128)
    level = lax.broadcasted_iota(jnp.int32, old.shape, 1)
    new = jnp.where(level == end, rows.reshape(lines, 1, 128), old)
    ref[plane, span, lanes] = new.reshape(16 * lines, 128).astype(BF16)


def clear_margin(padded_ref):
    empty = jnp.zeros((288, 384), BF16)
    padded_ref[0] = empty
    padded_ref[17] = empty
    line = jnp.zeros((16, 384), BF16)
    for x in range(1, 17):
        padded_ref[x, 0:16, :] = line
        padded_ref[x, 272:288, :] = line


def put_region(padded, offset, rows):
    dx, dy, dz = offset
    zeros = [d == 0 for d in offset]
    x = 17 if dx == 1 else 0
    y = 17 if dy == 1 else 0
    if zeros == [False, True, True]:
        put_lines(padded, [(x, 16, 256)], rows)
    elif zeros == [True, False, True]:
        put_lines(padded, [(at + 1, y * 16, 16) for at in range(16)], rows)
    elif zeros == [False, False, True]:
        put_lines(padded, [(x, y * 16, 16)], rows)
    elif zeros == [True, True, False]:
        for at in range(16):
            put_ends(padded, at + 1, 16, rows[at * 16 : at * 16 + 16], dz)
    elif zeros == [False, True, False]:
        put_ends(padded, x, 16, rows, dz)
    elif zeros == [True, False, False]:
        for at in range(16):
            put_ends(padded, at + 1, y * 16, rows[at : at + 1], dz)
    else:
        put_ends(padded, x, y * 16, rows[0:1], dz)


def face_source(place, block):
    away = place[1] - block
    return jnp.where(away > 0, 0, 1) == place[0], jnp.clip(jnp.abs(away) - 1, 0, 3)


def fill_margin(padded, near_ref, own_ref, other_ref, start=0, faces=None, z_faces=True):
    for k in FILL_ORDER:
        offset = DIRECTIONS[k]
        block = near_ref[0, k]
        face = offset.count(0) == 2
        if face and offset[2] and not z_faces:
            continue
        if face and faces is not None:
            place, own_faces_ref, other_faces_ref = faces
            here, slot = face_source(place, block)

            @pl.when((block >= 0) & here)
            def _(offset=offset, slot=slot):
                put_region(padded, offset, own_faces_ref[slot].astype(F32))

            @pl.when((block >= 0) & jnp.logical_not(here))
            def _(offset=offset, slot=slot):
                rows = swap_halves(other_faces_ref[slot].astype(F32))
                put_region(padded, offset, rows)

            continue

        @pl.when(block >= 0)
        def _(offset=offset, block=block, face=face):
            height = 128 if face else 16
            own = own_ref[block, start : start + height, :].astype(F32)
            other = other_ref[block, 0:height, :].astype(F32)
            first = jnp.where(low_lanes(own), own, swap_halves(other))
            second = jnp.where(low_lanes(own), swap_halves(own), other)
            if face:
                rows = jnp.concatenate([first, second])
            elif offset[0] == 0:
                rows = jnp.concatenate([first[:8], second[:8]])
            else:
                rows = first if offset[0] == 1 else second
            put_region(padded, offset, rows)


def send_features(
    near_hbm, heights_hbm, features_hbm, slots_ref,
    near_ref, heights_ref, features_ref, rows_ref, arrived
):
    copies = [
        pltpu.make_async_copy(near_hbm, near_ref, arrived.at[8]),
        pltpu.make_async_copy(heights_hbm, heights_ref, arrived.at[9]),
    ]
    order = (0, 1, 2, 3, 4, 5, 6, 7)
    bricks = [
        pltpu.make_async_copy(features_hbm.at[i], features_ref.at[i], arrived.at[i]) for i in order
    ]
    for copy in copies + bricks:
        copy.start()
    copies[1].wait()
    filled = filled_voxels(heights_ref).astype(BF16)
    for oz in range(2):
        for oy in range(2):
            pair = []
            for ox in range(2):
                brick = ox + 2 * oy + 4 * oz
                bricks[brick].wait()
                pair.append(features_ref[brick] * filled[brick : brick + 1])
            turned = jnp.concatenate(pair).T.astype(F32)
            for vx in range(8):
                for vy in range(8):
                    at = vx * 256 + (8 * oy + vy) * 16 + 8 * oz
                    source = (vx * 8 + vy) * 8
                    rows_ref[at : at + 8, :] = turned[source : source + 8]
    copies[0].wait()
    fill_slots(rows_ref, near_ref, slots_ref)


def own_first_taps(shift, conv_ref, yz):
    taps = []
    for ex in range(3):
        tap = conv_ref[ex * 9 + yz].astype(F32)
        taps.append(pltpu.roll(pltpu.roll(tap, shift, 0), shift, 1))
    return taps


def forward_weights(shift, conv_ref, down_in_ref, cot_in_ref, two_ref, down_ref, cot_ref):
    empty = jnp.zeros((128, 128), BF16)
    for yz in range(9):
        taps = own_first_taps(shift, conv_ref, yz)
        whole = [empty] + [tap.astype(BF16) for tap in taps] + [empty]
        for p in range(4):
            rows = slice((p * 9 + yz) * 128, (p * 9 + yz) * 128 + 128)
            two_ref[rows, 0:128] = whole[p + 1] if p < 3 else empty
            two_ref[rows, 128:256] = whole[p]
    for tap in range(8):
        rows = down_in_ref[tap].astype(F32)
        rows = pltpu.roll(rows, shift, 0)
        down_ref[tap * 128 : tap * 128 + 128, :] = pltpu.roll(rows, 2 * shift, 1).astype(BF16)
    cot_ref[...] = pltpu.roll(cot_in_ref[...].astype(F32), 2 * shift, 1).astype(BF16)


def backward_weights(shift, conv_ref, four_ref):
    empty = jnp.zeros((128, 128), BF16)
    none = jnp.zeros((64, 128), F32)
    for yz in range(9):
        taps = own_first_taps(shift, conv_ref, yz)
        own = [none] + [taps[2 - ex][:64] for ex in range(3)] + [none]
        pairs = [jnp.concatenate([own[i + 1], own[i]]).T.astype(BF16) for i in range(4)]
        for p in range(6):
            at = (p * 9 + 8 - yz) * 128
            four_ref[at : at + 128, 0:128] = pairs[p] if p < 4 else empty
            four_ref[at : at + 128, 128:256] = pairs[p - 2] if p >= 2 else empty


def own_lanes(triple):
    below, here = triple[:, 0:128].astype(F32), triple[:, 128:256].astype(F32)
    both = jnp.where(low_lanes(below), below, swap_halves(here)).astype(BF16)
    return both, triple[:, 256:384]


def prepare(
    core_ref, conv_hbm, down_hbm, cot_hbm, heights_hbm, own_hbm, other_hbm,
    lanes_hbm, active_hbm, slope_hbm, inner_hbm, taps_hbm, down_out_hbm, cot_out_hbm,
    conv_in_ref, down_in_ref, cot_in_ref, heights_ref, own_ref, other_ref,
    two_ref, down_ref, cot_ref, own_cot_ref, padded_ref, rows_ref, mask_ref, lanes_ref, active_ref,
    slope_ref, inner_ref, arrived, left, left_inner
):
    came = start_all(
        [
            (conv_hbm, conv_in_ref),
            (down_hbm, down_in_ref),
            (cot_hbm, cot_in_ref),
            (heights_hbm, heights_ref),
            (own_hbm, own_ref),
            (other_hbm, other_ref),
        ],
        arrived,
    )
    gone = [
        pltpu.make_async_copy(source, target, left.at[i])
        for i, (source, target) in enumerate(
            [
                (two_ref.at[0:3456, 0:128], taps_hbm),
                (down_ref, down_out_hbm),
                (own_cot_ref, cot_out_hbm),
                (lanes_ref, lanes_hbm),
                (active_ref, active_hbm),
                (slope_ref, slope_hbm),
            ]
        )
    ]
    for copy in came[:3]:
        copy.wait()
    forward_weights(
        core_ref[0] * 64, conv_in_ref, down_in_ref, cot_in_ref, two_ref, down_ref, cot_ref
    )
    own_cot_ref[...] = cot_ref[:, 0:128].T
    for copy in gone[:3]:
        copy.start()
    for copy in came[3:]:
        copy.wait()
    filled = filled_voxels(heights_ref)
    upright = filled.T
    for brick in range(8):
        ox, oy, oz = brick % 2, brick // 2 % 2, brick // 4
        both = jnp.concatenate([own_ref[brick].astype(F32), other_ref[brick].astype(F32)])
        turned = (both * filled[brick : brick + 1]).T
        mask = jnp.broadcast_to(upright[:, brick : brick + 1], (512, 128))
        for vx in range(8):
            for vy in range(8):
                at = (8 * ox + vx) * 256 + (8 * oy + vy) * 16 + 8 * oz
                source = (vx * 8 + vy) * 8
                rows_ref[at : at + 8, :] = turned[source : source + 8]
                mask_ref[at : at + 8, :] = mask[source : source + 8]
    clear_margin(padded_ref)
    for x in range(16):
        put_lines(Whole(padded_ref), [(x + 1, 16, 256)], rows_ref[x * 256 : x * 256 + 256, :])
        active_ref[x * 256 : x * 256 + 256, :] = mask_ref[x * 256 : x * 256 + 256, :].astype(BF16)
    for x in range(18):
        lanes_ref[x, :, 0:128], lanes_ref[x, :, 128:256] = own_lanes(padded_ref[x])
    gone[3].start()
    gone[4].start()
    for tap in range(8):
        tx, ty, tz = tap // 4, tap // 2 % 2, tap % 2
        part = lax.dot_general(
            cot_ref[...],
            down_ref[tap * 128 : tap * 128 + 128, :],
            (((1,), (1,)), ((), ())),
            preferred_element_type=F32,
        )
        for ux in range(8):
            for uy in range(8):
                at = (2 * ux + tx) * 256 + (2 * uy + ty) * 16 + tz
                source = (ux * 8 + uy) * 8
                rows = pl.ds(at, 8, stride=2)
                slope_ref[rows, :] = part[source : source + 8] * mask_ref[rows, :]
    gone[5].start()

    def leave(group):
        rows = pl.ds(pl.multiple_of(group * 1024, 1024), 1024)
        return pltpu.make_async_copy(
            inner_ref.at[rows], inner_hbm.at[rows], left_inner.at[group]
        )


    def step(group, carry):
        lhs = []
        for pair in range(2):
            pieces = []
            for p in range(4):
                for ey in range(3):
                    pieces.append(
                        padded_ref[group * 4 + pair * 2 + p, ey * 16 : ey * 16 + 256, :]
                    )
            lhs.append(jnp.concatenate(pieces, axis=1))
        summed = jnp.dot(jnp.concatenate(lhs), two_ref[...], preferred_element_type=F32)
        for pair in range(2):
            for phase in range(2):
                at = pl.multiple_of((group * 4 + pair * 2 + phase) * 256, 256)
                part = summed[pair * 256 : pair * 256 + 256, phase * 128 : phase * 128 + 128]
                rows = pl.ds(at, 256)
                inner_ref[rows, :] = jnp.where(mask_ref[rows, :] > 0, part, INACTIVE)
        leave(group).start()
        return carry

    lax.fori_loop(0, 4, step, 0)
    for copy in gone:
        copy.wait()
    for group in range(4):
        leave(group).wait()


def tap_rows(taps_ref, taps):
    starts = [((ex * 3 + ey) * 3 + ez) * 128 for ex, ey, ez in taps]
    return jnp.concatenate([taps_ref[at : at + 128, :] for at in starts])


def any_block(near_ref, axis, step):
    found = [near_ref[0, k] >= 0 for k, offset in enumerate(DIRECTIONS) if offset[axis] == step]
    return functools.reduce(jnp.logical_or, found)


def margin_plane(planes_ref, taps_ref, side):
    lhs = jnp.concatenate(
        [planes_ref[side, ey * 16 : ey * 16 + 256, :] for ey in range(3)], axis=1
    )
    rhs = taps_ref[side * 2304 : side * 2304 + 1152, :]
    return jnp.dot(lhs, rhs, preferred_element_type=F32)


def margin_lines(lines_ref, taps_ref, side):
    none = jnp.zeros((16, 384), BF16)
    lines = lines_ref[side]
    lhs = jnp.concatenate(
        [
            jnp.concatenate([none, lines[:240]]),
            lines,
            jnp.concatenate([lines[16:], none]),
        ],
        axis=1,
    )
    rhs = tap_rows(taps_ref, [(ex, 2 * side, ez) for ex in range(3) for ez in range(3)])
    return jnp.dot(lhs, rhs, preferred_element_type=F32)


def margin_ends(face, ez, taps_ref):
    line = lax.broadcasted_iota(jnp.int32, face.shape, 0) % 16
    shifted = [
        jnp.where(line == 0, 0.0, pltpu.roll(face, 1, 0)),
        face,
        jnp.where(line == 15, 0.0, pltpu.roll(face, 255, 0)),
    ]
    border = jnp.zeros((16, 128), F32)
    lhs = []
    for ex in range(3):
        for part in shifted:
            if ex == 0:
                part = jnp.concatenate([border, part[:240]])
            elif ex == 2:
                part = jnp.concatenate([part[16:], border])
            lhs.append(part.astype(BF16))
    rhs = tap_rows(taps_ref, [(ex, ey, ez) for ex in range(3) for ey in range(3)])
    return jnp.dot(jnp.concatenate(lhs, axis=1), rhs, preferred_element_type=F32)


Z_FACES = ((DIRECTIONS.index((0, 0, -1)), 0), (DIRECTIONS.index((0, 0, 1)), 2))


def joined_face(own_ref, other_ref, block):
    own = own_ref[block].astype(F32)
    other = other_ref[block].astype(F32)
    return jnp.concatenate(
        [
            jnp.where(low_lanes(own), own, swap_halves(other)),
            jnp.where(low_lanes(own), swap_halves(own), other),
        ]
    )


def add_margin(planes_ref, lines_ref, near_ref, own_ref, other_ref, taps_ref, pre_ref):
    for side in range(2):

        @pl.when(any_block(near_ref, 0, 2 * side - 1))
        def _(side=side):
            at = side * 15 * 256
            pre_ref[at : at + 256, :] += margin_plane(planes_ref, taps_ref, side)

        @pl.when(any_block(near_ref, 1, 2 * side - 1))
        def _(side=side):
            added = margin_lines(lines_ref, taps_ref, side)
            for x in range(16):
                at = x * 256 + side * 240
                pre_ref[at : at + 16, :] += added[x * 16 : x * 16 + 16]

    for k, ez in Z_FACES:
        block = near_ref[0, k]

        @pl.when(block >= 0)
        def _(block=block, ez=ez):
            added = margin_ends(joined_face(own_ref, other_ref, block), ez, taps_ref)
            rows = pl.ds(0 if ez == 0 else 15, 256, stride=16)
            pre_ref[rows, :] = pre_ref[rows, :] + added


def put_own_margin(planes_ref, lines_ref, near_ref, own_ref, other_ref, lanes_ref):
    for side in range(2):
        plane = side * 17
        lanes_ref[plane, :, 0:128], lanes_ref[plane, :, 128:256] = own_lanes(planes_ref[side])
        both, above = own_lanes(lines_ref[side])
        rows = slice(side * 272, side * 272 + 16)
        for x in range(16):
            lanes_ref[x + 1, rows, 0:128] = both[x * 16 : x * 16 + 16]
            lanes_ref[x + 1, rows, 128:256] = above[x * 16 : x * 16 + 16]
    for k, ez in Z_FACES:
        block = near_ref[0, k]

        @pl.when(block >= 0)
        def _(block=block, ez=ez):
            face = joined_face(own_ref, other_ref, block)
            lanes = slice(ez * 64, ez * 64 + 128)
            for x in range(16):
                old = lanes_ref[x + 1, 16:272, lanes].astype(F32).reshape(16, 16, 128)
                level = lax.broadcasted_iota(jnp.int32, old.shape, 1)
                lane = lax.broadcasted_iota(jnp.int32, old.shape, 2)
                here = (level == (0 if ez == 0 else 15)) & (lane < 64)
                new = jnp.where(here, face[x * 16 : x * 16 + 16].reshape(16, 1, 128), old)
                lanes_ref[x + 1, 16:272, lanes] = new.reshape(256, 128).astype(BF16)


def forward(
    near_ref, core_ref, at_ref, own_ref, other_ref, taps_ref, slope_ref,
    inner_hbm, lanes_hbm, down_hbm, cot_hbm,
    slots_hbm, faces_ref, coarse_hbm, grad_pre_hbm,
    planes_ref, lines_ref, pre_ref, grad_ref, turned_ref, lanes_ref,
    down_ref, cot_ref, coarse_ref, grad_pre_ref, slots_ref, arrived, left, left_slots
):
    came = start_all(
        [
            (inner_hbm, pre_ref),
            (lanes_hbm, lanes_ref),
            (down_hbm, down_ref),
            (cot_hbm, cot_ref),
        ],
        arrived,
    )
    planes_ref[...] = jnp.zeros(planes_ref.shape, BF16)
    lines_ref[...] = jnp.zeros(lines_ref.shape, BF16)
    margin = Margin(planes_ref, lines_ref)
    fill_margin(margin, near_ref, own_ref, other_ref, z_faces=False)
    came[0].wait()
    add_margin(planes_ref, lines_ref, near_ref, own_ref, other_ref, taps_ref, pre_ref)

    turned_ref[:, 0:512] = jnp.zeros((128, 512), BF16)
    turned_ref[:, 4608:5120] = jnp.zeros((128, 512), BF16)
    for x in range(16):
        rows = slice(x * 256, x * 256 + 256)
        pre = pre_ref[rows, :]
        sigmoid = 0.5 + 0.5 * jnp.tanh(0.5 * pre)
        pre_ref[rows, :] = jnp.where(pre > 0.5 * INACTIVE, pre * sigmoid, 0.0)
        grad = slope_ref[rows, :] * sigmoid * (1.0 + pre * (1.0 - sigmoid))
        grad_ref[rows, :] = grad
        grad = grad.astype(BF16)
        grad_pre_ref[rows, :] = grad
        turned_ref[:, 512 + x * 256 : 768 + x * 256] = grad.T

    gone = [
        pltpu.make_async_copy(grad_pre_ref, grad_pre_hbm, left.at[0]),
        pltpu.make_async_copy(coarse_ref, coarse_hbm, left.at[1]),
    ]
    gone[0].start()
    fill_faces(grad_ref, near_ref, (core_ref[0], at_ref[0]), faces_ref)
    share = slots_ref.shape[1] - 16
    fill_edges(grad_ref, near_ref, slots_ref, share)

    def put_terms(at, rows):
        while rows.shape[0]:
            owner, row = at // share, at % share
            count = min(rows.shape[0], share - row)
            slots_ref[owner, row : row + count, :] = rows[:count]
            rows = rows[count:]
            at += count

    ends = [1024 // share] + [(1024 + 576 * i) // share for i in (1, 2)] + [slots_ref.shape[0]]
    leaving = [
        pltpu.make_async_copy(
            slots_ref.at[first:last], slots_hbm.at[first:last], left_slots.at[i]
        )
        for i, (first, last) in enumerate(zip([0] + ends, ends))
    ]

    came[2].wait()
    came[3].wait()
    patches = []
    for tap in range(8):
        tx, ty, tz = tap // 4, tap // 2 % 2, tap % 2
        pieces = []
        for ux in range(8):
            for uy in range(8):
                at = (2 * ux + tx) * 256 + (2 * uy + ty) * 16 + tz
                pieces.append(pre_ref[pl.ds(at, 8, stride=2), :])
        patches.append(jnp.concatenate(pieces).astype(BF16))
    patches = jnp.concatenate(patches, axis=1)
    coarse = jnp.dot(patches, down_ref[...], preferred_element_type=F32)
    coarse_ref[...] = coarse[:, :128].astype(BF16)
    gone[1].start()
    grad_down = jnp.dot(cot_ref[...], patches, preferred_element_type=F32).astype(BF16)
    for tap in range(8):
        put_terms(tap * 128, grad_down[:, tap * 128 : tap * 128 + 128].T)
    leaving[0].start()

    came[1].wait()
    put_own_margin(planes_ref, lines_ref, near_ref, own_ref, other_ref, lanes_ref)
    lhs = jnp.concatenate(
        [turned_ref[:, (2 - ex) * 256 : (2 - ex) * 256 + 4608] for ex in range(3)]
    )
    for ey in range(3):
        rhs = lanes_ref[:, ey * 16 : ey * 16 + 256, :].reshape(4608, 256)
        summed = jnp.dot(lhs, rhs, preferred_element_type=F32)
        for ex in range(3):
            part = summed[ex * 128 : ex * 128 + 128].astype(BF16).T
            put_terms(1024 + (ey * 3 + ex) * 192, part[0:192])
        leaving[ey + 1].start()
    for copy in gone + leaving:
        copy.wait()


def fetch(taps_hbm, slope_hbm, taps_ref, slope_ref, arrived):
    for copy in start_all([(taps_hbm, taps_ref), (slope_hbm, slope_ref)], arrived):
        copy.wait()


def total(slots_ref, out_ref):
    devices, share, _ = out_ref.shape
    summed = slots_ref[0, 0:share, :].astype(F32)
    for device in range(1, devices):
        summed = summed + slots_ref[device, 0:share, :].astype(F32)
    summed = (summed / devices).astype(BF16)
    for device in range(devices):
        out_ref[device] = summed


def backward(
    near_ref, core_ref, at_ref, own_ref, other_ref, own_faces_ref, other_faces_ref,
    grad_pre_hbm, active_hbm, conv_hbm, out_ref,
    padded_ref, grad_pre_ref, active_ref, conv_ref, back_ref, arrived
):
    came = start_all(
        [(conv_hbm, conv_ref), (grad_pre_hbm, grad_pre_ref), (active_hbm, active_ref)], arrived
    )
    came[0].wait()
    backward_weights(core_ref[0] * 64, conv_ref, back_ref)
    clear_margin(padded_ref)
    came[1].wait()
    for x in range(16):
        rows = grad_pre_ref[x * 256 : x * 256 + 256, :].astype(F32)
        put_lines(Whole(padded_ref), [(x + 1, 16, 256)], rows)
    fill_margin(
        Whole(padded_ref), near_ref, own_ref, other_ref, own_ref.shape[1] - 16,
        ((core_ref[0], at_ref[0]), own_faces_ref, other_faces_ref),
    )
    came[2].wait()
    for half in range(2):
        lhs = []
        for quad in range(2):
            pieces = []
            for p in range(6):
                for ey in range(3):
                    pieces.append(
                        padded_ref[half * 8 + quad * 4 + p, ey * 16 : ey * 16 + 256, :]
                    )
            lhs.append(jnp.concatenate(pieces, axis=1))
        summed = jnp.dot(jnp.concatenate(lhs), back_ref[...], preferred_element_type=F32)
        for quad in range(2):
            for two in range(2):
                part = summed[quad * 256 : quad * 256 + 256, two * 128 : two * 128 + 128]
                x = half * 8 + quad * 4 + two * 2
                even = active_ref[x * 256 : x * 256 + 256, :].astype(F32)
                odd = active_ref[x * 256 + 256 : x * 256 + 512, :].astype(F32)
                part = part * jnp.where(low_lanes(part), even, odd)
                for oy in range(2):
                    rows = [
                        part[(8 * oy + vy) * 16 + 8 * oz : (8 * oy + vy) * 16 + 8 * oz + 8]
                        for oz in range(2)
                        for vy in range(8)
                    ]
                    turned = jnp.concatenate(rows).T
                    first, second = turned[:64], turned[64:]
                    lanes = slice(x % 8 * 64, x % 8 * 64 + 128)
                    brick = half + 2 * oy
                    near = jnp.where(low_lanes(first), first, swap_halves(second))
                    far = jnp.where(low_lanes(first), swap_halves(first), second)
                    out_ref[brick, :, lanes] = near.astype(BF16)
                    out_ref[brick + 4, :, lanes] = far.astype(BF16)


def finish(core_ref, sums_ref, conv_ref, down_ref):
    shift = core_ref[0] * 64
    for tap in range(27):
        ex, ey, ez = tap // 9, tap // 3 % 3, tap % 3
        at = 1024 + ((ey * 3 + ex) * 3 + ez) * 64
        rows = sums_ref[at : at + 64, :].astype(F32)
        conv_ref[tap] = pltpu.roll(rows, shift, 1)
    for tap in range(8):
        rows = sums_ref[tap * 128 : tap * 128 + 128, :].astype(F32)
        down_ref[tap, pl.ds(shift, 64), :] = rows[:64]
        down_ref[tap, pl.ds(64 - shift, 64), :] = rows[64:]


def over_space(block, distance):
    blocks = range(lax.axis_size("space"))
    route = [(2 * i, 2 * (i + distance)) for i in blocks if i + distance in blocks]
    route += [(2 * i + 1, 2 * (i - distance) + 1) for i in blocks if i - distance in blocks]
    return lax.ppermute(block, ("space", "chan"), route)


def over_chan(block):
    return lax.ppermute(block, "chan", [(0, 1), (1, 0)])


def to_all(slots):
    return lax.all_to_all(slots, "space", 0, 0, tiled=True)


def local(features, heights, neighbours, w_conv, w_down, cotangent):
    devices = lax.axis_size("space")
    member = lax.axis_index("chan")

    def out(*shape, dtype=BF16):
        return jax.ShapeDtypeStruct(shape, dtype)

    def held_out(*shape, dtype=BF16):
        return pltpu.HBM(shape, dtype)

    def memory(*shape, dtype=BF16):
        return pltpu.VMEM(shape, dtype)

    def copies(count):
        return pltpu.SemaphoreType.DMA((count,))

    core = member.reshape(1)
    place = (core, lax.axis_index("space").reshape(1))
    turned = features.transpose(0, 2, 1)
    slots = kernel_call(
        send_features,
        out(devices, 128, 128),
        [hbm()] * 3,
        vmem(),
        [
            pltpu.SMEM(neighbours.shape, jnp.int32),
            memory(8, 64, dtype=jnp.int32),
            memory(8, 64, 512),
            memory(2048, 128, dtype=F32),
            copies(10),
        ],
    )(neighbours, heights, turned)
    came = to_all(slots)
    other_turned = over_chan(turned)

    held = [
        held_out(18, 288, 256),
        held_out(4096, 128),
        held_out(4096, 128, dtype=F32),
        held_out(4096, 128, dtype=F32),
        held_out(3456, 128),
        held_out(1024, 256),
        held_out(128, 512),
    ]
    lanes, active, slope, inner, taps, down, cot = kernel_call(
        prepare,
        held,
        [smem()] + [hbm()] * 5 + [pl.BlockSpec(memory_space=pl.ANY)],
        [hbm()] * 7,
        [
            memory(27, 128, 128),
            memory(8, 128, 256),
            memory(512, 256),
            memory(8, 64, dtype=jnp.int32),
            memory(8, 64, 512),
            memory(8, 64, 512),
            memory(4608, 256),
            memory(1024, 256),
            memory(512, 256),
            memory(128, 512),
            memory(18, 288, 384),
            memory(4096, 128, dtype=F32),
            memory(4096, 128, dtype=F32),
            memory(18, 288, 256),
            memory(4096, 128),
            memory(4096, 128, dtype=F32),
            memory(4096, 128, dtype=F32),
            copies(6),
            copies(6),
            copies(4),
        ],
        flops=5 << 30,
        mib=36,
    )(core, w_conv, w_down, cotangent[0], heights, turned, other_turned)
    came, taps, slope, inner = lax.optimization_barrier((came, taps, slope, inner))
    came_other = over_chan(came)
    taps, slope = kernel_call(
        fetch,
        [out(3456, 128), out(4096, 128, dtype=F32)],
        [hbm()] * 2,
        [vmem()] * 2,
        [copies(2)],
    )(taps, slope)

    share = -(-2752 // (devices * 16)) * 16
    terms, faces, coarse, grad_pre = kernel_call(
        forward,
        [
            held_out(devices, share + 16, 128),
            out(4, 256, 128),
            held_out(512, 128),
            held_out(4096, 128),
        ],
        [smem()] * 3 + [vmem()] * 4 + [hbm()] * 4,
        [hbm(), vmem(), hbm(), hbm()],
        [
            memory(2, 288, 384),
            memory(2, 256, 384),
            memory(4096, 128, dtype=F32),
            memory(4096, 128, dtype=F32),
            memory(128, 5120),
            memory(18, 288, 256),
            memory(1024, 256),
            memory(128, 512),
            memory(512, 128),
            memory(4096, 128),
            memory(devices, share + 16, 128),
            copies(4),
            copies(2),
            copies(4),
        ],
        flops=5 << 30,
        mib=24,
    )(
        neighbours, *place, came, came_other, taps, slope, inner, lanes, down, cot
    )

    arrived = to_all(terms)
    came_faces = [over_space(faces[i], i + 1) for i in range(4)]
    arrived, *came_faces = lax.optimization_barrier((arrived, *came_faces))
    came_faces = jnp.stack(came_faces)
    other_faces = over_chan(came_faces)
    sums = to_all(
        kernel_call(total, out(devices, share, 128), [vmem()], vmem())(arrived)
    )
    arrived_other = over_chan(arrived[:, share:])
    grad_features = kernel_call(
        backward,
        out(8, 64, 512),
        [smem()] * 3 + [vmem()] * 4 + [hbm()] * 3,
        vmem(),
        [
            memory(18, 288, 384),
            memory(4096, 128),
            memory(4096, 128),
            memory(27, 128, 128),
            memory(6912, 256),
            copies(3),
        ],
        flops=5 << 30,
        mib=24,
    )(
        neighbours, *place, arrived, arrived_other, came_faces, other_faces, grad_pre, active,
        w_conv,
    )

    grad_conv, grad_down = kernel_call(
        finish,
        [out(27, 64, 128, dtype=F32), out(8, 128, 128, dtype=F32)],
        [smem(), vmem()],
        [vmem()] * 2,
    )(core, sums.reshape(-1, 128))
    return coarse[None], grad_conv, grad_down, grad_features.transpose(0, 2, 1)


def solution(mesh):
    placed = (
        P("space", None, "chan"),
        P("space", None),
        P("space", None),
        P(),
        P(),
        P("space", None, None),
    )
    return jax.shard_map(
        local,
        mesh=mesh,
        in_specs=placed,
        out_specs=(
            P("space", None, "chan"),
            P(None, "chan", None),
            P(None, None, "chan"),
            P("space", None, "chan"),
        ),
        check_vma=False,
    )
```

```python
import jax
import jax.numpy as jnp
from jax import lax
from jax.experimental import pallas as pl
from jax.experimental.pallas import tpu as pltpu
from jax.sharding import PartitionSpec as P

OFFSETS = [
    (along_x, along_y, along_z)
    for along_x in (-1, 0, 1)
    for along_y in (-1, 0, 1)
    for along_z in (-1, 0, 1)
]
DIRECTIONS = [offset for offset in OFFSETS if offset != (0, 0, 0)]
FILL_ORDER = sorted(range(26), key=lambda k: (abs(DIRECTIONS[k][2]), k))
INACTIVE = -1e30
EDGE = 8
F32 = jnp.float32
BF16 = jnp.bfloat16


def vmem():
    return pl.BlockSpec(memory_space=pltpu.VMEM)


def smem():
    return pl.BlockSpec(memory_space=pltpu.SMEM)


def hbm():
    return pl.BlockSpec(memory_space=pltpu.HBM)


def kernel_call(body, outs, specs, out_specs, scratch=(), flops=0, mib=16):
    call = pl.pallas_call(
        body,
        out_shape=outs,
        in_specs=specs,
        out_specs=out_specs,
        scratch_shapes=list(scratch),
        compiler_params=pltpu.CompilerParams(vmem_limit_bytes=mib * 1024 * 1024),
        cost_estimate=pl.CostEstimate(flops=flops, bytes_accessed=1 << 22, transcendentals=0),
    )

    def run(*operands):
        placed = []
        for spec, operand in zip(specs, operands):
            if spec.memory_space == pltpu.HBM:
                operand = pltpu.with_memory_space_constraint(operand, pltpu.HBM)
            placed.append(operand)
        return call(*placed)

    return run


def start_all(pairs, arrived):
    copies = [
        pltpu.make_async_copy(source, target, arrived.at[i])
        for i, (source, target) in enumerate(pairs)
    ]
    for copy in copies:
        copy.start()
    return copies


def swap_halves(rows):
    return pltpu.roll(rows, 64, 1)


def low_lanes(rows):
    return lax.broadcasted_iota(jnp.int32, rows.shape, 1) < 64


def filled_voxels(heights_ref):
    columns = lax.broadcasted_iota(jnp.int32, (64, 512), 0)
    voxels = lax.broadcasted_iota(jnp.int32, (64, 512), 1)
    spread = (voxels // 8 == columns).astype(F32)
    tall = jnp.dot(heights_ref[...].astype(F32), spread, preferred_element_type=F32)
    level = lax.broadcasted_iota(jnp.int32, tall.shape, 1) % 8
    return (level.astype(F32) < tall).astype(F32)


def fill_slots(rows_ref, near_ref, slots_ref):
    for k, (dx, dy, dz) in enumerate(DIRECTIONS):
        block = near_ref[0, k]
        xh = 7 if dx == 1 else 0
        y = 15 if dy == 1 else 0
        z = 15 if dz == 1 else 0

        @pl.when(block >= 0)
        def _(dx=dx, dy=dy, dz=dz, xh=xh, y=y, z=z, block=block):
            zeros = [d == 0 for d in (dx, dy, dz)]
            if zeros == [False, True, True]:
                plane = rows_ref[xh * 256 : xh * 256 + 256, :]
                first, second = plane[:128], plane[128:]
                if dx == -1:
                    second = swap_halves(second)
                else:
                    first = swap_halves(first)
                region = jnp.where(low_lanes(first), first, second)
            elif zeros == [True, False, True]:
                region = jnp.concatenate(
                    [rows_ref[x * 256 + y * 16 : x * 256 + y * 16 + 16, :] for x in range(8)]
                )
            elif zeros == [True, True, False]:
                region = rows_ref[pl.ds(z, 128, stride=16), :]
            elif zeros == [False, False, True]:
                region = rows_ref[xh * 256 + y * 16 : xh * 256 + y * 16 + 16, :]
            elif zeros == [False, True, False]:
                region = rows_ref[pl.ds(xh * 256 + z, 16, stride=16), :]
            elif zeros == [True, False, False]:
                line = rows_ref[pl.ds(y * 16 + z, 8, stride=256), :]
                region = jnp.concatenate([line, line])
            else:
                at = xh * 256 + y * 16 + z
                region = jnp.broadcast_to(rows_ref[at : at + 1, :], (16, 128))
            slots_ref[block, 0 : region.shape[0], :] = region.astype(BF16)


def fill_edges(rows_ref, near_ref, slots_ref, start):
    for k, (dx, dy, dz) in enumerate(DIRECTIONS):
        if (dx, dy, dz).count(0) == 2:
            continue
        block = near_ref[0, k]
        x, y, z = (15 if d == 1 else 0 for d in (dx, dy, dz))

        @pl.when(block >= 0)
        def _(dx=dx, dy=dy, dz=dz, x=x, y=y, z=z, block=block):
            if dx == 0:
                rows = rows_ref[pl.ds(y * 16 + z, 16, stride=256), :]
            elif dz == 0:
                rows = rows_ref[x * 256 + y * 16 : x * 256 + y * 16 + 16, :]
            elif dy == 0:
                rows = rows_ref[pl.ds(x * 256 + z, 16, stride=16), :]
            else:
                at = x * 256 + y * 16 + z
                rows = jnp.broadcast_to(rows_ref[at : at + 1, :], (16, 128))
            low, high = rows[:EDGE], swap_halves(rows[EDGE:])
            rows = jnp.where(low_lanes(low), low, high)
            slots_ref[block, start : start + EDGE, :] = rows.astype(BF16)


def fill_faces(rows_ref, near_ref, place, faces_ref):
    member, own = place
    for k, (dx, dy, dz) in enumerate(DIRECTIONS):
        if (dx, dy, dz).count(0) != 2:
            continue
        block = near_ref[0, k]
        distance = jnp.where(member == 0, block - own, own - block)
        end = 15 if dx + dy + dz == 1 else 0

        @pl.when((block >= 0) & (distance >= 1))
        def _(dx=dx, dy=dy, end=end, distance=distance):
            if dx:
                region = rows_ref[end * 256 : end * 256 + 256, :]
            elif dy:
                region = jnp.concatenate(
                    [rows_ref[x * 256 + end * 16 : x * 256 + end * 16 + 16, :] for x in range(16)]
                )
            else:
                region = rows_ref[pl.ds(end, 256, stride=16), :]
            faces_ref[distance - 1] = region.astype(BF16)


class Whole:
    def __init__(self, ref):
        self.ref = ref

    def at(self, x, row, height):
        return self.ref, x, row


class Margin:
    def __init__(self, planes_ref, lines_ref):
        self.planes_ref, self.lines_ref = planes_ref, lines_ref

    def at(self, x, row, height):
        if x in (0, 17):
            return self.planes_ref, x // 17, row
        return self.lines_ref, row // 272, (x - 1) * 16


def put_lines(padded, places, rows):
    count = rows.shape[0]
    level = lax.broadcasted_iota(jnp.int32, rows.shape, 0) % 16
    below = jnp.where(level == 0, 0.0, pltpu.roll(rows, 1, 0)).astype(BF16)
    above = jnp.where(level == 15, 0.0, pltpu.roll(rows, count - 1, 0)).astype(BF16)
    here = rows.astype(BF16)
    at = 0
    for x, row, height in places:
        ref, plane, first = padded.at(x, row, height)
        for j, part in enumerate((below, here, above)):
            ref[plane, first : first + height, j * 128 : j * 128 + 128] = part[at : at + height]
        at += height


def put_ends(padded, x, row, rows, dz):
    lines = rows.shape[0]
    j = 0 if dz == -1 else 2
    end = 0 if dz == -1 else 15
    lanes = slice(j * 128, j * 128 + 128)
    ref, plane, first = padded.at(x, row, 16 * lines)
    span = slice(first, first + 16 * lines)
    old = ref[plane, span, lanes].astype(F32).reshape(lines, 16, 128)
    level = lax.broadcasted_iota(jnp.int32, old.shape, 1)
    new = jnp.where(level == end, rows.reshape(lines, 1, 128), old)
    ref[plane, span, lanes] = new.reshape(16 * lines, 128).astype(BF16)


def clear_margin(padded_ref):
    empty = jnp.zeros((288, 384), BF16)
    padded_ref[0] = empty
    padded_ref[17] = empty
    line = jnp.zeros((16, 384), BF16)
    for x in range(1, 17):
        padded_ref[x, 0:16, :] = line
        padded_ref[x, 272:288, :] = line


def put_region(padded, offset, rows):
    dx, dy, dz = offset
    zeros = [d == 0 for d in offset]
    x = 17 if dx == 1 else 0
    y = 17 if dy == 1 else 0
    if zeros == [False, True, True]:
        put_lines(padded, [(x, 16, 256)], rows)
    elif zeros == [True, False, True]:
        put_lines(padded, [(at + 1, y * 16, 16) for at in range(16)], rows)
    elif zeros == [False, False, True]:
        put_lines(padded, [(x, y * 16, 16)], rows)
    elif zeros == [True, True, False]:
        for at in range(16):
            put_ends(padded, at + 1, 16, rows[at * 16 : at * 16 + 16], dz)
    elif zeros == [False, True, False]:
        put_ends(padded, x, 16, rows, dz)
    elif zeros == [True, False, False]:
        for at in range(16):
            put_ends(padded, at + 1, y * 16, rows[at : at + 1], dz)
    else:
        put_ends(padded, x, y * 16, rows[0:1], dz)


def face_source(place, block):
    away = place[1] - block
    return jnp.where(away > 0, 0, 1) == place[0], jnp.clip(jnp.abs(away) - 1, 0, 3)


def fill_margin(padded, near_ref, own_ref, other_ref, start=0, faces=None, z_faces=True):
    for k in FILL_ORDER:
        offset = DIRECTIONS[k]
        block = near_ref[0, k]
        face = offset.count(0) == 2
        if face and offset[2] and not z_faces:
            continue
        if face and faces is not None:
            place, own_faces_ref, other_faces_ref = faces
            here, slot = face_source(place, block)

            @pl.when((block >= 0) & here)
            def _(offset=offset, slot=slot):
                put_region(padded, offset, own_faces_ref[slot].astype(F32))

            @pl.when((block >= 0) & jnp.logical_not(here))
            def _(offset=offset, slot=slot):
                rows = swap_halves(other_faces_ref[slot].astype(F32))
                put_region(padded, offset, rows)

            continue

        @pl.when(block >= 0)
        def _(offset=offset, block=block, face=face):
            height = 128 if face else 16 if start == 0 else EDGE
            own = own_ref[block, start : start + height, :].astype(F32)
            other = other_ref[block, 0:height, :].astype(F32)
            first = jnp.where(low_lanes(own), own, swap_halves(other))
            second = jnp.where(low_lanes(own), swap_halves(own), other)
            if face or start:
                rows = jnp.concatenate([first, second])
            elif offset[0] == 0:
                rows = jnp.concatenate([first[:8], second[:8]])
            else:
                rows = first if offset[0] == 1 else second
            put_region(padded, offset, rows)


def send_features(
    near_hbm, heights_hbm, features_hbm, slots_ref,
    near_ref, heights_ref, features_ref, rows_ref, arrived
):
    copies = [
        pltpu.make_async_copy(near_hbm, near_ref, arrived.at[8]),
        pltpu.make_async_copy(heights_hbm, heights_ref, arrived.at[9]),
    ]
    order = (0, 1, 2, 3, 4, 5, 6, 7)
    bricks = [
        pltpu.make_async_copy(features_hbm.at[i], features_ref.at[i], arrived.at[i]) for i in order
    ]
    for copy in copies + bricks:
        copy.start()
    copies[1].wait()
    filled = filled_voxels(heights_ref).astype(BF16)
    for oz in range(2):
        for oy in range(2):
            pair = []
            for ox in range(2):
                brick = ox + 2 * oy + 4 * oz
                bricks[brick].wait()
                pair.append(features_ref[brick] * filled[brick : brick + 1])
            turned = jnp.concatenate(pair).T.astype(F32)
            for vx in range(8):
                for vy in range(8):
                    at = vx * 256 + (8 * oy + vy) * 16 + 8 * oz
                    source = (vx * 8 + vy) * 8
                    rows_ref[at : at + 8, :] = turned[source : source + 8]
    copies[0].wait()
    fill_slots(rows_ref, near_ref, slots_ref)


def own_first_taps(shift, conv_ref, yz):
    taps = []
    for ex in range(3):
        tap = conv_ref[ex * 9 + yz].astype(F32)
        taps.append(pltpu.roll(pltpu.roll(tap, shift, 0), shift, 1))
    return taps


def forward_weights(shift, conv_ref, down_in_ref, cot_in_ref, two_ref, down_ref, cot_ref):
    empty = jnp.zeros((128, 128), BF16)
    for yz in range(9):
        taps = own_first_taps(shift, conv_ref, yz)
        whole = [empty] + [tap.astype(BF16) for tap in taps] + [empty]
        for p in range(4):
            rows = slice((p * 9 + yz) * 128, (p * 9 + yz) * 128 + 128)
            two_ref[rows, 0:128] = whole[p + 1] if p < 3 else empty
            two_ref[rows, 128:256] = whole[p]
    for tap in range(8):
        rows = down_in_ref[tap].astype(F32)
        rows = pltpu.roll(rows, shift, 0)
        down_ref[tap * 128 : tap * 128 + 128, :] = pltpu.roll(rows, 2 * shift, 1).astype(BF16)
    cot_ref[...] = pltpu.roll(cot_in_ref[...].astype(F32), 2 * shift, 1).astype(BF16)


def backward_weights(shift, conv_ref, four_ref):
    empty = jnp.zeros((128, 128), BF16)
    none = jnp.zeros((64, 128), F32)
    for yz in range(9):
        taps = own_first_taps(shift, conv_ref, yz)
        own = [none] + [taps[2 - ex][:64] for ex in range(3)] + [none]
        pairs = [jnp.concatenate([own[i + 1], own[i]]).T.astype(BF16) for i in range(4)]
        for p in range(6):
            at = (p * 9 + 8 - yz) * 128
            four_ref[at : at + 128, 0:128] = pairs[p] if p < 4 else empty
            four_ref[at : at + 128, 128:256] = pairs[p - 2] if p >= 2 else empty


def own_lanes(triple):
    below, here = triple[:, 0:128].astype(F32), triple[:, 128:256].astype(F32)
    both = jnp.where(low_lanes(below), below, swap_halves(here)).astype(BF16)
    return both, triple[:, 256:384]


def prepare(
    core_ref, conv_hbm, down_hbm, cot_hbm, heights_hbm, own_hbm, other_hbm,
    lanes_hbm, active_hbm, slope_hbm, inner_hbm, taps_hbm, down_out_hbm, cot_out_hbm,
    conv_in_ref, down_in_ref, cot_in_ref, heights_ref, own_ref, other_ref,
    two_ref, down_ref, cot_ref, own_cot_ref, padded_ref, rows_ref, mask_ref, lanes_ref, active_ref,
    slope_ref, inner_ref, arrived, left, left_inner
):
    came = start_all(
        [
            (conv_hbm, conv_in_ref),
            (down_hbm, down_in_ref),
            (cot_hbm, cot_in_ref),
            (heights_hbm, heights_ref),
            (own_hbm, own_ref),
            (other_hbm, other_ref),
        ],
        arrived,
    )
    gone = [
        pltpu.make_async_copy(source, target, left.at[i])
        for i, (source, target) in enumerate(
            [
                (two_ref.at[0:3456, 0:128], taps_hbm),
                (down_ref, down_out_hbm),
                (own_cot_ref, cot_out_hbm),
                (lanes_ref, lanes_hbm),
                (active_ref, active_hbm),
                (slope_ref, slope_hbm),
            ]
        )
    ]
    for copy in came[:3]:
        copy.wait()
    forward_weights(
        core_ref[0] * 64, conv_in_ref, down_in_ref, cot_in_ref, two_ref, down_ref, cot_ref
    )
    own_cot_ref[...] = cot_ref[:, 0:128].T
    for copy in gone[:3]:
        copy.start()
    for copy in came[3:]:
        copy.wait()
    filled = filled_voxels(heights_ref)
    upright = filled.T
    for brick in range(8):
        ox, oy, oz = brick % 2, brick // 2 % 2, brick // 4
        both = jnp.concatenate([own_ref[brick].astype(F32), other_ref[brick].astype(F32)])
        turned = (both * filled[brick : brick + 1]).T
        mask = jnp.broadcast_to(upright[:, brick : brick + 1], (512, 128))
        for vx in range(8):
            for vy in range(8):
                at = (8 * ox + vx) * 256 + (8 * oy + vy) * 16 + 8 * oz
                source = (vx * 8 + vy) * 8
                rows_ref[at : at + 8, :] = turned[source : source + 8]
                mask_ref[at : at + 8, :] = mask[source : source + 8]
    clear_margin(padded_ref)
    for x in range(16):
        put_lines(Whole(padded_ref), [(x + 1, 16, 256)], rows_ref[x * 256 : x * 256 + 256, :])
        active_ref[x * 256 : x * 256 + 256, :] = mask_ref[x * 256 : x * 256 + 256, :].astype(BF16)
    for x in range(18):
        lanes_ref[x, :, 0:128], lanes_ref[x, :, 128:256] = own_lanes(padded_ref[x])
    gone[3].start()
    gone[4].start()
    for tap in range(8):
        tx, ty, tz = tap // 4, tap // 2 % 2, tap % 2
        part = lax.dot_general(
            cot_ref[...],
            down_ref[tap * 128 : tap * 128 + 128, :],
            (((1,), (1,)), ((), ())),
            preferred_element_type=F32,
        )
        for ux in range(8):
            for uy in range(8):
                at = (2 * ux + tx) * 256 + (2 * uy + ty) * 16 + tz
                source = (ux * 8 + uy) * 8
                rows = pl.ds(at, 8, stride=2)
                slope_ref[rows, :] = part[source : source + 8] * mask_ref[rows, :]
    gone[5].start()

    def leave(group):
        rows = pl.ds(pl.multiple_of(group * 1024, 1024), 1024)
        return pltpu.make_async_copy(
            inner_ref.at[rows], inner_hbm.at[rows], left_inner.at[group]
        )


    def step(group, carry):
        lhs = []
        for pair in range(2):
            pieces = []
            for p in range(4):
                for ey in range(3):
                    pieces.append(
                        padded_ref[group * 4 + pair * 2 + p, ey * 16 : ey * 16 + 256, :]
                    )
            lhs.append(jnp.concatenate(pieces, axis=1))
        summed = jnp.dot(jnp.concatenate(lhs), two_ref[...], preferred_element_type=F32)
        for pair in range(2):
            for phase in range(2):
                at = pl.multiple_of((group * 4 + pair * 2 + phase) * 256, 256)
                part = summed[pair * 256 : pair * 256 + 256, phase * 128 : phase * 128 + 128]
                rows = pl.ds(at, 256)
                inner_ref[rows, :] = jnp.where(mask_ref[rows, :] > 0, part, INACTIVE)
        leave(group).start()
        return carry

    lax.fori_loop(0, 4, step, 0)
    for copy in gone:
        copy.wait()
    for group in range(4):
        leave(group).wait()


def tap_rows(taps_ref, taps):
    starts = [((ex * 3 + ey) * 3 + ez) * 128 for ex, ey, ez in taps]
    return jnp.concatenate([taps_ref[at : at + 128, :] for at in starts])


def margin_planes(planes_ref, taps_ref):
    sums = []
    for side, ex in ((0, 0), (1, 2)):
        lhs = jnp.concatenate(
            [planes_ref[side, ey * 16 : ey * 16 + 256, :] for ey in range(3)], axis=1
        )
        rhs = taps_ref[ex * 1152 : ex * 1152 + 1152, :]
        sums.append(jnp.dot(lhs, rhs, preferred_element_type=F32))
    return sums


def margin_lines(lines_ref, taps_ref):
    sums = []
    none = jnp.zeros((16, 384), BF16)
    for side, ey in ((0, 0), (1, 2)):
        lines = lines_ref[side]
        lhs = jnp.concatenate(
            [
                jnp.concatenate([none, lines[:240]]),
                lines,
                jnp.concatenate([lines[16:], none]),
            ],
            axis=1,
        )
        rhs = tap_rows(taps_ref, [(ex, ey, ez) for ex in range(3) for ez in range(3)])
        sums.append(jnp.dot(lhs, rhs, preferred_element_type=F32))
    return sums


def margin_ends(face, ez, taps_ref):
    line = lax.broadcasted_iota(jnp.int32, face.shape, 0) % 16
    shifted = [
        jnp.where(line == 0, 0.0, pltpu.roll(face, 1, 0)),
        face,
        jnp.where(line == 15, 0.0, pltpu.roll(face, 255, 0)),
    ]
    border = jnp.zeros((16, 128), F32)
    lhs = []
    for ex in range(3):
        for part in shifted:
            if ex == 0:
                part = jnp.concatenate([border, part[:240]])
            elif ex == 2:
                part = jnp.concatenate([part[16:], border])
            lhs.append(part.astype(BF16))
    rhs = tap_rows(taps_ref, [(ex, ey, ez) for ex in range(3) for ey in range(3)])
    return jnp.dot(jnp.concatenate(lhs, axis=1), rhs, preferred_element_type=F32)


Z_FACES = ((DIRECTIONS.index((0, 0, -1)), 0), (DIRECTIONS.index((0, 0, 1)), 2))


def joined_face(own_ref, other_ref, block):
    own = own_ref[block].astype(F32)
    other = other_ref[block].astype(F32)
    return jnp.concatenate(
        [
            jnp.where(low_lanes(own), own, swap_halves(other)),
            jnp.where(low_lanes(own), swap_halves(own), other),
        ]
    )


def add_margin(planes_ref, lines_ref, near_ref, own_ref, other_ref, taps_ref, pre_ref):
    for side, added in enumerate(margin_planes(planes_ref, taps_ref)):
        at = side * 15 * 256
        pre_ref[at : at + 256, :] += added
    for side, added in enumerate(margin_lines(lines_ref, taps_ref)):
        for x in range(16):
            at = x * 256 + side * 240
            pre_ref[at : at + 16, :] += added[x * 16 : x * 16 + 16]
    for k, ez in Z_FACES:
        block = near_ref[0, k]

        @pl.when(block >= 0)
        def _(block=block, ez=ez):
            added = margin_ends(joined_face(own_ref, other_ref, block), ez, taps_ref)
            rows = pl.ds(0 if ez == 0 else 15, 256, stride=16)
            pre_ref[rows, :] = pre_ref[rows, :] + added


def put_own_margin(planes_ref, lines_ref, near_ref, own_ref, other_ref, lanes_ref):
    for side in range(2):
        plane = side * 17
        lanes_ref[plane, :, 0:128], lanes_ref[plane, :, 128:256] = own_lanes(planes_ref[side])
        both, above = own_lanes(lines_ref[side])
        rows = slice(side * 272, side * 272 + 16)
        for x in range(16):
            lanes_ref[x + 1, rows, 0:128] = both[x * 16 : x * 16 + 16]
            lanes_ref[x + 1, rows, 128:256] = above[x * 16 : x * 16 + 16]
    for k, ez in Z_FACES:
        block = near_ref[0, k]

        @pl.when(block >= 0)
        def _(block=block, ez=ez):
            face = joined_face(own_ref, other_ref, block)
            lanes = slice(ez * 64, ez * 64 + 128)
            for x in range(16):
                old = lanes_ref[x + 1, 16:272, lanes].astype(F32).reshape(16, 16, 128)
                level = lax.broadcasted_iota(jnp.int32, old.shape, 1)
                lane = lax.broadcasted_iota(jnp.int32, old.shape, 2)
                here = (level == (0 if ez == 0 else 15)) & (lane < 64)
                new = jnp.where(here, face[x * 16 : x * 16 + 16].reshape(16, 1, 128), old)
                lanes_ref[x + 1, 16:272, lanes] = new.reshape(256, 128).astype(BF16)


def forward(
    near_ref, core_ref, at_ref, own_ref, other_ref, taps_ref, inner_ref,
    slope_hbm, lanes_hbm, down_hbm, cot_hbm,
    slots_hbm, faces_ref, coarse_hbm, grad_pre_hbm,
    planes_ref, lines_ref, pre_ref, grad_ref, turned_ref, slope_ref, lanes_ref,
    down_ref, cot_ref, coarse_ref, grad_pre_ref, slots_ref, arrived, left, left_slots
):
    came = start_all(
        [
            (lanes_hbm, lanes_ref),
            (slope_hbm, slope_ref),
            (down_hbm, down_ref),
            (cot_hbm, cot_ref),
        ],
        arrived,
    )
    pre_ref[...] = inner_ref[...]
    planes_ref[...] = jnp.zeros(planes_ref.shape, BF16)
    lines_ref[...] = jnp.zeros(lines_ref.shape, BF16)
    margin = Margin(planes_ref, lines_ref)
    fill_margin(margin, near_ref, own_ref, other_ref, z_faces=False)
    add_margin(planes_ref, lines_ref, near_ref, own_ref, other_ref, taps_ref, pre_ref)
    came[0].wait()
    put_own_margin(planes_ref, lines_ref, near_ref, own_ref, other_ref, lanes_ref)
    for copy in came[1:]:
        copy.wait()

    turned_ref[:, 0:512] = jnp.zeros((128, 512), BF16)
    turned_ref[:, 4608:5120] = jnp.zeros((128, 512), BF16)
    for x in range(16):
        rows = slice(x * 256, x * 256 + 256)
        pre = pre_ref[rows, :]
        sigmoid = 0.5 + 0.5 * jnp.tanh(0.5 * pre)
        pre_ref[rows, :] = jnp.where(pre > 0.5 * INACTIVE, pre * sigmoid, 0.0)
        grad = slope_ref[rows, :] * sigmoid * (1.0 + pre * (1.0 - sigmoid))
        grad_ref[rows, :] = grad
        grad = grad.astype(BF16)
        grad_pre_ref[rows, :] = grad
        turned_ref[:, 512 + x * 256 : 768 + x * 256] = grad.T

    gone = [
        pltpu.make_async_copy(grad_pre_ref, grad_pre_hbm, left.at[0]),
        pltpu.make_async_copy(coarse_ref, coarse_hbm, left.at[1]),
    ]
    gone[0].start()
    share = slots_ref.shape[1] - EDGE
    def put_terms(at, rows):
        while rows.shape[0]:
            owner, row = at // share, at % share
            count = min(rows.shape[0], share - row)
            slots_ref[owner, row : row + count, :] = rows[:count]
            rows = rows[count:]
            at += count

    leaving = [pltpu.make_async_copy(slots_ref, slots_hbm, left_slots.at[0])]

    patches = []
    for tap in range(8):
        tx, ty, tz = tap // 4, tap // 2 % 2, tap % 2
        pieces = []
        for ux in range(8):
            for uy in range(8):
                at = (2 * ux + tx) * 256 + (2 * uy + ty) * 16 + tz
                pieces.append(pre_ref[pl.ds(at, 8, stride=2), :])
        patches.append(jnp.concatenate(pieces).astype(BF16))
    patches = jnp.concatenate(patches, axis=1)
    coarse = jnp.dot(patches, down_ref[...], preferred_element_type=F32)
    coarse_ref[...] = coarse[:, :128].astype(BF16)
    gone[1].start()
    grad_down = jnp.dot(cot_ref[...], patches, preferred_element_type=F32).astype(BF16)
    for tap in range(8):
        put_terms(tap * 128, grad_down[:, tap * 128 : tap * 128 + 128].T)
    lhs = jnp.concatenate(
        [turned_ref[:, (2 - ex) * 256 : (2 - ex) * 256 + 4608] for ex in range(3)]
    )
    for ey in range(3):
        rhs = lanes_ref[:, ey * 16 : ey * 16 + 256, :].reshape(4608, 256)
        summed = jnp.dot(lhs, rhs, preferred_element_type=F32)
        for ex in range(3):
            part = summed[ex * 128 : ex * 128 + 128].astype(BF16).T
            put_terms(1024 + (ey * 3 + ex) * 192, part[0:192])
    fill_edges(grad_ref, near_ref, slots_ref, share)
    for copy in leaving:
        copy.start()
    fill_faces(grad_ref, near_ref, (core_ref[0], at_ref[0]), faces_ref)
    for copy in gone + leaving:
        copy.wait()


def fetch(taps_hbm, inner_hbm, taps_ref, inner_ref, arrived):
    for copy in start_all([(taps_hbm, taps_ref), (inner_hbm, inner_ref)], arrived):
        copy.wait()


def total(slots_ref, out_ref):
    devices, share, _ = out_ref.shape
    summed = slots_ref[0, 0:share, :].astype(F32)
    for device in range(1, devices):
        summed = summed + slots_ref[device, 0:share, :].astype(F32)
    summed = (summed / devices).astype(BF16)
    for device in range(devices):
        out_ref[device] = summed


def backward(
    near_ref, core_ref, at_ref, own_ref, other_ref, own_faces_ref, other_faces_ref,
    grad_pre_hbm, active_hbm, conv_hbm, out_ref,
    padded_ref, grad_pre_ref, active_ref, conv_ref, back_ref, arrived
):
    came = start_all(
        [(conv_hbm, conv_ref), (grad_pre_hbm, grad_pre_ref), (active_hbm, active_ref)], arrived
    )
    came[0].wait()
    backward_weights(core_ref[0] * 64, conv_ref, back_ref)
    clear_margin(padded_ref)
    came[1].wait()
    for x in range(16):
        rows = grad_pre_ref[x * 256 : x * 256 + 256, :].astype(F32)
        put_lines(Whole(padded_ref), [(x + 1, 16, 256)], rows)
    fill_margin(
        Whole(padded_ref), near_ref, own_ref, other_ref, own_ref.shape[1] - EDGE,
        ((core_ref[0], at_ref[0]), own_faces_ref, other_faces_ref),
    )
    came[2].wait()
    for half in range(2):
        lhs = []
        for quad in range(2):
            pieces = []
            for p in range(6):
                for ey in range(3):
                    pieces.append(
                        padded_ref[half * 8 + quad * 4 + p, ey * 16 : ey * 16 + 256, :]
                    )
            lhs.append(jnp.concatenate(pieces, axis=1))
        summed = jnp.dot(jnp.concatenate(lhs), back_ref[...], preferred_element_type=F32)
        for quad in range(2):
            for two in range(2):
                part = summed[quad * 256 : quad * 256 + 256, two * 128 : two * 128 + 128]
                x = half * 8 + quad * 4 + two * 2
                even = active_ref[x * 256 : x * 256 + 256, :].astype(F32)
                odd = active_ref[x * 256 + 256 : x * 256 + 512, :].astype(F32)
                part = part * jnp.where(low_lanes(part), even, odd)
                for oy in range(2):
                    rows = [
                        part[(8 * oy + vy) * 16 + 8 * oz : (8 * oy + vy) * 16 + 8 * oz + 8]
                        for oz in range(2)
                        for vy in range(8)
                    ]
                    turned = jnp.concatenate(rows).T
                    first, second = turned[:64], turned[64:]
                    lanes = slice(x % 8 * 64, x % 8 * 64 + 128)
                    brick = half + 2 * oy
                    near = jnp.where(low_lanes(first), first, swap_halves(second))
                    far = jnp.where(low_lanes(first), swap_halves(first), second)
                    out_ref[brick, :, lanes] = near.astype(BF16)
                    out_ref[brick + 4, :, lanes] = far.astype(BF16)


def finish(core_ref, sums_ref, conv_ref, down_ref):
    shift = core_ref[0] * 64
    for tap in range(27):
        ex, ey, ez = tap // 9, tap // 3 % 3, tap % 3
        at = 1024 + ((ey * 3 + ex) * 3 + ez) * 64
        rows = sums_ref[at : at + 64, :].astype(F32)
        conv_ref[tap] = pltpu.roll(rows, shift, 1)
    for tap in range(8):
        rows = sums_ref[tap * 128 : tap * 128 + 128, :].astype(F32)
        down_ref[tap, pl.ds(shift, 64), :] = rows[:64]
        down_ref[tap, pl.ds(64 - shift, 64), :] = rows[64:]


def over_space(block, distance):
    blocks = range(lax.axis_size("space"))
    route = [(2 * i, 2 * (i + distance)) for i in blocks if i + distance in blocks]
    route += [(2 * i + 1, 2 * (i - distance) + 1) for i in blocks if i - distance in blocks]
    return lax.ppermute(block, ("space", "chan"), route)


def over_chan(block):
    return lax.ppermute(block, "chan", [(0, 1), (1, 0)])


def to_all(slots):
    return lax.all_to_all(slots, "space", 0, 0, tiled=True)


def local(features, heights, neighbours, w_conv, w_down, cotangent):
    devices = lax.axis_size("space")
    member = lax.axis_index("chan")

    def out(*shape, dtype=BF16):
        return jax.ShapeDtypeStruct(shape, dtype)

    def held_out(*shape, dtype=BF16):
        return pltpu.HBM(shape, dtype)

    def memory(*shape, dtype=BF16):
        return pltpu.VMEM(shape, dtype)

    def copies(count):
        return pltpu.SemaphoreType.DMA((count,))

    core = member.reshape(1)
    place = (core, lax.axis_index("space").reshape(1))
    turned = features.transpose(0, 2, 1)
    slots = kernel_call(
        send_features,
        out(devices, 128, 128),
        [hbm()] * 3,
        vmem(),
        [
            pltpu.SMEM(neighbours.shape, jnp.int32),
            memory(8, 64, dtype=jnp.int32),
            memory(8, 64, 512),
            memory(2048, 128, dtype=F32),
            copies(10),
        ],
    )(neighbours, heights, turned)
    came = to_all(slots)
    other_turned = over_chan(turned)

    held = [
        held_out(18, 288, 256),
        held_out(4096, 128),
        held_out(4096, 128, dtype=F32),
        held_out(4096, 128, dtype=F32),
        held_out(3456, 128),
        held_out(1024, 256),
        held_out(128, 512),
    ]
    lanes, active, slope, inner, taps, down, cot = kernel_call(
        prepare,
        held,
        [smem()] + [hbm()] * 5 + [pl.BlockSpec(memory_space=pl.ANY)],
        [hbm()] * 7,
        [
            memory(27, 128, 128),
            memory(8, 128, 256),
            memory(512, 256),
            memory(8, 64, dtype=jnp.int32),
            memory(8, 64, 512),
            memory(8, 64, 512),
            memory(4608, 256),
            memory(1024, 256),
            memory(512, 256),
            memory(128, 512),
            memory(18, 288, 384),
            memory(4096, 128, dtype=F32),
            memory(4096, 128, dtype=F32),
            memory(18, 288, 256),
            memory(4096, 128),
            memory(4096, 128, dtype=F32),
            memory(4096, 128, dtype=F32),
            copies(6),
            copies(6),
            copies(4),
        ],
        flops=5 << 30,
        mib=36,
    )(core, w_conv, w_down, cotangent[0], heights, turned, other_turned)
    came, taps, inner = lax.optimization_barrier((came, taps, inner))
    came_other = over_chan(came)
    taps, inner = kernel_call(
        fetch,
        [out(3456, 128), out(4096, 128, dtype=F32)],
        [hbm()] * 2,
        [vmem()] * 2,
        [copies(2)],
    )(taps, inner)

    share = -(-2752 // (devices * 16)) * 16
    terms, faces, coarse, grad_pre = kernel_call(
        forward,
        [
            held_out(devices, share + EDGE, 128),
            out(4, 256, 128),
            held_out(512, 128),
            held_out(4096, 128),
        ],
        [smem()] * 3 + [vmem()] * 4 + [hbm()] * 4,
        [hbm(), vmem(), hbm(), hbm()],
        [
            memory(2, 288, 384),
            memory(2, 256, 384),
            memory(4096, 128, dtype=F32),
            memory(4096, 128, dtype=F32),
            memory(128, 5120),
            memory(4096, 128, dtype=F32),
            memory(18, 288, 256),
            memory(1024, 256),
            memory(128, 512),
            memory(512, 128),
            memory(4096, 128),
            memory(devices, share + EDGE, 128),
            copies(4),
            copies(2),
            copies(1),
        ],
        flops=5 << 30,
        mib=24,
    )(
        neighbours, *place, came, came_other, taps, inner, slope, lanes, down, cot
    )

    arrived = to_all(terms)
    came_faces = [over_space(faces[i], i + 1) for i in range(4)]
    arrived, *came_faces = lax.optimization_barrier((arrived, *came_faces))
    came_faces = jnp.stack(came_faces)
    other_faces = over_chan(came_faces)
    sums = to_all(
        kernel_call(total, out(devices, share, 128), [vmem()], vmem())(arrived)
    )
    arrived_other = over_chan(arrived[:, share:])
    grad_features = kernel_call(
        backward,
        out(8, 64, 512),
        [smem()] * 3 + [vmem()] * 4 + [hbm()] * 3,
        vmem(),
        [
            memory(18, 288, 384),
            memory(4096, 128),
            memory(4096, 128),
            memory(27, 128, 128),
            memory(6912, 256),
            copies(3),
        ],
        flops=5 << 30,
        mib=24,
    )(
        neighbours, *place, arrived, arrived_other, came_faces, other_faces, grad_pre, active,
        w_conv,
    )

    grad_conv, grad_down = kernel_call(
        finish,
        [out(27, 64, 128, dtype=F32), out(8, 128, 128, dtype=F32)],
        [smem(), vmem()],
        [vmem()] * 2,
    )(core, sums.reshape(-1, 128))
    return coarse[None], grad_conv, grad_down, grad_features.transpose(0, 2, 1)


def solution(mesh):
    placed = (
        P("space", None, "chan"),
        P("space", None),
        P("space", None),
        P(),
        P(),
        P("space", None, None),
    )
    return jax.shard_map(
        local,
        mesh=mesh,
        in_specs=placed,
        out_specs=(
            P("space", None, "chan"),
            P(None, "chan", None),
            P(None, None, "chan"),
            P("space", None, "chan"),
        ),
        check_vma=False,
    )
```

```python
import jax
import jax.numpy as jnp
from jax import lax
from jax.experimental import pallas as pl
from jax.experimental.pallas import tpu as pltpu
from jax.sharding import PartitionSpec as P

OFFSETS = [
    (along_x, along_y, along_z)
    for along_x in (-1, 0, 1)
    for along_y in (-1, 0, 1)
    for along_z in (-1, 0, 1)
]
DIRECTIONS = [offset for offset in OFFSETS if offset != (0, 0, 0)]
FILL_ORDER = sorted(range(26), key=lambda k: (abs(DIRECTIONS[k][2]), k))
INACTIVE = -1e30
EDGE = 8
F32 = jnp.float32
BF16 = jnp.bfloat16


def vmem():
    return pl.BlockSpec(memory_space=pltpu.VMEM)


def smem():
    return pl.BlockSpec(memory_space=pltpu.SMEM)


def hbm():
    return pl.BlockSpec(memory_space=pltpu.HBM)


def kernel_call(body, outs, specs, out_specs, scratch=(), flops=0, mib=16):
    call = pl.pallas_call(
        body,
        out_shape=outs,
        in_specs=specs,
        out_specs=out_specs,
        scratch_shapes=list(scratch),
        compiler_params=pltpu.CompilerParams(vmem_limit_bytes=mib * 1024 * 1024),
        cost_estimate=pl.CostEstimate(flops=flops, bytes_accessed=1 << 22, transcendentals=0),
    )

    def run(*operands):
        placed = []
        for spec, operand in zip(specs, operands):
            if spec.memory_space == pltpu.HBM:
                operand = pltpu.with_memory_space_constraint(operand, pltpu.HBM)
            placed.append(operand)
        return call(*placed)

    return run


def start_all(pairs, arrived):
    copies = [
        pltpu.make_async_copy(source, target, arrived.at[i])
        for i, (source, target) in enumerate(pairs)
    ]
    for copy in copies:
        copy.start()
    return copies


def swap_halves(rows):
    return pltpu.roll(rows, 64, 1)


def low_lanes(rows):
    return lax.broadcasted_iota(jnp.int32, rows.shape, 1) < 64


def filled_voxels(heights_ref):
    columns = lax.broadcasted_iota(jnp.int32, (64, 512), 0)
    voxels = lax.broadcasted_iota(jnp.int32, (64, 512), 1)
    spread = (voxels // 8 == columns).astype(F32)
    tall = jnp.dot(heights_ref[...].astype(F32), spread, preferred_element_type=F32)
    level = lax.broadcasted_iota(jnp.int32, tall.shape, 1) % 8
    return (level.astype(F32) < tall).astype(F32)


def fill_slots(rows_ref, near_ref, slots_ref, slots_hbm, left):
    def leave(k):
        block = near_ref[0, k]
        rows = slice(0, 128 if DIRECTIONS[k].count(0) == 2 else 16)
        return pltpu.make_async_copy(
            slots_ref.at[block, rows], slots_hbm.at[block, rows], left.at[k]
        )

    for k, (dx, dy, dz) in enumerate(DIRECTIONS):
        block = near_ref[0, k]
        xh = 7 if dx == 1 else 0
        y = 15 if dy == 1 else 0
        z = 15 if dz == 1 else 0

        @pl.when(block >= 0)
        def _(k=k, dx=dx, dy=dy, dz=dz, xh=xh, y=y, z=z, block=block):
            zeros = [d == 0 for d in (dx, dy, dz)]
            if zeros == [False, True, True]:
                plane = rows_ref[xh * 256 : xh * 256 + 256, :]
                first, second = plane[:128], plane[128:]
                if dx == -1:
                    second = swap_halves(second)
                else:
                    first = swap_halves(first)
                region = jnp.where(low_lanes(first), first, second)
            elif zeros == [True, False, True]:
                region = jnp.concatenate(
                    [rows_ref[x * 256 + y * 16 : x * 256 + y * 16 + 16, :] for x in range(8)]
                )
            elif zeros == [True, True, False]:
                region = rows_ref[pl.ds(z, 128, stride=16), :]
            elif zeros == [False, False, True]:
                region = rows_ref[xh * 256 + y * 16 : xh * 256 + y * 16 + 16, :]
            elif zeros == [False, True, False]:
                region = rows_ref[pl.ds(xh * 256 + z, 16, stride=16), :]
            elif zeros == [True, False, False]:
                line = rows_ref[pl.ds(y * 16 + z, 8, stride=256), :]
                region = jnp.concatenate([line, line])
            else:
                at = xh * 256 + y * 16 + z
                region = jnp.broadcast_to(rows_ref[at : at + 1, :], (16, 128))
            slots_ref[block, 0 : region.shape[0], :] = region.astype(BF16)
            leave(k).start()

    for k in range(26):

        @pl.when(near_ref[0, k] >= 0)
        def _(k=k):
            leave(k).wait()


def fill_edges(rows_ref, near_ref, slots_ref, start):
    for k, (dx, dy, dz) in enumerate(DIRECTIONS):
        if (dx, dy, dz).count(0) == 2:
            continue
        block = near_ref[0, k]
        x, y, z = (15 if d == 1 else 0 for d in (dx, dy, dz))

        @pl.when(block >= 0)
        def _(dx=dx, dy=dy, dz=dz, x=x, y=y, z=z, block=block):
            if dx == 0:
                rows = rows_ref[pl.ds(y * 16 + z, 16, stride=256), :]
            elif dz == 0:
                rows = rows_ref[x * 256 + y * 16 : x * 256 + y * 16 + 16, :]
            elif dy == 0:
                rows = rows_ref[pl.ds(x * 256 + z, 16, stride=16), :]
            else:
                at = x * 256 + y * 16 + z
                rows = jnp.broadcast_to(rows_ref[at : at + 1, :], (16, 128))
            low, high = rows[:EDGE], swap_halves(rows[EDGE:])
            rows = jnp.where(low_lanes(low), low, high)
            slots_ref[block, start : start + EDGE, :] = rows.astype(BF16)


def fill_faces(rows_ref, near_ref, place, faces_ref):
    member, own = place
    for k, (dx, dy, dz) in enumerate(DIRECTIONS):
        if (dx, dy, dz).count(0) != 2:
            continue
        block = near_ref[0, k]
        distance = jnp.where(member == 0, block - own, own - block)
        end = 15 if dx + dy + dz == 1 else 0

        @pl.when((block >= 0) & (distance >= 1))
        def _(dx=dx, dy=dy, end=end, distance=distance):
            if dx:
                region = rows_ref[end * 256 : end * 256 + 256, :]
            elif dy:
                region = jnp.concatenate(
                    [rows_ref[x * 256 + end * 16 : x * 256 + end * 16 + 16, :] for x in range(16)]
                )
            else:
                region = rows_ref[pl.ds(end, 256, stride=16), :]
            faces_ref[distance - 1] = region.astype(BF16)


class Whole:
    def __init__(self, ref):
        self.ref = ref

    def at(self, x, row, height):
        return self.ref, x, row


class Margin:
    def __init__(self, planes_ref, lines_ref):
        self.planes_ref, self.lines_ref = planes_ref, lines_ref

    def at(self, x, row, height):
        if x in (0, 17):
            return self.planes_ref, x // 17, row
        return self.lines_ref, row // 272, (x - 1) * 16


def put_lines(padded, places, rows):
    count = rows.shape[0]
    level = lax.broadcasted_iota(jnp.int32, rows.shape, 0) % 16
    below = jnp.where(level == 0, 0.0, pltpu.roll(rows, 1, 0)).astype(BF16)
    above = jnp.where(level == 15, 0.0, pltpu.roll(rows, count - 1, 0)).astype(BF16)
    here = rows.astype(BF16)
    at = 0
    for x, row, height in places:
        ref, plane, first = padded.at(x, row, height)
        for j, part in enumerate((below, here, above)):
            ref[plane, first : first + height, j * 128 : j * 128 + 128] = part[at : at + height]
        at += height


def put_ends(padded, x, row, rows, dz):
    lines = rows.shape[0]
    j = 0 if dz == -1 else 2
    end = 0 if dz == -1 else 15
    lanes = slice(j * 128, j * 128 + 128)
    ref, plane, first = padded.at(x, row, 16 * lines)
    span = slice(first, first + 16 * lines)
    old = ref[plane, span, lanes].astype(F32).reshape(lines, 16, 128)
    level = lax.broadcasted_iota(jnp.int32, old.shape, 1)
    new = jnp.where(level == end, rows.reshape(lines, 1, 128), old)
    ref[plane, span, lanes] = new.reshape(16 * lines, 128).astype(BF16)


def clear_margin(padded_ref):
    empty = jnp.zeros((288, 384), BF16)
    padded_ref[0] = empty
    padded_ref[17] = empty
    line = jnp.zeros((16, 384), BF16)
    for x in range(1, 17):
        padded_ref[x, 0:16, :] = line
        padded_ref[x, 272:288, :] = line


def put_region(padded, offset, rows):
    dx, dy, dz = offset
    zeros = [d == 0 for d in offset]
    x = 17 if dx == 1 else 0
    y = 17 if dy == 1 else 0
    if zeros == [False, True, True]:
        put_lines(padded, [(x, 16, 256)], rows)
    elif zeros == [True, False, True]:
        put_lines(padded, [(at + 1, y * 16, 16) for at in range(16)], rows)
    elif zeros == [False, False, True]:
        put_lines(padded, [(x, y * 16, 16)], rows)
    elif zeros == [True, True, False]:
        for at in range(16):
            put_ends(padded, at + 1, 16, rows[at * 16 : at * 16 + 16], dz)
    elif zeros == [False, True, False]:
        put_ends(padded, x, 16, rows, dz)
    elif zeros == [True, False, False]:
        for at in range(16):
            put_ends(padded, at + 1, y * 16, rows[at : at + 1], dz)
    else:
        put_ends(padded, x, y * 16, rows[0:1], dz)


def face_source(place, block):
    away = place[1] - block
    return jnp.where(away > 0, 0, 1) == place[0], jnp.clip(jnp.abs(away) - 1, 0, 3)


def fill_margin(padded, near_ref, own_ref, other_ref, start=0, faces=None, z_faces=True):
    for k in FILL_ORDER:
        offset = DIRECTIONS[k]
        block = near_ref[0, k]
        face = offset.count(0) == 2
        if face and offset[2] and not z_faces:
            continue
        if face and faces is not None:
            place, own_faces_ref, other_faces_ref = faces
            here, slot = face_source(place, block)

            @pl.when((block >= 0) & here)
            def _(offset=offset, slot=slot):
                put_region(padded, offset, own_faces_ref[slot].astype(F32))

            @pl.when((block >= 0) & jnp.logical_not(here))
            def _(offset=offset, slot=slot):
                rows = swap_halves(other_faces_ref[slot].astype(F32))
                put_region(padded, offset, rows)

            continue

        @pl.when(block >= 0)
        def _(offset=offset, block=block, face=face):
            height = 128 if face else 16 if start == 0 else EDGE
            own = own_ref[block, start : start + height, :].astype(F32)
            other = other_ref[block, 0:height, :].astype(F32)
            first = jnp.where(low_lanes(own), own, swap_halves(other))
            second = jnp.where(low_lanes(own), swap_halves(own), other)
            if face or start:
                rows = jnp.concatenate([first, second])
            elif offset[0] == 0:
                rows = jnp.concatenate([first[:8], second[:8]])
            else:
                rows = first if offset[0] == 1 else second
            put_region(padded, offset, rows)


def send_features(
    near_hbm, heights_hbm, features_hbm, slots_hbm,
    near_ref, heights_ref, features_ref, rows_ref, slots_ref, arrived, left
):
    copies = [
        pltpu.make_async_copy(near_hbm, near_ref, arrived.at[8]),
        pltpu.make_async_copy(heights_hbm, heights_ref, arrived.at[9]),
    ]
    order = (0, 1, 2, 3, 4, 5, 6, 7)
    bricks = [
        pltpu.make_async_copy(features_hbm.at[i], features_ref.at[i], arrived.at[i]) for i in order
    ]
    for copy in copies + bricks:
        copy.start()
    copies[1].wait()
    filled = filled_voxels(heights_ref).astype(BF16)
    for oz in range(2):
        for oy in range(2):
            pair = []
            for ox in range(2):
                brick = ox + 2 * oy + 4 * oz
                bricks[brick].wait()
                pair.append(features_ref[brick] * filled[brick : brick + 1])
            turned = jnp.concatenate(pair).T.astype(F32)
            for vx in range(8):
                for vy in range(8):
                    at = vx * 256 + (8 * oy + vy) * 16 + 8 * oz
                    source = (vx * 8 + vy) * 8
                    rows_ref[at : at + 8, :] = turned[source : source + 8]
    copies[0].wait()
    fill_slots(rows_ref, near_ref, slots_ref, slots_hbm, left)


def own_first_taps(shift, conv_ref, yz):
    taps = []
    for ex in range(3):
        tap = conv_ref[ex * 9 + yz].astype(F32)
        taps.append(pltpu.roll(pltpu.roll(tap, shift, 0), shift, 1))
    return taps


def forward_weights(shift, conv_ref, down_in_ref, cot_in_ref, two_ref, down_ref, cot_ref):
    empty = jnp.zeros((128, 128), BF16)
    for yz in range(9):
        taps = own_first_taps(shift, conv_ref, yz)
        whole = [empty] + [tap.astype(BF16) for tap in taps] + [empty]
        for p in range(4):
            rows = slice((p * 9 + yz) * 128, (p * 9 + yz) * 128 + 128)
            two_ref[rows, 0:128] = whole[p + 1] if p < 3 else empty
            two_ref[rows, 128:256] = whole[p]
    for tap in range(8):
        rows = down_in_ref[tap].astype(F32)
        rows = pltpu.roll(rows, shift, 0)
        down_ref[tap * 128 : tap * 128 + 128, :] = pltpu.roll(rows, 2 * shift, 1).astype(BF16)
    cot_ref[...] = pltpu.roll(cot_in_ref[...].astype(F32), 2 * shift, 1).astype(BF16)


def backward_weights(shift, conv_ref, four_ref):
    empty = jnp.zeros((128, 128), BF16)
    none = jnp.zeros((64, 128), F32)
    for yz in range(9):
        taps = own_first_taps(shift, conv_ref, yz)
        own = [none] + [taps[2 - ex][:64] for ex in range(3)] + [none]
        pairs = [jnp.concatenate([own[i + 1], own[i]]).T.astype(BF16) for i in range(4)]
        for p in range(6):
            at = (p * 9 + 8 - yz) * 128
            four_ref[at : at + 128, 0:128] = pairs[p] if p < 4 else empty
            four_ref[at : at + 128, 128:256] = pairs[p - 2] if p >= 2 else empty


def own_lanes(triple):
    below, here = triple[:, 0:128].astype(F32), triple[:, 128:256].astype(F32)
    both = jnp.where(low_lanes(below), below, swap_halves(here)).astype(BF16)
    return both, triple[:, 256:384]


def prepare(
    core_ref, conv_hbm, down_hbm, cot_hbm, heights_hbm, own_hbm, other_hbm,
    lanes_hbm, active_hbm, slope_hbm, inner_hbm, taps_hbm, down_out_hbm, cot_out_hbm,
    conv_in_ref, down_in_ref, cot_in_ref, heights_ref, own_ref, other_ref,
    two_ref, down_ref, cot_ref, own_cot_ref, padded_ref, rows_ref, mask_ref, lanes_ref, active_ref,
    slope_ref, inner_ref, arrived, left, left_inner
):
    came = start_all(
        [
            (conv_hbm, conv_in_ref),
            (down_hbm, down_in_ref),
            (cot_hbm, cot_in_ref),
            (heights_hbm, heights_ref),
            (own_hbm, own_ref),
            (other_hbm, other_ref),
        ],
        arrived,
    )
    gone = [
        pltpu.make_async_copy(source, target, left.at[i])
        for i, (source, target) in enumerate(
            [
                (two_ref.at[0:3456, 0:128], taps_hbm),
                (down_ref, down_out_hbm),
                (own_cot_ref, cot_out_hbm),
                (lanes_ref, lanes_hbm),
                (active_ref, active_hbm),
                (slope_ref, slope_hbm),
            ]
        )
    ]
    for copy in came[:3]:
        copy.wait()
    forward_weights(
        core_ref[0] * 64, conv_in_ref, down_in_ref, cot_in_ref, two_ref, down_ref, cot_ref
    )
    own_cot_ref[...] = cot_ref[:, 0:128].T
    for copy in gone[:3]:
        copy.start()
    for copy in came[3:]:
        copy.wait()
    filled = filled_voxels(heights_ref)
    upright = filled.T
    for brick in range(8):
        ox, oy, oz = brick % 2, brick // 2 % 2, brick // 4
        both = jnp.concatenate([own_ref[brick].astype(F32), other_ref[brick].astype(F32)])
        turned = (both * filled[brick : brick + 1]).T
        mask = jnp.broadcast_to(upright[:, brick : brick + 1], (512, 128))
        for vx in range(8):
            for vy in range(8):
                at = (8 * ox + vx) * 256 + (8 * oy + vy) * 16 + 8 * oz
                source = (vx * 8 + vy) * 8
                rows_ref[at : at + 8, :] = turned[source : source + 8]
                mask_ref[at : at + 8, :] = mask[source : source + 8]
    clear_margin(padded_ref)
    for x in range(16):
        put_lines(Whole(padded_ref), [(x + 1, 16, 256)], rows_ref[x * 256 : x * 256 + 256, :])
        active_ref[x * 256 : x * 256 + 256, :] = mask_ref[x * 256 : x * 256 + 256, :].astype(BF16)
    for x in range(18):
        lanes_ref[x, :, 0:128], lanes_ref[x, :, 128:256] = own_lanes(padded_ref[x])
    gone[3].start()
    gone[4].start()
    for tap in range(8):
        tx, ty, tz = tap // 4, tap // 2 % 2, tap % 2
        part = lax.dot_general(
            cot_ref[...],
            down_ref[tap * 128 : tap * 128 + 128, :],
            (((1,), (1,)), ((), ())),
            preferred_element_type=F32,
        )
        for ux in range(8):
            for uy in range(8):
                at = (2 * ux + tx) * 256 + (2 * uy + ty) * 16 + tz
                source = (ux * 8 + uy) * 8
                rows = pl.ds(at, 8, stride=2)
                slope_ref[rows, :] = part[source : source + 8] * mask_ref[rows, :]
    gone[5].start()

    def leave(group):
        rows = pl.ds(pl.multiple_of(group * 1024, 1024), 1024)
        return pltpu.make_async_copy(
            inner_ref.at[rows], inner_hbm.at[rows], left_inner.at[group]
        )


    def step(group, carry):
        lhs = []
        for pair in range(2):
            pieces = []
            for p in range(4):
                for ey in range(3):
                    pieces.append(
                        padded_ref[group * 4 + pair * 2 + p, ey * 16 : ey * 16 + 256, :]
                    )
            lhs.append(jnp.concatenate(pieces, axis=1))
        summed = jnp.dot(jnp.concatenate(lhs), two_ref[...], preferred_element_type=F32)
        for pair in range(2):
            for phase in range(2):
                at = pl.multiple_of((group * 4 + pair * 2 + phase) * 256, 256)
                part = summed[pair * 256 : pair * 256 + 256, phase * 128 : phase * 128 + 128]
                rows = pl.ds(at, 256)
                inner_ref[rows, :] = jnp.where(mask_ref[rows, :] > 0, part, INACTIVE)
        leave(group).start()
        return carry

    lax.fori_loop(0, 4, step, 0)
    for copy in gone:
        copy.wait()
    for group in range(4):
        leave(group).wait()


def tap_rows(taps_ref, taps):
    starts = [((ex * 3 + ey) * 3 + ez) * 128 for ex, ey, ez in taps]
    return jnp.concatenate([taps_ref[at : at + 128, :] for at in starts])


def margin_planes(planes_ref, taps_ref):
    sums = []
    for side, ex in ((0, 0), (1, 2)):
        lhs = jnp.concatenate(
            [planes_ref[side, ey * 16 : ey * 16 + 256, :] for ey in range(3)], axis=1
        )
        rhs = taps_ref[ex * 1152 : ex * 1152 + 1152, :]
        sums.append(jnp.dot(lhs, rhs, preferred_element_type=F32))
    return sums


def margin_lines(lines_ref, taps_ref):
    sums = []
    none = jnp.zeros((16, 384), BF16)
    for side, ey in ((0, 0), (1, 2)):
        lines = lines_ref[side]
        lhs = jnp.concatenate(
            [
                jnp.concatenate([none, lines[:240]]),
                lines,
                jnp.concatenate([lines[16:], none]),
            ],
            axis=1,
        )
        rhs = tap_rows(taps_ref, [(ex, ey, ez) for ex in range(3) for ez in range(3)])
        sums.append(jnp.dot(lhs, rhs, preferred_element_type=F32))
    return sums


def margin_ends(face, ez, taps_ref):
    line = lax.broadcasted_iota(jnp.int32, face.shape, 0) % 16
    shifted = [
        jnp.where(line == 0, 0.0, pltpu.roll(face, 1, 0)),
        face,
        jnp.where(line == 15, 0.0, pltpu.roll(face, 255, 0)),
    ]
    border = jnp.zeros((16, 128), F32)
    lhs = []
    for ex in range(3):
        for part in shifted:
            if ex == 0:
                part = jnp.concatenate([border, part[:240]])
            elif ex == 2:
                part = jnp.concatenate([part[16:], border])
            lhs.append(part.astype(BF16))
    rhs = tap_rows(taps_ref, [(ex, ey, ez) for ex in range(3) for ey in range(3)])
    return jnp.dot(jnp.concatenate(lhs, axis=1), rhs, preferred_element_type=F32)


Z_FACES = ((DIRECTIONS.index((0, 0, -1)), 0), (DIRECTIONS.index((0, 0, 1)), 2))


def joined_face(own_ref, other_ref, block):
    own = own_ref[block].astype(F32)
    other = other_ref[block].astype(F32)
    return jnp.concatenate(
        [
            jnp.where(low_lanes(own), own, swap_halves(other)),
            jnp.where(low_lanes(own), swap_halves(own), other),
        ]
    )


def add_margin(planes_ref, lines_ref, near_ref, own_ref, other_ref, taps_ref, pre_ref):
    for side, added in enumerate(margin_planes(planes_ref, taps_ref)):
        at = side * 15 * 256
        pre_ref[at : at + 256, :] += added
    for side, added in enumerate(margin_lines(lines_ref, taps_ref)):
        for x in range(16):
            at = x * 256 + side * 240
            pre_ref[at : at + 16, :] += added[x * 16 : x * 16 + 16]
    for k, ez in Z_FACES:
        block = near_ref[0, k]

        @pl.when(block >= 0)
        def _(block=block, ez=ez):
            added = margin_ends(joined_face(own_ref, other_ref, block), ez, taps_ref)
            rows = pl.ds(0 if ez == 0 else 15, 256, stride=16)
            pre_ref[rows, :] = pre_ref[rows, :] + added


def put_own_margin(planes_ref, lines_ref, near_ref, own_ref, other_ref, lanes_ref):
    for side in range(2):
        plane = side * 17
        lanes_ref[plane, :, 0:128], lanes_ref[plane, :, 128:256] = own_lanes(planes_ref[side])
        both, above = own_lanes(lines_ref[side])
        rows = slice(side * 272, side * 272 + 16)
        for x in range(16):
            lanes_ref[x + 1, rows, 0:128] = both[x * 16 : x * 16 + 16]
            lanes_ref[x + 1, rows, 128:256] = above[x * 16 : x * 16 + 16]
    for k, ez in Z_FACES:
        block = near_ref[0, k]

        @pl.when(block >= 0)
        def _(block=block, ez=ez):
            face = joined_face(own_ref, other_ref, block)
            lanes = slice(ez * 64, ez * 64 + 128)
            for x in range(16):
                old = lanes_ref[x + 1, 16:272, lanes].astype(F32).reshape(16, 16, 128)
                level = lax.broadcasted_iota(jnp.int32, old.shape, 1)
                lane = lax.broadcasted_iota(jnp.int32, old.shape, 2)
                here = (level == (0 if ez == 0 else 15)) & (lane < 64)
                new = jnp.where(here, face[x * 16 : x * 16 + 16].reshape(16, 1, 128), old)
                lanes_ref[x + 1, 16:272, lanes] = new.reshape(256, 128).astype(BF16)


def forward(
    near_ref, core_ref, at_ref, own_ref, other_ref, taps_ref, inner_ref,
    slope_hbm, lanes_hbm, down_hbm, cot_hbm,
    slots_hbm, faces_ref, coarse_hbm, grad_pre_hbm,
    planes_ref, lines_ref, pre_ref, grad_ref, turned_ref, slope_ref, lanes_ref,
    down_ref, cot_ref, coarse_ref, grad_pre_ref, slots_ref, arrived, left, left_slots
):
    came = start_all(
        [
            (lanes_hbm, lanes_ref),
            (slope_hbm, slope_ref),
            (down_hbm, down_ref),
            (cot_hbm, cot_ref),
        ],
        arrived,
    )
    pre_ref[...] = inner_ref[...]
    planes_ref[...] = jnp.zeros(planes_ref.shape, BF16)
    lines_ref[...] = jnp.zeros(lines_ref.shape, BF16)
    margin = Margin(planes_ref, lines_ref)
    fill_margin(margin, near_ref, own_ref, other_ref, z_faces=False)
    add_margin(planes_ref, lines_ref, near_ref, own_ref, other_ref, taps_ref, pre_ref)
    came[0].wait()
    put_own_margin(planes_ref, lines_ref, near_ref, own_ref, other_ref, lanes_ref)
    for copy in came[1:]:
        copy.wait()

    turned_ref[:, 0:512] = jnp.zeros((128, 512), BF16)
    turned_ref[:, 4608:5120] = jnp.zeros((128, 512), BF16)
    for x in range(16):
        rows = slice(x * 256, x * 256 + 256)
        pre = pre_ref[rows, :]
        sigmoid = 0.5 + 0.5 * jnp.tanh(0.5 * pre)
        pre_ref[rows, :] = jnp.where(pre > 0.5 * INACTIVE, pre * sigmoid, 0.0)
        grad = slope_ref[rows, :] * sigmoid * (1.0 + pre * (1.0 - sigmoid))
        grad_ref[rows, :] = grad
        grad = grad.astype(BF16)
        grad_pre_ref[rows, :] = grad
        turned_ref[:, 512 + x * 256 : 768 + x * 256] = grad.T

    gone = [
        pltpu.make_async_copy(grad_pre_ref, grad_pre_hbm, left.at[0]),
        pltpu.make_async_copy(coarse_ref, coarse_hbm, left.at[1]),
    ]
    gone[0].start()
    share = slots_ref.shape[1] - EDGE
    def put_terms(at, rows):
        while rows.shape[0]:
            owner, row = at // share, at % share
            count = min(rows.shape[0], share - row)
            slots_ref[owner, row : row + count, :] = rows[:count]
            rows = rows[count:]
            at += count

    leaving = [pltpu.make_async_copy(slots_ref, slots_hbm, left_slots.at[0])]

    patches = []
    for tap in range(8):
        tx, ty, tz = tap // 4, tap // 2 % 2, tap % 2
        pieces = []
        for ux in range(8):
            for uy in range(8):
                at = (2 * ux + tx) * 256 + (2 * uy + ty) * 16 + tz
                pieces.append(pre_ref[pl.ds(at, 8, stride=2), :])
        patches.append(jnp.concatenate(pieces).astype(BF16))
    patches = jnp.concatenate(patches, axis=1)
    coarse = jnp.dot(patches, down_ref[...], preferred_element_type=F32)
    coarse_ref[...] = coarse[:, :128].astype(BF16)
    gone[1].start()
    grad_down = jnp.dot(cot_ref[...], patches, preferred_element_type=F32).astype(BF16)
    for tap in range(8):
        put_terms(tap * 128, grad_down[:, tap * 128 : tap * 128 + 128].T)
    lhs = jnp.concatenate(
        [turned_ref[:, (2 - ex) * 256 : (2 - ex) * 256 + 4608] for ex in range(3)]
    )
    for ey in range(3):
        rhs = lanes_ref[:, ey * 16 : ey * 16 + 256, :].reshape(4608, 256)
        summed = jnp.dot(lhs, rhs, preferred_element_type=F32)
        for ex in range(3):
            part = summed[ex * 128 : ex * 128 + 128].astype(BF16).T
            put_terms(1024 + (ey * 3 + ex) * 192, part[0:192])
    fill_edges(grad_ref, near_ref, slots_ref, share)
    for copy in leaving:
        copy.start()
    fill_faces(grad_ref, near_ref, (core_ref[0], at_ref[0]), faces_ref)
    for copy in gone + leaving:
        copy.wait()


def fetch(taps_hbm, inner_hbm, taps_ref, inner_ref, arrived):
    for copy in start_all([(taps_hbm, taps_ref), (inner_hbm, inner_ref)], arrived):
        copy.wait()


def total(slots_ref, out_ref):
    devices, share, _ = out_ref.shape
    summed = slots_ref[0, 0:share, :].astype(F32)
    for device in range(1, devices):
        summed = summed + slots_ref[device, 0:share, :].astype(F32)
    summed = (summed / devices).astype(BF16)
    for device in range(devices):
        out_ref[device] = summed


def backward(
    near_ref, core_ref, at_ref, own_ref, other_ref, own_faces_ref, other_faces_ref,
    grad_pre_hbm, active_hbm, conv_hbm, out_ref,
    padded_ref, grad_pre_ref, active_ref, conv_ref, back_ref, arrived
):
    came = start_all(
        [(conv_hbm, conv_ref), (grad_pre_hbm, grad_pre_ref), (active_hbm, active_ref)], arrived
    )
    came[0].wait()
    backward_weights(core_ref[0] * 64, conv_ref, back_ref)
    clear_margin(padded_ref)
    came[1].wait()
    for x in range(16):
        rows = grad_pre_ref[x * 256 : x * 256 + 256, :].astype(F32)
        put_lines(Whole(padded_ref), [(x + 1, 16, 256)], rows)
    fill_margin(
        Whole(padded_ref), near_ref, own_ref, other_ref, own_ref.shape[1] - EDGE,
        ((core_ref[0], at_ref[0]), own_faces_ref, other_faces_ref),
    )
    came[2].wait()
    for half in range(2):
        lhs = []
        for quad in range(2):
            pieces = []
            for p in range(6):
                for ey in range(3):
                    pieces.append(
                        padded_ref[half * 8 + quad * 4 + p, ey * 16 : ey * 16 + 256, :]
                    )
            lhs.append(jnp.concatenate(pieces, axis=1))
        summed = jnp.dot(jnp.concatenate(lhs), back_ref[...], preferred_element_type=F32)
        for quad in range(2):
            for two in range(2):
                part = summed[quad * 256 : quad * 256 + 256, two * 128 : two * 128 + 128]
                x = half * 8 + quad * 4 + two * 2
                even = active_ref[x * 256 : x * 256 + 256, :].astype(F32)
                odd = active_ref[x * 256 + 256 : x * 256 + 512, :].astype(F32)
                part = part * jnp.where(low_lanes(part), even, odd)
                for oy in range(2):
                    rows = [
                        part[(8 * oy + vy) * 16 + 8 * oz : (8 * oy + vy) * 16 + 8 * oz + 8]
                        for oz in range(2)
                        for vy in range(8)
                    ]
                    turned = jnp.concatenate(rows).T
                    first, second = turned[:64], turned[64:]
                    lanes = slice(x % 8 * 64, x % 8 * 64 + 128)
                    brick = half + 2 * oy
                    near = jnp.where(low_lanes(first), first, swap_halves(second))
                    far = jnp.where(low_lanes(first), swap_halves(first), second)
                    out_ref[brick, :, lanes] = near.astype(BF16)
                    out_ref[brick + 4, :, lanes] = far.astype(BF16)


def finish(core_ref, sums_ref, conv_ref, down_ref):
    shift = core_ref[0] * 64
    for tap in range(27):
        ex, ey, ez = tap // 9, tap // 3 % 3, tap % 3
        at = 1024 + ((ey * 3 + ex) * 3 + ez) * 64
        rows = sums_ref[at : at + 64, :].astype(F32)
        conv_ref[tap] = pltpu.roll(rows, shift, 1)
    for tap in range(8):
        rows = sums_ref[tap * 128 : tap * 128 + 128, :].astype(F32)
        down_ref[tap, pl.ds(shift, 64), :] = rows[:64]
        down_ref[tap, pl.ds(64 - shift, 64), :] = rows[64:]


def over_space(block, distance):
    blocks = range(lax.axis_size("space"))
    route = [(2 * i, 2 * (i + distance)) for i in blocks if i + distance in blocks]
    route += [(2 * i + 1, 2 * (i - distance) + 1) for i in blocks if i - distance in blocks]
    return lax.ppermute(block, ("space", "chan"), route)


def over_chan(block):
    return lax.ppermute(block, "chan", [(0, 1), (1, 0)])


def to_all(slots):
    return lax.all_to_all(slots, "space", 0, 0, tiled=True)


def local(features, heights, neighbours, w_conv, w_down, cotangent):
    devices = lax.axis_size("space")
    member = lax.axis_index("chan")

    def out(*shape, dtype=BF16):
        return jax.ShapeDtypeStruct(shape, dtype)

    def held_out(*shape, dtype=BF16):
        return pltpu.HBM(shape, dtype)

    def memory(*shape, dtype=BF16):
        return pltpu.VMEM(shape, dtype)

    def copies(count):
        return pltpu.SemaphoreType.DMA((count,))

    core = member.reshape(1)
    place = (core, lax.axis_index("space").reshape(1))
    turned = features.transpose(0, 2, 1)
    slots = kernel_call(
        send_features,
        held_out(devices, 128, 128),
        [hbm()] * 3,
        hbm(),
        [
            pltpu.SMEM(neighbours.shape, jnp.int32),
            memory(8, 64, dtype=jnp.int32),
            memory(8, 64, 512),
            memory(2048, 128, dtype=F32),
            memory(devices, 128, 128),
            copies(10),
            copies(26),
        ],
    )(neighbours, heights, turned)
    slots, turned_after = lax.optimization_barrier((slots, turned))
    came = to_all(slots)
    other_turned = over_chan(turned_after)

    held = [
        held_out(18, 288, 256),
        held_out(4096, 128),
        held_out(4096, 128, dtype=F32),
        held_out(4096, 128, dtype=F32),
        held_out(3456, 128),
        held_out(1024, 256),
        held_out(128, 512),
    ]
    lanes, active, slope, inner, taps, down, cot = kernel_call(
        prepare,
        held,
        [smem()] + [hbm()] * 5 + [pl.BlockSpec(memory_space=pl.ANY)],
        [hbm()] * 7,
        [
            memory(27, 128, 128),
            memory(8, 128, 256),
            memory(512, 256),
            memory(8, 64, dtype=jnp.int32),
            memory(8, 64, 512),
            memory(8, 64, 512),
            memory(4608, 256),
            memory(1024, 256),
            memory(512, 256),
            memory(128, 512),
            memory(18, 288, 384),
            memory(4096, 128, dtype=F32),
            memory(4096, 128, dtype=F32),
            memory(18, 288, 256),
            memory(4096, 128),
            memory(4096, 128, dtype=F32),
            memory(4096, 128, dtype=F32),
            copies(6),
            copies(6),
            copies(4),
        ],
        flops=5 << 30,
        mib=36,
    )(core, w_conv, w_down, cotangent[0], heights, turned, other_turned)
    came, taps, inner = lax.optimization_barrier((came, taps, inner))
    came_other = over_chan(came)
    taps, inner = kernel_call(
        fetch,
        [out(3456, 128), out(4096, 128, dtype=F32)],
        [hbm()] * 2,
        [vmem()] * 2,
        [copies(2)],
    )(taps, inner)

    share = -(-2752 // (devices * 16)) * 16
    terms, faces, coarse, grad_pre = kernel_call(
        forward,
        [
            held_out(devices, share + EDGE, 128),
            out(4, 256, 128),
            held_out(512, 128),
            held_out(4096, 128),
        ],
        [smem()] * 3 + [vmem()] * 4 + [hbm()] * 4,
        [hbm(), vmem(), hbm(), hbm()],
        [
            memory(2, 288, 384),
            memory(2, 256, 384),
            memory(4096, 128, dtype=F32),
            memory(4096, 128, dtype=F32),
            memory(128, 5120),
            memory(4096, 128, dtype=F32),
            memory(18, 288, 256),
            memory(1024, 256),
            memory(128, 512),
            memory(512, 128),
            memory(4096, 128),
            memory(devices, share + EDGE, 128),
            copies(4),
            copies(2),
            copies(1),
        ],
        flops=5 << 30,
        mib=24,
    )(
        neighbours, *place, came, came_other, taps, inner, slope, lanes, down, cot
    )

    arrived = to_all(terms)
    came_faces = [over_space(faces[i], i + 1) for i in range(4)]
    arrived, *came_faces = lax.optimization_barrier((arrived, *came_faces))
    came_faces = jnp.stack(came_faces)
    other_faces = over_chan(came_faces)
    sums = to_all(
        kernel_call(total, out(devices, share, 128), [vmem()], vmem())(arrived)
    )
    arrived_other = over_chan(arrived[:, share:])
    grad_features = kernel_call(
        backward,
        out(8, 64, 512),
        [smem()] * 3 + [vmem()] * 4 + [hbm()] * 3,
        vmem(),
        [
            memory(18, 288, 384),
            memory(4096, 128),
            memory(4096, 128),
            memory(27, 128, 128),
            memory(6912, 256),
            copies(3),
        ],
        flops=5 << 30,
        mib=24,
    )(
        neighbours, *place, arrived, arrived_other, came_faces, other_faces, grad_pre, active,
        w_conv,
    )

    grad_conv, grad_down = kernel_call(
        finish,
        [out(27, 64, 128, dtype=F32), out(8, 128, 128, dtype=F32)],
        [smem(), vmem()],
        [vmem()] * 2,
    )(core, sums.reshape(-1, 128))
    return coarse[None], grad_conv, grad_down, grad_features.transpose(0, 2, 1)


def solution(mesh):
    placed = (
        P("space", None, "chan"),
        P("space", None),
        P("space", None),
        P(),
        P(),
        P("space", None, None),
    )
    return jax.shard_map(
        local,
        mesh=mesh,
        in_specs=placed,
        out_specs=(
            P("space", None, "chan"),
            P(None, "chan", None),
            P(None, None, "chan"),
            P("space", None, "chan"),
        ),
        check_vma=False,
    )
```

```python
import jax
import jax.numpy as jnp
from jax import lax
from jax.experimental import pallas as pl
from jax.experimental.pallas import tpu as pltpu
from jax.sharding import PartitionSpec as P

OFFSETS = [
    (along_x, along_y, along_z)
    for along_x in (-1, 0, 1)
    for along_y in (-1, 0, 1)
    for along_z in (-1, 0, 1)
]
DIRECTIONS = [offset for offset in OFFSETS if offset != (0, 0, 0)]
FILL_ORDER = sorted(range(26), key=lambda k: (abs(DIRECTIONS[k][2]), k))
INACTIVE = -1e30
EDGE = 8
INNER = 4
F32 = jnp.float32
BF16 = jnp.bfloat16


def vmem():
    return pl.BlockSpec(memory_space=pltpu.VMEM)


def smem():
    return pl.BlockSpec(memory_space=pltpu.SMEM)


def hbm():
    return pl.BlockSpec(memory_space=pltpu.HBM)


def kernel_call(body, outs, specs, out_specs, scratch=(), flops=0, mib=16):
    call = pl.pallas_call(
        body,
        out_shape=outs,
        in_specs=specs,
        out_specs=out_specs,
        scratch_shapes=list(scratch),
        compiler_params=pltpu.CompilerParams(vmem_limit_bytes=mib * 1024 * 1024),
        cost_estimate=pl.CostEstimate(flops=flops, bytes_accessed=1 << 22, transcendentals=0),
    )

    def run(*operands):
        placed = []
        for spec, operand in zip(specs, operands):
            if spec.memory_space == pltpu.HBM:
                operand = pltpu.with_memory_space_constraint(operand, pltpu.HBM)
            placed.append(operand)
        return call(*placed)

    return run


def start_all(pairs, arrived):
    copies = [
        pltpu.make_async_copy(source, target, arrived.at[i])
        for i, (source, target) in enumerate(pairs)
    ]
    for copy in copies:
        copy.start()
    return copies


def swap_halves(rows):
    return pltpu.roll(rows, 64, 1)


def low_lanes(rows):
    return lax.broadcasted_iota(jnp.int32, rows.shape, 1) < 64


def filled_voxels(heights_ref):
    columns = lax.broadcasted_iota(jnp.int32, (64, 512), 0)
    voxels = lax.broadcasted_iota(jnp.int32, (64, 512), 1)
    spread = (voxels // 8 == columns).astype(F32)
    tall = jnp.dot(heights_ref[...].astype(F32), spread, preferred_element_type=F32)
    level = lax.broadcasted_iota(jnp.int32, tall.shape, 1) % 8
    return (level.astype(F32) < tall).astype(F32)


def slot_of(slots_ref, block):
    return block % INNER * (slots_ref.shape[0] // INNER) + block // INNER


def fill_slots(rows_ref, near_ref, slots_ref, slots_hbm, left):
    def leave(k):
        slot = slot_of(slots_ref, near_ref[0, k])
        rows = slice(0, 128 if DIRECTIONS[k].count(0) == 2 else 16)
        return pltpu.make_async_copy(
            slots_ref.at[slot, rows], slots_hbm.at[slot, rows], left.at[k]
        )

    for k, (dx, dy, dz) in enumerate(DIRECTIONS):
        block = near_ref[0, k]
        xh = 7 if dx == 1 else 0
        y = 15 if dy == 1 else 0
        z = 15 if dz == 1 else 0

        @pl.when(block >= 0)
        def _(k=k, dx=dx, dy=dy, dz=dz, xh=xh, y=y, z=z, block=block):
            zeros = [d == 0 for d in (dx, dy, dz)]
            if zeros == [False, True, True]:
                plane = rows_ref[xh * 256 : xh * 256 + 256, :]
                first, second = plane[:128], plane[128:]
                if dx == -1:
                    second = swap_halves(second)
                else:
                    first = swap_halves(first)
                region = jnp.where(low_lanes(first), first, second)
            elif zeros == [True, False, True]:
                region = jnp.concatenate(
                    [rows_ref[x * 256 + y * 16 : x * 256 + y * 16 + 16, :] for x in range(8)]
                )
            elif zeros == [True, True, False]:
                region = rows_ref[pl.ds(z, 128, stride=16), :]
            elif zeros == [False, False, True]:
                region = rows_ref[xh * 256 + y * 16 : xh * 256 + y * 16 + 16, :]
            elif zeros == [False, True, False]:
                region = rows_ref[pl.ds(xh * 256 + z, 16, stride=16), :]
            elif zeros == [True, False, False]:
                line = rows_ref[pl.ds(y * 16 + z, 8, stride=256), :]
                region = jnp.concatenate([line, line])
            else:
                at = xh * 256 + y * 16 + z
                region = jnp.broadcast_to(rows_ref[at : at + 1, :], (16, 128))
            slots_ref[slot_of(slots_ref, block), 0 : region.shape[0], :] = region.astype(BF16)
            leave(k).start()

    for k in range(26):

        @pl.when(near_ref[0, k] >= 0)
        def _(k=k):
            leave(k).wait()


def fill_edges(rows_ref, near_ref, slots_ref, start):
    for k, (dx, dy, dz) in enumerate(DIRECTIONS):
        if (dx, dy, dz).count(0) == 2:
            continue
        block = near_ref[0, k]
        x, y, z = (15 if d == 1 else 0 for d in (dx, dy, dz))

        @pl.when(block >= 0)
        def _(dx=dx, dy=dy, dz=dz, x=x, y=y, z=z, block=block):
            if dx == 0:
                rows = rows_ref[pl.ds(y * 16 + z, 16, stride=256), :]
            elif dz == 0:
                rows = rows_ref[x * 256 + y * 16 : x * 256 + y * 16 + 16, :]
            elif dy == 0:
                rows = rows_ref[pl.ds(x * 256 + z, 16, stride=16), :]
            else:
                at = x * 256 + y * 16 + z
                rows = jnp.broadcast_to(rows_ref[at : at + 1, :], (16, 128))
            low, high = rows[:EDGE], swap_halves(rows[EDGE:])
            rows = jnp.where(low_lanes(low), low, high)
            slots_ref[slot_of(slots_ref, block), start : start + EDGE, :] = rows.astype(BF16)


def fill_faces(rows_ref, near_ref, place, faces_ref):
    member, own = place
    for k, (dx, dy, dz) in enumerate(DIRECTIONS):
        if (dx, dy, dz).count(0) != 2:
            continue
        block = near_ref[0, k]
        distance = jnp.where(member == 0, block - own, own - block)
        end = 15 if dx + dy + dz == 1 else 0

        @pl.when((block >= 0) & (distance >= 1))
        def _(dx=dx, dy=dy, end=end, distance=distance):
            if dx:
                region = rows_ref[end * 256 : end * 256 + 256, :]
            elif dy:
                region = jnp.concatenate(
                    [rows_ref[x * 256 + end * 16 : x * 256 + end * 16 + 16, :] for x in range(16)]
                )
            else:
                region = rows_ref[pl.ds(end, 256, stride=16), :]
            faces_ref[distance - 1] = region.astype(BF16)


class Whole:
    def __init__(self, ref):
        self.ref = ref

    def at(self, x, row, height):
        return self.ref, x, row


class Margin:
    def __init__(self, planes_ref, lines_ref):
        self.planes_ref, self.lines_ref = planes_ref, lines_ref

    def at(self, x, row, height):
        if x in (0, 17):
            return self.planes_ref, x // 17, row
        return self.lines_ref, row // 272, (x - 1) * 16


def put_lines(padded, places, rows):
    count = rows.shape[0]
    level = lax.broadcasted_iota(jnp.int32, rows.shape, 0) % 16
    below = jnp.where(level == 0, 0.0, pltpu.roll(rows, 1, 0)).astype(BF16)
    above = jnp.where(level == 15, 0.0, pltpu.roll(rows, count - 1, 0)).astype(BF16)
    here = rows.astype(BF16)
    at = 0
    for x, row, height in places:
        ref, plane, first = padded.at(x, row, height)
        for j, part in enumerate((below, here, above)):
            ref[plane, first : first + height, j * 128 : j * 128 + 128] = part[at : at + height]
        at += height


def put_ends(padded, x, row, rows, dz):
    lines = rows.shape[0]
    j = 0 if dz == -1 else 2
    end = 0 if dz == -1 else 15
    lanes = slice(j * 128, j * 128 + 128)
    ref, plane, first = padded.at(x, row, 16 * lines)
    span = slice(first, first + 16 * lines)
    old = ref[plane, span, lanes].astype(F32).reshape(lines, 16, 128)
    level = lax.broadcasted_iota(jnp.int32, old.shape, 1)
    new = jnp.where(level == end, rows.reshape(lines, 1, 128), old)
    ref[plane, span, lanes] = new.reshape(16 * lines, 128).astype(BF16)


def clear_margin(padded_ref):
    empty = jnp.zeros((288, 384), BF16)
    padded_ref[0] = empty
    padded_ref[17] = empty
    line = jnp.zeros((16, 384), BF16)
    for x in range(1, 17):
        padded_ref[x, 0:16, :] = line
        padded_ref[x, 272:288, :] = line


def put_region(padded, offset, rows):
    dx, dy, dz = offset
    zeros = [d == 0 for d in offset]
    x = 17 if dx == 1 else 0
    y = 17 if dy == 1 else 0
    if zeros == [False, True, True]:
        put_lines(padded, [(x, 16, 256)], rows)
    elif zeros == [True, False, True]:
        put_lines(padded, [(at + 1, y * 16, 16) for at in range(16)], rows)
    elif zeros == [False, False, True]:
        put_lines(padded, [(x, y * 16, 16)], rows)
    elif zeros == [True, True, False]:
        for at in range(16):
            put_ends(padded, at + 1, 16, rows[at * 16 : at * 16 + 16], dz)
    elif zeros == [False, True, False]:
        put_ends(padded, x, 16, rows, dz)
    elif zeros == [True, False, False]:
        for at in range(16):
            put_ends(padded, at + 1, y * 16, rows[at : at + 1], dz)
    else:
        put_ends(padded, x, y * 16, rows[0:1], dz)


def face_source(place, block):
    away = place[1] - block
    return jnp.where(away > 0, 0, 1) == place[0], jnp.clip(jnp.abs(away) - 1, 0, 3)


def fill_margin(padded, near_ref, own_ref, other_ref, start=0, faces=None, z_faces=True):
    for k in FILL_ORDER:
        offset = DIRECTIONS[k]
        block = near_ref[0, k]
        face = offset.count(0) == 2
        if face and offset[2] and not z_faces:
            continue
        if face and faces is not None:
            place, own_faces_ref, other_faces_ref = faces
            here, slot = face_source(place, block)

            @pl.when((block >= 0) & here)
            def _(offset=offset, slot=slot):
                put_region(padded, offset, own_faces_ref[slot].astype(F32))

            @pl.when((block >= 0) & jnp.logical_not(here))
            def _(offset=offset, slot=slot):
                rows = swap_halves(other_faces_ref[slot].astype(F32))
                put_region(padded, offset, rows)

            continue

        @pl.when(block >= 0)
        def _(offset=offset, block=block, face=face):
            height = 128 if face else 16 if start == 0 else EDGE
            slot = slot_of(own_ref, block)
            own = own_ref[slot, start : start + height, :].astype(F32)
            other = other_ref[slot, 0:height, :].astype(F32)
            first = jnp.where(low_lanes(own), own, swap_halves(other))
            second = jnp.where(low_lanes(own), swap_halves(own), other)
            if face or start:
                rows = jnp.concatenate([first, second])
            elif offset[0] == 0:
                rows = jnp.concatenate([first[:8], second[:8]])
            else:
                rows = first if offset[0] == 1 else second
            put_region(padded, offset, rows)


def send_features(
    near_hbm, heights_hbm, features_hbm, slots_hbm,
    near_ref, heights_ref, features_ref, rows_ref, slots_ref, arrived, left
):
    copies = [
        pltpu.make_async_copy(near_hbm, near_ref, arrived.at[8]),
        pltpu.make_async_copy(heights_hbm, heights_ref, arrived.at[9]),
    ]
    order = (0, 1, 2, 3, 4, 5, 6, 7)
    bricks = [
        pltpu.make_async_copy(features_hbm.at[i], features_ref.at[i], arrived.at[i]) for i in order
    ]
    for copy in copies + bricks:
        copy.start()
    copies[1].wait()
    filled = filled_voxels(heights_ref).astype(BF16)
    for oz in range(2):
        for oy in range(2):
            pair = []
            for ox in range(2):
                brick = ox + 2 * oy + 4 * oz
                bricks[brick].wait()
                pair.append(features_ref[brick] * filled[brick : brick + 1])
            turned = jnp.concatenate(pair).T.astype(F32)
            for vx in range(8):
                for vy in range(8):
                    at = vx * 256 + (8 * oy + vy) * 16 + 8 * oz
                    source = (vx * 8 + vy) * 8
                    rows_ref[at : at + 8, :] = turned[source : source + 8]
    copies[0].wait()
    fill_slots(rows_ref, near_ref, slots_ref, slots_hbm, left)


def own_first_taps(shift, conv_ref, yz):
    taps = []
    for ex in range(3):
        tap = conv_ref[ex * 9 + yz].astype(F32)
        taps.append(pltpu.roll(pltpu.roll(tap, shift, 0), shift, 1))
    return taps


def forward_weights(shift, conv_ref, down_in_ref, cot_in_ref, two_ref, down_ref, cot_ref):
    empty = jnp.zeros((128, 128), BF16)
    for yz in range(9):
        taps = own_first_taps(shift, conv_ref, yz)
        whole = [empty] + [tap.astype(BF16) for tap in taps] + [empty]
        for p in range(4):
            rows = slice((p * 9 + yz) * 128, (p * 9 + yz) * 128 + 128)
            two_ref[rows, 0:128] = whole[p + 1] if p < 3 else empty
            two_ref[rows, 128:256] = whole[p]
    for tap in range(8):
        rows = down_in_ref[tap].astype(F32)
        rows = pltpu.roll(rows, shift, 0)
        down_ref[tap * 128 : tap * 128 + 128, :] = pltpu.roll(rows, 2 * shift, 1).astype(BF16)
    cot_ref[...] = pltpu.roll(cot_in_ref[...].astype(F32), 2 * shift, 1).astype(BF16)


def backward_weights(shift, conv_ref, four_ref):
    empty = jnp.zeros((128, 128), BF16)
    none = jnp.zeros((64, 128), F32)
    for yz in range(9):
        taps = own_first_taps(shift, conv_ref, yz)
        own = [none] + [taps[2 - ex][:64] for ex in range(3)] + [none]
        pairs = [jnp.concatenate([own[i + 1], own[i]]).T.astype(BF16) for i in range(4)]
        for p in range(6):
            at = (p * 9 + 8 - yz) * 128
            four_ref[at : at + 128, 0:128] = pairs[p] if p < 4 else empty
            four_ref[at : at + 128, 128:256] = pairs[p - 2] if p >= 2 else empty


def own_lanes(triple):
    below, here = triple[:, 0:128].astype(F32), triple[:, 128:256].astype(F32)
    both = jnp.where(low_lanes(below), below, swap_halves(here)).astype(BF16)
    return both, triple[:, 256:384]


def prepare(
    core_ref, conv_hbm, down_hbm, cot_hbm, heights_hbm, own_hbm, other_hbm,
    lanes_hbm, active_hbm, slope_hbm, inner_hbm, taps_hbm, down_out_hbm, cot_out_hbm,
    conv_in_ref, down_in_ref, cot_in_ref, heights_ref, own_ref, other_ref,
    two_ref, down_ref, cot_ref, own_cot_ref, padded_ref, rows_ref, mask_ref, lanes_ref, active_ref,
    slope_ref, inner_ref, arrived, left, left_inner
):
    came = start_all(
        [
            (conv_hbm, conv_in_ref),
            (down_hbm, down_in_ref),
            (cot_hbm, cot_in_ref),
            (heights_hbm, heights_ref),
            (own_hbm, own_ref),
            (other_hbm, other_ref),
        ],
        arrived,
    )
    gone = [
        pltpu.make_async_copy(source, target, left.at[i])
        for i, (source, target) in enumerate(
            [
                (two_ref.at[0:3456, 0:128], taps_hbm),
                (down_ref, down_out_hbm),
                (own_cot_ref, cot_out_hbm),
                (lanes_ref, lanes_hbm),
                (active_ref, active_hbm),
                (slope_ref, slope_hbm),
            ]
        )
    ]
    for copy in came[:3]:
        copy.wait()
    forward_weights(
        core_ref[0] * 64, conv_in_ref, down_in_ref, cot_in_ref, two_ref, down_ref, cot_ref
    )
    own_cot_ref[...] = cot_ref[:, 0:128].T
    for copy in gone[:3]:
        copy.start()
    for copy in came[3:]:
        copy.wait()
    filled = filled_voxels(heights_ref)
    upright = filled.T
    for brick in range(8):
        ox, oy, oz = brick % 2, brick // 2 % 2, brick // 4
        both = jnp.concatenate([own_ref[brick].astype(F32), other_ref[brick].astype(F32)])
        turned = (both * filled[brick : brick + 1]).T
        mask = jnp.broadcast_to(upright[:, brick : brick + 1], (512, 128))
        for vx in range(8):
            for vy in range(8):
                at = (8 * ox + vx) * 256 + (8 * oy + vy) * 16 + 8 * oz
                source = (vx * 8 + vy) * 8
                rows_ref[at : at + 8, :] = turned[source : source + 8]
                mask_ref[at : at + 8, :] = mask[source : source + 8]
    clear_margin(padded_ref)
    for x in range(16):
        put_lines(Whole(padded_ref), [(x + 1, 16, 256)], rows_ref[x * 256 : x * 256 + 256, :])
        active_ref[x * 256 : x * 256 + 256, :] = mask_ref[x * 256 : x * 256 + 256, :].astype(BF16)
    for x in range(18):
        lanes_ref[x, :, 0:128], lanes_ref[x, :, 128:256] = own_lanes(padded_ref[x])
    gone[3].start()
    gone[4].start()
    for tap in range(8):
        tx, ty, tz = tap // 4, tap // 2 % 2, tap % 2
        part = lax.dot_general(
            cot_ref[...],
            down_ref[tap * 128 : tap * 128 + 128, :],
            (((1,), (1,)), ((), ())),
            preferred_element_type=F32,
        )
        for ux in range(8):
            for uy in range(8):
                at = (2 * ux + tx) * 256 + (2 * uy + ty) * 16 + tz
                source = (ux * 8 + uy) * 8
                rows = pl.ds(at, 8, stride=2)
                slope_ref[rows, :] = part[source : source + 8] * mask_ref[rows, :]
    gone[5].start()

    def leave(group):
        rows = pl.ds(pl.multiple_of(group * 1024, 1024), 1024)
        return pltpu.make_async_copy(
            inner_ref.at[rows], inner_hbm.at[rows], left_inner.at[group]
        )


    def step(group, carry):
        lhs = []
        for pair in range(2):
            pieces = []
            for p in range(4):
                for ey in range(3):
                    pieces.append(
                        padded_ref[group * 4 + pair * 2 + p, ey * 16 : ey * 16 + 256, :]
                    )
            lhs.append(jnp.concatenate(pieces, axis=1))
        summed = jnp.dot(jnp.concatenate(lhs), two_ref[...], preferred_element_type=F32)
        for pair in range(2):
            for phase in range(2):
                at = pl.multiple_of((group * 4 + pair * 2 + phase) * 256, 256)
                part = summed[pair * 256 : pair * 256 + 256, phase * 128 : phase * 128 + 128]
                rows = pl.ds(at, 256)
                inner_ref[rows, :] = jnp.where(mask_ref[rows, :] > 0, part, INACTIVE)
        leave(group).start()
        return carry

    lax.fori_loop(0, 4, step, 0)
    for copy in gone:
        copy.wait()
    for group in range(4):
        leave(group).wait()


def tap_rows(taps_ref, taps):
    starts = [((ex * 3 + ey) * 3 + ez) * 128 for ex, ey, ez in taps]
    return jnp.concatenate([taps_ref[at : at + 128, :] for at in starts])


def margin_planes(planes_ref, taps_ref):
    sums = []
    for side, ex in ((0, 0), (1, 2)):
        lhs = jnp.concatenate(
            [planes_ref[side, ey * 16 : ey * 16 + 256, :] for ey in range(3)], axis=1
        )
        rhs = taps_ref[ex * 1152 : ex * 1152 + 1152, :]
        sums.append(jnp.dot(lhs, rhs, preferred_element_type=F32))
    return sums


def margin_lines(lines_ref, taps_ref):
    sums = []
    none = jnp.zeros((16, 384), BF16)
    for side, ey in ((0, 0), (1, 2)):
        lines = lines_ref[side]
        lhs = jnp.concatenate(
            [
                jnp.concatenate([none, lines[:240]]),
                lines,
                jnp.concatenate([lines[16:], none]),
            ],
            axis=1,
        )
        rhs = tap_rows(taps_ref, [(ex, ey, ez) for ex in range(3) for ez in range(3)])
        sums.append(jnp.dot(lhs, rhs, preferred_element_type=F32))
    return sums


def margin_ends(face, ez, taps_ref):
    line = lax.broadcasted_iota(jnp.int32, face.shape, 0) % 16
    shifted = [
        jnp.where(line == 0, 0.0, pltpu.roll(face, 1, 0)),
        face,
        jnp.where(line == 15, 0.0, pltpu.roll(face, 255, 0)),
    ]
    border = jnp.zeros((16, 128), F32)
    lhs = []
    for ex in range(3):
        for part in shifted:
            if ex == 0:
                part = jnp.concatenate([border, part[:240]])
            elif ex == 2:
                part = jnp.concatenate([part[16:], border])
            lhs.append(part.astype(BF16))
    rhs = tap_rows(taps_ref, [(ex, ey, ez) for ex in range(3) for ey in range(3)])
    return jnp.dot(jnp.concatenate(lhs, axis=1), rhs, preferred_element_type=F32)


Z_FACES = ((DIRECTIONS.index((0, 0, -1)), 0), (DIRECTIONS.index((0, 0, 1)), 2))


def joined_face(own_ref, other_ref, block):
    slot = slot_of(own_ref, block)
    own = own_ref[slot].astype(F32)
    other = other_ref[slot].astype(F32)
    return jnp.concatenate(
        [
            jnp.where(low_lanes(own), own, swap_halves(other)),
            jnp.where(low_lanes(own), swap_halves(own), other),
        ]
    )


def add_margin(planes_ref, lines_ref, near_ref, own_ref, other_ref, taps_ref, pre_ref):
    for side, added in enumerate(margin_planes(planes_ref, taps_ref)):
        at = side * 15 * 256
        pre_ref[at : at + 256, :] += added
    for side, added in enumerate(margin_lines(lines_ref, taps_ref)):
        for x in range(16):
            at = x * 256 + side * 240
            pre_ref[at : at + 16, :] += added[x * 16 : x * 16 + 16]
    for k, ez in Z_FACES:
        block = near_ref[0, k]

        @pl.when(block >= 0)
        def _(block=block, ez=ez):
            added = margin_ends(joined_face(own_ref, other_ref, block), ez, taps_ref)
            rows = pl.ds(0 if ez == 0 else 15, 256, stride=16)
            pre_ref[rows, :] = pre_ref[rows, :] + added


def put_own_margin(planes_ref, lines_ref, near_ref, own_ref, other_ref, lanes_ref):
    for side in range(2):
        plane = side * 17
        lanes_ref[plane, :, 0:128], lanes_ref[plane, :, 128:256] = own_lanes(planes_ref[side])
        both, above = own_lanes(lines_ref[side])
        rows = slice(side * 272, side * 272 + 16)
        for x in range(16):
            lanes_ref[x + 1, rows, 0:128] = both[x * 16 : x * 16 + 16]
            lanes_ref[x + 1, rows, 128:256] = above[x * 16 : x * 16 + 16]
    for k, ez in Z_FACES:
        block = near_ref[0, k]

        @pl.when(block >= 0)
        def _(block=block, ez=ez):
            face = joined_face(own_ref, other_ref, block)
            lanes = slice(ez * 64, ez * 64 + 128)
            for x in range(16):
                old = lanes_ref[x + 1, 16:272, lanes].astype(F32).reshape(16, 16, 128)
                level = lax.broadcasted_iota(jnp.int32, old.shape, 1)
                lane = lax.broadcasted_iota(jnp.int32, old.shape, 2)
                here = (level == (0 if ez == 0 else 15)) & (lane < 64)
                new = jnp.where(here, face[x * 16 : x * 16 + 16].reshape(16, 1, 128), old)
                lanes_ref[x + 1, 16:272, lanes] = new.reshape(256, 128).astype(BF16)


def forward(
    near_ref, core_ref, at_ref, own_ref, other_ref, taps_ref, inner_ref,
    slope_hbm, lanes_hbm, down_hbm, cot_hbm,
    slots_hbm, faces_ref, coarse_hbm, grad_pre_hbm,
    planes_ref, lines_ref, pre_ref, grad_ref, turned_ref, slope_ref, lanes_ref,
    down_ref, cot_ref, coarse_ref, grad_pre_ref, slots_ref, arrived, left, left_slots
):
    came = start_all(
        [
            (lanes_hbm, lanes_ref),
            (slope_hbm, slope_ref),
            (down_hbm, down_ref),
            (cot_hbm, cot_ref),
        ],
        arrived,
    )
    pre_ref[...] = inner_ref[...]
    planes_ref[...] = jnp.zeros(planes_ref.shape, BF16)
    lines_ref[...] = jnp.zeros(lines_ref.shape, BF16)
    margin = Margin(planes_ref, lines_ref)
    fill_margin(margin, near_ref, own_ref, other_ref, z_faces=False)
    add_margin(planes_ref, lines_ref, near_ref, own_ref, other_ref, taps_ref, pre_ref)
    came[0].wait()
    put_own_margin(planes_ref, lines_ref, near_ref, own_ref, other_ref, lanes_ref)
    for copy in came[1:]:
        copy.wait()

    turned_ref[:, 0:512] = jnp.zeros((128, 512), BF16)
    turned_ref[:, 4608:5120] = jnp.zeros((128, 512), BF16)
    for x in range(16):
        rows = slice(x * 256, x * 256 + 256)
        pre = pre_ref[rows, :]
        sigmoid = 0.5 + 0.5 * jnp.tanh(0.5 * pre)
        pre_ref[rows, :] = jnp.where(pre > 0.5 * INACTIVE, pre * sigmoid, 0.0)
        grad = slope_ref[rows, :] * sigmoid * (1.0 + pre * (1.0 - sigmoid))
        grad_ref[rows, :] = grad
        grad = grad.astype(BF16)
        grad_pre_ref[rows, :] = grad
        turned_ref[:, 512 + x * 256 : 768 + x * 256] = grad.T

    gone = [
        pltpu.make_async_copy(grad_pre_ref, grad_pre_hbm, left.at[0]),
        pltpu.make_async_copy(coarse_ref, coarse_hbm, left.at[1]),
    ]
    gone[0].start()
    share = slots_ref.shape[1] - EDGE
    def put_terms(at, rows):
        while rows.shape[0]:
            owner, row = at // share, at % share
            count = min(rows.shape[0], share - row)
            slots_ref[owner, row : row + count, :] = rows[:count]
            rows = rows[count:]
            at += count

    leaving = [pltpu.make_async_copy(slots_ref, slots_hbm, left_slots.at[0])]

    patches = []
    for tap in range(8):
        tx, ty, tz = tap // 4, tap // 2 % 2, tap % 2
        pieces = []
        for ux in range(8):
            for uy in range(8):
                at = (2 * ux + tx) * 256 + (2 * uy + ty) * 16 + tz
                pieces.append(pre_ref[pl.ds(at, 8, stride=2), :])
        patches.append(jnp.concatenate(pieces).astype(BF16))
    patches = jnp.concatenate(patches, axis=1)
    coarse = jnp.dot(patches, down_ref[...], preferred_element_type=F32)
    coarse_ref[...] = coarse[:, :128].astype(BF16)
    gone[1].start()
    grad_down = jnp.dot(cot_ref[...], patches, preferred_element_type=F32).astype(BF16)
    for tap in range(8):
        put_terms(tap * 128, grad_down[:, tap * 128 : tap * 128 + 128].T)
    lhs = jnp.concatenate(
        [turned_ref[:, (2 - ex) * 256 : (2 - ex) * 256 + 4608] for ex in range(3)]
    )
    for ey in range(3):
        rhs = lanes_ref[:, ey * 16 : ey * 16 + 256, :].reshape(4608, 256)
        summed = jnp.dot(lhs, rhs, preferred_element_type=F32)
        for ex in range(3):
            part = summed[ex * 128 : ex * 128 + 128].astype(BF16).T
            put_terms(1024 + (ey * 3 + ex) * 192, part[0:192])
    fill_edges(grad_ref, near_ref, slots_ref, share)
    for copy in leaving:
        copy.start()
    fill_faces(grad_ref, near_ref, (core_ref[0], at_ref[0]), faces_ref)
    for copy in gone + leaving:
        copy.wait()


def fetch(taps_hbm, inner_hbm, taps_ref, inner_ref, arrived):
    for copy in start_all([(taps_hbm, taps_ref), (inner_hbm, inner_ref)], arrived):
        copy.wait()


def total(slots_ref, out_ref):
    devices, share, _ = out_ref.shape
    summed = slots_ref[0, 0:share, :].astype(F32)
    for device in range(1, devices):
        summed = summed + slots_ref[device, 0:share, :].astype(F32)
    summed = (summed / devices).astype(BF16)
    for device in range(devices):
        out_ref[device] = summed


def backward(
    near_ref, core_ref, at_ref, own_ref, other_ref, own_faces_ref, other_faces_ref,
    grad_pre_hbm, active_hbm, conv_hbm, out_ref,
    padded_ref, grad_pre_ref, active_ref, conv_ref, back_ref, arrived
):
    came = start_all(
        [(conv_hbm, conv_ref), (grad_pre_hbm, grad_pre_ref), (active_hbm, active_ref)], arrived
    )
    came[0].wait()
    backward_weights(core_ref[0] * 64, conv_ref, back_ref)
    clear_margin(padded_ref)
    came[1].wait()
    for x in range(16):
        rows = grad_pre_ref[x * 256 : x * 256 + 256, :].astype(F32)
        put_lines(Whole(padded_ref), [(x + 1, 16, 256)], rows)
    fill_margin(
        Whole(padded_ref), near_ref, own_ref, other_ref, own_ref.shape[1] - EDGE,
        ((core_ref[0], at_ref[0]), own_faces_ref, other_faces_ref),
    )
    came[2].wait()
    for half in range(2):
        lhs = []
        for quad in range(2):
            pieces = []
            for p in range(6):
                for ey in range(3):
                    pieces.append(
                        padded_ref[half * 8 + quad * 4 + p, ey * 16 : ey * 16 + 256, :]
                    )
            lhs.append(jnp.concatenate(pieces, axis=1))
        summed = jnp.dot(jnp.concatenate(lhs), back_ref[...], preferred_element_type=F32)
        for quad in range(2):
            for two in range(2):
                part = summed[quad * 256 : quad * 256 + 256, two * 128 : two * 128 + 128]
                x = half * 8 + quad * 4 + two * 2
                even = active_ref[x * 256 : x * 256 + 256, :].astype(F32)
                odd = active_ref[x * 256 + 256 : x * 256 + 512, :].astype(F32)
                part = part * jnp.where(low_lanes(part), even, odd)
                for oy in range(2):
                    rows = [
                        part[(8 * oy + vy) * 16 + 8 * oz : (8 * oy + vy) * 16 + 8 * oz + 8]
                        for oz in range(2)
                        for vy in range(8)
                    ]
                    turned = jnp.concatenate(rows).T
                    first, second = turned[:64], turned[64:]
                    lanes = slice(x % 8 * 64, x % 8 * 64 + 128)
                    brick = half + 2 * oy
                    near = jnp.where(low_lanes(first), first, swap_halves(second))
                    far = jnp.where(low_lanes(first), swap_halves(first), second)
                    out_ref[brick, :, lanes] = near.astype(BF16)
                    out_ref[brick + 4, :, lanes] = far.astype(BF16)


def finish(core_ref, sums_ref, conv_ref, down_ref):
    shift = core_ref[0] * 64
    for tap in range(27):
        ex, ey, ez = tap // 9, tap // 3 % 3, tap % 3
        at = 1024 + ((ey * 3 + ex) * 3 + ez) * 64
        rows = sums_ref[at : at + 64, :].astype(F32)
        conv_ref[tap] = pltpu.roll(rows, shift, 1)
    for tap in range(8):
        rows = sums_ref[tap * 128 : tap * 128 + 128, :].astype(F32)
        down_ref[tap, pl.ds(shift, 64), :] = rows[:64]
        down_ref[tap, pl.ds(64 - shift, 64), :] = rows[64:]


def over_space(block, distance):
    blocks = range(lax.axis_size("space"))
    route = [(2 * i, 2 * (i + distance)) for i in blocks if i + distance in blocks]
    route += [(2 * i + 1, 2 * (i - distance) + 1) for i in blocks if i - distance in blocks]
    return lax.ppermute(block, ("space", "chan"), route)


def over_chan(block):
    return lax.ppermute(block, "chan", [(0, 1), (1, 0)])


def to_all(slots):
    outer = lax.axis_size("space") // INNER
    order = [plane * INNER + j for j in range(INNER) for plane in range(outer)]
    return lax.all_to_all(slots, "space", 0, 0, axis_index_groups=[order], tiled=True)


def local(features, heights, neighbours, w_conv, w_down, cotangent):
    devices = lax.axis_size("space")
    member = lax.axis_index("chan")

    def out(*shape, dtype=BF16):
        return jax.ShapeDtypeStruct(shape, dtype)

    def held_out(*shape, dtype=BF16):
        return pltpu.HBM(shape, dtype)

    def memory(*shape, dtype=BF16):
        return pltpu.VMEM(shape, dtype)

    def copies(count):
        return pltpu.SemaphoreType.DMA((count,))

    core = member.reshape(1)
    place = (core, lax.axis_index("space").reshape(1))
    turned = features.transpose(0, 2, 1)
    slots = kernel_call(
        send_features,
        held_out(devices, 128, 128),
        [hbm()] * 3,
        hbm(),
        [
            pltpu.SMEM(neighbours.shape, jnp.int32),
            memory(8, 64, dtype=jnp.int32),
            memory(8, 64, 512),
            memory(2048, 128, dtype=F32),
            memory(devices, 128, 128),
            copies(10),
            copies(26),
        ],
    )(neighbours, heights, turned)
    slots, turned_after = lax.optimization_barrier((slots, turned))
    came = to_all(slots)
    other_turned = over_chan(turned_after)

    held = [
        held_out(18, 288, 256),
        held_out(4096, 128),
        held_out(4096, 128, dtype=F32),
        held_out(4096, 128, dtype=F32),
        held_out(3456, 128),
        held_out(1024, 256),
        held_out(128, 512),
    ]
    lanes, active, slope, inner, taps, down, cot = kernel_call(
        prepare,
        held,
        [smem()] + [hbm()] * 5 + [pl.BlockSpec(memory_space=pl.ANY)],
        [hbm()] * 7,
        [
            memory(27, 128, 128),
            memory(8, 128, 256),
            memory(512, 256),
            memory(8, 64, dtype=jnp.int32),
            memory(8, 64, 512),
            memory(8, 64, 512),
            memory(4608, 256),
            memory(1024, 256),
            memory(512, 256),
            memory(128, 512),
            memory(18, 288, 384),
            memory(4096, 128, dtype=F32),
            memory(4096, 128, dtype=F32),
            memory(18, 288, 256),
            memory(4096, 128),
            memory(4096, 128, dtype=F32),
            memory(4096, 128, dtype=F32),
            copies(6),
            copies(6),
            copies(4),
        ],
        flops=5 << 30,
        mib=36,
    )(core, w_conv, w_down, cotangent[0], heights, turned, other_turned)
    came, taps, inner = lax.optimization_barrier((came, taps, inner))
    came_other = over_chan(came)
    taps, inner = kernel_call(
        fetch,
        [out(3456, 128), out(4096, 128, dtype=F32)],
        [hbm()] * 2,
        [vmem()] * 2,
        [copies(2)],
    )(taps, inner)

    share = -(-2752 // (devices * 16)) * 16
    terms, faces, coarse, grad_pre = kernel_call(
        forward,
        [
            held_out(devices, share + EDGE, 128),
            out(4, 256, 128),
            held_out(512, 128),
            held_out(4096, 128),
        ],
        [smem()] * 3 + [vmem()] * 4 + [hbm()] * 4,
        [hbm(), vmem(), hbm(), hbm()],
        [
            memory(2, 288, 384),
            memory(2, 256, 384),
            memory(4096, 128, dtype=F32),
            memory(4096, 128, dtype=F32),
            memory(128, 5120),
            memory(4096, 128, dtype=F32),
            memory(18, 288, 256),
            memory(1024, 256),
            memory(128, 512),
            memory(512, 128),
            memory(4096, 128),
            memory(devices, share + EDGE, 128),
            copies(4),
            copies(2),
            copies(1),
        ],
        flops=5 << 30,
        mib=24,
    )(
        neighbours, *place, came, came_other, taps, inner, slope, lanes, down, cot
    )

    arrived = to_all(terms)
    came_faces = [over_space(faces[i], i + 1) for i in range(4)]
    arrived, *came_faces = lax.optimization_barrier((arrived, *came_faces))
    came_faces = jnp.stack(came_faces)
    other_faces = over_chan(came_faces)
    sums = to_all(
        kernel_call(total, out(devices, share, 128), [vmem()], vmem())(arrived)
    )
    arrived_other = over_chan(arrived[:, share:])
    grad_features = kernel_call(
        backward,
        out(8, 64, 512),
        [smem()] * 3 + [vmem()] * 4 + [hbm()] * 3,
        vmem(),
        [
            memory(18, 288, 384),
            memory(4096, 128),
            memory(4096, 128),
            memory(27, 128, 128),
            memory(6912, 256),
            copies(3),
        ],
        flops=5 << 30,
        mib=24,
    )(
        neighbours, *place, arrived, arrived_other, came_faces, other_faces, grad_pre, active,
        w_conv,
    )

    grad_conv, grad_down = kernel_call(
        finish,
        [out(27, 64, 128, dtype=F32), out(8, 128, 128, dtype=F32)],
        [smem(), vmem()],
        [vmem()] * 2,
    )(core, sums.reshape(-1, 128))
    return coarse[None], grad_conv, grad_down, grad_features.transpose(0, 2, 1)


def solution(mesh):
    placed = (
        P("space", None, "chan"),
        P("space", None),
        P("space", None),
        P(),
        P(),
        P("space", None, None),
    )
    return jax.shard_map(
        local,
        mesh=mesh,
        in_specs=placed,
        out_specs=(
            P("space", None, "chan"),
            P(None, "chan", None),
            P(None, None, "chan"),
            P("space", None, "chan"),
        ),
        check_vma=False,
    )
```

```python
import jax
import jax.numpy as jnp
from jax import lax
from jax.experimental import pallas as pl
from jax.experimental.pallas import tpu as pltpu
from jax.sharding import PartitionSpec as P

OFFSETS = [
    (along_x, along_y, along_z)
    for along_x in (-1, 0, 1)
    for along_y in (-1, 0, 1)
    for along_z in (-1, 0, 1)
]
DIRECTIONS = [offset for offset in OFFSETS if offset != (0, 0, 0)]
FILL_ORDER = sorted(range(26), key=lambda k: (abs(DIRECTIONS[k][2]), k))
INACTIVE = -1e30
EDGE = 8
INNER = 4
F32 = jnp.float32
BF16 = jnp.bfloat16


def vmem():
    return pl.BlockSpec(memory_space=pltpu.VMEM)


def smem():
    return pl.BlockSpec(memory_space=pltpu.SMEM)


def hbm():
    return pl.BlockSpec(memory_space=pltpu.HBM)


def kernel_call(body, outs, specs, out_specs, scratch=(), flops=0, mib=16):
    call = pl.pallas_call(
        body,
        out_shape=outs,
        in_specs=specs,
        out_specs=out_specs,
        scratch_shapes=list(scratch),
        compiler_params=pltpu.CompilerParams(vmem_limit_bytes=mib * 1024 * 1024),
        cost_estimate=pl.CostEstimate(flops=flops, bytes_accessed=1 << 22, transcendentals=0),
    )

    def run(*operands):
        placed = []
        for spec, operand in zip(specs, operands):
            if spec.memory_space == pltpu.HBM:
                operand = pltpu.with_memory_space_constraint(operand, pltpu.HBM)
            placed.append(operand)
        return call(*placed)

    return run


def start_all(pairs, arrived):
    copies = [
        pltpu.make_async_copy(source, target, arrived.at[i])
        for i, (source, target) in enumerate(pairs)
    ]
    for copy in copies:
        copy.start()
    return copies


def swap_halves(rows):
    return pltpu.roll(rows, 64, 1)


def low_lanes(rows):
    return lax.broadcasted_iota(jnp.int32, rows.shape, 1) < 64


def filled_voxels(heights_ref):
    columns = lax.broadcasted_iota(jnp.int32, (64, 512), 0)
    voxels = lax.broadcasted_iota(jnp.int32, (64, 512), 1)
    spread = (voxels // 8 == columns).astype(F32)
    tall = jnp.dot(heights_ref[...].astype(F32), spread, preferred_element_type=F32)
    level = lax.broadcasted_iota(jnp.int32, tall.shape, 1) % 8
    return (level.astype(F32) < tall).astype(F32)


def slot_of(slots_ref, block):
    planes = slots_ref.shape[0] // INNER
    column = block % INNER
    column = column ^ (column >> 1)
    plane = block // INNER
    return column * planes + jnp.where(column % 2 == 0, plane, planes - 1 - plane)


def block_order(devices):
    planes = devices // INNER
    order = []
    for at, column in enumerate((0, 1, 3, 2)):
        up = range(planes) if at % 2 == 0 else reversed(range(planes))
        order += [plane * INNER + column for plane in up]
    return order


def fill_slots(rows_ref, near_ref, slots_ref, slots_hbm, left):
    def leave(k):
        slot = slot_of(slots_ref, near_ref[0, k])
        rows = slice(0, 128 if DIRECTIONS[k].count(0) == 2 else 16)
        return pltpu.make_async_copy(
            slots_ref.at[slot, rows], slots_hbm.at[slot, rows], left.at[k]
        )

    for k, (dx, dy, dz) in enumerate(DIRECTIONS):
        block = near_ref[0, k]
        xh = 7 if dx == 1 else 0
        y = 15 if dy == 1 else 0
        z = 15 if dz == 1 else 0

        @pl.when(block >= 0)
        def _(k=k, dx=dx, dy=dy, dz=dz, xh=xh, y=y, z=z, block=block):
            zeros = [d == 0 for d in (dx, dy, dz)]
            if zeros == [False, True, True]:
                plane = rows_ref[xh * 256 : xh * 256 + 256, :]
                first, second = plane[:128], plane[128:]
                if dx == -1:
                    second = swap_halves(second)
                else:
                    first = swap_halves(first)
                region = jnp.where(low_lanes(first), first, second)
            elif zeros == [True, False, True]:
                region = jnp.concatenate(
                    [rows_ref[x * 256 + y * 16 : x * 256 + y * 16 + 16, :] for x in range(8)]
                )
            elif zeros == [True, True, False]:
                region = rows_ref[pl.ds(z, 128, stride=16), :]
            elif zeros == [False, False, True]:
                region = rows_ref[xh * 256 + y * 16 : xh * 256 + y * 16 + 16, :]
            elif zeros == [False, True, False]:
                region = rows_ref[pl.ds(xh * 256 + z, 16, stride=16), :]
            elif zeros == [True, False, False]:
                line = rows_ref[pl.ds(y * 16 + z, 8, stride=256), :]
                region = jnp.concatenate([line, line])
            else:
                at = xh * 256 + y * 16 + z
                region = jnp.broadcast_to(rows_ref[at : at + 1, :], (16, 128))
            slots_ref[slot_of(slots_ref, block), 0 : region.shape[0], :] = region.astype(BF16)
            leave(k).start()

    for k in range(26):

        @pl.when(near_ref[0, k] >= 0)
        def _(k=k):
            leave(k).wait()


def fill_edges(rows_ref, near_ref, slots_ref, start):
    for k, (dx, dy, dz) in enumerate(DIRECTIONS):
        if (dx, dy, dz).count(0) == 2:
            continue
        block = near_ref[0, k]
        x, y, z = (15 if d == 1 else 0 for d in (dx, dy, dz))

        @pl.when(block >= 0)
        def _(dx=dx, dy=dy, dz=dz, x=x, y=y, z=z, block=block):
            if dx == 0:
                rows = rows_ref[pl.ds(y * 16 + z, 16, stride=256), :]
            elif dz == 0:
                rows = rows_ref[x * 256 + y * 16 : x * 256 + y * 16 + 16, :]
            elif dy == 0:
                rows = rows_ref[pl.ds(x * 256 + z, 16, stride=16), :]
            else:
                at = x * 256 + y * 16 + z
                rows = jnp.broadcast_to(rows_ref[at : at + 1, :], (16, 128))
            low, high = rows[:EDGE], swap_halves(rows[EDGE:])
            rows = jnp.where(low_lanes(low), low, high)
            slots_ref[slot_of(slots_ref, block), start : start + EDGE, :] = rows.astype(BF16)


def fill_faces(rows_ref, near_ref, place, faces_ref):
    member, own = place
    for k, (dx, dy, dz) in enumerate(DIRECTIONS):
        if (dx, dy, dz).count(0) != 2:
            continue
        block = near_ref[0, k]
        distance = jnp.where(member == 0, block - own, own - block)
        end = 15 if dx + dy + dz == 1 else 0

        @pl.when((block >= 0) & (distance >= 1))
        def _(dx=dx, dy=dy, end=end, distance=distance):
            if dx:
                region = rows_ref[end * 256 : end * 256 + 256, :]
            elif dy:
                region = jnp.concatenate(
                    [rows_ref[x * 256 + end * 16 : x * 256 + end * 16 + 16, :] for x in range(16)]
                )
            else:
                region = rows_ref[pl.ds(end, 256, stride=16), :]
            faces_ref[distance - 1] = region.astype(BF16)


class Whole:
    def __init__(self, ref):
        self.ref = ref

    def at(self, x, row, height):
        return self.ref, x, row


class Margin:
    def __init__(self, planes_ref, lines_ref):
        self.planes_ref, self.lines_ref = planes_ref, lines_ref

    def at(self, x, row, height):
        if x in (0, 17):
            return self.planes_ref, x // 17, row
        return self.lines_ref, row // 272, (x - 1) * 16


def put_lines(padded, places, rows):
    count = rows.shape[0]
    level = lax.broadcasted_iota(jnp.int32, rows.shape, 0) % 16
    below = jnp.where(level == 0, 0.0, pltpu.roll(rows, 1, 0)).astype(BF16)
    above = jnp.where(level == 15, 0.0, pltpu.roll(rows, count - 1, 0)).astype(BF16)
    here = rows.astype(BF16)
    at = 0
    for x, row, height in places:
        ref, plane, first = padded.at(x, row, height)
        for j, part in enumerate((below, here, above)):
            ref[plane, first : first + height, j * 128 : j * 128 + 128] = part[at : at + height]
        at += height


def put_ends(padded, x, row, rows, dz):
    lines = rows.shape[0]
    j = 0 if dz == -1 else 2
    end = 0 if dz == -1 else 15
    lanes = slice(j * 128, j * 128 + 128)
    ref, plane, first = padded.at(x, row, 16 * lines)
    span = slice(first, first + 16 * lines)
    old = ref[plane, span, lanes].astype(F32).reshape(lines, 16, 128)
    level = lax.broadcasted_iota(jnp.int32, old.shape, 1)
    new = jnp.where(level == end, rows.reshape(lines, 1, 128), old)
    ref[plane, span, lanes] = new.reshape(16 * lines, 128).astype(BF16)


def clear_margin(padded_ref):
    empty = jnp.zeros((288, 384), BF16)
    padded_ref[0] = empty
    padded_ref[17] = empty
    line = jnp.zeros((16, 384), BF16)
    for x in range(1, 17):
        padded_ref[x, 0:16, :] = line
        padded_ref[x, 272:288, :] = line


def put_region(padded, offset, rows):
    dx, dy, dz = offset
    zeros = [d == 0 for d in offset]
    x = 17 if dx == 1 else 0
    y = 17 if dy == 1 else 0
    if zeros == [False, True, True]:
        put_lines(padded, [(x, 16, 256)], rows)
    elif zeros == [True, False, True]:
        put_lines(padded, [(at + 1, y * 16, 16) for at in range(16)], rows)
    elif zeros == [False, False, True]:
        put_lines(padded, [(x, y * 16, 16)], rows)
    elif zeros == [True, True, False]:
        for at in range(16):
            put_ends(padded, at + 1, 16, rows[at * 16 : at * 16 + 16], dz)
    elif zeros == [False, True, False]:
        put_ends(padded, x, 16, rows, dz)
    elif zeros == [True, False, False]:
        for at in range(16):
            put_ends(padded, at + 1, y * 16, rows[at : at + 1], dz)
    else:
        put_ends(padded, x, y * 16, rows[0:1], dz)


def face_source(place, block):
    away = place[1] - block
    return jnp.where(away > 0, 0, 1) == place[0], jnp.clip(jnp.abs(away) - 1, 0, 3)


def fill_margin(padded, near_ref, own_ref, other_ref, start=0, faces=None, z_faces=True):
    for k in FILL_ORDER:
        offset = DIRECTIONS[k]
        block = near_ref[0, k]
        face = offset.count(0) == 2
        if face and offset[2] and not z_faces:
            continue
        if face and faces is not None:
            place, own_faces_ref, other_faces_ref = faces
            here, slot = face_source(place, block)

            @pl.when((block >= 0) & here)
            def _(offset=offset, slot=slot):
                put_region(padded, offset, own_faces_ref[slot].astype(F32))

            @pl.when((block >= 0) & jnp.logical_not(here))
            def _(offset=offset, slot=slot):
                rows = swap_halves(other_faces_ref[slot].astype(F32))
                put_region(padded, offset, rows)

            continue

        @pl.when(block >= 0)
        def _(offset=offset, block=block, face=face):
            height = 128 if face else 16 if start == 0 else EDGE
            slot = slot_of(own_ref, block)
            own = own_ref[slot, start : start + height, :].astype(F32)
            other = other_ref[slot, 0:height, :].astype(F32)
            first = jnp.where(low_lanes(own), own, swap_halves(other))
            second = jnp.where(low_lanes(own), swap_halves(own), other)
            if face or start:
                rows = jnp.concatenate([first, second])
            elif offset[0] == 0:
                rows = jnp.concatenate([first[:8], second[:8]])
            else:
                rows = first if offset[0] == 1 else second
            put_region(padded, offset, rows)


def send_features(
    near_hbm, heights_hbm, features_hbm, slots_hbm,
    near_ref, heights_ref, features_ref, rows_ref, slots_ref, arrived, left
):
    copies = [
        pltpu.make_async_copy(near_hbm, near_ref, arrived.at[8]),
        pltpu.make_async_copy(heights_hbm, heights_ref, arrived.at[9]),
    ]
    order = (0, 1, 2, 3, 4, 5, 6, 7)
    bricks = [
        pltpu.make_async_copy(features_hbm.at[i], features_ref.at[i], arrived.at[i]) for i in order
    ]
    for copy in copies + bricks:
        copy.start()
    copies[1].wait()
    filled = filled_voxels(heights_ref).astype(BF16)
    for oz in range(2):
        for oy in range(2):
            pair = []
            for ox in range(2):
                brick = ox + 2 * oy + 4 * oz
                bricks[brick].wait()
                pair.append(features_ref[brick] * filled[brick : brick + 1])
            turned = jnp.concatenate(pair).T.astype(F32)
            for vx in range(8):
                for vy in range(8):
                    at = vx * 256 + (8 * oy + vy) * 16 + 8 * oz
                    source = (vx * 8 + vy) * 8
                    rows_ref[at : at + 8, :] = turned[source : source + 8]
    copies[0].wait()
    fill_slots(rows_ref, near_ref, slots_ref, slots_hbm, left)


def own_first_taps(shift, conv_ref, yz):
    taps = []
    for ex in range(3):
        tap = conv_ref[ex * 9 + yz].astype(F32)
        taps.append(pltpu.roll(pltpu.roll(tap, shift, 0), shift, 1))
    return taps


def forward_weights(shift, conv_ref, down_in_ref, cot_in_ref, two_ref, down_ref, cot_ref):
    empty = jnp.zeros((128, 128), BF16)
    for yz in range(9):
        taps = own_first_taps(shift, conv_ref, yz)
        whole = [empty] + [tap.astype(BF16) for tap in taps] + [empty]
        for p in range(4):
            rows = slice((p * 9 + yz) * 128, (p * 9 + yz) * 128 + 128)
            two_ref[rows, 0:128] = whole[p + 1] if p < 3 else empty
            two_ref[rows, 128:256] = whole[p]
    for tap in range(8):
        rows = down_in_ref[tap].astype(F32)
        rows = pltpu.roll(rows, shift, 0)
        down_ref[tap * 128 : tap * 128 + 128, :] = pltpu.roll(rows, 2 * shift, 1).astype(BF16)
    cot_ref[...] = pltpu.roll(cot_in_ref[...].astype(F32), 2 * shift, 1).astype(BF16)


def backward_weights(shift, conv_ref, four_ref):
    empty = jnp.zeros((128, 128), BF16)
    none = jnp.zeros((64, 128), F32)
    for yz in range(9):
        taps = own_first_taps(shift, conv_ref, yz)
        own = [none] + [taps[2 - ex][:64] for ex in range(3)] + [none]
        pairs = [jnp.concatenate([own[i + 1], own[i]]).T.astype(BF16) for i in range(4)]
        for p in range(6):
            at = (p * 9 + 8 - yz) * 128
            four_ref[at : at + 128, 0:128] = pairs[p] if p < 4 else empty
            four_ref[at : at + 128, 128:256] = pairs[p - 2] if p >= 2 else empty


def own_lanes(triple):
    below, here = triple[:, 0:128].astype(F32), triple[:, 128:256].astype(F32)
    both = jnp.where(low_lanes(below), below, swap_halves(here)).astype(BF16)
    return both, triple[:, 256:384]


def prepare(
    core_ref, conv_hbm, down_hbm, cot_hbm, heights_hbm, own_hbm, other_hbm,
    lanes_hbm, active_hbm, slope_hbm, inner_hbm, taps_hbm, down_out_hbm, cot_out_hbm,
    conv_in_ref, down_in_ref, cot_in_ref, heights_ref, own_ref, other_ref,
    two_ref, down_ref, cot_ref, own_cot_ref, padded_ref, rows_ref, mask_ref, lanes_ref, active_ref,
    slope_ref, inner_ref, arrived, left, left_inner
):
    came = start_all(
        [
            (conv_hbm, conv_in_ref),
            (down_hbm, down_in_ref),
            (cot_hbm, cot_in_ref),
            (heights_hbm, heights_ref),
            (own_hbm, own_ref),
            (other_hbm, other_ref),
        ],
        arrived,
    )
    gone = [
        pltpu.make_async_copy(source, target, left.at[i])
        for i, (source, target) in enumerate(
            [
                (two_ref.at[0:3456, 0:128], taps_hbm),
                (down_ref, down_out_hbm),
                (own_cot_ref, cot_out_hbm),
                (lanes_ref, lanes_hbm),
                (active_ref, active_hbm),
                (slope_ref, slope_hbm),
            ]
        )
    ]
    for copy in came[:3]:
        copy.wait()
    forward_weights(
        core_ref[0] * 64, conv_in_ref, down_in_ref, cot_in_ref, two_ref, down_ref, cot_ref
    )
    own_cot_ref[...] = cot_ref[:, 0:128].T
    for copy in gone[:3]:
        copy.start()
    for copy in came[3:]:
        copy.wait()
    filled = filled_voxels(heights_ref)
    upright = filled.T
    for brick in range(8):
        ox, oy, oz = brick % 2, brick // 2 % 2, brick // 4
        both = jnp.concatenate([own_ref[brick].astype(F32), other_ref[brick].astype(F32)])
        turned = (both * filled[brick : brick + 1]).T
        mask = jnp.broadcast_to(upright[:, brick : brick + 1], (512, 128))
        for vx in range(8):
            for vy in range(8):
                at = (8 * ox + vx) * 256 + (8 * oy + vy) * 16 + 8 * oz
                source = (vx * 8 + vy) * 8
                rows_ref[at : at + 8, :] = turned[source : source + 8]
                mask_ref[at : at + 8, :] = mask[source : source + 8]
    clear_margin(padded_ref)
    for x in range(16):
        put_lines(Whole(padded_ref), [(x + 1, 16, 256)], rows_ref[x * 256 : x * 256 + 256, :])
        active_ref[x * 256 : x * 256 + 256, :] = mask_ref[x * 256 : x * 256 + 256, :].astype(BF16)
    for x in range(18):
        lanes_ref[x, :, 0:128], lanes_ref[x, :, 128:256] = own_lanes(padded_ref[x])
    gone[3].start()
    gone[4].start()
    for tap in range(8):
        tx, ty, tz = tap // 4, tap // 2 % 2, tap % 2
        part = lax.dot_general(
            cot_ref[...],
            down_ref[tap * 128 : tap * 128 + 128, :],
            (((1,), (1,)), ((), ())),
            preferred_element_type=F32,
        )
        for ux in range(8):
            for uy in range(8):
                at = (2 * ux + tx) * 256 + (2 * uy + ty) * 16 + tz
                source = (ux * 8 + uy) * 8
                rows = pl.ds(at, 8, stride=2)
                slope_ref[rows, :] = part[source : source + 8] * mask_ref[rows, :]
    gone[5].start()

    def leave(group):
        rows = pl.ds(pl.multiple_of(group * 1024, 1024), 1024)
        return pltpu.make_async_copy(
            inner_ref.at[rows], inner_hbm.at[rows], left_inner.at[group]
        )


    def step(group, carry):
        lhs = []
        for pair in range(2):
            pieces = []
            for p in range(4):
                for ey in range(3):
                    pieces.append(
                        padded_ref[group * 4 + pair * 2 + p, ey * 16 : ey * 16 + 256, :]
                    )
            lhs.append(jnp.concatenate(pieces, axis=1))
        summed = jnp.dot(jnp.concatenate(lhs), two_ref[...], preferred_element_type=F32)
        for pair in range(2):
            for phase in range(2):
                at = pl.multiple_of((group * 4 + pair * 2 + phase) * 256, 256)
                part = summed[pair * 256 : pair * 256 + 256, phase * 128 : phase * 128 + 128]
                rows = pl.ds(at, 256)
                inner_ref[rows, :] = jnp.where(mask_ref[rows, :] > 0, part, INACTIVE)
        leave(group).start()
        return carry

    lax.fori_loop(0, 4, step, 0)
    for copy in gone:
        copy.wait()
    for group in range(4):
        leave(group).wait()


def tap_rows(taps_ref, taps):
    starts = [((ex * 3 + ey) * 3 + ez) * 128 for ex, ey, ez in taps]
    return jnp.concatenate([taps_ref[at : at + 128, :] for at in starts])


def margin_planes(planes_ref, taps_ref):
    sums = []
    for side, ex in ((0, 0), (1, 2)):
        lhs = jnp.concatenate(
            [planes_ref[side, ey * 16 : ey * 16 + 256, :] for ey in range(3)], axis=1
        )
        rhs = taps_ref[ex * 1152 : ex * 1152 + 1152, :]
        sums.append(jnp.dot(lhs, rhs, preferred_element_type=F32))
    return sums


def margin_lines(lines_ref, taps_ref):
    sums = []
    none = jnp.zeros((16, 384), BF16)
    for side, ey in ((0, 0), (1, 2)):
        lines = lines_ref[side]
        lhs = jnp.concatenate(
            [
                jnp.concatenate([none, lines[:240]]),
                lines,
                jnp.concatenate([lines[16:], none]),
            ],
            axis=1,
        )
        rhs = tap_rows(taps_ref, [(ex, ey, ez) for ex in range(3) for ez in range(3)])
        sums.append(jnp.dot(lhs, rhs, preferred_element_type=F32))
    return sums


def margin_ends(face, ez, taps_ref):
    line = lax.broadcasted_iota(jnp.int32, face.shape, 0) % 16
    shifted = [
        jnp.where(line == 0, 0.0, pltpu.roll(face, 1, 0)),
        face,
        jnp.where(line == 15, 0.0, pltpu.roll(face, 255, 0)),
    ]
    border = jnp.zeros((16, 128), F32)
    lhs = []
    for ex in range(3):
        for part in shifted:
            if ex == 0:
                part = jnp.concatenate([border, part[:240]])
            elif ex == 2:
                part = jnp.concatenate([part[16:], border])
            lhs.append(part.astype(BF16))
    rhs = tap_rows(taps_ref, [(ex, ey, ez) for ex in range(3) for ey in range(3)])
    return jnp.dot(jnp.concatenate(lhs, axis=1), rhs, preferred_element_type=F32)


Z_FACES = ((DIRECTIONS.index((0, 0, -1)), 0), (DIRECTIONS.index((0, 0, 1)), 2))


def joined_face(own_ref, other_ref, block):
    slot = slot_of(own_ref, block)
    own = own_ref[slot].astype(F32)
    other = other_ref[slot].astype(F32)
    return jnp.concatenate(
        [
            jnp.where(low_lanes(own), own, swap_halves(other)),
            jnp.where(low_lanes(own), swap_halves(own), other),
        ]
    )


def add_margin(planes_ref, lines_ref, near_ref, own_ref, other_ref, taps_ref, pre_ref):
    for side, added in enumerate(margin_planes(planes_ref, taps_ref)):
        at = side * 15 * 256
        pre_ref[at : at + 256, :] += added
    for side, added in enumerate(margin_lines(lines_ref, taps_ref)):
        for x in range(16):
            at = x * 256 + side * 240
            pre_ref[at : at + 16, :] += added[x * 16 : x * 16 + 16]
    for k, ez in Z_FACES:
        block = near_ref[0, k]

        @pl.when(block >= 0)
        def _(block=block, ez=ez):
            added = margin_ends(joined_face(own_ref, other_ref, block), ez, taps_ref)
            rows = pl.ds(0 if ez == 0 else 15, 256, stride=16)
            pre_ref[rows, :] = pre_ref[rows, :] + added


def put_own_margin(planes_ref, lines_ref, near_ref, own_ref, other_ref, lanes_ref):
    for side in range(2):
        plane = side * 17
        lanes_ref[plane, :, 0:128], lanes_ref[plane, :, 128:256] = own_lanes(planes_ref[side])
        both, above = own_lanes(lines_ref[side])
        rows = slice(side * 272, side * 272 + 16)
        for x in range(16):
            lanes_ref[x + 1, rows, 0:128] = both[x * 16 : x * 16 + 16]
            lanes_ref[x + 1, rows, 128:256] = above[x * 16 : x * 16 + 16]
    for k, ez in Z_FACES:
        block = near_ref[0, k]

        @pl.when(block >= 0)
        def _(block=block, ez=ez):
            face = joined_face(own_ref, other_ref, block)
            lanes = slice(ez * 64, ez * 64 + 128)
            for x in range(16):
                old = lanes_ref[x + 1, 16:272, lanes].astype(F32).reshape(16, 16, 128)
                level = lax.broadcasted_iota(jnp.int32, old.shape, 1)
                lane = lax.broadcasted_iota(jnp.int32, old.shape, 2)
                here = (level == (0 if ez == 0 else 15)) & (lane < 64)
                new = jnp.where(here, face[x * 16 : x * 16 + 16].reshape(16, 1, 128), old)
                lanes_ref[x + 1, 16:272, lanes] = new.reshape(256, 128).astype(BF16)


def forward(
    near_ref, core_ref, at_ref, own_ref, other_ref, taps_ref, inner_ref,
    slope_hbm, lanes_hbm, down_hbm, cot_hbm,
    slots_hbm, faces_ref, coarse_hbm, grad_pre_hbm,
    planes_ref, lines_ref, pre_ref, grad_ref, turned_ref, slope_ref, lanes_ref,
    down_ref, cot_ref, coarse_ref, grad_pre_ref, slots_ref, arrived, left, left_slots
):
    came = start_all(
        [
            (lanes_hbm, lanes_ref),
            (slope_hbm, slope_ref),
            (down_hbm, down_ref),
            (cot_hbm, cot_ref),
        ],
        arrived,
    )
    pre_ref[...] = inner_ref[...]
    planes_ref[...] = jnp.zeros(planes_ref.shape, BF16)
    lines_ref[...] = jnp.zeros(lines_ref.shape, BF16)
    margin = Margin(planes_ref, lines_ref)
    fill_margin(margin, near_ref, own_ref, other_ref, z_faces=False)
    add_margin(planes_ref, lines_ref, near_ref, own_ref, other_ref, taps_ref, pre_ref)
    came[0].wait()
    put_own_margin(planes_ref, lines_ref, near_ref, own_ref, other_ref, lanes_ref)
    for copy in came[1:]:
        copy.wait()

    turned_ref[:, 0:512] = jnp.zeros((128, 512), BF16)
    turned_ref[:, 4608:5120] = jnp.zeros((128, 512), BF16)
    for x in range(16):
        rows = slice(x * 256, x * 256 + 256)
        pre = pre_ref[rows, :]
        sigmoid = 0.5 + 0.5 * jnp.tanh(0.5 * pre)
        pre_ref[rows, :] = jnp.where(pre > 0.5 * INACTIVE, pre * sigmoid, 0.0)
        grad = slope_ref[rows, :] * sigmoid * (1.0 + pre * (1.0 - sigmoid))
        grad_ref[rows, :] = grad
        grad = grad.astype(BF16)
        grad_pre_ref[rows, :] = grad
        turned_ref[:, 512 + x * 256 : 768 + x * 256] = grad.T

    gone = [
        pltpu.make_async_copy(grad_pre_ref, grad_pre_hbm, left.at[0]),
        pltpu.make_async_copy(coarse_ref, coarse_hbm, left.at[1]),
    ]
    gone[0].start()
    share = slots_ref.shape[1] - EDGE
    def put_terms(at, rows):
        while rows.shape[0]:
            owner, row = at // share, at % share
            count = min(rows.shape[0], share - row)
            slots_ref[owner, row : row + count, :] = rows[:count]
            rows = rows[count:]
            at += count

    leaving = [pltpu.make_async_copy(slots_ref, slots_hbm, left_slots.at[0])]

    patches = []
    for tap in range(8):
        tx, ty, tz = tap // 4, tap // 2 % 2, tap % 2
        pieces = []
        for ux in range(8):
            for uy in range(8):
                at = (2 * ux + tx) * 256 + (2 * uy + ty) * 16 + tz
                pieces.append(pre_ref[pl.ds(at, 8, stride=2), :])
        patches.append(jnp.concatenate(pieces).astype(BF16))
    patches = jnp.concatenate(patches, axis=1)
    coarse = jnp.dot(patches, down_ref[...], preferred_element_type=F32)
    coarse_ref[...] = coarse[:, :128].astype(BF16)
    gone[1].start()
    grad_down = jnp.dot(cot_ref[...], patches, preferred_element_type=F32).astype(BF16)
    for tap in range(8):
        put_terms(tap * 128, grad_down[:, tap * 128 : tap * 128 + 128].T)
    lhs = jnp.concatenate(
        [turned_ref[:, (2 - ex) * 256 : (2 - ex) * 256 + 4608] for ex in range(3)]
    )
    for ey in range(3):
        rhs = lanes_ref[:, ey * 16 : ey * 16 + 256, :].reshape(4608, 256)
        summed = jnp.dot(lhs, rhs, preferred_element_type=F32)
        for ex in range(3):
            part = summed[ex * 128 : ex * 128 + 128].astype(BF16).T
            put_terms(1024 + (ey * 3 + ex) * 192, part[0:192])
    fill_edges(grad_ref, near_ref, slots_ref, share)
    for copy in leaving:
        copy.start()
    fill_faces(grad_ref, near_ref, (core_ref[0], at_ref[0]), faces_ref)
    for copy in gone + leaving:
        copy.wait()


def fetch(taps_hbm, inner_hbm, taps_ref, inner_ref, arrived):
    for copy in start_all([(taps_hbm, taps_ref), (inner_hbm, inner_ref)], arrived):
        copy.wait()


def total(slots_ref, out_ref):
    devices, share, _ = out_ref.shape
    summed = slots_ref[0, 0:share, :].astype(F32)
    for device in range(1, devices):
        summed = summed + slots_ref[device, 0:share, :].astype(F32)
    summed = (summed / devices).astype(BF16)
    for device in range(devices):
        out_ref[device] = summed


def backward(
    near_ref, core_ref, at_ref, own_ref, other_ref, own_faces_ref, other_faces_ref,
    grad_pre_hbm, active_hbm, conv_hbm, out_ref,
    padded_ref, grad_pre_ref, active_ref, conv_ref, back_ref, arrived
):
    came = start_all(
        [(conv_hbm, conv_ref), (grad_pre_hbm, grad_pre_ref), (active_hbm, active_ref)], arrived
    )
    came[0].wait()
    backward_weights(core_ref[0] * 64, conv_ref, back_ref)
    clear_margin(padded_ref)
    came[1].wait()
    for x in range(16):
        rows = grad_pre_ref[x * 256 : x * 256 + 256, :].astype(F32)
        put_lines(Whole(padded_ref), [(x + 1, 16, 256)], rows)
    fill_margin(
        Whole(padded_ref), near_ref, own_ref, other_ref, own_ref.shape[1] - EDGE,
        ((core_ref[0], at_ref[0]), own_faces_ref, other_faces_ref),
    )
    came[2].wait()
    for half in range(2):
        lhs = []
        for quad in range(2):
            pieces = []
            for p in range(6):
                for ey in range(3):
                    pieces.append(
                        padded_ref[half * 8 + quad * 4 + p, ey * 16 : ey * 16 + 256, :]
                    )
            lhs.append(jnp.concatenate(pieces, axis=1))
        summed = jnp.dot(jnp.concatenate(lhs), back_ref[...], preferred_element_type=F32)
        for quad in range(2):
            for two in range(2):
                part = summed[quad * 256 : quad * 256 + 256, two * 128 : two * 128 + 128]
                x = half * 8 + quad * 4 + two * 2
                even = active_ref[x * 256 : x * 256 + 256, :].astype(F32)
                odd = active_ref[x * 256 + 256 : x * 256 + 512, :].astype(F32)
                part = part * jnp.where(low_lanes(part), even, odd)
                for oy in range(2):
                    rows = [
                        part[(8 * oy + vy) * 16 + 8 * oz : (8 * oy + vy) * 16 + 8 * oz + 8]
                        for oz in range(2)
                        for vy in range(8)
                    ]
                    turned = jnp.concatenate(rows).T
                    first, second = turned[:64], turned[64:]
                    lanes = slice(x % 8 * 64, x % 8 * 64 + 128)
                    brick = half + 2 * oy
                    near = jnp.where(low_lanes(first), first, swap_halves(second))
                    far = jnp.where(low_lanes(first), swap_halves(first), second)
                    out_ref[brick, :, lanes] = near.astype(BF16)
                    out_ref[brick + 4, :, lanes] = far.astype(BF16)


def finish(core_ref, sums_ref, conv_ref, down_ref):
    shift = core_ref[0] * 64
    for tap in range(27):
        ex, ey, ez = tap // 9, tap // 3 % 3, tap % 3
        at = 1024 + ((ey * 3 + ex) * 3 + ez) * 64
        rows = sums_ref[at : at + 64, :].astype(F32)
        conv_ref[tap] = pltpu.roll(rows, shift, 1)
    for tap in range(8):
        rows = sums_ref[tap * 128 : tap * 128 + 128, :].astype(F32)
        down_ref[tap, pl.ds(shift, 64), :] = rows[:64]
        down_ref[tap, pl.ds(64 - shift, 64), :] = rows[64:]


def over_space(block, distance):
    blocks = range(lax.axis_size("space"))
    route = [(2 * i, 2 * (i + distance)) for i in blocks if i + distance in blocks]
    route += [(2 * i + 1, 2 * (i - distance) + 1) for i in blocks if i - distance in blocks]
    return lax.ppermute(block, ("space", "chan"), route)


def over_chan(block):
    return lax.ppermute(block, "chan", [(0, 1), (1, 0)])


def to_all(slots):
    order = block_order(lax.axis_size("space"))
    return lax.all_to_all(slots, "space", 0, 0, axis_index_groups=[order], tiled=True)


def local(features, heights, neighbours, w_conv, w_down, cotangent):
    devices = lax.axis_size("space")
    member = lax.axis_index("chan")

    def out(*shape, dtype=BF16):
        return jax.ShapeDtypeStruct(shape, dtype)

    def held_out(*shape, dtype=BF16):
        return pltpu.HBM(shape, dtype)

    def memory(*shape, dtype=BF16):
        return pltpu.VMEM(shape, dtype)

    def copies(count):
        return pltpu.SemaphoreType.DMA((count,))

    core = member.reshape(1)
    place = (core, lax.axis_index("space").reshape(1))
    turned = features.transpose(0, 2, 1)
    slots = kernel_call(
        send_features,
        held_out(devices, 128, 128),
        [hbm()] * 3,
        hbm(),
        [
            pltpu.SMEM(neighbours.shape, jnp.int32),
            memory(8, 64, dtype=jnp.int32),
            memory(8, 64, 512),
            memory(2048, 128, dtype=F32),
            memory(devices, 128, 128),
            copies(10),
            copies(26),
        ],
    )(neighbours, heights, turned)
    slots, turned_after = lax.optimization_barrier((slots, turned))
    came = to_all(slots)
    other_turned = over_chan(turned_after)

    held = [
        held_out(18, 288, 256),
        held_out(4096, 128),
        held_out(4096, 128, dtype=F32),
        held_out(4096, 128, dtype=F32),
        held_out(3456, 128),
        held_out(1024, 256),
        held_out(128, 512),
    ]
    lanes, active, slope, inner, taps, down, cot = kernel_call(
        prepare,
        held,
        [smem()] + [hbm()] * 5 + [pl.BlockSpec(memory_space=pl.ANY)],
        [hbm()] * 7,
        [
            memory(27, 128, 128),
            memory(8, 128, 256),
            memory(512, 256),
            memory(8, 64, dtype=jnp.int32),
            memory(8, 64, 512),
            memory(8, 64, 512),
            memory(4608, 256),
            memory(1024, 256),
            memory(512, 256),
            memory(128, 512),
            memory(18, 288, 384),
            memory(4096, 128, dtype=F32),
            memory(4096, 128, dtype=F32),
            memory(18, 288, 256),
            memory(4096, 128),
            memory(4096, 128, dtype=F32),
            memory(4096, 128, dtype=F32),
            copies(6),
            copies(6),
            copies(4),
        ],
        flops=5 << 30,
        mib=36,
    )(core, w_conv, w_down, cotangent[0], heights, turned, other_turned)
    came, taps, inner = lax.optimization_barrier((came, taps, inner))
    came_other = over_chan(came)
    taps, inner = kernel_call(
        fetch,
        [out(3456, 128), out(4096, 128, dtype=F32)],
        [hbm()] * 2,
        [vmem()] * 2,
        [copies(2)],
    )(taps, inner)

    share = -(-2752 // (devices * 16)) * 16
    terms, faces, coarse, grad_pre = kernel_call(
        forward,
        [
            held_out(devices, share + EDGE, 128),
            out(4, 256, 128),
            held_out(512, 128),
            held_out(4096, 128),
        ],
        [smem()] * 3 + [vmem()] * 4 + [hbm()] * 4,
        [hbm(), vmem(), hbm(), hbm()],
        [
            memory(2, 288, 384),
            memory(2, 256, 384),
            memory(4096, 128, dtype=F32),
            memory(4096, 128, dtype=F32),
            memory(128, 5120),
            memory(4096, 128, dtype=F32),
            memory(18, 288, 256),
            memory(1024, 256),
            memory(128, 512),
            memory(512, 128),
            memory(4096, 128),
            memory(devices, share + EDGE, 128),
            copies(4),
            copies(2),
            copies(1),
        ],
        flops=5 << 30,
        mib=24,
    )(
        neighbours, *place, came, came_other, taps, inner, slope, lanes, down, cot
    )

    arrived = to_all(terms)
    came_faces = [over_space(faces[i], i + 1) for i in range(4)]
    arrived, *came_faces = lax.optimization_barrier((arrived, *came_faces))
    came_faces = jnp.stack(came_faces)
    other_faces = over_chan(came_faces)
    sums = to_all(
        kernel_call(total, out(devices, share, 128), [vmem()], vmem())(arrived)
    )
    arrived_other = over_chan(arrived[:, share:])
    grad_features = kernel_call(
        backward,
        out(8, 64, 512),
        [smem()] * 3 + [vmem()] * 4 + [hbm()] * 3,
        vmem(),
        [
            memory(18, 288, 384),
            memory(4096, 128),
            memory(4096, 128),
            memory(27, 128, 128),
            memory(6912, 256),
            copies(3),
        ],
        flops=5 << 30,
        mib=24,
    )(
        neighbours, *place, arrived, arrived_other, came_faces, other_faces, grad_pre, active,
        w_conv,
    )

    grad_conv, grad_down = kernel_call(
        finish,
        [out(27, 64, 128, dtype=F32), out(8, 128, 128, dtype=F32)],
        [smem(), vmem()],
        [vmem()] * 2,
    )(core, sums.reshape(-1, 128))
    return coarse[None], grad_conv, grad_down, grad_features.transpose(0, 2, 1)


def solution(mesh):
    placed = (
        P("space", None, "chan"),
        P("space", None),
        P("space", None),
        P(),
        P(),
        P("space", None, None),
    )
    return jax.shard_map(
        local,
        mesh=mesh,
        in_specs=placed,
        out_specs=(
            P("space", None, "chan"),
            P(None, "chan", None),
            P(None, None, "chan"),
            P("space", None, "chan"),
        ),
        check_vma=False,
    )
```

```python
import jax
import jax.numpy as jnp
from jax import lax
from jax.experimental import pallas as pl
from jax.experimental.pallas import tpu as pltpu
from jax.sharding import PartitionSpec as P

OFFSETS = [
    (along_x, along_y, along_z)
    for along_x in (-1, 0, 1)
    for along_y in (-1, 0, 1)
    for along_z in (-1, 0, 1)
]
DIRECTIONS = [offset for offset in OFFSETS if offset != (0, 0, 0)]
FILL_ORDER = sorted(range(26), key=lambda k: (abs(DIRECTIONS[k][2]), k))
INACTIVE = -1e30
EDGE = 8
INNER = 4
F32 = jnp.float32
BF16 = jnp.bfloat16


def vmem():
    return pl.BlockSpec(memory_space=pltpu.VMEM)


def smem():
    return pl.BlockSpec(memory_space=pltpu.SMEM)


def hbm():
    return pl.BlockSpec(memory_space=pltpu.HBM)


def kernel_call(body, outs, specs, out_specs, scratch=(), flops=0, mib=16):
    call = pl.pallas_call(
        body,
        out_shape=outs,
        in_specs=specs,
        out_specs=out_specs,
        scratch_shapes=list(scratch),
        compiler_params=pltpu.CompilerParams(vmem_limit_bytes=mib * 1024 * 1024),
        cost_estimate=pl.CostEstimate(flops=flops, bytes_accessed=1 << 22, transcendentals=0),
    )

    def run(*operands):
        placed = []
        for spec, operand in zip(specs, operands):
            if spec.memory_space == pltpu.HBM:
                operand = pltpu.with_memory_space_constraint(operand, pltpu.HBM)
            placed.append(operand)
        return call(*placed)

    return run


def start_all(pairs, arrived):
    copies = [
        pltpu.make_async_copy(source, target, arrived.at[i])
        for i, (source, target) in enumerate(pairs)
    ]
    for copy in copies:
        copy.start()
    return copies


def swap_halves(rows):
    return pltpu.roll(rows, 64, 1)


def low_lanes(rows):
    return lax.broadcasted_iota(jnp.int32, rows.shape, 1) < 64


def filled_voxels(heights_ref):
    columns = lax.broadcasted_iota(jnp.int32, (64, 512), 0)
    voxels = lax.broadcasted_iota(jnp.int32, (64, 512), 1)
    spread = (voxels // 8 == columns).astype(F32)
    tall = jnp.dot(heights_ref[...].astype(F32), spread, preferred_element_type=F32)
    level = lax.broadcasted_iota(jnp.int32, tall.shape, 1) % 8
    return (level.astype(F32) < tall).astype(F32)


def slot_of(slots_ref, block):
    planes = slots_ref.shape[0] // INNER
    column = block % INNER
    column = column ^ (column >> 1)
    plane = block // INNER
    return column * planes + jnp.where(column % 2 == 0, planes - 1 - plane, plane)


def block_order(devices):
    planes = devices // INNER
    order = []
    for at, column in enumerate((0, 1, 3, 2)):
        up = range(planes) if at % 2 else reversed(range(planes))
        order += [plane * INNER + column for plane in up]
    return order


def fill_slots(rows_ref, near_ref, slots_ref, slots_hbm, left):
    def leave(k):
        slot = slot_of(slots_ref, near_ref[0, k])
        rows = slice(0, 128 if DIRECTIONS[k].count(0) == 2 else 16)
        return pltpu.make_async_copy(
            slots_ref.at[slot, rows], slots_hbm.at[slot, rows], left.at[k]
        )

    for k, (dx, dy, dz) in enumerate(DIRECTIONS):
        block = near_ref[0, k]
        xh = 7 if dx == 1 else 0
        y = 15 if dy == 1 else 0
        z = 15 if dz == 1 else 0

        @pl.when(block >= 0)
        def _(k=k, dx=dx, dy=dy, dz=dz, xh=xh, y=y, z=z, block=block):
            zeros = [d == 0 for d in (dx, dy, dz)]
            if zeros == [False, True, True]:
                plane = rows_ref[xh * 256 : xh * 256 + 256, :]
                first, second = plane[:128], plane[128:]
                if dx == -1:
                    second = swap_halves(second)
                else:
                    first = swap_halves(first)
                region = jnp.where(low_lanes(first), first, second)
            elif zeros == [True, False, True]:
                region = jnp.concatenate(
                    [rows_ref[x * 256 + y * 16 : x * 256 + y * 16 + 16, :] for x in range(8)]
                )
            elif zeros == [True, True, False]:
                region = rows_ref[pl.ds(z, 128, stride=16), :]
            elif zeros == [False, False, True]:
                region = rows_ref[xh * 256 + y * 16 : xh * 256 + y * 16 + 16, :]
            elif zeros == [False, True, False]:
                region = rows_ref[pl.ds(xh * 256 + z, 16, stride=16), :]
            elif zeros == [True, False, False]:
                line = rows_ref[pl.ds(y * 16 + z, 8, stride=256), :]
                region = jnp.concatenate([line, line])
            else:
                at = xh * 256 + y * 16 + z
                region = jnp.broadcast_to(rows_ref[at : at + 1, :], (16, 128))
            slots_ref[slot_of(slots_ref, block), 0 : region.shape[0], :] = region.astype(BF16)
            leave(k).start()

    for k in range(26):

        @pl.when(near_ref[0, k] >= 0)
        def _(k=k):
            leave(k).wait()


def fill_edges(rows_ref, near_ref, slots_ref, start):
    for k, (dx, dy, dz) in enumerate(DIRECTIONS):
        if (dx, dy, dz).count(0) == 2:
            continue
        block = near_ref[0, k]
        x, y, z = (15 if d == 1 else 0 for d in (dx, dy, dz))

        @pl.when(block >= 0)
        def _(dx=dx, dy=dy, dz=dz, x=x, y=y, z=z, block=block):
            if dx == 0:
                rows = rows_ref[pl.ds(y * 16 + z, 16, stride=256), :]
            elif dz == 0:
                rows = rows_ref[x * 256 + y * 16 : x * 256 + y * 16 + 16, :]
            elif dy == 0:
                rows = rows_ref[pl.ds(x * 256 + z, 16, stride=16), :]
            else:
                at = x * 256 + y * 16 + z
                rows = jnp.broadcast_to(rows_ref[at : at + 1, :], (16, 128))
            low, high = rows[:EDGE], swap_halves(rows[EDGE:])
            rows = jnp.where(low_lanes(low), low, high)
            slots_ref[slot_of(slots_ref, block), start : start + EDGE, :] = rows.astype(BF16)


def fill_faces(rows_ref, near_ref, place, faces_ref):
    member, own = place
    for k, (dx, dy, dz) in enumerate(DIRECTIONS):
        if (dx, dy, dz).count(0) != 2:
            continue
        block = near_ref[0, k]
        distance = jnp.where(member == 0, block - own, own - block)
        end = 15 if dx + dy + dz == 1 else 0

        @pl.when((block >= 0) & (distance >= 1))
        def _(dx=dx, dy=dy, end=end, distance=distance):
            if dx:
                region = rows_ref[end * 256 : end * 256 + 256, :]
            elif dy:
                region = jnp.concatenate(
                    [rows_ref[x * 256 + end * 16 : x * 256 + end * 16 + 16, :] for x in range(16)]
                )
            else:
                region = rows_ref[pl.ds(end, 256, stride=16), :]
            faces_ref[distance - 1] = region.astype(BF16)


class Whole:
    def __init__(self, ref):
        self.ref = ref

    def at(self, x, row, height):
        return self.ref, x, row


class Margin:
    def __init__(self, planes_ref, lines_ref):
        self.planes_ref, self.lines_ref = planes_ref, lines_ref

    def at(self, x, row, height):
        if x in (0, 17):
            return self.planes_ref, x // 17, row
        return self.lines_ref, row // 272, (x - 1) * 16


def put_lines(padded, places, rows):
    count = rows.shape[0]
    level = lax.broadcasted_iota(jnp.int32, rows.shape, 0) % 16
    below = jnp.where(level == 0, 0.0, pltpu.roll(rows, 1, 0)).astype(BF16)
    above = jnp.where(level == 15, 0.0, pltpu.roll(rows, count - 1, 0)).astype(BF16)
    here = rows.astype(BF16)
    at = 0
    for x, row, height in places:
        ref, plane, first = padded.at(x, row, height)
        for j, part in enumerate((below, here, above)):
            ref[plane, first : first + height, j * 128 : j * 128 + 128] = part[at : at + height]
        at += height


def put_ends(padded, x, row, rows, dz):
    lines = rows.shape[0]
    j = 0 if dz == -1 else 2
    end = 0 if dz == -1 else 15
    lanes = slice(j * 128, j * 128 + 128)
    ref, plane, first = padded.at(x, row, 16 * lines)
    span = slice(first, first + 16 * lines)
    old = ref[plane, span, lanes].astype(F32).reshape(lines, 16, 128)
    level = lax.broadcasted_iota(jnp.int32, old.shape, 1)
    new = jnp.where(level == end, rows.reshape(lines, 1, 128), old)
    ref[plane, span, lanes] = new.reshape(16 * lines, 128).astype(BF16)


def clear_margin(padded_ref):
    empty = jnp.zeros((288, 384), BF16)
    padded_ref[0] = empty
    padded_ref[17] = empty
    line = jnp.zeros((16, 384), BF16)
    for x in range(1, 17):
        padded_ref[x, 0:16, :] = line
        padded_ref[x, 272:288, :] = line


def put_region(padded, offset, rows):
    dx, dy, dz = offset
    zeros = [d == 0 for d in offset]
    x = 17 if dx == 1 else 0
    y = 17 if dy == 1 else 0
    if zeros == [False, True, True]:
        put_lines(padded, [(x, 16, 256)], rows)
    elif zeros == [True, False, True]:
        put_lines(padded, [(at + 1, y * 16, 16) for at in range(16)], rows)
    elif zeros == [False, False, True]:
        put_lines(padded, [(x, y * 16, 16)], rows)
    elif zeros == [True, True, False]:
        for at in range(16):
            put_ends(padded, at + 1, 16, rows[at * 16 : at * 16 + 16], dz)
    elif zeros == [False, True, False]:
        put_ends(padded, x, 16, rows, dz)
    elif zeros == [True, False, False]:
        for at in range(16):
            put_ends(padded, at + 1, y * 16, rows[at : at + 1], dz)
    else:
        put_ends(padded, x, y * 16, rows[0:1], dz)


def face_source(place, block):
    away = place[1] - block
    return jnp.where(away > 0, 0, 1) == place[0], jnp.clip(jnp.abs(away) - 1, 0, 3)


def fill_margin(padded, near_ref, own_ref, other_ref, start=0, faces=None, z_faces=True):
    for k in FILL_ORDER:
        offset = DIRECTIONS[k]
        block = near_ref[0, k]
        face = offset.count(0) == 2
        if face and offset[2] and not z_faces:
            continue
        if face and faces is not None:
            place, own_faces_ref, other_faces_ref = faces
            here, slot = face_source(place, block)

            @pl.when((block >= 0) & here)
            def _(offset=offset, slot=slot):
                put_region(padded, offset, own_faces_ref[slot].astype(F32))

            @pl.when((block >= 0) & jnp.logical_not(here))
            def _(offset=offset, slot=slot):
                rows = swap_halves(other_faces_ref[slot].astype(F32))
                put_region(padded, offset, rows)

            continue

        @pl.when(block >= 0)
        def _(offset=offset, block=block, face=face):
            height = 128 if face else 16 if start == 0 else EDGE
            slot = slot_of(own_ref, block)
            own = own_ref[slot, start : start + height, :].astype(F32)
            other = other_ref[slot, 0:height, :].astype(F32)
            first = jnp.where(low_lanes(own), own, swap_halves(other))
            second = jnp.where(low_lanes(own), swap_halves(own), other)
            if face or start:
                rows = jnp.concatenate([first, second])
            elif offset[0] == 0:
                rows = jnp.concatenate([first[:8], second[:8]])
            else:
                rows = first if offset[0] == 1 else second
            put_region(padded, offset, rows)


def send_features(
    near_hbm, heights_hbm, features_hbm, slots_hbm,
    near_ref, heights_ref, features_ref, rows_ref, slots_ref, arrived, left
):
    copies = [
        pltpu.make_async_copy(near_hbm, near_ref, arrived.at[8]),
        pltpu.make_async_copy(heights_hbm, heights_ref, arrived.at[9]),
    ]
    order = (0, 1, 2, 3, 4, 5, 6, 7)
    bricks = [
        pltpu.make_async_copy(features_hbm.at[i], features_ref.at[i], arrived.at[i]) for i in order
    ]
    for copy in copies + bricks:
        copy.start()
    copies[1].wait()
    filled = filled_voxels(heights_ref).astype(BF16)
    for oz in range(2):
        for oy in range(2):
            pair = []
            for ox in range(2):
                brick = ox + 2 * oy + 4 * oz
                bricks[brick].wait()
                pair.append(features_ref[brick] * filled[brick : brick + 1])
            turned = jnp.concatenate(pair).T.astype(F32)
            for vx in range(8):
                for vy in range(8):
                    at = vx * 256 + (8 * oy + vy) * 16 + 8 * oz
                    source = (vx * 8 + vy) * 8
                    rows_ref[at : at + 8, :] = turned[source : source + 8]
    copies[0].wait()
    fill_slots(rows_ref, near_ref, slots_ref, slots_hbm, left)


def own_first_taps(shift, conv_ref, yz):
    taps = []
    for ex in range(3):
        tap = conv_ref[ex * 9 + yz].astype(F32)
        taps.append(pltpu.roll(pltpu.roll(tap, shift, 0), shift, 1))
    return taps


def forward_weights(shift, conv_ref, down_in_ref, cot_in_ref, two_ref, down_ref, cot_ref):
    empty = jnp.zeros((128, 128), BF16)
    for yz in range(9):
        taps = own_first_taps(shift, conv_ref, yz)
        whole = [empty] + [tap.astype(BF16) for tap in taps] + [empty]
        for p in range(4):
            rows = slice((p * 9 + yz) * 128, (p * 9 + yz) * 128 + 128)
            two_ref[rows, 0:128] = whole[p + 1] if p < 3 else empty
            two_ref[rows, 128:256] = whole[p]
    for tap in range(8):
        rows = down_in_ref[tap].astype(F32)
        rows = pltpu.roll(rows, shift, 0)
        down_ref[tap * 128 : tap * 128 + 128, :] = pltpu.roll(rows, 2 * shift, 1).astype(BF16)
    cot_ref[...] = pltpu.roll(cot_in_ref[...].astype(F32), 2 * shift, 1).astype(BF16)


def backward_weights(shift, conv_ref, four_ref):
    empty = jnp.zeros((128, 128), BF16)
    none = jnp.zeros((64, 128), F32)
    for yz in range(9):
        taps = own_first_taps(shift, conv_ref, yz)
        own = [none] + [taps[2 - ex][:64] for ex in range(3)] + [none]
        pairs = [jnp.concatenate([own[i + 1], own[i]]).T.astype(BF16) for i in range(4)]
        for p in range(6):
            at = (p * 9 + 8 - yz) * 128
            four_ref[at : at + 128, 0:128] = pairs[p] if p < 4 else empty
            four_ref[at : at + 128, 128:256] = pairs[p - 2] if p >= 2 else empty


def own_lanes(triple):
    below, here = triple[:, 0:128].astype(F32), triple[:, 128:256].astype(F32)
    both = jnp.where(low_lanes(below), below, swap_halves(here)).astype(BF16)
    return both, triple[:, 256:384]


def prepare(
    core_ref, conv_hbm, down_hbm, cot_hbm, heights_hbm, own_hbm, other_hbm,
    lanes_hbm, active_hbm, slope_hbm, inner_hbm, taps_hbm, down_out_hbm, cot_out_hbm,
    conv_in_ref, down_in_ref, cot_in_ref, heights_ref, own_ref, other_ref,
    two_ref, down_ref, cot_ref, own_cot_ref, padded_ref, rows_ref, mask_ref, lanes_ref, active_ref,
    slope_ref, inner_ref, arrived, left, left_inner
):
    came = start_all(
        [
            (conv_hbm, conv_in_ref),
            (down_hbm, down_in_ref),
            (cot_hbm, cot_in_ref),
            (heights_hbm, heights_ref),
            (own_hbm, own_ref),
            (other_hbm, other_ref),
        ],
        arrived,
    )
    gone = [
        pltpu.make_async_copy(source, target, left.at[i])
        for i, (source, target) in enumerate(
            [
                (two_ref.at[0:3456, 0:128], taps_hbm),
                (down_ref, down_out_hbm),
                (own_cot_ref, cot_out_hbm),
                (lanes_ref, lanes_hbm),
                (active_ref, active_hbm),
                (slope_ref, slope_hbm),
            ]
        )
    ]
    for copy in came[:3]:
        copy.wait()
    forward_weights(
        core_ref[0] * 64, conv_in_ref, down_in_ref, cot_in_ref, two_ref, down_ref, cot_ref
    )
    own_cot_ref[...] = cot_ref[:, 0:128].T
    for copy in gone[:3]:
        copy.start()
    for copy in came[3:]:
        copy.wait()
    filled = filled_voxels(heights_ref)
    upright = filled.T
    for brick in range(8):
        ox, oy, oz = brick % 2, brick // 2 % 2, brick // 4
        both = jnp.concatenate([own_ref[brick].astype(F32), other_ref[brick].astype(F32)])
        turned = (both * filled[brick : brick + 1]).T
        mask = jnp.broadcast_to(upright[:, brick : brick + 1], (512, 128))
        for vx in range(8):
            for vy in range(8):
                at = (8 * ox + vx) * 256 + (8 * oy + vy) * 16 + 8 * oz
                source = (vx * 8 + vy) * 8
                rows_ref[at : at + 8, :] = turned[source : source + 8]
                mask_ref[at : at + 8, :] = mask[source : source + 8]
    clear_margin(padded_ref)
    for x in range(16):
        put_lines(Whole(padded_ref), [(x + 1, 16, 256)], rows_ref[x * 256 : x * 256 + 256, :])
        active_ref[x * 256 : x * 256 + 256, :] = mask_ref[x * 256 : x * 256 + 256, :].astype(BF16)
    for x in range(18):
        lanes_ref[x, :, 0:128], lanes_ref[x, :, 128:256] = own_lanes(padded_ref[x])
    gone[3].start()
    gone[4].start()
    for tap in range(8):
        tx, ty, tz = tap // 4, tap // 2 % 2, tap % 2
        part = lax.dot_general(
            cot_ref[...],
            down_ref[tap * 128 : tap * 128 + 128, :],
            (((1,), (1,)), ((), ())),
            preferred_element_type=F32,
        )
        for ux in range(8):
            for uy in range(8):
                at = (2 * ux + tx) * 256 + (2 * uy + ty) * 16 + tz
                source = (ux * 8 + uy) * 8
                rows = pl.ds(at, 8, stride=2)
                slope_ref[rows, :] = part[source : source + 8] * mask_ref[rows, :]
    gone[5].start()

    def leave(group):
        rows = pl.ds(pl.multiple_of(group * 1024, 1024), 1024)
        return pltpu.make_async_copy(
            inner_ref.at[rows], inner_hbm.at[rows], left_inner.at[group]
        )


    def step(group, carry):
        lhs = []
        for pair in range(2):
            pieces = []
            for p in range(4):
                for ey in range(3):
                    pieces.append(
                        padded_ref[group * 4 + pair * 2 + p, ey * 16 : ey * 16 + 256, :]
                    )
            lhs.append(jnp.concatenate(pieces, axis=1))
        summed = jnp.dot(jnp.concatenate(lhs), two_ref[...], preferred_element_type=F32)
        for pair in range(2):
            for phase in range(2):
                at = pl.multiple_of((group * 4 + pair * 2 + phase) * 256, 256)
                part = summed[pair * 256 : pair * 256 + 256, phase * 128 : phase * 128 + 128]
                rows = pl.ds(at, 256)
                inner_ref[rows, :] = jnp.where(mask_ref[rows, :] > 0, part, INACTIVE)
        leave(group).start()
        return carry

    lax.fori_loop(0, 4, step, 0)
    for copy in gone:
        copy.wait()
    for group in range(4):
        leave(group).wait()


def tap_rows(taps_ref, taps):
    starts = [((ex * 3 + ey) * 3 + ez) * 128 for ex, ey, ez in taps]
    return jnp.concatenate([taps_ref[at : at + 128, :] for at in starts])


def margin_planes(planes_ref, taps_ref):
    sums = []
    for side, ex in ((0, 0), (1, 2)):
        lhs = jnp.concatenate(
            [planes_ref[side, ey * 16 : ey * 16 + 256, :] for ey in range(3)], axis=1
        )
        rhs = taps_ref[ex * 1152 : ex * 1152 + 1152, :]
        sums.append(jnp.dot(lhs, rhs, preferred_element_type=F32))
    return sums


def margin_lines(lines_ref, taps_ref):
    sums = []
    none = jnp.zeros((16, 384), BF16)
    for side, ey in ((0, 0), (1, 2)):
        lines = lines_ref[side]
        lhs = jnp.concatenate(
            [
                jnp.concatenate([none, lines[:240]]),
                lines,
                jnp.concatenate([lines[16:], none]),
            ],
            axis=1,
        )
        rhs = tap_rows(taps_ref, [(ex, ey, ez) for ex in range(3) for ez in range(3)])
        sums.append(jnp.dot(lhs, rhs, preferred_element_type=F32))
    return sums


def margin_ends(face, ez, taps_ref):
    line = lax.broadcasted_iota(jnp.int32, face.shape, 0) % 16
    shifted = [
        jnp.where(line == 0, 0.0, pltpu.roll(face, 1, 0)),
        face,
        jnp.where(line == 15, 0.0, pltpu.roll(face, 255, 0)),
    ]
    border = jnp.zeros((16, 128), F32)
    lhs = []
    for ex in range(3):
        for part in shifted:
            if ex == 0:
                part = jnp.concatenate([border, part[:240]])
            elif ex == 2:
                part = jnp.concatenate([part[16:], border])
            lhs.append(part.astype(BF16))
    rhs = tap_rows(taps_ref, [(ex, ey, ez) for ex in range(3) for ey in range(3)])
    return jnp.dot(jnp.concatenate(lhs, axis=1), rhs, preferred_element_type=F32)


Z_FACES = ((DIRECTIONS.index((0, 0, -1)), 0), (DIRECTIONS.index((0, 0, 1)), 2))


def joined_face(own_ref, other_ref, block):
    slot = slot_of(own_ref, block)
    own = own_ref[slot].astype(F32)
    other = other_ref[slot].astype(F32)
    return jnp.concatenate(
        [
            jnp.where(low_lanes(own), own, swap_halves(other)),
            jnp.where(low_lanes(own), swap_halves(own), other),
        ]
    )


def add_margin(planes_ref, lines_ref, near_ref, own_ref, other_ref, taps_ref, pre_ref):
    for side, added in enumerate(margin_planes(planes_ref, taps_ref)):
        at = side * 15 * 256
        pre_ref[at : at + 256, :] += added
    for side, added in enumerate(margin_lines(lines_ref, taps_ref)):
        for x in range(16):
            at = x * 256 + side * 240
            pre_ref[at : at + 16, :] += added[x * 16 : x * 16 + 16]
    for k, ez in Z_FACES:
        block = near_ref[0, k]

        @pl.when(block >= 0)
        def _(block=block, ez=ez):
            added = margin_ends(joined_face(own_ref, other_ref, block), ez, taps_ref)
            rows = pl.ds(0 if ez == 0 else 15, 256, stride=16)
            pre_ref[rows, :] = pre_ref[rows, :] + added


def put_own_margin(planes_ref, lines_ref, near_ref, own_ref, other_ref, lanes_ref):
    for side in range(2):
        plane = side * 17
        lanes_ref[plane, :, 0:128], lanes_ref[plane, :, 128:256] = own_lanes(planes_ref[side])
        both, above = own_lanes(lines_ref[side])
        rows = slice(side * 272, side * 272 + 16)
        for x in range(16):
            lanes_ref[x + 1, rows, 0:128] = both[x * 16 : x * 16 + 16]
            lanes_ref[x + 1, rows, 128:256] = above[x * 16 : x * 16 + 16]
    for k, ez in Z_FACES:
        block = near_ref[0, k]

        @pl.when(block >= 0)
        def _(block=block, ez=ez):
            face = joined_face(own_ref, other_ref, block)
            lanes = slice(ez * 64, ez * 64 + 128)
            for x in range(16):
                old = lanes_ref[x + 1, 16:272, lanes].astype(F32).reshape(16, 16, 128)
                level = lax.broadcasted_iota(jnp.int32, old.shape, 1)
                lane = lax.broadcasted_iota(jnp.int32, old.shape, 2)
                here = (level == (0 if ez == 0 else 15)) & (lane < 64)
                new = jnp.where(here, face[x * 16 : x * 16 + 16].reshape(16, 1, 128), old)
                lanes_ref[x + 1, 16:272, lanes] = new.reshape(256, 128).astype(BF16)


def forward(
    near_ref, core_ref, at_ref, own_ref, other_ref, taps_ref, inner_ref,
    slope_hbm, lanes_hbm, down_hbm, cot_hbm,
    slots_hbm, faces_ref, coarse_hbm, grad_pre_hbm,
    planes_ref, lines_ref, pre_ref, grad_ref, turned_ref, slope_ref, lanes_ref,
    down_ref, cot_ref, coarse_ref, grad_pre_ref, slots_ref, arrived, left, left_slots
):
    came = start_all(
        [
            (lanes_hbm, lanes_ref),
            (slope_hbm, slope_ref),
            (down_hbm, down_ref),
            (cot_hbm, cot_ref),
        ],
        arrived,
    )
    pre_ref[...] = inner_ref[...]
    planes_ref[...] = jnp.zeros(planes_ref.shape, BF16)
    lines_ref[...] = jnp.zeros(lines_ref.shape, BF16)
    margin = Margin(planes_ref, lines_ref)
    fill_margin(margin, near_ref, own_ref, other_ref, z_faces=False)
    add_margin(planes_ref, lines_ref, near_ref, own_ref, other_ref, taps_ref, pre_ref)
    came[0].wait()
    put_own_margin(planes_ref, lines_ref, near_ref, own_ref, other_ref, lanes_ref)
    for copy in came[1:]:
        copy.wait()

    turned_ref[:, 0:512] = jnp.zeros((128, 512), BF16)
    turned_ref[:, 4608:5120] = jnp.zeros((128, 512), BF16)
    for x in range(16):
        rows = slice(x * 256, x * 256 + 256)
        pre = pre_ref[rows, :]
        sigmoid = 0.5 + 0.5 * jnp.tanh(0.5 * pre)
        pre_ref[rows, :] = jnp.where(pre > 0.5 * INACTIVE, pre * sigmoid, 0.0)
        grad = slope_ref[rows, :] * sigmoid * (1.0 + pre * (1.0 - sigmoid))
        grad_ref[rows, :] = grad
        grad = grad.astype(BF16)
        grad_pre_ref[rows, :] = grad
        turned_ref[:, 512 + x * 256 : 768 + x * 256] = grad.T

    gone = [
        pltpu.make_async_copy(grad_pre_ref, grad_pre_hbm, left.at[0]),
        pltpu.make_async_copy(coarse_ref, coarse_hbm, left.at[1]),
    ]
    gone[0].start()
    share = slots_ref.shape[1] - EDGE
    def put_terms(at, rows):
        while rows.shape[0]:
            owner, row = at // share, at % share
            count = min(rows.shape[0], share - row)
            slots_ref[owner, row : row + count, :] = rows[:count]
            rows = rows[count:]
            at += count

    leaving = [pltpu.make_async_copy(slots_ref, slots_hbm, left_slots.at[0])]

    patches = []
    for tap in range(8):
        tx, ty, tz = tap // 4, tap // 2 % 2, tap % 2
        pieces = []
        for ux in range(8):
            for uy in range(8):
                at = (2 * ux + tx) * 256 + (2 * uy + ty) * 16 + tz
                pieces.append(pre_ref[pl.ds(at, 8, stride=2), :])
        patches.append(jnp.concatenate(pieces).astype(BF16))
    patches = jnp.concatenate(patches, axis=1)
    coarse = jnp.dot(patches, down_ref[...], preferred_element_type=F32)
    coarse_ref[...] = coarse[:, :128].astype(BF16)
    gone[1].start()
    grad_down = jnp.dot(cot_ref[...], patches, preferred_element_type=F32).astype(BF16)
    for tap in range(8):
        put_terms(tap * 128, grad_down[:, tap * 128 : tap * 128 + 128].T)
    lhs = jnp.concatenate(
        [turned_ref[:, (2 - ex) * 256 : (2 - ex) * 256 + 4608] for ex in range(3)]
    )
    for ey in range(3):
        rhs = lanes_ref[:, ey * 16 : ey * 16 + 256, :].reshape(4608, 256)
        summed = jnp.dot(lhs, rhs, preferred_element_type=F32)
        for ex in range(3):
            part = summed[ex * 128 : ex * 128 + 128].astype(BF16).T
            put_terms(1024 + (ey * 3 + ex) * 192, part[0:192])
    fill_edges(grad_ref, near_ref, slots_ref, share)
    for copy in leaving:
        copy.start()
    fill_faces(grad_ref, near_ref, (core_ref[0], at_ref[0]), faces_ref)
    for copy in gone + leaving:
        copy.wait()


def fetch(taps_hbm, inner_hbm, taps_ref, inner_ref, arrived):
    for copy in start_all([(taps_hbm, taps_ref), (inner_hbm, inner_ref)], arrived):
        copy.wait()


def total(slots_ref, out_ref):
    devices, share, _ = out_ref.shape
    summed = slots_ref[0, 0:share, :].astype(F32)
    for device in range(1, devices):
        summed = summed + slots_ref[device, 0:share, :].astype(F32)
    summed = (summed / devices).astype(BF16)
    for device in range(devices):
        out_ref[device] = summed


def backward(
    near_ref, core_ref, at_ref, own_ref, other_ref, own_faces_ref, other_faces_ref,
    grad_pre_hbm, active_hbm, conv_hbm, out_ref,
    padded_ref, grad_pre_ref, active_ref, conv_ref, back_ref, arrived
):
    came = start_all(
        [(conv_hbm, conv_ref), (grad_pre_hbm, grad_pre_ref), (active_hbm, active_ref)], arrived
    )
    came[0].wait()
    backward_weights(core_ref[0] * 64, conv_ref, back_ref)
    clear_margin(padded_ref)
    came[1].wait()
    for x in range(16):
        rows = grad_pre_ref[x * 256 : x * 256 + 256, :].astype(F32)
        put_lines(Whole(padded_ref), [(x + 1, 16, 256)], rows)
    fill_margin(
        Whole(padded_ref), near_ref, own_ref, other_ref, own_ref.shape[1] - EDGE,
        ((core_ref[0], at_ref[0]), own_faces_ref, other_faces_ref),
    )
    came[2].wait()
    for half in range(2):
        lhs = []
        for quad in range(2):
            pieces = []
            for p in range(6):
                for ey in range(3):
                    pieces.append(
                        padded_ref[half * 8 + quad * 4 + p, ey * 16 : ey * 16 + 256, :]
                    )
            lhs.append(jnp.concatenate(pieces, axis=1))
        summed = jnp.dot(jnp.concatenate(lhs), back_ref[...], preferred_element_type=F32)
        for quad in range(2):
            for two in range(2):
                part = summed[quad * 256 : quad * 256 + 256, two * 128 : two * 128 + 128]
                x = half * 8 + quad * 4 + two * 2
                even = active_ref[x * 256 : x * 256 + 256, :].astype(F32)
                odd = active_ref[x * 256 + 256 : x * 256 + 512, :].astype(F32)
                part = part * jnp.where(low_lanes(part), even, odd)
                for oy in range(2):
                    rows = [
                        part[(8 * oy + vy) * 16 + 8 * oz : (8 * oy + vy) * 16 + 8 * oz + 8]
                        for oz in range(2)
                        for vy in range(8)
                    ]
                    turned = jnp.concatenate(rows).T
                    first, second = turned[:64], turned[64:]
                    lanes = slice(x % 8 * 64, x % 8 * 64 + 128)
                    brick = half + 2 * oy
                    near = jnp.where(low_lanes(first), first, swap_halves(second))
                    far = jnp.where(low_lanes(first), swap_halves(first), second)
                    out_ref[brick, :, lanes] = near.astype(BF16)
                    out_ref[brick + 4, :, lanes] = far.astype(BF16)


def finish(core_ref, sums_ref, conv_ref, down_ref):
    shift = core_ref[0] * 64
    for tap in range(27):
        ex, ey, ez = tap // 9, tap // 3 % 3, tap % 3
        at = 1024 + ((ey * 3 + ex) * 3 + ez) * 64
        rows = sums_ref[at : at + 64, :].astype(F32)
        conv_ref[tap] = pltpu.roll(rows, shift, 1)
    for tap in range(8):
        rows = sums_ref[tap * 128 : tap * 128 + 128, :].astype(F32)
        down_ref[tap, pl.ds(shift, 64), :] = rows[:64]
        down_ref[tap, pl.ds(64 - shift, 64), :] = rows[64:]


def over_space(block, distance):
    blocks = range(lax.axis_size("space"))
    route = [(2 * i, 2 * (i + distance)) for i in blocks if i + distance in blocks]
    route += [(2 * i + 1, 2 * (i - distance) + 1) for i in blocks if i - distance in blocks]
    return lax.ppermute(block, ("space", "chan"), route)


def over_chan(block):
    return lax.ppermute(block, "chan", [(0, 1), (1, 0)])


def to_all(slots):
    order = block_order(lax.axis_size("space"))
    return lax.all_to_all(slots, "space", 0, 0, axis_index_groups=[order], tiled=True)


def local(features, heights, neighbours, w_conv, w_down, cotangent):
    devices = lax.axis_size("space")
    member = lax.axis_index("chan")

    def out(*shape, dtype=BF16):
        return jax.ShapeDtypeStruct(shape, dtype)

    def held_out(*shape, dtype=BF16):
        return pltpu.HBM(shape, dtype)

    def memory(*shape, dtype=BF16):
        return pltpu.VMEM(shape, dtype)

    def copies(count):
        return pltpu.SemaphoreType.DMA((count,))

    core = member.reshape(1)
    place = (core, lax.axis_index("space").reshape(1))
    turned = features.transpose(0, 2, 1)
    slots = kernel_call(
        send_features,
        held_out(devices, 128, 128),
        [hbm()] * 3,
        hbm(),
        [
            pltpu.SMEM(neighbours.shape, jnp.int32),
            memory(8, 64, dtype=jnp.int32),
            memory(8, 64, 512),
            memory(2048, 128, dtype=F32),
            memory(devices, 128, 128),
            copies(10),
            copies(26),
        ],
    )(neighbours, heights, turned)
    slots, turned_after = lax.optimization_barrier((slots, turned))
    came = to_all(slots)
    other_turned = over_chan(turned_after)

    held = [
        held_out(18, 288, 256),
        held_out(4096, 128),
        held_out(4096, 128, dtype=F32),
        held_out(4096, 128, dtype=F32),
        held_out(3456, 128),
        held_out(1024, 256),
        held_out(128, 512),
    ]
    lanes, active, slope, inner, taps, down, cot = kernel_call(
        prepare,
        held,
        [smem()] + [hbm()] * 5 + [pl.BlockSpec(memory_space=pl.ANY)],
        [hbm()] * 7,
        [
            memory(27, 128, 128),
            memory(8, 128, 256),
            memory(512, 256),
            memory(8, 64, dtype=jnp.int32),
            memory(8, 64, 512),
            memory(8, 64, 512),
            memory(4608, 256),
            memory(1024, 256),
            memory(512, 256),
            memory(128, 512),
            memory(18, 288, 384),
            memory(4096, 128, dtype=F32),
            memory(4096, 128, dtype=F32),
            memory(18, 288, 256),
            memory(4096, 128),
            memory(4096, 128, dtype=F32),
            memory(4096, 128, dtype=F32),
            copies(6),
            copies(6),
            copies(4),
        ],
        flops=5 << 30,
        mib=36,
    )(core, w_conv, w_down, cotangent[0], heights, turned, other_turned)
    came, taps, inner = lax.optimization_barrier((came, taps, inner))
    came_other = over_chan(came)
    taps, inner = kernel_call(
        fetch,
        [out(3456, 128), out(4096, 128, dtype=F32)],
        [hbm()] * 2,
        [vmem()] * 2,
        [copies(2)],
    )(taps, inner)

    share = -(-2752 // (devices * 16)) * 16
    terms, faces, coarse, grad_pre = kernel_call(
        forward,
        [
            held_out(devices, share + EDGE, 128),
            out(4, 256, 128),
            held_out(512, 128),
            held_out(4096, 128),
        ],
        [smem()] * 3 + [vmem()] * 4 + [hbm()] * 4,
        [hbm(), vmem(), hbm(), hbm()],
        [
            memory(2, 288, 384),
            memory(2, 256, 384),
            memory(4096, 128, dtype=F32),
            memory(4096, 128, dtype=F32),
            memory(128, 5120),
            memory(4096, 128, dtype=F32),
            memory(18, 288, 256),
            memory(1024, 256),
            memory(128, 512),
            memory(512, 128),
            memory(4096, 128),
            memory(devices, share + EDGE, 128),
            copies(4),
            copies(2),
            copies(1),
        ],
        flops=5 << 30,
        mib=24,
    )(
        neighbours, *place, came, came_other, taps, inner, slope, lanes, down, cot
    )

    arrived = to_all(terms)
    came_faces = [over_space(faces[i], i + 1) for i in range(4)]
    arrived, *came_faces = lax.optimization_barrier((arrived, *came_faces))
    came_faces = jnp.stack(came_faces)
    other_faces = over_chan(came_faces)
    sums = to_all(
        kernel_call(total, out(devices, share, 128), [vmem()], vmem())(arrived)
    )
    arrived_other = over_chan(arrived[:, share:])
    grad_features = kernel_call(
        backward,
        out(8, 64, 512),
        [smem()] * 3 + [vmem()] * 4 + [hbm()] * 3,
        vmem(),
        [
            memory(18, 288, 384),
            memory(4096, 128),
            memory(4096, 128),
            memory(27, 128, 128),
            memory(6912, 256),
            copies(3),
        ],
        flops=5 << 30,
        mib=24,
    )(
        neighbours, *place, arrived, arrived_other, came_faces, other_faces, grad_pre, active,
        w_conv,
    )

    grad_conv, grad_down = kernel_call(
        finish,
        [out(27, 64, 128, dtype=F32), out(8, 128, 128, dtype=F32)],
        [smem(), vmem()],
        [vmem()] * 2,
    )(core, sums.reshape(-1, 128))
    return coarse[None], grad_conv, grad_down, grad_features.transpose(0, 2, 1)


def solution(mesh):
    placed = (
        P("space", None, "chan"),
        P("space", None),
        P("space", None),
        P(),
        P(),
        P("space", None, None),
    )
    return jax.shard_map(
        local,
        mesh=mesh,
        in_specs=placed,
        out_specs=(
            P("space", None, "chan"),
            P(None, "chan", None),
            P(None, None, "chan"),
            P("space", None, "chan"),
        ),
        check_vma=False,
    )
```

```python
import jax
import jax.numpy as jnp
from jax import lax
from jax.experimental import pallas as pl
from jax.experimental.pallas import tpu as pltpu
from jax.sharding import PartitionSpec as P

OFFSETS = [
    (along_x, along_y, along_z)
    for along_x in (-1, 0, 1)
    for along_y in (-1, 0, 1)
    for along_z in (-1, 0, 1)
]
DIRECTIONS = [offset for offset in OFFSETS if offset != (0, 0, 0)]
FILL_ORDER = sorted(range(26), key=lambda k: (abs(DIRECTIONS[k][2]), k))
INACTIVE = -1e30
EDGE = 8
INNER = 4
F32 = jnp.float32
BF16 = jnp.bfloat16


def vmem():
    return pl.BlockSpec(memory_space=pltpu.VMEM)


def smem():
    return pl.BlockSpec(memory_space=pltpu.SMEM)


def hbm():
    return pl.BlockSpec(memory_space=pltpu.HBM)


def kernel_call(body, outs, specs, out_specs, scratch=(), flops=0, mib=16):
    call = pl.pallas_call(
        body,
        out_shape=outs,
        in_specs=specs,
        out_specs=out_specs,
        scratch_shapes=list(scratch),
        compiler_params=pltpu.CompilerParams(vmem_limit_bytes=mib * 1024 * 1024),
        cost_estimate=pl.CostEstimate(flops=flops, bytes_accessed=1 << 22, transcendentals=0),
    )

    def run(*operands):
        placed = []
        for spec, operand in zip(specs, operands):
            if spec.memory_space == pltpu.HBM:
                operand = pltpu.with_memory_space_constraint(operand, pltpu.HBM)
            placed.append(operand)
        return call(*placed)

    return run


def start_all(pairs, arrived):
    copies = [
        pltpu.make_async_copy(source, target, arrived.at[i])
        for i, (source, target) in enumerate(pairs)
    ]
    for copy in copies:
        copy.start()
    return copies


def swap_halves(rows):
    return pltpu.roll(rows, 64, 1)


def low_lanes(rows):
    return lax.broadcasted_iota(jnp.int32, rows.shape, 1) < 64


def filled_voxels(heights_ref):
    columns = lax.broadcasted_iota(jnp.int32, (64, 512), 0)
    voxels = lax.broadcasted_iota(jnp.int32, (64, 512), 1)
    spread = (voxels // 8 == columns).astype(F32)
    tall = jnp.dot(heights_ref[...].astype(F32), spread, preferred_element_type=F32)
    level = lax.broadcasted_iota(jnp.int32, tall.shape, 1) % 8
    return (level.astype(F32) < tall).astype(F32)


def slot_of(slots_ref, block):
    planes = slots_ref.shape[0] // INNER
    column = block % INNER
    column = ((column ^ (column >> 1)) + 2) % INNER
    plane = block // INNER
    return column * planes + jnp.where(column % 2 == 0, planes - 1 - plane, plane)


def block_order(devices):
    planes = devices // INNER
    order = []
    for at, column in enumerate((3, 2, 0, 1)):
        up = range(planes) if at % 2 else reversed(range(planes))
        order += [plane * INNER + column for plane in up]
    return order


def fill_slots(rows_ref, near_ref, slots_ref, slots_hbm, left):
    def leave(k):
        slot = slot_of(slots_ref, near_ref[0, k])
        rows = slice(0, 128 if DIRECTIONS[k].count(0) == 2 else 16)
        return pltpu.make_async_copy(
            slots_ref.at[slot, rows], slots_hbm.at[slot, rows], left.at[k]
        )

    for k, (dx, dy, dz) in enumerate(DIRECTIONS):
        block = near_ref[0, k]
        xh = 7 if dx == 1 else 0
        y = 15 if dy == 1 else 0
        z = 15 if dz == 1 else 0

        @pl.when(block >= 0)
        def _(k=k, dx=dx, dy=dy, dz=dz, xh=xh, y=y, z=z, block=block):
            zeros = [d == 0 for d in (dx, dy, dz)]
            if zeros == [False, True, True]:
                plane = rows_ref[xh * 256 : xh * 256 + 256, :]
                first, second = plane[:128], plane[128:]
                if dx == -1:
                    second = swap_halves(second)
                else:
                    first = swap_halves(first)
                region = jnp.where(low_lanes(first), first, second)
            elif zeros == [True, False, True]:
                region = jnp.concatenate(
                    [rows_ref[x * 256 + y * 16 : x * 256 + y * 16 + 16, :] for x in range(8)]
                )
            elif zeros == [True, True, False]:
                region = rows_ref[pl.ds(z, 128, stride=16), :]
            elif zeros == [False, False, True]:
                region = rows_ref[xh * 256 + y * 16 : xh * 256 + y * 16 + 16, :]
            elif zeros == [False, True, False]:
                region = rows_ref[pl.ds(xh * 256 + z, 16, stride=16), :]
            elif zeros == [True, False, False]:
                line = rows_ref[pl.ds(y * 16 + z, 8, stride=256), :]
                region = jnp.concatenate([line, line])
            else:
                at = xh * 256 + y * 16 + z
                region = jnp.broadcast_to(rows_ref[at : at + 1, :], (16, 128))
            slots_ref[slot_of(slots_ref, block), 0 : region.shape[0], :] = region.astype(BF16)
            leave(k).start()

    for k in range(26):

        @pl.when(near_ref[0, k] >= 0)
        def _(k=k):
            leave(k).wait()


def fill_edges(rows_ref, near_ref, slots_ref, start):
    for k, (dx, dy, dz) in enumerate(DIRECTIONS):
        if (dx, dy, dz).count(0) == 2:
            continue
        block = near_ref[0, k]
        x, y, z = (15 if d == 1 else 0 for d in (dx, dy, dz))

        @pl.when(block >= 0)
        def _(dx=dx, dy=dy, dz=dz, x=x, y=y, z=z, block=block):
            if dx == 0:
                rows = rows_ref[pl.ds(y * 16 + z, 16, stride=256), :]
            elif dz == 0:
                rows = rows_ref[x * 256 + y * 16 : x * 256 + y * 16 + 16, :]
            elif dy == 0:
                rows = rows_ref[pl.ds(x * 256 + z, 16, stride=16), :]
            else:
                at = x * 256 + y * 16 + z
                rows = jnp.broadcast_to(rows_ref[at : at + 1, :], (16, 128))
            low, high = rows[:EDGE], swap_halves(rows[EDGE:])
            rows = jnp.where(low_lanes(low), low, high)
            slots_ref[slot_of(slots_ref, block), start : start + EDGE, :] = rows.astype(BF16)


def fill_faces(rows_ref, near_ref, place, faces_ref):
    member, own = place
    for k, (dx, dy, dz) in enumerate(DIRECTIONS):
        if (dx, dy, dz).count(0) != 2:
            continue
        block = near_ref[0, k]
        distance = jnp.where(member == 0, block - own, own - block)
        end = 15 if dx + dy + dz == 1 else 0

        @pl.when((block >= 0) & (distance >= 1))
        def _(dx=dx, dy=dy, end=end, distance=distance):
            if dx:
                region = rows_ref[end * 256 : end * 256 + 256, :]
            elif dy:
                region = jnp.concatenate(
                    [rows_ref[x * 256 + end * 16 : x * 256 + end * 16 + 16, :] for x in range(16)]
                )
            else:
                region = rows_ref[pl.ds(end, 256, stride=16), :]
            faces_ref[distance - 1] = region.astype(BF16)


class Whole:
    def __init__(self, ref):
        self.ref = ref

    def at(self, x, row, height):
        return self.ref, x, row


class Margin:
    def __init__(self, planes_ref, lines_ref):
        self.planes_ref, self.lines_ref = planes_ref, lines_ref

    def at(self, x, row, height):
        if x in (0, 17):
            return self.planes_ref, x // 17, row
        return self.lines_ref, row // 272, (x - 1) * 16


def put_lines(padded, places, rows):
    count = rows.shape[0]
    level = lax.broadcasted_iota(jnp.int32, rows.shape, 0) % 16
    below = jnp.where(level == 0, 0.0, pltpu.roll(rows, 1, 0)).astype(BF16)
    above = jnp.where(level == 15, 0.0, pltpu.roll(rows, count - 1, 0)).astype(BF16)
    here = rows.astype(BF16)
    at = 0
    for x, row, height in places:
        ref, plane, first = padded.at(x, row, height)
        for j, part in enumerate((below, here, above)):
            ref[plane, first : first + height, j * 128 : j * 128 + 128] = part[at : at + height]
        at += height


def put_ends(padded, x, row, rows, dz):
    lines = rows.shape[0]
    j = 0 if dz == -1 else 2
    end = 0 if dz == -1 else 15
    lanes = slice(j * 128, j * 128 + 128)
    ref, plane, first = padded.at(x, row, 16 * lines)
    span = slice(first, first + 16 * lines)
    old = ref[plane, span, lanes].astype(F32).reshape(lines, 16, 128)
    level = lax.broadcasted_iota(jnp.int32, old.shape, 1)
    new = jnp.where(level == end, rows.reshape(lines, 1, 128), old)
    ref[plane, span, lanes] = new.reshape(16 * lines, 128).astype(BF16)


def clear_margin(padded_ref):
    empty = jnp.zeros((288, 384), BF16)
    padded_ref[0] = empty
    padded_ref[17] = empty
    line = jnp.zeros((16, 384), BF16)
    for x in range(1, 17):
        padded_ref[x, 0:16, :] = line
        padded_ref[x, 272:288, :] = line


def put_region(padded, offset, rows):
    dx, dy, dz = offset
    zeros = [d == 0 for d in offset]
    x = 17 if dx == 1 else 0
    y = 17 if dy == 1 else 0
    if zeros == [False, True, True]:
        put_lines(padded, [(x, 16, 256)], rows)
    elif zeros == [True, False, True]:
        put_lines(padded, [(at + 1, y * 16, 16) for at in range(16)], rows)
    elif zeros == [False, False, True]:
        put_lines(padded, [(x, y * 16, 16)], rows)
    elif zeros == [True, True, False]:
        for at in range(16):
            put_ends(padded, at + 1, 16, rows[at * 16 : at * 16 + 16], dz)
    elif zeros == [False, True, False]:
        put_ends(padded, x, 16, rows, dz)
    elif zeros == [True, False, False]:
        for at in range(16):
            put_ends(padded, at + 1, y * 16, rows[at : at + 1], dz)
    else:
        put_ends(padded, x, y * 16, rows[0:1], dz)


def face_source(place, block):
    away = place[1] - block
    return jnp.where(away > 0, 0, 1) == place[0], jnp.clip(jnp.abs(away) - 1, 0, 3)


def fill_margin(padded, near_ref, own_ref, other_ref, start=0, faces=None, z_faces=True):
    for k in FILL_ORDER:
        offset = DIRECTIONS[k]
        block = near_ref[0, k]
        face = offset.count(0) == 2
        if face and offset[2] and not z_faces:
            continue
        if face and faces is not None:
            place, own_faces_ref, other_faces_ref = faces
            here, slot = face_source(place, block)

            @pl.when((block >= 0) & here)
            def _(offset=offset, slot=slot):
                put_region(padded, offset, own_faces_ref[slot].astype(F32))

            @pl.when((block >= 0) & jnp.logical_not(here))
            def _(offset=offset, slot=slot):
                rows = swap_halves(other_faces_ref[slot].astype(F32))
                put_region(padded, offset, rows)

            continue

        @pl.when(block >= 0)
        def _(offset=offset, block=block, face=face):
            height = 128 if face else 16 if start == 0 else EDGE
            slot = slot_of(own_ref, block)
            own = own_ref[slot, start : start + height, :].astype(F32)
            other = other_ref[slot, 0:height, :].astype(F32)
            first = jnp.where(low_lanes(own), own, swap_halves(other))
            second = jnp.where(low_lanes(own), swap_halves(own), other)
            if face or start:
                rows = jnp.concatenate([first, second])
            elif offset[0] == 0:
                rows = jnp.concatenate([first[:8], second[:8]])
            else:
                rows = first if offset[0] == 1 else second
            put_region(padded, offset, rows)


def send_features(
    near_hbm, heights_hbm, features_hbm, slots_hbm,
    near_ref, heights_ref, features_ref, rows_ref, slots_ref, arrived, left
):
    copies = [
        pltpu.make_async_copy(near_hbm, near_ref, arrived.at[8]),
        pltpu.make_async_copy(heights_hbm, heights_ref, arrived.at[9]),
    ]
    order = (0, 1, 2, 3, 4, 5, 6, 7)
    bricks = [
        pltpu.make_async_copy(features_hbm.at[i], features_ref.at[i], arrived.at[i]) for i in order
    ]
    for copy in copies + bricks:
        copy.start()
    copies[1].wait()
    filled = filled_voxels(heights_ref).astype(BF16)
    for oz in range(2):
        for oy in range(2):
            pair = []
            for ox in range(2):
                brick = ox + 2 * oy + 4 * oz
                bricks[brick].wait()
                pair.append(features_ref[brick] * filled[brick : brick + 1])
            turned = jnp.concatenate(pair).T.astype(F32)
            for vx in range(8):
                for vy in range(8):
                    at = vx * 256 + (8 * oy + vy) * 16 + 8 * oz
                    source = (vx * 8 + vy) * 8
                    rows_ref[at : at + 8, :] = turned[source : source + 8]
    copies[0].wait()
    fill_slots(rows_ref, near_ref, slots_ref, slots_hbm, left)


def own_first_taps(shift, conv_ref, yz):
    taps = []
    for ex in range(3):
        tap = conv_ref[ex * 9 + yz].astype(F32)
        taps.append(pltpu.roll(pltpu.roll(tap, shift, 0), shift, 1))
    return taps


def forward_weights(shift, conv_ref, down_in_ref, cot_in_ref, two_ref, down_ref, cot_ref):
    empty = jnp.zeros((128, 128), BF16)
    for yz in range(9):
        taps = own_first_taps(shift, conv_ref, yz)
        whole = [empty] + [tap.astype(BF16) for tap in taps] + [empty]
        for p in range(4):
            rows = slice((p * 9 + yz) * 128, (p * 9 + yz) * 128 + 128)
            two_ref[rows, 0:128] = whole[p + 1] if p < 3 else empty
            two_ref[rows, 128:256] = whole[p]
    for tap in range(8):
        rows = down_in_ref[tap].astype(F32)
        rows = pltpu.roll(rows, shift, 0)
        down_ref[tap * 128 : tap * 128 + 128, :] = pltpu.roll(rows, 2 * shift, 1).astype(BF16)
    cot_ref[...] = pltpu.roll(cot_in_ref[...].astype(F32), 2 * shift, 1).astype(BF16)


def backward_weights(shift, conv_ref, four_ref):
    empty = jnp.zeros((128, 128), BF16)
    none = jnp.zeros((64, 128), F32)
    for yz in range(9):
        taps = own_first_taps(shift, conv_ref, yz)
        own = [none] + [taps[2 - ex][:64] for ex in range(3)] + [none]
        pairs = [jnp.concatenate([own[i + 1], own[i]]).T.astype(BF16) for i in range(4)]
        for p in range(6):
            at = (p * 9 + 8 - yz) * 128
            four_ref[at : at + 128, 0:128] = pairs[p] if p < 4 else empty
            four_ref[at : at + 128, 128:256] = pairs[p - 2] if p >= 2 else empty


def own_lanes(triple):
    below, here = triple[:, 0:128].astype(F32), triple[:, 128:256].astype(F32)
    both = jnp.where(low_lanes(below), below, swap_halves(here)).astype(BF16)
    return both, triple[:, 256:384]


def prepare(
    core_ref, conv_hbm, down_hbm, cot_hbm, heights_hbm, own_hbm, other_hbm,
    lanes_hbm, active_hbm, slope_hbm, inner_hbm, taps_hbm, down_out_hbm, cot_out_hbm,
    conv_in_ref, down_in_ref, cot_in_ref, heights_ref, own_ref, other_ref,
    two_ref, down_ref, cot_ref, own_cot_ref, padded_ref, rows_ref, mask_ref, lanes_ref, active_ref,
    slope_ref, inner_ref, arrived, left, left_inner
):
    came = start_all(
        [
            (conv_hbm, conv_in_ref),
            (down_hbm, down_in_ref),
            (cot_hbm, cot_in_ref),
            (heights_hbm, heights_ref),
            (own_hbm, own_ref),
            (other_hbm, other_ref),
        ],
        arrived,
    )
    gone = [
        pltpu.make_async_copy(source, target, left.at[i])
        for i, (source, target) in enumerate(
            [
                (two_ref.at[0:3456, 0:128], taps_hbm),
                (down_ref, down_out_hbm),
                (own_cot_ref, cot_out_hbm),
                (lanes_ref, lanes_hbm),
                (active_ref, active_hbm),
                (slope_ref, slope_hbm),
            ]
        )
    ]
    for copy in came[:3]:
        copy.wait()
    forward_weights(
        core_ref[0] * 64, conv_in_ref, down_in_ref, cot_in_ref, two_ref, down_ref, cot_ref
    )
    own_cot_ref[...] = cot_ref[:, 0:128].T
    for copy in gone[:3]:
        copy.start()
    for copy in came[3:]:
        copy.wait()
    filled = filled_voxels(heights_ref)
    upright = filled.T
    for brick in range(8):
        ox, oy, oz = brick % 2, brick // 2 % 2, brick // 4
        both = jnp.concatenate([own_ref[brick].astype(F32), other_ref[brick].astype(F32)])
        turned = (both * filled[brick : brick + 1]).T
        mask = jnp.broadcast_to(upright[:, brick : brick + 1], (512, 128))
        for vx in range(8):
            for vy in range(8):
                at = (8 * ox + vx) * 256 + (8 * oy + vy) * 16 + 8 * oz
                source = (vx * 8 + vy) * 8
                rows_ref[at : at + 8, :] = turned[source : source + 8]
                mask_ref[at : at + 8, :] = mask[source : source + 8]
    clear_margin(padded_ref)
    for x in range(16):
        put_lines(Whole(padded_ref), [(x + 1, 16, 256)], rows_ref[x * 256 : x * 256 + 256, :])
        active_ref[x * 256 : x * 256 + 256, :] = mask_ref[x * 256 : x * 256 + 256, :].astype(BF16)
    for x in range(18):
        lanes_ref[x, :, 0:128], lanes_ref[x, :, 128:256] = own_lanes(padded_ref[x])
    gone[3].start()
    gone[4].start()
    for tap in range(8):
        tx, ty, tz = tap // 4, tap // 2 % 2, tap % 2
        part = lax.dot_general(
            cot_ref[...],
            down_ref[tap * 128 : tap * 128 + 128, :],
            (((1,), (1,)), ((), ())),
            preferred_element_type=F32,
        )
        for ux in range(8):
            for uy in range(8):
                at = (2 * ux + tx) * 256 + (2 * uy + ty) * 16 + tz
                source = (ux * 8 + uy) * 8
                rows = pl.ds(at, 8, stride=2)
                slope_ref[rows, :] = part[source : source + 8] * mask_ref[rows, :]
    gone[5].start()

    def leave(group):
        rows = pl.ds(pl.multiple_of(group * 1024, 1024), 1024)
        return pltpu.make_async_copy(
            inner_ref.at[rows], inner_hbm.at[rows], left_inner.at[group]
        )


    def step(group, carry):
        lhs = []
        for pair in range(2):
            pieces = []
            for p in range(4):
                for ey in range(3):
                    pieces.append(
                        padded_ref[group * 4 + pair * 2 + p, ey * 16 : ey * 16 + 256, :]
                    )
            lhs.append(jnp.concatenate(pieces, axis=1))
        summed = jnp.dot(jnp.concatenate(lhs), two_ref[...], preferred_element_type=F32)
        for pair in range(2):
            for phase in range(2):
                at = pl.multiple_of((group * 4 + pair * 2 + phase) * 256, 256)
                part = summed[pair * 256 : pair * 256 + 256, phase * 128 : phase * 128 + 128]
                rows = pl.ds(at, 256)
                inner_ref[rows, :] = jnp.where(mask_ref[rows, :] > 0, part, INACTIVE)
        leave(group).start()
        return carry

    lax.fori_loop(0, 4, step, 0)
    for copy in gone:
        copy.wait()
    for group in range(4):
        leave(group).wait()


def tap_rows(taps_ref, taps):
    starts = [((ex * 3 + ey) * 3 + ez) * 128 for ex, ey, ez in taps]
    return jnp.concatenate([taps_ref[at : at + 128, :] for at in starts])


def margin_planes(planes_ref, taps_ref):
    sums = []
    for side, ex in ((0, 0), (1, 2)):
        lhs = jnp.concatenate(
            [planes_ref[side, ey * 16 : ey * 16 + 256, :] for ey in range(3)], axis=1
        )
        rhs = taps_ref[ex * 1152 : ex * 1152 + 1152, :]
        sums.append(jnp.dot(lhs, rhs, preferred_element_type=F32))
    return sums


def margin_lines(lines_ref, taps_ref):
    sums = []
    none = jnp.zeros((16, 384), BF16)
    for side, ey in ((0, 0), (1, 2)):
        lines = lines_ref[side]
        lhs = jnp.concatenate(
            [
                jnp.concatenate([none, lines[:240]]),
                lines,
                jnp.concatenate([lines[16:], none]),
            ],
            axis=1,
        )
        rhs = tap_rows(taps_ref, [(ex, ey, ez) for ex in range(3) for ez in range(3)])
        sums.append(jnp.dot(lhs, rhs, preferred_element_type=F32))
    return sums


def margin_ends(face, ez, taps_ref):
    line = lax.broadcasted_iota(jnp.int32, face.shape, 0) % 16
    shifted = [
        jnp.where(line == 0, 0.0, pltpu.roll(face, 1, 0)),
        face,
        jnp.where(line == 15, 0.0, pltpu.roll(face, 255, 0)),
    ]
    border = jnp.zeros((16, 128), F32)
    lhs = []
    for ex in range(3):
        for part in shifted:
            if ex == 0:
                part = jnp.concatenate([border, part[:240]])
            elif ex == 2:
                part = jnp.concatenate([part[16:], border])
            lhs.append(part.astype(BF16))
    rhs = tap_rows(taps_ref, [(ex, ey, ez) for ex in range(3) for ey in range(3)])
    return jnp.dot(jnp.concatenate(lhs, axis=1), rhs, preferred_element_type=F32)


Z_FACES = ((DIRECTIONS.index((0, 0, -1)), 0), (DIRECTIONS.index((0, 0, 1)), 2))


def joined_face(own_ref, other_ref, block):
    slot = slot_of(own_ref, block)
    own = own_ref[slot].astype(F32)
    other = other_ref[slot].astype(F32)
    return jnp.concatenate(
        [
            jnp.where(low_lanes(own), own, swap_halves(other)),
            jnp.where(low_lanes(own), swap_halves(own), other),
        ]
    )


def add_margin(planes_ref, lines_ref, near_ref, own_ref, other_ref, taps_ref, pre_ref):
    for side, added in enumerate(margin_planes(planes_ref, taps_ref)):
        at = side * 15 * 256
        pre_ref[at : at + 256, :] += added
    for side, added in enumerate(margin_lines(lines_ref, taps_ref)):
        for x in range(16):
            at = x * 256 + side * 240
            pre_ref[at : at + 16, :] += added[x * 16 : x * 16 + 16]
    for k, ez in Z_FACES:
        block = near_ref[0, k]

        @pl.when(block >= 0)
        def _(block=block, ez=ez):
            added = margin_ends(joined_face(own_ref, other_ref, block), ez, taps_ref)
            rows = pl.ds(0 if ez == 0 else 15, 256, stride=16)
            pre_ref[rows, :] = pre_ref[rows, :] + added


def put_own_margin(planes_ref, lines_ref, near_ref, own_ref, other_ref, lanes_ref):
    for side in range(2):
        plane = side * 17
        lanes_ref[plane, :, 0:128], lanes_ref[plane, :, 128:256] = own_lanes(planes_ref[side])
        both, above = own_lanes(lines_ref[side])
        rows = slice(side * 272, side * 272 + 16)
        for x in range(16):
            lanes_ref[x + 1, rows, 0:128] = both[x * 16 : x * 16 + 16]
            lanes_ref[x + 1, rows, 128:256] = above[x * 16 : x * 16 + 16]
    for k, ez in Z_FACES:
        block = near_ref[0, k]

        @pl.when(block >= 0)
        def _(block=block, ez=ez):
            face = joined_face(own_ref, other_ref, block)
            lanes = slice(ez * 64, ez * 64 + 128)
            for x in range(16):
                old = lanes_ref[x + 1, 16:272, lanes].astype(F32).reshape(16, 16, 128)
                level = lax.broadcasted_iota(jnp.int32, old.shape, 1)
                lane = lax.broadcasted_iota(jnp.int32, old.shape, 2)
                here = (level == (0 if ez == 0 else 15)) & (lane < 64)
                new = jnp.where(here, face[x * 16 : x * 16 + 16].reshape(16, 1, 128), old)
                lanes_ref[x + 1, 16:272, lanes] = new.reshape(256, 128).astype(BF16)


def forward(
    near_ref, core_ref, at_ref, own_ref, other_ref, taps_ref, inner_ref,
    slope_hbm, lanes_hbm, down_hbm, cot_hbm,
    slots_hbm, faces_ref, coarse_hbm, grad_pre_hbm,
    planes_ref, lines_ref, pre_ref, grad_ref, turned_ref, slope_ref, lanes_ref,
    down_ref, cot_ref, coarse_ref, grad_pre_ref, slots_ref, arrived, left, left_slots
):
    came = start_all(
        [
            (lanes_hbm, lanes_ref),
            (slope_hbm, slope_ref),
            (down_hbm, down_ref),
            (cot_hbm, cot_ref),
        ],
        arrived,
    )
    pre_ref[...] = inner_ref[...]
    planes_ref[...] = jnp.zeros(planes_ref.shape, BF16)
    lines_ref[...] = jnp.zeros(lines_ref.shape, BF16)
    margin = Margin(planes_ref, lines_ref)
    fill_margin(margin, near_ref, own_ref, other_ref, z_faces=False)
    add_margin(planes_ref, lines_ref, near_ref, own_ref, other_ref, taps_ref, pre_ref)
    came[0].wait()
    put_own_margin(planes_ref, lines_ref, near_ref, own_ref, other_ref, lanes_ref)
    for copy in came[1:]:
        copy.wait()

    turned_ref[:, 0:512] = jnp.zeros((128, 512), BF16)
    turned_ref[:, 4608:5120] = jnp.zeros((128, 512), BF16)
    for x in range(16):
        rows = slice(x * 256, x * 256 + 256)
        pre = pre_ref[rows, :]
        sigmoid = 0.5 + 0.5 * jnp.tanh(0.5 * pre)
        pre_ref[rows, :] = jnp.where(pre > 0.5 * INACTIVE, pre * sigmoid, 0.0)
        grad = slope_ref[rows, :] * sigmoid * (1.0 + pre * (1.0 - sigmoid))
        grad_ref[rows, :] = grad
        grad = grad.astype(BF16)
        grad_pre_ref[rows, :] = grad
        turned_ref[:, 512 + x * 256 : 768 + x * 256] = grad.T

    gone = [
        pltpu.make_async_copy(grad_pre_ref, grad_pre_hbm, left.at[0]),
        pltpu.make_async_copy(coarse_ref, coarse_hbm, left.at[1]),
    ]
    gone[0].start()
    share = slots_ref.shape[1] - EDGE
    def put_terms(at, rows):
        while rows.shape[0]:
            owner, row = at // share, at % share
            count = min(rows.shape[0], share - row)
            slots_ref[owner, row : row + count, :] = rows[:count]
            rows = rows[count:]
            at += count

    leaving = [pltpu.make_async_copy(slots_ref, slots_hbm, left_slots.at[0])]

    patches = []
    for tap in range(8):
        tx, ty, tz = tap // 4, tap // 2 % 2, tap % 2
        pieces = []
        for ux in range(8):
            for uy in range(8):
                at = (2 * ux + tx) * 256 + (2 * uy + ty) * 16 + tz
                pieces.append(pre_ref[pl.ds(at, 8, stride=2), :])
        patches.append(jnp.concatenate(pieces).astype(BF16))
    patches = jnp.concatenate(patches, axis=1)
    coarse = jnp.dot(patches, down_ref[...], preferred_element_type=F32)
    coarse_ref[...] = coarse[:, :128].astype(BF16)
    gone[1].start()
    grad_down = jnp.dot(cot_ref[...], patches, preferred_element_type=F32).astype(BF16)
    for tap in range(8):
        put_terms(tap * 128, grad_down[:, tap * 128 : tap * 128 + 128].T)
    lhs = jnp.concatenate(
        [turned_ref[:, (2 - ex) * 256 : (2 - ex) * 256 + 4608] for ex in range(3)]
    )
    for ey in range(3):
        rhs = lanes_ref[:, ey * 16 : ey * 16 + 256, :].reshape(4608, 256)
        summed = jnp.dot(lhs, rhs, preferred_element_type=F32)
        for ex in range(3):
            part = summed[ex * 128 : ex * 128 + 128].astype(BF16).T
            put_terms(1024 + (ey * 3 + ex) * 192, part[0:192])
    fill_edges(grad_ref, near_ref, slots_ref, share)
    for copy in leaving:
        copy.start()
    fill_faces(grad_ref, near_ref, (core_ref[0], at_ref[0]), faces_ref)
    for copy in gone + leaving:
        copy.wait()


def fetch(taps_hbm, inner_hbm, taps_ref, inner_ref, arrived):
    for copy in start_all([(taps_hbm, taps_ref), (inner_hbm, inner_ref)], arrived):
        copy.wait()


def total(slots_ref, out_ref):
    devices, share, _ = out_ref.shape
    summed = slots_ref[0, 0:share, :].astype(F32)
    for device in range(1, devices):
        summed = summed + slots_ref[device, 0:share, :].astype(F32)
    summed = (summed / devices).astype(BF16)
    for device in range(devices):
        out_ref[device] = summed


def backward(
    near_ref, core_ref, at_ref, own_ref, other_ref, own_faces_ref, other_faces_ref,
    grad_pre_hbm, active_hbm, conv_hbm, out_ref,
    padded_ref, grad_pre_ref, active_ref, conv_ref, back_ref, arrived
):
    came = start_all(
        [(conv_hbm, conv_ref), (grad_pre_hbm, grad_pre_ref), (active_hbm, active_ref)], arrived
    )
    came[0].wait()
    backward_weights(core_ref[0] * 64, conv_ref, back_ref)
    clear_margin(padded_ref)
    came[1].wait()
    for x in range(16):
        rows = grad_pre_ref[x * 256 : x * 256 + 256, :].astype(F32)
        put_lines(Whole(padded_ref), [(x + 1, 16, 256)], rows)
    fill_margin(
        Whole(padded_ref), near_ref, own_ref, other_ref, own_ref.shape[1] - EDGE,
        ((core_ref[0], at_ref[0]), own_faces_ref, other_faces_ref),
    )
    came[2].wait()
    for half in range(2):
        lhs = []
        for quad in range(2):
            pieces = []
            for p in range(6):
                for ey in range(3):
                    pieces.append(
                        padded_ref[half * 8 + quad * 4 + p, ey * 16 : ey * 16 + 256, :]
                    )
            lhs.append(jnp.concatenate(pieces, axis=1))
        summed = jnp.dot(jnp.concatenate(lhs), back_ref[...], preferred_element_type=F32)
        for quad in range(2):
            for two in range(2):
                part = summed[quad * 256 : quad * 256 + 256, two * 128 : two * 128 + 128]
                x = half * 8 + quad * 4 + two * 2
                even = active_ref[x * 256 : x * 256 + 256, :].astype(F32)
                odd = active_ref[x * 256 + 256 : x * 256 + 512, :].astype(F32)
                part = part * jnp.where(low_lanes(part), even, odd)
                for oy in range(2):
                    rows = [
                        part[(8 * oy + vy) * 16 + 8 * oz : (8 * oy + vy) * 16 + 8 * oz + 8]
                        for oz in range(2)
                        for vy in range(8)
                    ]
                    turned = jnp.concatenate(rows).T
                    first, second = turned[:64], turned[64:]
                    lanes = slice(x % 8 * 64, x % 8 * 64 + 128)
                    brick = half + 2 * oy
                    near = jnp.where(low_lanes(first), first, swap_halves(second))
                    far = jnp.where(low_lanes(first), swap_halves(first), second)
                    out_ref[brick, :, lanes] = near.astype(BF16)
                    out_ref[brick + 4, :, lanes] = far.astype(BF16)


def finish(core_ref, sums_ref, conv_ref, down_ref):
    shift = core_ref[0] * 64
    for tap in range(27):
        ex, ey, ez = tap // 9, tap // 3 % 3, tap % 3
        at = 1024 + ((ey * 3 + ex) * 3 + ez) * 64
        rows = sums_ref[at : at + 64, :].astype(F32)
        conv_ref[tap] = pltpu.roll(rows, shift, 1)
    for tap in range(8):
        rows = sums_ref[tap * 128 : tap * 128 + 128, :].astype(F32)
        down_ref[tap, pl.ds(shift, 64), :] = rows[:64]
        down_ref[tap, pl.ds(64 - shift, 64), :] = rows[64:]


def over_space(block, distance):
    blocks = range(lax.axis_size("space"))
    route = [(2 * i, 2 * (i + distance)) for i in blocks if i + distance in blocks]
    route += [(2 * i + 1, 2 * (i - distance) + 1) for i in blocks if i - distance in blocks]
    return lax.ppermute(block, ("space", "chan"), route)


def over_chan(block):
    return lax.ppermute(block, "chan", [(0, 1), (1, 0)])


def to_all(slots):
    order = block_order(lax.axis_size("space"))
    return lax.all_to_all(slots, "space", 0, 0, axis_index_groups=[order], tiled=True)


def local(features, heights, neighbours, w_conv, w_down, cotangent):
    devices = lax.axis_size("space")
    member = lax.axis_index("chan")

    def out(*shape, dtype=BF16):
        return jax.ShapeDtypeStruct(shape, dtype)

    def held_out(*shape, dtype=BF16):
        return pltpu.HBM(shape, dtype)

    def memory(*shape, dtype=BF16):
        return pltpu.VMEM(shape, dtype)

    def copies(count):
        return pltpu.SemaphoreType.DMA((count,))

    core = member.reshape(1)
    place = (core, lax.axis_index("space").reshape(1))
    turned = features.transpose(0, 2, 1)
    slots = kernel_call(
        send_features,
        held_out(devices, 128, 128),
        [hbm()] * 3,
        hbm(),
        [
            pltpu.SMEM(neighbours.shape, jnp.int32),
            memory(8, 64, dtype=jnp.int32),
            memory(8, 64, 512),
            memory(2048, 128, dtype=F32),
            memory(devices, 128, 128),
            copies(10),
            copies(26),
        ],
    )(neighbours, heights, turned)
    slots, turned_after = lax.optimization_barrier((slots, turned))
    came = to_all(slots)
    other_turned = over_chan(turned_after)

    held = [
        held_out(18, 288, 256),
        held_out(4096, 128),
        held_out(4096, 128, dtype=F32),
        held_out(4096, 128, dtype=F32),
        held_out(3456, 128),
        held_out(1024, 256),
        held_out(128, 512),
    ]
    lanes, active, slope, inner, taps, down, cot = kernel_call(
        prepare,
        held,
        [smem()] + [hbm()] * 5 + [pl.BlockSpec(memory_space=pl.ANY)],
        [hbm()] * 7,
        [
            memory(27, 128, 128),
            memory(8, 128, 256),
            memory(512, 256),
            memory(8, 64, dtype=jnp.int32),
            memory(8, 64, 512),
            memory(8, 64, 512),
            memory(4608, 256),
            memory(1024, 256),
            memory(512, 256),
            memory(128, 512),
            memory(18, 288, 384),
            memory(4096, 128, dtype=F32),
            memory(4096, 128, dtype=F32),
            memory(18, 288, 256),
            memory(4096, 128),
            memory(4096, 128, dtype=F32),
            memory(4096, 128, dtype=F32),
            copies(6),
            copies(6),
            copies(4),
        ],
        flops=5 << 30,
        mib=36,
    )(core, w_conv, w_down, cotangent[0], heights, turned, other_turned)
    came, taps, inner = lax.optimization_barrier((came, taps, inner))
    came_other = over_chan(came)
    taps, inner = kernel_call(
        fetch,
        [out(3456, 128), out(4096, 128, dtype=F32)],
        [hbm()] * 2,
        [vmem()] * 2,
        [copies(2)],
    )(taps, inner)

    share = -(-2752 // (devices * 16)) * 16
    terms, faces, coarse, grad_pre = kernel_call(
        forward,
        [
            held_out(devices, share + EDGE, 128),
            out(4, 256, 128),
            held_out(512, 128),
            held_out(4096, 128),
        ],
        [smem()] * 3 + [vmem()] * 4 + [hbm()] * 4,
        [hbm(), vmem(), hbm(), hbm()],
        [
            memory(2, 288, 384),
            memory(2, 256, 384),
            memory(4096, 128, dtype=F32),
            memory(4096, 128, dtype=F32),
            memory(128, 5120),
            memory(4096, 128, dtype=F32),
            memory(18, 288, 256),
            memory(1024, 256),
            memory(128, 512),
            memory(512, 128),
            memory(4096, 128),
            memory(devices, share + EDGE, 128),
            copies(4),
            copies(2),
            copies(1),
        ],
        flops=5 << 30,
        mib=24,
    )(
        neighbours, *place, came, came_other, taps, inner, slope, lanes, down, cot
    )

    arrived = to_all(terms)
    came_faces = [over_space(faces[i], i + 1) for i in range(4)]
    arrived, *came_faces = lax.optimization_barrier((arrived, *came_faces))
    came_faces = jnp.stack(came_faces)
    other_faces = over_chan(came_faces)
    sums = to_all(
        kernel_call(total, out(devices, share, 128), [vmem()], vmem())(arrived)
    )
    arrived_other = over_chan(arrived[:, share:])
    grad_features = kernel_call(
        backward,
        out(8, 64, 512),
        [smem()] * 3 + [vmem()] * 4 + [hbm()] * 3,
        vmem(),
        [
            memory(18, 288, 384),
            memory(4096, 128),
            memory(4096, 128),
            memory(27, 128, 128),
            memory(6912, 256),
            copies(3),
        ],
        flops=5 << 30,
        mib=24,
    )(
        neighbours, *place, arrived, arrived_other, came_faces, other_faces, grad_pre, active,
        w_conv,
    )

    grad_conv, grad_down = kernel_call(
        finish,
        [out(27, 64, 128, dtype=F32), out(8, 128, 128, dtype=F32)],
        [smem(), vmem()],
        [vmem()] * 2,
    )(core, sums.reshape(-1, 128))
    return coarse[None], grad_conv, grad_down, grad_features.transpose(0, 2, 1)


def solution(mesh):
    placed = (
        P("space", None, "chan"),
        P("space", None),
        P("space", None),
        P(),
        P(),
        P("space", None, None),
    )
    return jax.shard_map(
        local,
        mesh=mesh,
        in_specs=placed,
        out_specs=(
            P("space", None, "chan"),
            P(None, "chan", None),
            P(None, None, "chan"),
            P("space", None, "chan"),
        ),
        check_vma=False,
    )
```
